32 devices in a mesh: dp: 16 (over z, y, x), mp: 2 (over core).
Axes of the slice: x: 2, y: 2, z: 4, core: 2. Of those that a mesh axis runs over, the one named last changes fastest.
Arguments:
- tokens: bfloat16 [15760, 768], P('dp'), may hold values from -6 to 6
- ln1_gain: bfloat16 [768], P('dp'), may hold values from 0.5 to 1.5
- w_qkv: bfloat16 [768, 3, 768], P('dp', None, 'mp'), may hold values from -0.21875 to 0.21875
- w_out: bfloat16 [768, 768], P('mp', 'dp'), may hold values from -0.625 to 0.625
- out_bias: bfloat16 [768], P('dp'), may hold values from -3 to 3
- ln2_gain: bfloat16 [768], P('dp'), may hold values from 0.5 to 1.5
- router: bfloat16 [768, 16], P('dp'), may hold values from -0.15625 to 0.15625
- w_in: bfloat16 [16, 768, 3072], P('dp', None, 'mp'), may hold values from -0.21875 to 0.21875
- in_bias: bfloat16 [16, 3072], P('dp', 'mp'), may hold values from -3 to 3
- w_back: bfloat16 [16, 3072, 768], P('dp', 'mp'), may hold values from -0.875 to 0.875
- back_bias: bfloat16 [16, 768], P('dp'), may hold values from -4 to 4
- routes: int32 [15760, 2], P('dp'), may hold values from 0 to 15, all different within a row; in each aligned block of 985 rows (0 to 984, 985 to 1969, ...) at most 306 rows name the same one
- priority: int32 [16, 985], P('dp'), may hold values from 0 to 984, each once within a row
- cotangent: bfloat16 [15760, 768], P('dp'), may hold values from -6 to 6
Outputs:
- output: bfloat16 [15760, 768], P('dp')
- token_gradient: bfloat16 [15760, 768], P('dp')
- grad_ln1_gain: float32 [768], P('dp')
- grad_w_qkv: float32 [768, 3, 768], P('dp', None, 'mp')
- grad_w_out: float32 [768, 768], P('mp', 'dp')
- grad_out_bias: float32 [768], P('dp')
- grad_ln2_gain: float32 [768], P('dp')
- grad_router: float32 [768, 16], P('dp')
- grad_w_in: float32 [16, 768, 3072], P('dp', None, 'mp')
- grad_in_bias: float32 [16, 3072], P('dp', 'mp')
- grad_w_back: float32 [16, 3072, 768], P('dp', 'mp')
- grad_back_bias: float32 [16, 768], P('dp')
The draws below stay inside these ranges and needn't reach their ends.
Inputs may be any that keep to these rules, and one draw needn't show every extreme that they name: `routes`: in the rows of one index of dp no expert is named by more than 306 rows; a row never names one expert twice. `priority`: each row orders the 985 tokens of its group, each rank once.
All inputs are finite; a program needn't handle non-finite values.
Results may differ from the reference program's by a relative error of at most 0.017.
Values may be sent and summed in bfloat16 or wider, within the bound.
A program may use at most 192 MiB of HBM per device.

```python
import math
import jax
import jax.numpy as jnp
import numpy as np
from jax import lax

D = 768
HEADS = 12
HD = 64
FF = 3072
SEQ = 197
IMG_DEV = 5
TOK_DEV = 985
EXPERTS = 16
GROUPS = 16
CAP = 153
TOKENS = 15760
N_DP = 16


def block_scale(stream_key, extent, cuts, smallest, high):
    factor_of, own = 1.0, jax.random.fold_in(stream_key, 6)
    for dim, parts in cuts:
        heights = jnp.exp(jax.random.uniform(jax.random.fold_in(own, dim), (parts,), jnp.float32, smallest / len(cuts), high / len(cuts)))
        factor_of = factor_of * jnp.repeat(heights, extent[dim] // parts).reshape([-1 if axis == dim else 1 for axis in range(len(extent))])
    return factor_of


def routed_block(own_key, own, number, rows, count, top, most, slope):
    sequence = jax.random.permutation(own_key, count)
    heavy_load, ordinary = portions_of(count, rows * top, most, slope, True), portions_of(count, rows * top, most, slope, False)
    places = jnp.arange(count)

    def named(sizes, rotation):
        used = int((sizes > 0).sum())
        fixed = max(1, used // 4)
        moved = fixed + (places - fixed + rotation * (used - fixed)) % max(1, count - fixed)
        return jnp.zeros((count,), jnp.int32).at[sequence[jnp.where(places < fixed, places, moved)]].set(jnp.asarray(sizes, jnp.int32))

    sizes = jnp.where(number % 4 == 0, named(heavy_load, number // 4), named(ordinary, number - number // 4 - 1))
    mixed = jax.random.permutation(jax.random.fold_in(own, 3), count)
    giver, receiver = mixed[0:count // 2 * 2:2], mixed[1:count // 2 * 2:2]
    slack = jnp.minimum(sizes[giver] - 1, most - sizes[receiver]) // 2
    slack = jnp.where((giver == sequence[0]) | (receiver == sequence[0]) | (sizes[receiver] == 0), 0, jnp.maximum(slack, 0))
    moved = jax.random.randint(jax.random.fold_in(own, 4), (count // 2,), 0, 1 << 20) % (slack + 1)
    sizes = sizes.at[giver].add(-moved).at[receiver].add(moved)
    items = jnp.searchsorted(jnp.cumsum(sizes), jnp.arange(rows * top), side="right").astype(jnp.int32)
    table = items.reshape(top, rows).T
    table = table[jax.random.permutation(jax.random.fold_in(own, 1), rows)]
    rotation = jax.random.randint(jax.random.fold_in(own, 2), (rows, 1), 0, top)
    return jnp.take_along_axis(table, (jnp.arange(top)[None, :] + rotation) % top, axis=1)


def portions_of(number_of, total, limit, slope, full):
    weights = [(1 << 20) // math.isqrt(rank ** slope) + 1 for rank in range(1, number_of + 1)]
    largest = limit if full else min(limit, max(-(-total // number_of), total * weights[0] // sum(weights)))
    least = 1 if total - largest >= number_of - 1 else 0
    counts, surplus = [largest] + [least] * (number_of - 1), total - largest - least * (number_of - 1)
    while surplus > 0:
        movable = [i for i in range(1, number_of) if counts[i] < largest] or [i for i in range(1, number_of) if counts[i] < limit]
        whole, budget = sum([weights[i] for i in movable]), surplus
        for i in movable:
            extra = min(limit - counts[i], max(1, budget * weights[i] // whole), surplus)
            counts[i] = counts[i] + extra
            surplus = surplus - extra
    return np.array(counts)


def centred(key, extent, deviation, bound, split=(), held_as=jnp.bfloat16):
    drawn = jax.random.normal(key, extent, jnp.float32) * deviation
    if len(split) > 0:
        drawn = block_scale(key, extent, split, -0.22, 0.18) * drawn
    return jnp.clip(drawn, min=-bound, max=bound).astype(held_as)


def setup_inputs(seed: int = 0) -> dict:
    arg_keys = jax.random.split(jax.random.key(seed), 15)
    tokens = centred(arg_keys[0], (TOKENS, D), 1.0, 6.0, ((0, 16),))
    ln1_gain = jnp.clip(0.5 + 1.0 * jax.random.uniform(arg_keys[1], (D,), jnp.float32) ** block_scale(arg_keys[1], (D,), ((0, 16),), -0.2, 0.2), 0.5, 1.5).astype(jnp.bfloat16)
    w_qkv = centred(arg_keys[2], (D, 3, D), D ** -0.5, 0.21875, ((0, 16), (2, 2)))
    w_out = centred(arg_keys[3], (D, D), (D // 8) ** -0.5, 0.625, ((0, 2), (1, 16)))
    out_bias = centred(arg_keys[4], (D,), 0.5, 3.0, ((0, 16),))
    ln2_gain = jnp.clip(0.5 + 1.0 * jax.random.uniform(arg_keys[5], (D,), jnp.float32) ** block_scale(arg_keys[5], (D,), ((0, 16),), -0.2, 0.2), 0.5, 1.5).astype(jnp.bfloat16)
    router = centred(arg_keys[6], (D, EXPERTS), (2 * D) ** -0.5, 0.15625, ((0, 16),))
    w_in = centred(arg_keys[7], (EXPERTS, D, FF), D ** -0.5, 0.21875, ((0, 16), (2, 2)))
    in_bias = centred(arg_keys[8], (EXPERTS, FF), 0.5, 3.0, ((0, 16), (1, 2)))
    w_back = centred(arg_keys[9], (EXPERTS, FF, D), (max(1, 12100 // (EXPERTS * EXPERTS))) ** -0.5, 0.875, ((0, 16), (1, 2)))
    back_bias = centred(arg_keys[10], (EXPERTS, D), 1.0, 4.0, ((0, 16),))
    routes_keys = jax.random.split(jax.random.fold_in(arg_keys[11], 1), TOKENS // TOK_DEV)
    routes_turns = jax.random.permutation(jax.random.fold_in(arg_keys[11], 3), TOKENS // TOK_DEV)
    routes = jax.vmap(lambda own, number: routed_block(jax.random.fold_in(arg_keys[11], 2), own, number, TOK_DEV, EXPERTS, 2, 2 * CAP, 1))(routes_keys, routes_turns).reshape((TOKENS, 2))
    priority = jax.vmap(lambda own: jax.random.permutation(own, TOK_DEV))(jax.random.split(arg_keys[12], GROUPS)).reshape((GROUPS, TOK_DEV)).astype(jnp.int32)
    cotangent = centred(arg_keys[13], (TOKENS, D), 1.0, 6.0, ((0, 16),))
    return {"tokens": tokens, "ln1_gain": ln1_gain, "w_qkv": w_qkv, "w_out": w_out, "out_bias": out_bias, "ln2_gain": ln2_gain, "router": router, "w_in": w_in, "in_bias": in_bias, "w_back": w_back, "back_bias": back_bias, "routes": routes, "priority": priority, "cotangent": cotangent}


epsilon = 1e-06
highest = lax.Precision.HIGHEST

@jax.custom_vjp
def low(v):
    return lax.optimization_barrier(v.astype(jnp.bfloat16)).astype(jnp.float32)

@jax.custom_vjp
def low_back(v):
    return v

def low_keep(v):
    return (low(v), None)

def low_pass(kept, grad):
    return (grad,)

def back_keep(v):
    return (v, None)

def back_low(kept, grad):
    return (low(grad),)
low.defvjp(low_keep, low_pass)
low_back.defvjp(back_keep, back_low)

def layer_norm(values, scale_factor):
    average = lax.optimization_barrier(jnp.mean(values, axis=-1, keepdims=True))
    centered = values - average
    spread = lax.optimization_barrier(jnp.mean(centered * centered, axis=-1, keepdims=True))
    return centered * lax.rsqrt(spread + epsilon) * scale_factor

def routing(route_rows, ranking, experts, capacity):
    tok_rows = route_rows.shape[0]
    ranked = jnp.arange(2, dtype=jnp.int32)[None, :] * tok_rows + ranking[:, None]
    by_order = jnp.zeros((2 * tok_rows,), jnp.int32).at[ranked.reshape(-1)].set(route_rows.reshape(-1))
    onehot = (by_order[:, None] == jnp.arange(experts, dtype=jnp.int32)[None, :]).astype(jnp.int32)
    earlier = jnp.cumsum(onehot, axis=0, dtype=jnp.int32) - onehot
    slot_of = lax.optimization_barrier(jnp.sum(earlier * onehot, axis=1, dtype=jnp.int32))
    slot_ids = slot_of[ranked]
    return jnp.where(slot_ids < capacity, route_rows * capacity + slot_ids, experts * capacity).astype(jnp.int32)

def pair_of_slot(slot_index, experts, capacity):
    pair_count = slot_index.shape[0] * slot_index.shape[1]
    empty = jnp.full((experts * capacity,), pair_count, jnp.int32)
    return empty.at[slot_index.reshape(-1)].set(jnp.arange(pair_count, dtype=jnp.int32), mode='drop')

def attend(group_rows, w_qkv, w_out):
    merged_qkv = jnp.dot(group_rows, w_qkv.reshape(D, 3 * D), precision=highest)
    merged_qkv = low_back(low(merged_qkv)).reshape(IMG_DEV, SEQ, 3, HEADS, HD)
    queries = merged_qkv[:, :, 0]
    keys_all = merged_qkv[:, :, 1]
    values_all = merged_qkv[:, :, 2]
    scores = low_back(jnp.einsum('bqhd,bkhd->bhqk', queries, keys_all, precision=highest) * HD ** (-0.5))
    weights = jax.nn.softmax(scores, axis=-1)
    attended = jnp.einsum('bhqk,bkhd->bqhd', low(weights), values_all, precision=highest).reshape(TOK_DEV, D)
    attended = low_back(low(attended))
    return low_back(jnp.dot(attended, w_out, precision=highest))

def expert(expert_rows, w_first, b_first, w_second, b_second):
    inner_sum = low_back(jnp.dot(expert_rows, w_first, precision=highest) + b_first)
    active = low(jax.nn.gelu(inner_sum, approximate=False))
    return low_back(low(jnp.dot(active, w_second, precision=highest) + b_second))

def forward(params, routes, slot_index, slot_pair):
    input_tokens, gain_one, w_qkv, w_out, out_bias, gain_two, router, w_in, in_bias, w_back, back_bias = params
    first_normalized = low(layer_norm(input_tokens, gain_one))
    attention = lax.map(jax.checkpoint(lambda group_rows: attend(group_rows, w_qkv, w_out)), first_normalized.reshape(N_DP, TOK_DEV, D)).reshape(TOKENS, D)
    hidden_state = input_tokens + attention + out_bias
    second_normalized = low(layer_norm(hidden_state, gain_two))
    logits = low_back(jnp.dot(second_normalized, router, precision=highest))
    weights = jax.nn.softmax(logits, axis=-1)
    gate_values = jnp.take_along_axis(weights, routes, axis=1)
    padded = jnp.concatenate([second_normalized.reshape(N_DP, TOK_DEV, D), jnp.zeros((N_DP, 1, D), jnp.float32)], axis=1)
    outgoing = jax.vmap(lambda source, indices: source[indices // 2])(padded, slot_pair)
    expert_in = low_back(outgoing.reshape(N_DP, EXPERTS, CAP, D).transpose(1, 0, 2, 3).reshape(EXPERTS, N_DP * CAP, D))
    expert_out = lax.map(jax.checkpoint(lambda packed: expert(*packed)), (expert_in, w_in, in_bias, w_back, back_bias))
    returned = expert_out.reshape(EXPERTS, N_DP, CAP, D).transpose(1, 0, 2, 3).reshape(N_DP, EXPERTS * CAP, D)
    returned = jnp.concatenate([returned, jnp.zeros((N_DP, 1, D), jnp.float32)], axis=1)
    picked = jax.vmap(lambda source, indices: source[indices])(returned, slot_index).reshape(TOKENS, 2, D)
    return hidden_state + lax.optimization_barrier(jnp.sum(gate_values[:, :, None] * picked, axis=1))

def reference(tokens, ln1_gain, w_qkv, w_out, out_bias, ln2_gain, router, w_in, in_bias, w_back, back_bias, routes, priority, cotangent):
    slot_index = jax.vmap(lambda route_rows, ranking: routing(route_rows, ranking, EXPERTS, CAP))(routes.reshape(N_DP, TOK_DEV, 2), priority)
    slot_pair = jax.vmap(lambda indices: pair_of_slot(indices, EXPERTS, CAP))(slot_index)
    params = tuple((array.astype(jnp.float32) for array in (tokens, ln1_gain, w_qkv, w_out, out_bias, ln2_gain, router, w_in, in_bias, w_back, back_bias)))
    result, pullback = jax.vjp(lambda *values: forward(values, routes, slot_index, slot_pair), *params)
    gradients = pullback(cotangent.astype(jnp.float32))
    return (result.astype(jnp.bfloat16), gradients[0].astype(jnp.bfloat16), gradients[1], gradients[2], gradients[3], gradients[4], gradients[5], gradients[6], gradients[7], gradients[8], gradients[9], gradients[10])
```

```python
import functools

import jax
import jax.numpy as jnp
from jax import lax
from jax.experimental import pallas as pl
from jax.experimental.pallas import tpu as pltpu
from jax.sharding import PartitionSpec as P

D = 768
HD = 64
SEQ = 197
EPS = 1e-06
F32 = jnp.float32
BF = jnp.bfloat16
MESH = pl.DeviceIdType.MESH
VMEM_LIMIT = 62 * 1024 * 1024
LINE = 4
FREE = 3


def up(value, step):
    return (value + step - 1) // step * step


SEQ_PAD = up(SEQ, 16)


def mm(left, right, cl, cr):
    return lax.dot_general(
        left, right, (((cl,), (cr,)), ((), ())), preferred_element_type=F32
    )


def norm_rows(values):
    average = jnp.mean(values, axis=-1, keepdims=True)
    centered = values - average
    inverse = lax.rsqrt(jnp.mean(centered * centered, axis=-1, keepdims=True) + EPS)
    return centered * inverse, inverse


def norm_back(grad, gain, xhat, inverse):
    scaled = grad * gain
    return inverse * (
        scaled
        - jnp.mean(scaled, axis=-1, keepdims=True)
        - xhat * jnp.mean(scaled * xhat, axis=-1, keepdims=True)
    )


def split_two(value):
    high = value.astype(BF)
    return high, (value - high.astype(F32)).astype(BF)


def whole():
    return pl.BlockSpec(memory_space=pltpu.VMEM)


def params(**more):
    return pltpu.CompilerParams(vmem_limit_bytes=VMEM_LIMIT, **more)


def greet(peers):
    barrier = pltpu.get_barrier_semaphore()
    for peer in peers:
        pl.semaphore_signal(barrier, inc=1, device_id=peer, device_id_type=MESH)
    pl.semaphore_wait(barrier, len(peers))


def remote(src, dst, send_sem, recv_sem, peer):
    return pltpu.make_async_remote_copy(
        src_ref=src, dst_ref=dst, send_sem=send_sem, recv_sem=recv_sem,
        device_id=peer, device_id_type=MESH,
    )


def slot_matrix(idx_ref, first, rows):
    number = lax.broadcasted_iota(jnp.int32, (rows, idx_ref.shape[1]), 0) + first
    hit = (number == idx_ref[0:1, :]) | (number == idx_ref[1:2, :])
    return jnp.where(hit, 1.0, 0.0).astype(BF)


def route_kernel(experts, cap, half, slots, prow_ref, pcol_ref, rt_ref, ct_ref, idx_ref, out_ref, ctp):
    lanes = rt_ref.shape[1]
    tok = ct_ref.shape[0]
    mine = lax.axis_index("mp")
    ctp[...] = jnp.zeros_like(ctp)
    ctp[0:tok, :] = ct_ref[...]
    number = lax.broadcasted_iota(jnp.int32, (experts, lanes), 0)
    hot = [jnp.where(number == rt_ref[j : j + 1, :], 1.0, 0.0) for j in range(2)]
    before = jnp.where(pcol_ref[...] < prow_ref[...], 1.0, 0.0).astype(BF)
    counts = [mm(h.astype(BF), before, 1, 0) for h in hot]
    counts[1] = counts[1] + jnp.sum(hot[0], axis=1, keepdims=True)
    for j in range(2):
        slot = jnp.sum(counts[j] * hot[j], axis=0, keepdims=True).astype(jnp.int32)
        place = slot - mine * half
        expert = rt_ref[j : j + 1, :]
        kept = (slot < cap) & (place >= 0) & (place < half) & (expert >= 0)
        idx_ref[j : j + 1, :] = jnp.where(kept, expert * slots + place, -1)

    group = 4 * slots

    def step(b, carry):
        rows = slot_matrix(idx_ref, b * group, group)
        block = mm(rows, ctp[...], 1, 0).astype(BF)
        out_ref[pl.ds(b * 4, 4)] = block.reshape(4, slots, D)
        return carry

    lax.fori_loop(0, experts // 4, step, 0)


def route(prow, pcol, rt, ct, experts, cap, half, slots):
    lanes = rt.shape[1]
    return pl.pallas_call(
        functools.partial(route_kernel, experts, cap, half, slots),
        out_shape=(
            jax.ShapeDtypeStruct((2, lanes), jnp.int32),
            jax.ShapeDtypeStruct((experts, slots, D), BF),
        ),
        in_specs=[whole()] * 4,
        out_specs=(whole(), whole()),
        scratch_shapes=[pltpu.VMEM((lanes, D), BF)],
        compiler_params=params(),
        name="route",
    )(prow, pcol, rt, ct)


def gather_kernel(n, w_ref, s_ref, wo_ref, so_ref, lsem, zs, zr, ps, pr):
    me = lax.axis_index("dp")
    plane = n // LINE
    z, q = me // plane, me % plane
    rp = w_ref.shape[1]
    zpeer = [((z + d) % LINE) * plane + q for d in range(1, LINE)]
    qpeer = [z * plane + (q + d) % plane for d in range(1, plane)]
    greet([{"dp": p} for p in zpeer + qpeer])

    def at(block):
        rows = pl.ds(pl.multiple_of(block * rp, rp), rp)
        return wo_ref.at[:, rows, :], so_ref.at[rows, :]

    own = at(me)
    local = [pltpu.make_async_copy(a, b, lsem.at[i]) for i, (a, b) in enumerate(zip((w_ref, s_ref), own))]
    for c in local:
        c.start()
    sends = []
    for d, p in enumerate(zpeer):
        for i, (a, b) in enumerate(zip((w_ref, s_ref), own)):
            c = remote(a, b, zs.at[d, i], zr.at[d, i], {"dp": p})
            c.start()
            sends.append(c)
    for d, p in enumerate(qpeer):
        for i, (a, b) in enumerate(zip((w_ref, s_ref), own)):
            c = remote(a, b, ps.at[d, 0, i], pr.at[d, 0, i], {"dp": p})
            c.start()
            sends.append(c)
    for k in range(1, LINE):
        block = at(((z + LINE - k) % LINE) * plane + q)
        for i in range(2):
            remote(block[i], block[i], zs.at[k - 1, i], zr.at[k - 1, i], {"dp": zpeer[0]}).wait_recv()
        for d, p in enumerate(qpeer):
            for i in range(2):
                c = remote(block[i], block[i], ps.at[d, k, i], pr.at[d, k, i], {"dp": p})
                c.start()
                sends.append(c)
    for d in range(1, plane):
        for k in range(LINE):
            block = at(((z + LINE - k) % LINE) * plane + (q + plane - d) % plane)
            for i in range(2):
                remote(block[i], block[i], ps.at[d - 1, k, i], pr.at[d - 1, k, i], {"dp": qpeer[0]}).wait_recv()
    for c in sends:
        c.wait_send()
    for c in local:
        c.wait()


def gather_weights(w, s, n):
    parts, rp, width = w.shape
    plane = n // LINE
    sem = pltpu.SemaphoreType.DMA
    return pl.pallas_call(
        functools.partial(gather_kernel, n),
        out_shape=(
            jax.ShapeDtypeStruct((parts, n * rp, width), BF),
            jax.ShapeDtypeStruct((n * rp, s.shape[1]), BF),
        ),
        in_specs=[whole()] * 2,
        out_specs=(whole(), whole()),
        scratch_shapes=[
            sem((2,)), sem((LINE - 1, 2)), sem((LINE - 1, 2)),
            sem((plane - 1, LINE, 2)), sem((plane - 1, LINE, 2)),
        ],
        compiler_params=params(collective_id=0, has_side_effects=True),
        name="gather_weights",
    )(w, s)


def attend_kernel(experts, tok_ref, small_ref, w_ref, qkv_ref, att_ref, part_ref, xp, pp):
    images = xp.shape[0]
    scale = HD ** (-0.5)
    gains = jnp.transpose(small_ref[...].astype(F32))
    gain = gains[experts : experts + 1, :]
    xp[:, SEQ_PAD - 16 : SEQ_PAD, :] = jnp.zeros((images, 16, D), F32)
    for i in range(images):
        xp[i, 0:SEQ, :] = tok_ref[i * SEQ : (i + 1) * SEQ, :].astype(F32)
    lane = lax.broadcasted_iota(jnp.int32, (1, 2 * HD), 1)
    masks = [jnp.where(lane // HD == h, 1.0, 0.0).astype(BF) for h in range(2)]
    valid = lax.broadcasted_iota(jnp.int32, (1, SEQ_PAD), 1) < SEQ

    def image(i, carry):
        xhat, _ = norm_rows(xp[i])
        normed = (xhat * gain).astype(BF)
        for c in range(3):
            qkv_ref[c, i] = mm(normed, w_ref[c], 1, 0).astype(BF)
        for p in range(w_ref.shape[2] // (2 * HD)):
            cols = slice(p * 2 * HD, (p + 1) * 2 * HD)
            q, k, v = (qkv_ref[c, i, :, cols] for c in range(3))
            outs = []
            for h in range(2):
                scores = mm(q * masks[h], k, 1, 1) * scale
                scores = jnp.where(valid, scores, -1e30)
                raised = jnp.exp(scores - jnp.max(scores, axis=-1, keepdims=True))
                weights = raised / jnp.sum(raised, axis=-1, keepdims=True)
                outs.append(mm(weights.astype(BF), v, 1, 0))
            att_ref[i, :, cols] = jnp.where(lane < HD, outs[0], outs[1]).astype(BF)
        pp[i] = mm(att_ref[i], w_ref[3], 1, 1)
        return carry

    lax.fori_loop(0, images, image, 0)
    for i in range(images):
        part_ref[i * SEQ : (i + 1) * SEQ, :] = pp[i, 0:SEQ, :]


def attend(tok, small, w, experts):
    images = tok.shape[0] // SEQ
    width = w.shape[2]
    return pl.pallas_call(
        functools.partial(attend_kernel, experts),
        out_shape=(
            jax.ShapeDtypeStruct((3, images, SEQ_PAD, width), BF),
            jax.ShapeDtypeStruct((images, SEQ_PAD, width), BF),
            jax.ShapeDtypeStruct(tok.shape, F32),
        ),
        in_specs=[whole()] * 3,
        out_specs=(whole(),) * 3,
        scratch_shapes=[
            pltpu.VMEM((images, SEQ_PAD, D), F32),
            pltpu.VMEM((images, SEQ_PAD, D), F32),
        ],
        compiler_params=params(),
        name="attend",
    )(tok, small, w)


def row_chunks(rows):
    return [(s, min(256, rows - s)) for s in range(0, rows, 256)]


def dispatch_kernel(
    n, half, part_ref, tok_ref, small_ref, idx_ref, hid_ref, n2_ref, prob_ref, x_ref,
    own, other, send, p2, hs, hr, ss, rs,
):
    me, mine = lax.axis_index("dp"), lax.axis_index("mp")
    tok = tok_ref.shape[0]
    slots = send.shape[1]
    experts = prob_ref.shape[0]
    sibling = {"mp": 1 - mine}
    greet([sibling] + [{"dp": (me + d) % n} for d in range(1, n)])
    own[own.shape[0] - 16 :, :] = jnp.zeros((16, D), BF)
    copies = []
    for c, (start, size) in enumerate(row_chunks(own.shape[0])):
        stop = min(start + size, tok)
        own[start:stop, :] = part_ref[start:stop, :].astype(BF)
        rows = pl.ds(start, size)
        copy = remote(own.at[rows, :], other.at[rows, :], hs.at[c], hr.at[c], sibling)
        copy.start()
        copies.append(copy)
    gains = jnp.transpose(small_ref[...].astype(F32))
    gain = gains[experts + 1 : experts + 2, :]
    bias = gains[experts + 2 : experts + 3, :]
    n2_ref[n2_ref.shape[0] - 64 :, :] = jnp.zeros((64, D), BF)
    for c, (start, size) in enumerate(row_chunks(own.shape[0])):
        stop = min(start + size, tok)
        copies[c].wait_recv()
        both = own[start:stop, :].astype(F32) + other[start:stop, :].astype(F32)
        hidden = tok_ref[start:stop, :].astype(F32) + both + bias
        hid_ref[start:stop, :] = hidden
        xhat, _ = norm_rows(hidden)
        n2_ref[start:stop, :] = (xhat * gain).astype(BF)
    logits = mm(gains[0:experts, :].astype(BF), n2_ref[...], 1, 1)
    raised = jnp.exp(logits - jnp.max(logits, axis=0, keepdims=True))
    probs = raised / jnp.sum(raised, axis=0, keepdims=True)
    prob_ref[...] = probs
    high, low = split_two(probs)
    p2[0:experts, :] = high
    p2[experts:, :] = low
    place = lax.broadcasted_iota(jnp.int32, (slots, slots), 0)
    number = lax.broadcasted_iota(jnp.int32, (2 * experts, slots), 0)

    def step(b, carry):
        hot = [slot_matrix(idx_ref, ((me + b * 4 + j) % n) * slots, slots) for j in range(4)]
        block = mm(jnp.concatenate(hot, axis=0), n2_ref[...], 1, 0)
        for j in range(4):
            d = b * 4 + j
            peer = (me + d) % n
            gates = mm(p2[...], hot[j], 1, 1)
            row_high = jnp.sum(jnp.where(number == peer, gates, 0.0), axis=0, keepdims=True)
            row_low = jnp.sum(jnp.where(number == peer + experts, gates, 0.0), axis=0, keepdims=True)
            rows = block[j * slots : (j + 1) * slots, :]
            left = jnp.where(place == half, row_high, jnp.where(place == half + 1, row_low, rows[:, 0:slots]))
            send[d, :, :] = rows.astype(BF)
            send[d, :, 0:slots] = left.astype(BF)

            @pl.when(d > 0)
            def _():
                remote(send.at[d], x_ref.at[me], ss.at[d], rs.at[d], {"dp": peer}).start()

        return carry

    lax.fori_loop(0, n // 4, step, 0)
    x_ref[me] = send[0]

    def finish(d, carry):
        source = (me + n - d) % n
        remote(send.at[d], x_ref.at[source], ss.at[d], rs.at[d], {"dp": source}).wait()
        return carry

    lax.fori_loop(1, n, finish, 0)
    for copy in copies:
        copy.wait_send()


def dispatch(part, tok, small, idx, n, experts, half, slots):
    lanes = idx.shape[1]
    tr = up(tok.shape[0], 16)
    sem = pltpu.SemaphoreType.DMA
    chunks = len(row_chunks(tr))
    return pl.pallas_call(
        functools.partial(dispatch_kernel, n, half),
        out_shape=(
            jax.ShapeDtypeStruct(tok.shape, F32),
            jax.ShapeDtypeStruct((lanes, D), BF),
            jax.ShapeDtypeStruct((experts, lanes), F32),
            jax.ShapeDtypeStruct((n, slots, D), BF),
        ),
        in_specs=[whole()] * 4,
        out_specs=(whole(),) * 4,
        scratch_shapes=[
            pltpu.VMEM((tr, D), BF),
            pltpu.VMEM((tr, D), BF),
            pltpu.VMEM((n, slots, D), BF),
            pltpu.VMEM((2 * experts, lanes), BF),
            sem((chunks,)), sem((chunks,)), sem((n,)), sem((n,)),
        ],
        compiler_params=params(collective_id=1, has_side_effects=True),
        name="dispatch",
    )(part, tok, small, idx)


def expert_kernel(
    n, half, slots,
    x_ref, ct_ref, wi_own, wi_sib, wb_own, wb_sib, bi_own, bi_sib, bb_ref,
    gi_own, gi_sib, gb_own, gb_sib, gbi_own, gbi_sib, gbb_ref, dx_ref, y_ref,
    xt, g_s, y_acc, dx_acc, act_s, dpre_s, gate_s, wi_s, wb_s,
):
    k, steps = pl.program_id(0), pl.num_programs(0)
    first = k < steps // 2
    rows_all = n * slots
    tile = 256
    tiles = rows_all // tile

    def in_group():
        row = lax.broadcasted_iota(jnp.int32, (tile, n), 0)
        return row, lax.broadcasted_iota(jnp.int32, (tile, n), 1)

    @pl.when(k == 0)
    def _():
        group = lax.broadcasted_iota(jnp.int32, (n, rows_all), 0)
        row = lax.broadcasted_iota(jnp.int32, (n, rows_all), 1)
        pick = jnp.where((row == group * slots + half) | (row == group * slots + half + 1), 1.0, 0.0)
        gates = mm(pick.astype(BF), x_ref[:, 0:128], 1, 0)
        high, low = split_two(gates)

        def start(r, total):
            at = pl.ds(pl.multiple_of(r * tile, tile), tile)
            row, group = in_group()
            mine = jnp.where((row + r * tile) // slots == group, 1.0, 0.0).astype(BF)
            wide = mm(mine, high, 1, 0) + mm(mine, low, 1, 0)
            spot = lax.broadcasted_iota(jnp.int32, (tile, 128), 0) + r * tile
            lane = lax.broadcasted_iota(jnp.int32, (tile, 128), 1)
            gate = jnp.sum(jnp.where(lane == spot % slots, wide, 0.0), axis=1, keepdims=True)
            gate_s[at, :] = gate
            scaled = (gate * ct_ref[at, :].astype(F32)).astype(BF)
            g_s[at, :] = scaled
            xt[:, at] = jnp.transpose(x_ref[at, :].astype(F32)).astype(BF)
            return total + jnp.sum(scaled.astype(F32), axis=0, keepdims=True)

        gbb_ref[...] = lax.fori_loop(0, tiles, start, jnp.zeros((1, D), F32))
        y_acc[...] = jnp.zeros_like(y_acc)
        dx_acc[...] = jnp.zeros_like(dx_acc)

    @pl.when(first)
    def _():
        wi_s[...] = wi_own[...]
        wb_s[...] = wb_own[...]

    @pl.when(jnp.logical_not(first))
    def _():
        wi_s[...] = wi_sib[...]
        wb_s[...] = wb_sib[...]

    bias = jnp.where(first, bi_own[...], bi_sib[...]).astype(F32)

    def forward(r, total):
        at = pl.ds(pl.multiple_of(r * tile, tile), tile)
        pre = mm(x_ref[at, :], wi_s[...], 1, 0) + bias
        phi = 0.5 * (1.0 + lax.erf(pre * (0.5**0.5)))
        slope = phi + pre * (jnp.exp(-0.5 * pre * pre) * ((2.0 * jnp.pi) ** -0.5))
        act = (pre * phi).astype(BF)
        act_s[at, :] = act
        grad = (mm(g_s[at, :], wb_s[...], 1, 1) * slope).astype(BF)
        dpre_s[at, :] = grad
        y_acc[at, :] += mm(act, wb_s[...], 1, 0)
        dx_acc[at, :] += mm(grad, wi_s[...], 1, 1)
        return total + jnp.sum(grad.astype(F32), axis=0, keepdims=True)

    total = lax.fori_loop(0, tiles, forward, jnp.zeros(bias.shape, F32))

    def first_weight(r, carry):
        at = pl.ds(pl.multiple_of(r * tile, tile), tile)
        grad = mm(xt[at, :], dpre_s[...], 1, 0)

        @pl.when(first)
        def _():
            gi_own[at, :] = grad

        @pl.when(jnp.logical_not(first))
        def _():
            gi_sib[at, :] = grad.astype(BF)

        return carry

    lax.fori_loop(0, D // tile, first_weight, 0)

    def second_weight(r, carry):
        at = pl.ds(pl.multiple_of(r * tile, tile), tile)
        grad = mm(act_s[:, at], g_s[...], 0, 0)

        @pl.when(first)
        def _():
            gb_own[at, :] = grad

        @pl.when(jnp.logical_not(first))
        def _():
            gb_sib[at, :] = grad.astype(BF)

        return carry

    lax.fori_loop(0, act_s.shape[1] // tile, second_weight, 0)

    @pl.when(first)
    def _():
        gbi_own[...] = total

    @pl.when(jnp.logical_not(first))
    def _():
        gbi_sib[...] = total

    @pl.when(k == steps - 1)
    def _():
        def finish(r, sums):
            at = pl.ds(pl.multiple_of(r * tile, tile), tile)
            y = (y_acc[at, :] + bb_ref[...].astype(F32)).astype(BF).astype(F32)
            y_ref[at, :] = (gate_s[at, :] * y).astype(BF)
            dots = jnp.sum(ct_ref[at, :].astype(F32) * y, axis=1, keepdims=True)
            spot = lax.broadcasted_iota(jnp.int32, (tile, 128), 0) + r * tile
            lane = lax.broadcasted_iota(jnp.int32, (tile, 128), 1)
            spread = jnp.where(lane == spot % slots, dots, 0.0)
            row, group = in_group()
            mine = jnp.where((row + r * tile) // slots == group, 1.0, 0.0).astype(BF)
            high, low = split_two(spread)
            return sums[0] + mm(mine, high, 0, 0), sums[1] + mm(mine, low, 0, 0)

        zero = jnp.zeros((n, 128), F32)
        high, low = lax.fori_loop(0, tiles, finish, (zero, zero))
        high, low = high.astype(BF), low.astype(BF)

        def leave(r, carry):
            at = pl.ds(pl.multiple_of(r * tile, tile), tile)
            row, group = in_group()
            spot = row + r * tile - group * slots
            put = [jnp.where(spot == half + i, 1.0, 0.0).astype(BF) for i in range(2)]
            dx_ref[at, :] = dx_acc[at, :].astype(BF)
            dx_ref[at, 0:128] = (dx_acc[at, 0:128] + mm(put[0], high, 1, 0) + mm(put[1], low, 1, 0)).astype(BF)
            return carry

        lax.fori_loop(0, tiles, leave, 0)


def expert(x, ct, wi, wb, bi, bb, n, half, slots):
    rows = n * slots
    hidden = wi[0].shape[1]
    chunk = 512
    each = hidden // chunk
    own = lambda k: jnp.minimum(k, each - 1)
    sib = lambda k: jnp.maximum(k - each, 0)
    cols = lambda at: pl.BlockSpec((D, chunk), lambda k: (0, at(k)))
    lines = lambda at: pl.BlockSpec((chunk, D), lambda k: (at(k), 0))
    strip = lambda at: pl.BlockSpec((1, chunk), lambda k: (0, at(k)))
    shape = jax.ShapeDtypeStruct
    return pl.pallas_call(
        functools.partial(expert_kernel, n, half, slots),
        grid=(2 * each,),
        out_shape=(
            shape((D, hidden), F32), shape((D, hidden), BF),
            shape((hidden, D), F32), shape((hidden, D), BF),
            shape((1, hidden), F32), shape((1, hidden), F32), shape((1, D), F32),
            shape((rows, D), BF), shape((rows, D), BF),
        ),
        in_specs=[whole(), whole(), cols(own), cols(sib), lines(own), lines(sib), strip(own), strip(sib), whole()],
        out_specs=(
            cols(own), cols(sib), lines(own), lines(sib), strip(own), strip(sib), whole(), whole(), whole(),
        ),
        scratch_shapes=[
            pltpu.VMEM((D, rows), BF),
            pltpu.VMEM((rows, D), BF),
            pltpu.VMEM((rows, D), F32),
            pltpu.VMEM((rows, D), F32),
            pltpu.VMEM((rows, chunk), BF),
            pltpu.VMEM((rows, chunk), BF),
            pltpu.VMEM((rows, 1), F32),
            pltpu.VMEM((D, chunk), BF),
            pltpu.VMEM((chunk, D), BF),
        ],
        compiler_params=params(dimension_semantics=("arbitrary",)),
        name="expert",
    )(x, ct, wi[0], wi[1], wb[0], wb[1], bi[0], bi[1], bb)


def return_kernel(
    n, half, dx_ref, idx_ref, prob_ref, n2_ref, hid_ref, ct_ref, small_ref, hg_ref, sg_ref,
    back, acc, own, other, gp, gp_other, ss, rs, hs, hr,
):
    me, mine = lax.axis_index("dp"), lax.axis_index("mp")
    tok = ct_ref.shape[0]
    slots = dx_ref.shape[1]
    experts = prob_ref.shape[0]
    sibling = {"mp": 1 - mine}
    greet([sibling] + [{"dp": (me + d) % n} for d in range(1, n)])

    def begin(d, carry):
        peer = (me + d) % n
        remote(dx_ref.at[peer], back.at[d], ss.at[d], rs.at[d], {"dp": peer}).start()
        return carry

    lax.fori_loop(1, n, begin, 0)
    back[0] = dx_ref[me]
    acc[...] = jnp.zeros_like(acc)
    gp[...] = jnp.zeros_like(gp)
    place = lax.broadcasted_iota(jnp.int32, (slots, 128), 0)
    number = lax.broadcasted_iota(jnp.int32, (2 * experts, slots), 0)

    def step(b, carry):
        hot = []
        for j in range(4):
            d = b * 4 + j
            source = (me + n - d) % n

            @pl.when(d > 0)
            def _():
                remote(dx_ref.at[source], back.at[d], ss.at[d], rs.at[d], {"dp": source}).wait_recv()

            hot.append(slot_matrix(idx_ref, source * slots, slots))
            extra = back[d, :, 0:128].astype(F32)
            high = jnp.sum(jnp.where(place == half, extra, 0.0), axis=0, keepdims=True)[:, 0:slots]
            low = jnp.sum(jnp.where(place == half + 1, extra, 0.0), axis=0, keepdims=True)[:, 0:slots]
            rows = jnp.where(number == source, high, jnp.where(number == source + experts, low, 0.0))
            gp[...] += mm(rows.astype(BF), hot[j], 1, 0)
        block = back[pl.ds(b * 4, 4)].reshape(4 * slots, D)
        acc[...] += mm(jnp.concatenate(hot, axis=0), block, 0, 0)
        return carry

    lax.fori_loop(0, n // 4, step, 0)
    copies = []
    own[own.shape[0] - 16 :, :] = jnp.zeros((16, D), BF)
    for c, (start, size) in enumerate(row_chunks(own.shape[0])):
        stop = min(start + size, tok)
        own[start:stop, :] = acc[start:stop, :].astype(BF)
        rows = pl.ds(start, size)
        copy = remote(own.at[rows, :], other.at[rows, :], hs.at[c], hr.at[c], sibling)
        copy.start()
        copies.append(copy)
    copy = remote(gp, gp_other, hs.at[len(copies)], hr.at[len(copies)], sibling)
    copy.start()
    copy.wait()
    probs = prob_ref[...]
    both = gp[...] + gp_other[...]
    grad_probs = both[0:experts, :] + both[experts:, :]
    logits = (probs * (grad_probs - jnp.sum(grad_probs * probs, axis=0, keepdims=True))).astype(BF)
    gains = jnp.transpose(small_ref[...].astype(F32))
    gain = gains[experts + 1 : experts + 2, :]
    acc[...] = mm(logits, gains[0:experts, :].astype(BF), 0, 0)
    sg_ref[...] = jnp.zeros_like(sg_ref)
    sg_ref[0:experts, :] = mm(logits, n2_ref[...], 1, 0)
    gain_sum = jnp.zeros((1, D), F32)
    bias_sum = jnp.zeros((1, D), F32)
    for c, (start, size) in enumerate(row_chunks(own.shape[0])):
        stop = min(start + size, tok)
        copies[c].wait_recv()
        grad = own[start:stop, :].astype(F32) + other[start:stop, :].astype(F32) + acc[start:stop, :]
        xhat, inverse = norm_rows(hid_ref[start:stop, :])
        hidden = ct_ref[start:stop, :].astype(F32) + norm_back(grad, gain, xhat, inverse)
        hg_ref[start:stop, :] = hidden
        gain_sum += jnp.sum(grad * xhat, axis=0, keepdims=True)
        bias_sum += jnp.sum(hidden, axis=0, keepdims=True)
    sg_ref[experts : experts + 1, :] = gain_sum
    sg_ref[experts + 1 : experts + 2, :] = bias_sum
    for copy in copies:
        copy.wait_send()

    def finish(d, carry):
        peer = (me + d) % n
        remote(dx_ref.at[peer], back.at[d], ss.at[d], rs.at[d], {"dp": peer}).wait_send()
        return carry

    lax.fori_loop(1, n, finish, 0)


def give_back(dx, idx, probs, n2, hid, ct, small, n, half):
    slots = dx.shape[1]
    experts, lanes = probs.shape
    tr = up(ct.shape[0], 16)
    chunks = len(row_chunks(tr))
    sem = pltpu.SemaphoreType.DMA
    return pl.pallas_call(
        functools.partial(return_kernel, n, half),
        out_shape=(
            jax.ShapeDtypeStruct(ct.shape, F32),
            jax.ShapeDtypeStruct((128, D), F32),
        ),
        in_specs=[whole()] * 7,
        out_specs=(whole(),) * 2,
        scratch_shapes=[
            pltpu.VMEM((n, slots, D), BF),
            pltpu.VMEM((lanes, D), F32),
            pltpu.VMEM((tr, D), BF),
            pltpu.VMEM((tr, D), BF),
            pltpu.VMEM((2 * experts, lanes), F32),
            pltpu.VMEM((2 * experts, lanes), F32),
            sem((n,)), sem((n,)), sem((chunks + 1,)), sem((chunks + 1,)),
        ],
        compiler_params=params(collective_id=2, has_side_effects=True),
        name="give_back",
    )(dx, idx, probs, n2, hid, ct, small)


def attend_back_kernel(
    experts, hg_ref, tok_ref, small_ref, w_ref, qkv_ref, att_ref, dn_ref, dw_ref,
    normed, low, dqkv, pp,
):
    images = normed.shape[0]
    scale = HD ** (-0.5)
    gains = jnp.transpose(small_ref[...].astype(F32))
    gain = gains[experts : experts + 1, :]
    tail = jnp.zeros((images, 16, D), F32)
    pp[:, SEQ_PAD - 16 : SEQ_PAD, :] = tail
    for i in range(images):
        pp[i, 0:SEQ, :] = hg_ref[i * SEQ : (i + 1) * SEQ, :]
    low[...] = pp[...].astype(BF)
    for i in range(images):
        pp[i, 0:SEQ, :] = tok_ref[i * SEQ : (i + 1) * SEQ, :].astype(F32)
    lane = lax.broadcasted_iota(jnp.int32, (1, 2 * HD), 1)
    masks = [jnp.where(lane // HD == h, 1.0, 0.0).astype(BF) for h in range(2)]
    valid = lax.broadcasted_iota(jnp.int32, (1, SEQ_PAD), 1) < SEQ

    def image(i, carry):
        xhat, _ = norm_rows(pp[i])
        normed[i] = (xhat * gain).astype(BF)
        grad_att = mm(low[i], w_ref[3], 1, 0).astype(BF)
        for p in range(w_ref.shape[2] // (2 * HD)):
            cols = slice(p * 2 * HD, (p + 1) * 2 * HD)
            q, k, v = (qkv_ref[c, i, :, cols] for c in range(3))
            pair = grad_att[:, cols]
            grads = []
            for h in range(2):
                scores = mm(q * masks[h], k, 1, 1) * scale
                scores = jnp.where(valid, scores, -1e30)
                raised = jnp.exp(scores - jnp.max(scores, axis=-1, keepdims=True))
                weights = raised / jnp.sum(raised, axis=-1, keepdims=True)
                grad_weights = mm(pair * masks[h], v, 1, 1)
                grad_scores = weights * (
                    grad_weights - jnp.sum(grad_weights * weights, axis=-1, keepdims=True)
                )
                scores_low = grad_scores.astype(BF)
                grads.append((
                    mm(scores_low, k, 1, 0) * scale,
                    mm(scores_low, q, 0, 0) * scale,
                    mm(weights.astype(BF), pair, 0, 0),
                ))
            for c in range(3):
                dqkv[c, i, :, cols] = jnp.where(lane < HD, grads[0][c], grads[1][c]).astype(BF)
        total = mm(dqkv[0, i], w_ref[0], 1, 1)
        for c in range(1, 3):
            total += mm(dqkv[c, i], w_ref[c], 1, 1)
        pp[i] = total
        return carry

    lax.fori_loop(0, images, image, 0)
    for i in range(images):
        dn_ref[i * SEQ : (i + 1) * SEQ, :] = pp[i, 0:SEQ, :]
    rows = images * SEQ_PAD

    def weight(r, carry):
        at = pl.ds(pl.multiple_of(r * 256, 256), 256)
        left = normed[:, :, at].reshape(rows, 256)
        for c in range(3):
            dw_ref[c, at, :] = mm(left, dqkv[c].reshape(rows, -1), 0, 0).astype(BF)
        left = low[:, :, at].reshape(rows, 256)
        dw_ref[3, at, :] = mm(left, att_ref[...].reshape(rows, -1), 0, 0).astype(BF)
        return carry

    lax.fori_loop(0, D // 256, weight, 0)


def attend_back(hg, tok, small, w, qkv, att, experts):
    images = tok.shape[0] // SEQ
    width = w.shape[2]
    return pl.pallas_call(
        functools.partial(attend_back_kernel, experts),
        out_shape=(
            jax.ShapeDtypeStruct(tok.shape, F32),
            jax.ShapeDtypeStruct((4, D, width), BF),
        ),
        in_specs=[whole()] * 6,
        out_specs=(whole(),) * 2,
        scratch_shapes=[
            pltpu.VMEM((images, SEQ_PAD, D), BF),
            pltpu.VMEM((images, SEQ_PAD, D), BF),
            pltpu.VMEM((3, images, SEQ_PAD, width), BF),
            pltpu.VMEM((images, SEQ_PAD, D), F32),
        ],
        compiler_params=params(),
        name="attend_back",
    )(hg, tok, small, w, qkv, att)


def last_kernel(
    n, experts, dw_ref, sg_ref, dn_ref, tok_ref, hg_ref, small_ref, y_ref, idx_ref, hid_ref,
    tg_ref, out_ref, gw_ref, gs_ref,
    own, other, mix, mix_other, sm, r1, q1, s1, t1, r2, q2, acc, hs, hr, as_, ar, bs, br,
):
    me, mine = lax.axis_index("dp"), lax.axis_index("mp")
    plane = n // LINE
    z, q = me // plane, me % plane
    tok = tok_ref.shape[0]
    rp = dw_ref.shape[3]
    sibling = {"mp": 1 - mine}
    zpeer = [((z + d) % LINE) * plane + q for d in range(1, LINE)]
    qpeer = [z * plane + (q + d) % plane for d in range(1, plane)]
    greet([sibling] + [{"dp": p} for p in zpeer + qpeer])
    sends = []
    for d, p in enumerate(qpeer):
        c = remote(dw_ref.at[:, :, (q + d + 1) % plane], r1.at[d], as_.at[d, 0], ar.at[d, 0], {"dp": p})
        c.start()
        sends.append(c)
    copies = []
    own[own.shape[0] - 16 :, :] = jnp.zeros((16, D), BF)
    for c, (start, size) in enumerate(row_chunks(own.shape[0])):
        stop = min(start + size, tok)
        own[start:stop, :] = dn_ref[start:stop, :].astype(BF)
        rows = pl.ds(start, size)
        copy = remote(own.at[rows, :], other.at[rows, :], hs.at[c], hr.at[c], sibling)
        copy.start()
        copies.append(copy)
    gains = jnp.transpose(small_ref[...].astype(F32))
    gain = gains[experts : experts + 1, :]
    gain_sum = jnp.zeros((1, D), F32)
    for c, (start, size) in enumerate(row_chunks(own.shape[0])):
        stop = min(start + size, tok)
        copies[c].wait()
        grad = own[start:stop, :].astype(F32) + other[start:stop, :].astype(F32)
        xhat, inverse = norm_rows(tok_ref[start:stop, :].astype(F32))
        tg_ref[start:stop, :] = (hg_ref[start:stop, :] + norm_back(grad, gain, xhat, inverse)).astype(BF)
        gain_sum += jnp.sum(grad * xhat, axis=0, keepdims=True)
    row = lax.broadcasted_iota(jnp.int32, sg_ref.shape, 0)
    rows = jnp.where(row == experts + 2, gain_sum, sg_ref[...])
    turned = jnp.transpose(rows).astype(BF)
    real = turned.shape[0] // n
    for b in range(n):
        at = (b // plane, b % plane)
        if real < rp:
            sm[at[0], at[1]] = jnp.zeros((rp, 128), BF)
        sm[at[0], at[1], 0:real, :] = turned[b * real : (b + 1) * real, :]
    for d, p in enumerate(qpeer):
        c = remote(sm.at[:, (q + d + 1) % plane], q1.at[d], as_.at[d, 1], ar.at[d, 1], {"dp": p})
        c.start()
        sends.append(c)
    slots = y_ref.shape[1]
    acc[...] = jnp.zeros_like(acc)

    def step(b, carry):
        hot = slot_matrix(idx_ref, b * 4 * slots, 4 * slots)
        acc[...] += mm(hot, y_ref[pl.ds(b * 4, 4)].reshape(4 * slots, D), 0, 0)
        return carry

    lax.fori_loop(0, n // 4, step, 0)
    mix[mix.shape[0] - 16 :, :] = jnp.zeros((16, D), BF)
    base = len(copies)
    late = []
    for c, (start, size) in enumerate(row_chunks(own.shape[0])):
        stop = min(start + size, tok)
        mix[start:stop, :] = acc[start:stop, :].astype(BF)
        rows = pl.ds(start, size)
        copy = remote(mix.at[rows, :], mix_other.at[rows, :], hs.at[base + c], hr.at[base + c], sibling)
        copy.start()
        late.append(copy)
    for c, (start, size) in enumerate(row_chunks(own.shape[0])):
        stop = min(start + size, tok)
        late[c].wait()
        both = mix[start:stop, :].astype(F32) + mix_other[start:stop, :].astype(F32)
        out_ref[start:stop, :] = (hid_ref[start:stop, :] + both).astype(BF)
    for d in range(plane - 1):
        remote(dw_ref.at[:, :, 0], r1.at[d], as_.at[d, 0], ar.at[d, 0], {"dp": qpeer[0]}).wait_recv()
        remote(sm.at[:, 0], q1.at[d], as_.at[d, 1], ar.at[d, 1], {"dp": qpeer[0]}).wait_recv()
    for b in range(LINE):
        value = dw_ref[:, b, q].astype(F32)
        little = sm[b, q].astype(F32)
        for d in range(plane - 1):
            value += r1[d, :, b].astype(F32)
            little += q1[d, b].astype(F32)
        s1[b] = value.astype(BF)
        t1[b] = little.astype(BF)
    for d, p in enumerate(zpeer):
        to = (z + d + 1) % LINE
        for i, (a, b) in enumerate(((s1, r2), (t1, q2))):
            c = remote(a.at[to], b.at[d], bs.at[d, i], br.at[d, i], {"dp": p})
            c.start()
            sends.append(c)
    value = s1[z].astype(F32)
    little = t1[z].astype(F32)
    for d in range(LINE - 1):
        for i, (a, b) in enumerate(((s1, r2), (t1, q2))):
            remote(a.at[0], b.at[d], bs.at[d, i], br.at[d, i], {"dp": zpeer[0]}).wait_recv()
        value += r2[d].astype(F32)
        little += q2[d].astype(F32)
    gw_ref[...] = value
    gs_ref[...] = little
    for c in sends:
        c.wait_send()


def last(dw, sg, dn, tok, hg, small, y, idx, hid, n, experts):
    parts, _, rows, width = dw.shape
    rp = rows
    plane = n // LINE
    dw = dw.reshape(parts, LINE, plane, rp, width)
    tr = up(tok.shape[0], 16)
    chunks = len(row_chunks(tr))
    sem = pltpu.SemaphoreType.DMA
    vmem = pltpu.VMEM
    return pl.pallas_call(
        functools.partial(last_kernel, n, experts),
        out_shape=(
            jax.ShapeDtypeStruct(tok.shape, BF),
            jax.ShapeDtypeStruct(tok.shape, BF),
            jax.ShapeDtypeStruct((parts, rp, width), F32),
            jax.ShapeDtypeStruct((rp, 128), F32),
        ),
        in_specs=[whole()] * 9,
        out_specs=(whole(),) * 4,
        scratch_shapes=[
            vmem((tr, D), BF), vmem((tr, D), BF), vmem((tr, D), BF), vmem((tr, D), BF),
            vmem((LINE, plane, rp, 128), BF),
            vmem((plane - 1, parts, LINE, rp, width), BF),
            vmem((plane - 1, LINE, rp, 128), BF),
            vmem((LINE, parts, rp, width), BF),
            vmem((LINE, rp, 128), BF),
            vmem((LINE - 1, parts, rp, width), BF),
            vmem((LINE - 1, rp, 128), BF),
            vmem((idx.shape[1], D), F32),
            sem((2 * chunks,)), sem((2 * chunks,)),
            sem((plane - 1, 2)), sem((plane - 1, 2)), sem((LINE - 1, 2)), sem((LINE - 1, 2)),
        ],
        compiler_params=params(collective_id=3, has_side_effects=True),
        name="last",
    )(dw, sg, dn, tok, hg, small, y, idx, hid)


def body(
    tokens, ln1_gain, w_qkv, w_out, out_bias, ln2_gain, router, w_in, in_bias,
    w_back, back_bias, routes, priority, cotangent,
):
    n = lax.axis_size("dp")
    tok = tokens.shape[0]
    experts = router.shape[1]
    cap = max(2, 5 * tok // (2 * experts))
    half = (cap + 1) // 2
    slots = up(half + FREE, 16)
    lanes = up(tok, 128)
    shard, width = w_qkv.shape[0], w_qkv.shape[2]
    rp = up(shard, 16)
    swap = [(0, 1), (1, 0)]

    wi = (w_in[0], lax.ppermute(w_in[0], "mp", swap))
    wb = (w_back[0], lax.ppermute(w_back[0], "mp", swap))
    bi = (in_bias, lax.ppermute(in_bias, "mp", swap))

    rt = jnp.pad(routes.T, ((0, 0), (0, lanes - tok)), constant_values=-1)
    ranks = jnp.pad(priority[0], (0, lanes - tok), constant_values=1 << 20)
    idx, ct_rows = route(ranks[None, :], ranks[:, None], rt, cotangent, experts, cap, half, slots)

    weights = jnp.concatenate([jnp.swapaxes(w_qkv, 0, 1), w_out.T[None]], axis=0)
    small = jnp.concatenate(
        [router, ln1_gain[:, None], ln2_gain[:, None], out_bias[:, None],
         jnp.zeros((shard, 128 - experts - 3), BF)], axis=1,
    )
    if rp > shard:
        weights = jnp.pad(weights, ((0, 0), (0, rp - shard), (0, 0)))
        small = jnp.pad(small, ((0, rp - shard), (0, 0)))
    weights, small = gather_weights(weights, small, n)
    if rp > shard:
        weights = weights.reshape(4, n, rp, width)[:, :, :shard].reshape(4, D, width)
        small = small.reshape(n, rp, 128)[:, :shard].reshape(D, 128)

    ct_rows, small = lax.optimization_barrier((ct_rows, small))
    ct_rows = lax.all_to_all(ct_rows, "dp", split_axis=0, concat_axis=0, tiled=True)

    qkv, att, part = attend(tokens, small, weights, experts)
    hid, n2, probs, x = dispatch(part, tokens, small, idx, n, experts, half, slots)
    rows = n * slots
    gi_own, gi_sib, gb_own, gb_sib, gbi_own, gbi_sib, gbb, dx, y = expert(
        x.reshape(rows, D), ct_rows.reshape(rows, D), wi, wb, bi, back_bias, n, half, slots
    )
    y = lax.all_to_all(y.reshape(n, slots, D), "dp", split_axis=0, concat_axis=0, tiled=True)
    gi_sib = lax.ppermute(gi_sib, "mp", swap)
    gb_sib = lax.ppermute(gb_sib, "mp", swap)
    little = jnp.concatenate([gbi_sib, gbb], axis=1)
    little = lax.ppermute(little, "mp", swap)
    hidden = gbi_own.shape[1]
    hg, sg = give_back(dx.reshape(n, slots, D), idx, probs, n2, hid, cotangent, small, n, half)
    dn, dw = attend_back(hg, tokens, small, weights, qkv, att, experts)
    dw = dw.reshape(4, n, shard, width)
    if rp > shard:
        dw = jnp.pad(dw, ((0, 0), (0, 0), (0, rp - shard), (0, 0)))
    tg, out, gw, gs = last(dw, sg, dn, tokens, hg, small, y, idx, hid, n, experts)
    gw, gs = gw[:, :shard], gs[:shard]
    return (
        out,
        tg,
        gs[:, experts + 2],
        jnp.swapaxes(gw[:3], 0, 1),
        gw[3].T,
        gs[:, experts + 1],
        gs[:, experts],
        gs[:, :experts],
        (gi_own + gi_sib.astype(F32))[None],
        gbi_own + little[:, :hidden],
        (gb_own + gb_sib.astype(F32))[None],
        gbb + little[:, hidden:],
    )


def solution(mesh):
    return jax.shard_map(
        body,
        mesh=mesh,
        in_specs=(
            P("dp", None),
            P("dp"),
            P("dp", None, "mp"),
            P("mp", "dp"),
            P("dp"),
            P("dp"),
            P("dp", None),
            P("dp", None, "mp"),
            P("dp", "mp"),
            P("dp", "mp", None),
            P("dp", None),
            P("dp", None),
            P("dp", None),
            P("dp", None),
        ),
        out_specs=(
            P("dp", None),
            P("dp", None),
            P("dp"),
            P("dp", None, "mp"),
            P("mp", "dp"),
            P("dp"),
            P("dp"),
            P("dp", None),
            P("dp", None, "mp"),
            P("dp", "mp"),
            P("dp", "mp", None),
            P("dp", None),
        ),
        check_vma=False,
    )
```

```python
import functools

import jax
import jax.numpy as jnp
from jax import lax
from jax.experimental import pallas as pl
from jax.experimental.pallas import tpu as pltpu
from jax.sharding import PartitionSpec as P

D = 768
HD = 64
SEQ = 197
EPS = 1e-06
F32 = jnp.float32
BF = jnp.bfloat16
MESH = pl.DeviceIdType.MESH
VMEM_LIMIT = 62 * 1024 * 1024
LINE = 4
FREE = 3


def up(value, step):
    return (value + step - 1) // step * step


SEQ_PAD = up(SEQ, 16)


def mm(left, right, cl, cr):
    return lax.dot_general(
        left, right, (((cl,), (cr,)), ((), ())), preferred_element_type=F32
    )


def norm_rows(values):
    average = jnp.mean(values, axis=-1, keepdims=True)
    centered = values - average
    inverse = lax.rsqrt(jnp.mean(centered * centered, axis=-1, keepdims=True) + EPS)
    return centered * inverse, inverse


def norm_back(grad, gain, xhat, inverse):
    scaled = grad * gain
    return inverse * (
        scaled
        - jnp.mean(scaled, axis=-1, keepdims=True)
        - xhat * jnp.mean(scaled * xhat, axis=-1, keepdims=True)
    )


def split_two(value):
    high = value.astype(BF)
    return high, (value - high.astype(F32)).astype(BF)


def whole():
    return pl.BlockSpec(memory_space=pltpu.VMEM)


def params(**more):
    return pltpu.CompilerParams(vmem_limit_bytes=VMEM_LIMIT, **more)


def greet(peers):
    barrier = pltpu.get_barrier_semaphore()
    for peer in peers:
        pl.semaphore_signal(barrier, inc=1, device_id=peer, device_id_type=MESH)
    pl.semaphore_wait(barrier, len(peers))


def remote(src, dst, send_sem, recv_sem, peer):
    return pltpu.make_async_remote_copy(
        src_ref=src, dst_ref=dst, send_sem=send_sem, recv_sem=recv_sem,
        device_id=peer, device_id_type=MESH,
    )


def slot_matrix(idx_ref, first, rows):
    number = lax.broadcasted_iota(jnp.int32, (rows, idx_ref.shape[1]), 0) + first
    hit = (number == idx_ref[0:1, :]) | (number == idx_ref[1:2, :])
    return jnp.where(hit, 1.0, 0.0).astype(BF)


def route_kernel(experts, cap, half, slots, prow_ref, pcol_ref, rt_ref, ct_ref, idx_ref, out_ref, ctp):
    lanes = rt_ref.shape[1]
    tok = ct_ref.shape[0]
    mine = lax.axis_index("mp")
    ctp[...] = jnp.zeros_like(ctp)
    ctp[0:tok, :] = ct_ref[...]
    number = lax.broadcasted_iota(jnp.int32, (experts, lanes), 0)
    hot = [jnp.where(number == rt_ref[j : j + 1, :], 1.0, 0.0) for j in range(2)]
    before = jnp.where(pcol_ref[...] < prow_ref[...], 1.0, 0.0).astype(BF)
    counts = [mm(h.astype(BF), before, 1, 0) for h in hot]
    counts[1] = counts[1] + jnp.sum(hot[0], axis=1, keepdims=True)
    for j in range(2):
        slot = jnp.sum(counts[j] * hot[j], axis=0, keepdims=True).astype(jnp.int32)
        place = slot - mine * half
        expert = rt_ref[j : j + 1, :]
        kept = (slot < cap) & (place >= 0) & (place < half) & (expert >= 0)
        idx_ref[j : j + 1, :] = jnp.where(kept, expert * slots + place, -1)

    group = 4 * slots

    def step(b, carry):
        rows = slot_matrix(idx_ref, b * group, group)
        block = mm(rows, ctp[...], 1, 0).astype(BF)
        out_ref[pl.ds(b * 4, 4)] = block.reshape(4, slots, D)
        return carry

    lax.fori_loop(0, experts // 4, step, 0)


def route(prow, pcol, rt, ct, experts, cap, half, slots):
    lanes = rt.shape[1]
    return pl.pallas_call(
        functools.partial(route_kernel, experts, cap, half, slots),
        out_shape=(
            jax.ShapeDtypeStruct((2, lanes), jnp.int32),
            jax.ShapeDtypeStruct((experts, slots, D), BF),
        ),
        in_specs=[whole()] * 4,
        out_specs=(whole(), whole()),
        scratch_shapes=[pltpu.VMEM((lanes, D), BF)],
        compiler_params=params(),
        name="route",
    )(prow, pcol, rt, ct)


def gather_kernel(n, w_ref, s_ref, wo_ref, so_ref, lsem, zs, zr, ps, pr):
    me = lax.axis_index("dp")
    plane = n // LINE
    z, q = me // plane, me % plane
    rp = w_ref.shape[1]
    zpeer = [((z + d) % LINE) * plane + q for d in range(1, LINE)]
    qpeer = [z * plane + (q + d) % plane for d in range(1, plane)]
    greet([{"dp": p} for p in zpeer + qpeer])

    def at(block):
        rows = pl.ds(pl.multiple_of(block * rp, rp), rp)
        return wo_ref.at[:, rows, :], so_ref.at[rows, :]

    own = at(me)
    local = [pltpu.make_async_copy(a, b, lsem.at[i]) for i, (a, b) in enumerate(zip((w_ref, s_ref), own))]
    for c in local:
        c.start()
    sends = []
    for d, p in enumerate(zpeer):
        for i, (a, b) in enumerate(zip((w_ref, s_ref), own)):
            c = remote(a, b, zs.at[d, i], zr.at[d, i], {"dp": p})
            c.start()
            sends.append(c)
    for d, p in enumerate(qpeer):
        for i, (a, b) in enumerate(zip((w_ref, s_ref), own)):
            c = remote(a, b, ps.at[d, 0, i], pr.at[d, 0, i], {"dp": p})
            c.start()
            sends.append(c)
    for k in range(1, LINE):
        block = at(((z + LINE - k) % LINE) * plane + q)
        for i in range(2):
            remote(block[i], block[i], zs.at[k - 1, i], zr.at[k - 1, i], {"dp": zpeer[0]}).wait_recv()
        for d, p in enumerate(qpeer):
            for i in range(2):
                c = remote(block[i], block[i], ps.at[d, k, i], pr.at[d, k, i], {"dp": p})
                c.start()
                sends.append(c)
    for d in range(1, plane):
        for k in range(LINE):
            block = at(((z + LINE - k) % LINE) * plane + (q + plane - d) % plane)
            for i in range(2):
                remote(block[i], block[i], ps.at[d - 1, k, i], pr.at[d - 1, k, i], {"dp": qpeer[0]}).wait_recv()
    for c in sends:
        c.wait_send()
    for c in local:
        c.wait()


def gather_weights(w, s, n):
    parts, rp, width = w.shape
    plane = n // LINE
    sem = pltpu.SemaphoreType.DMA
    return pl.pallas_call(
        functools.partial(gather_kernel, n),
        out_shape=(
            jax.ShapeDtypeStruct((parts, n * rp, width), BF),
            jax.ShapeDtypeStruct((n * rp, s.shape[1]), BF),
        ),
        in_specs=[whole()] * 2,
        out_specs=(whole(), whole()),
        scratch_shapes=[
            sem((2,)), sem((LINE - 1, 2)), sem((LINE - 1, 2)),
            sem((plane - 1, LINE, 2)), sem((plane - 1, LINE, 2)),
        ],
        compiler_params=params(collective_id=0, has_side_effects=True),
        name="gather_weights",
    )(w, s)


def attend_kernel(experts, tok_ref, small_ref, w_ref, qkv_ref, att_ref, part_ref, xp, pp):
    images = xp.shape[0]
    scale = HD ** (-0.5)
    gains = jnp.transpose(small_ref[...].astype(F32))
    gain = gains[experts : experts + 1, :]
    xp[:, SEQ_PAD - 16 : SEQ_PAD, :] = jnp.zeros((images, 16, D), F32)
    for i in range(images):
        xp[i, 0:SEQ, :] = tok_ref[i * SEQ : (i + 1) * SEQ, :].astype(F32)
    lane = lax.broadcasted_iota(jnp.int32, (1, 2 * HD), 1)
    masks = [jnp.where(lane // HD == h, 1.0, 0.0).astype(BF) for h in range(2)]
    valid = lax.broadcasted_iota(jnp.int32, (1, SEQ_PAD), 1) < SEQ

    def image(i, carry):
        xhat, _ = norm_rows(xp[i])
        normed = (xhat * gain).astype(BF)
        for c in range(3):
            qkv_ref[c, i] = mm(normed, w_ref[c], 1, 0).astype(BF)
        for p in range(w_ref.shape[2] // (2 * HD)):
            cols = slice(p * 2 * HD, (p + 1) * 2 * HD)
            q, k, v = (qkv_ref[c, i, :, cols] for c in range(3))
            outs = []
            for h in range(2):
                scores = mm(q * masks[h], k, 1, 1) * scale
                scores = jnp.where(valid, scores, -1e30)
                raised = jnp.exp(scores - jnp.max(scores, axis=-1, keepdims=True))
                weights = raised / jnp.sum(raised, axis=-1, keepdims=True)
                outs.append(mm(weights.astype(BF), v, 1, 0))
            att_ref[i, :, cols] = jnp.where(lane < HD, outs[0], outs[1]).astype(BF)
        pp[i] = mm(att_ref[i], w_ref[3], 1, 1)
        return carry

    lax.fori_loop(0, images, image, 0)
    for i in range(images):
        part_ref[i * SEQ : (i + 1) * SEQ, :] = pp[i, 0:SEQ, :]


def attend(tok, small, w, experts):
    images = tok.shape[0] // SEQ
    width = w.shape[2]
    return pl.pallas_call(
        functools.partial(attend_kernel, experts),
        out_shape=(
            jax.ShapeDtypeStruct((3, images, SEQ_PAD, width), BF),
            jax.ShapeDtypeStruct((images, SEQ_PAD, width), BF),
            jax.ShapeDtypeStruct(tok.shape, F32),
        ),
        in_specs=[whole()] * 3,
        out_specs=(whole(),) * 3,
        scratch_shapes=[
            pltpu.VMEM((images, SEQ_PAD, D), F32),
            pltpu.VMEM((images, SEQ_PAD, D), F32),
        ],
        compiler_params=params(),
        name="attend",
    )(tok, small, w)


def row_chunks(rows):
    return [(s, min(256, rows - s)) for s in range(0, rows, 256)]


def dispatch_kernel(
    n, half, part_ref, tok_ref, small_ref, idx_ref, hid_ref, n2_ref, prob_ref, x_ref,
    own, other, send, p2, hs, hr, ss, rs,
):
    me, mine = lax.axis_index("dp"), lax.axis_index("mp")
    tok = tok_ref.shape[0]
    slots = send.shape[1]
    experts = prob_ref.shape[0]
    sibling = {"mp": 1 - mine}
    greet([sibling] + [{"dp": (me + d) % n} for d in range(1, n)])
    own[own.shape[0] - 16 :, :] = jnp.zeros((16, D), BF)
    copies = []
    for c, (start, size) in enumerate(row_chunks(own.shape[0])):
        stop = min(start + size, tok)
        own[start:stop, :] = part_ref[start:stop, :].astype(BF)
        rows = pl.ds(start, size)
        copy = remote(own.at[rows, :], other.at[rows, :], hs.at[c], hr.at[c], sibling)
        copy.start()
        copies.append(copy)
    gains = jnp.transpose(small_ref[...].astype(F32))
    gain = gains[experts + 1 : experts + 2, :]
    bias = gains[experts + 2 : experts + 3, :]
    n2_ref[n2_ref.shape[0] - 64 :, :] = jnp.zeros((64, D), BF)
    for c, (start, size) in enumerate(row_chunks(own.shape[0])):
        stop = min(start + size, tok)
        copies[c].wait_recv()
        both = own[start:stop, :].astype(F32) + other[start:stop, :].astype(F32)
        hidden = tok_ref[start:stop, :].astype(F32) + both + bias
        hid_ref[start:stop, :] = hidden
        xhat, _ = norm_rows(hidden)
        n2_ref[start:stop, :] = (xhat * gain).astype(BF)
    logits = mm(gains[0:experts, :].astype(BF), n2_ref[...], 1, 1)
    raised = jnp.exp(logits - jnp.max(logits, axis=0, keepdims=True))
    probs = raised / jnp.sum(raised, axis=0, keepdims=True)
    prob_ref[...] = probs
    high, low = split_two(probs)
    p2[0:experts, :] = high
    p2[experts:, :] = low
    place = lax.broadcasted_iota(jnp.int32, (slots, slots), 0)
    number = lax.broadcasted_iota(jnp.int32, (2 * experts, slots), 0)

    def step(b, carry):
        hot = [slot_matrix(idx_ref, ((me + b * 4 + j) % n) * slots, slots) for j in range(4)]
        block = mm(jnp.concatenate(hot, axis=0), n2_ref[...], 1, 0)
        for j in range(4):
            d = b * 4 + j
            peer = (me + d) % n
            gates = mm(p2[...], hot[j], 1, 1)
            row_high = jnp.sum(jnp.where(number == peer, gates, 0.0), axis=0, keepdims=True)
            row_low = jnp.sum(jnp.where(number == peer + experts, gates, 0.0), axis=0, keepdims=True)
            rows = block[j * slots : (j + 1) * slots, :]
            left = jnp.where(place == half, row_high, jnp.where(place == half + 1, row_low, rows[:, 0:slots]))
            send[d, :, :] = rows.astype(BF)
            send[d, :, 0:slots] = left.astype(BF)

            @pl.when(d > 0)
            def _():
                remote(send.at[d], x_ref.at[d], ss.at[d], rs.at[d], {"dp": peer}).start()

        return carry

    lax.fori_loop(0, n // 4, step, 0)
    x_ref[0] = send[0]

    def finish(d, carry):
        source = (me + n - d) % n
        remote(send.at[d], x_ref.at[d], ss.at[d], rs.at[d], {"dp": source}).wait()
        return carry

    lax.fori_loop(1, n, finish, 0)
    for copy in copies:
        copy.wait_send()


def dispatch(part, tok, small, idx, n, experts, half, slots):
    lanes = idx.shape[1]
    tr = up(tok.shape[0], 16)
    sem = pltpu.SemaphoreType.DMA
    chunks = len(row_chunks(tr))
    return pl.pallas_call(
        functools.partial(dispatch_kernel, n, half),
        out_shape=(
            jax.ShapeDtypeStruct(tok.shape, F32),
            jax.ShapeDtypeStruct((lanes, D), BF),
            jax.ShapeDtypeStruct((experts, lanes), F32),
            jax.ShapeDtypeStruct((n, slots, D), BF),
        ),
        in_specs=[whole()] * 4,
        out_specs=(whole(),) * 4,
        scratch_shapes=[
            pltpu.VMEM((tr, D), BF),
            pltpu.VMEM((tr, D), BF),
            pltpu.VMEM((n, slots, D), BF),
            pltpu.VMEM((2 * experts, lanes), BF),
            sem((chunks,)), sem((chunks,)), sem((n,)), sem((n,)),
        ],
        compiler_params=params(collective_id=1, has_side_effects=True),
        name="dispatch",
    )(part, tok, small, idx)


def expert_kernel(
    n, half, experts,
    x_ref, ct_ref, wi_own, wi_sib, wb_own, wb_sib, bi_own, bi_sib, bb_ref,
    idx_ref, prob_ref, hid_ref, tok_ct, small_ref,
    hg_ref, sg_ref, y_ref, gi_ref, gi_in, gb_ref, gb_in, little_ref, little_in,
    vi_own, vi_sib, vb_own, vb_sib, g_s, act_own, act_sib, dp_own, dp_sib, dx_s, back, acc, other,
    ct_s, y_s, stage, gp, gp_other,
    lsem, ysem, gsem, ss, rs, hs, hr, ms, mr,
):
    me, mine = lax.axis_index("dp"), lax.axis_index("mp")
    sibling = {"mp": 1 - mine}
    slots = x_ref.shape[1]
    tok = tok_ct.shape[0]
    hidden = wi_own.shape[1]
    group = 4 * slots
    batches = n // 4
    loads = [
        pltpu.make_async_copy(a, b, lsem.at[i])
        for i, (a, b) in enumerate(
            ((wi_own, vi_own), (wb_own, vb_own), (wi_sib, vi_sib), (wb_sib, vb_sib), (hid_ref, hg_ref))
        )
    ]
    for c in loads:
        c.start()
    greet([sibling] + [{"dp": (me + d) % n} for d in range(1, n)])
    little_ref[...] = jnp.zeros_like(little_ref)

    def cts(b, j):
        return pltpu.make_async_copy(ct_ref.at[(me + n - b * 4 - j) % n], ct_s.at[j], ysem.at[0, j])

    def ys(b, j):
        return pltpu.make_async_copy(y_s.at[j], y_ref.at[(me + n - b * 4 - j) % n], ysem.at[1, j])

    for j in range(4):
        cts(0, j).start()
    for c in loads[:4]:
        c.wait()
    chunk = 768
    row = lax.broadcasted_iota(jnp.int32, (group, 16), 0)
    number = lax.broadcasted_iota(jnp.int32, (group, 16), 1)
    member = jnp.where(row // slots == number, 1.0, 0.0).astype(BF)
    spot = lax.broadcasted_iota(jnp.int32, (group, 128), 0) % slots
    here = spot == lax.broadcasted_iota(jnp.int32, (group, 128), 1)
    row_t = lax.broadcasted_iota(jnp.int32, (16, group), 1)
    number_t = lax.broadcasted_iota(jnp.int32, (16, group), 0)
    pick = jnp.where(
        (row_t == number_t * slots + half) | (row_t == number_t * slots + half + 1), 1.0, 0.0
    ).astype(BF)
    member_t = jnp.where(row_t // slots == number_t, 1.0, 0.0).astype(BF)
    puts = [jnp.where(row == number * slots + half + i, 1.0, 0.0).astype(BF) for i in range(2)]

    def batch(b, carry):
        at = pl.ds(pl.multiple_of(b * group, 16), group)
        x = x_ref[pl.ds(b * 4, 4)].reshape(group, D)
        high, low = split_two(mm(pick, x[:, 0:128], 1, 0))
        wide = mm(member, high, 1, 0) + mm(member, low, 1, 0)
        gate = jnp.sum(jnp.where(here, wide, 0.0), axis=1, keepdims=True)
        for j in range(4):
            cts(b, j).wait()
        g_s[at, :] = (gate * ct_s[...].reshape(group, D).astype(F32)).astype(BF)
        little_ref[0:1, 2 * hidden :] += jnp.sum(g_s[at, :].astype(F32), axis=0, keepdims=True)
        for part, (vi, vb, bi, acts, dps) in enumerate(
            ((vi_own, vb_own, bi_own, act_own, dp_own), (vi_sib, vb_sib, bi_sib, act_sib, dp_sib))
        ):
            for c in range(hidden // chunk):
                cols = slice(c * chunk, (c + 1) * chunk)
                pre = mm(x_ref[pl.ds(b * 4, 4)].reshape(group, D), vi[:, cols], 1, 0) + bi[:, cols].astype(F32)
                phi = 0.5 * (1.0 + lax.erf(pre * (0.5**0.5)))
                slope = phi + pre * (jnp.exp(-0.5 * pre * pre) * ((2.0 * jnp.pi) ** -0.5))
                acts[at, cols] = (pre * phi).astype(BF)
                grad = (mm(g_s[at, :], vb[cols, :], 1, 1) * slope).astype(BF)
                dps[at, cols] = grad
                place = slice(part * hidden + c * chunk, part * hidden + (c + 1) * chunk)
                little_ref[0:1, place] += jnp.sum(grad.astype(F32), axis=0, keepdims=True)
        dx = mm(dp_own[at, :], vi_own[...], 1, 1) + mm(dp_sib[at, :], vi_sib[...], 1, 1)
        y = mm(act_own[at, :], vb_own[...], 1, 0) + mm(act_sib[at, :], vb_sib[...], 1, 0)
        y = (y + bb_ref[...].astype(F32)).astype(BF).astype(F32)
        dots = jnp.sum(ct_s[...].reshape(group, D).astype(F32) * y, axis=1, keepdims=True)
        high, low = split_two(jnp.where(here, dots, 0.0))
        high, low = mm(member_t, high, 1, 0).astype(BF), mm(member_t, low, 1, 0).astype(BF)
        left = dx[:, 0:128] + mm(puts[0], high, 1, 0) + mm(puts[1], low, 1, 0)
        dx = jnp.concatenate([left, dx[:, 128:]], axis=1)
        dx_s[pl.ds(b * 4, 4)] = dx.astype(BF).reshape(4, slots, D)
        for j in range(4):
            d = b * 4 + j

            @pl.when(d > 0)
            def _():
                remote(dx_s.at[d], back.at[d], ss.at[d], rs.at[d], {"dp": (me + n - d) % n}).start()

        @pl.when(b > 0)
        def _():
            for j in range(4):
                ys(b - 1, j).wait()

        y_s[...] = (gate * y).astype(BF).reshape(4, slots, D)
        for j in range(4):
            ys(b, j).start()

        @pl.when(b + 1 < batches)
        def _():
            for j in range(4):
                cts(b + 1, j).start()

        return carry

    lax.fori_loop(0, batches, batch, 0)
    back[0] = dx_s[0]
    little = remote(little_ref, little_in, ms.at[2], mr.at[2], sibling)
    little.start()

    rows_all = n * slots
    steps = 3
    size = D // steps
    wide = hidden // 2
    swaps = []

    def out_i(r, c):
        return pltpu.make_async_copy(
            stage.at[r % 2, c * size : (c + 1) * size, :],
            gi_ref.at[r * size : (r + 1) * size, c * wide : (c + 1) * wide], gsem.at[c, r],
        )

    def out_b(r):
        return pltpu.make_async_copy(
            stage.at[r % 2], gb_ref.at[r * 2 * size : (r + 1) * 2 * size, :], gsem.at[2, r]
        )

    for r in range(steps):
        at = slice(r * size, (r + 1) * size)
        left = x_ref[:, :, at].reshape(rows_all, size)
        vi_sib[at, :] = mm(left, dp_sib[...], 0, 0).astype(BF)
        for c in range(2):
            if r >= 2:
                out_i(r - 2, c).wait()
            stage[r % 2, c * size : (c + 1) * size, :] = mm(left, dp_own[:, c * wide : (c + 1) * wide], 0, 0)
            out_i(r, c).start()
    copy = remote(vi_sib, gi_in, ms.at[0], mr.at[0], sibling)
    copy.start()
    swaps.append(copy)

    acc[...] = jnp.zeros_like(acc)
    gp[...] = jnp.zeros_like(gp)
    place = lax.broadcasted_iota(jnp.int32, (slots, 128), 0)
    count = lax.broadcasted_iota(jnp.int32, (experts, slots), 0)

    def combine(b, carry):
        hot = []
        for j in range(4):
            d = b * 4 + j
            source = (me + d) % n

            @pl.when(d > 0)
            def _():
                remote(dx_s.at[d], back.at[d], ss.at[d], rs.at[d], {"dp": source}).wait_recv()

            hot.append(slot_matrix(idx_ref, source * slots, slots))
            extra = back[d, :, 0:128].astype(F32)
            high = jnp.sum(jnp.where(place == half, extra, 0.0), axis=0, keepdims=True)[:, 0:slots]
            low = jnp.sum(jnp.where(place == half + 1, extra, 0.0), axis=0, keepdims=True)[:, 0:slots]
            for value in (high, low):
                gp[...] += mm(jnp.where(count == source, value, 0.0).astype(BF), hot[j], 1, 0)
        block = back[pl.ds(b * 4, 4)].reshape(group, D)
        acc[...] += mm(jnp.concatenate(hot, axis=0), block, 0, 0)
        return carry

    lax.fori_loop(0, batches // 2, combine, 0)
    for r in range(steps):
        at = slice(r * 2 * size, (r + 1) * 2 * size)
        vb_sib[at, :] = mm(act_sib[:, at], g_s[...], 0, 0).astype(BF)
        if r == 0:
            for c in range(2):
                out_i(1, c).wait()
                out_i(2, c).wait()
        if r >= 2:
            out_b(r - 2).wait()
        stage[r % 2] = mm(act_own[:, at], g_s[...], 0, 0)
        out_b(r).start()
    copy = remote(vb_sib, gb_in, ms.at[1], mr.at[1], sibling)
    copy.start()
    swaps.append(copy)
    lax.fori_loop(batches // 2, batches, combine, 0)

    copies = []
    own = g_s
    own[other.shape[0] - 16 : other.shape[0], :] = jnp.zeros((16, D), BF)
    for c, (start, length) in enumerate(row_chunks(other.shape[0])):
        stop = min(start + length, tok)
        own[start:stop, :] = acc[start:stop, :].astype(BF)
        rows = pl.ds(start, length)
        copy = remote(own.at[rows, :], other.at[rows, :], hs.at[c], hr.at[c], sibling)
        copy.start()
        copies.append(copy)
    copy = remote(gp, gp_other, hs.at[len(copies)], hr.at[len(copies)], sibling)
    copy.start()
    copy.wait()
    probs = prob_ref[...]
    grad_probs = gp[...] + gp_other[...]
    logits = (probs * (grad_probs - jnp.sum(grad_probs * probs, axis=0, keepdims=True))).astype(BF)
    gains = jnp.transpose(small_ref[...].astype(F32))
    gain = gains[experts + 1 : experts + 2, :]
    acc[...] = mm(logits, gains[0:experts, :].astype(BF), 0, 0)
    sg_ref[...] = jnp.zeros_like(sg_ref)
    gain_sum = jnp.zeros((1, D), F32)
    bias_sum = jnp.zeros((1, D), F32)
    lanes = acc.shape[0]
    act_own[lanes - 64 : lanes, 0:D] = jnp.zeros((64, D), BF)
    loads[4].wait()
    for c, (start, length) in enumerate(row_chunks(other.shape[0])):
        stop = min(start + length, tok)
        copies[c].wait_recv()
        grad = own[start:stop, :].astype(F32) + other[start:stop, :].astype(F32) + acc[start:stop, :]
        xhat, inverse = norm_rows(hg_ref[start:stop, :])
        act_own[start:stop, 0:D] = (xhat * gain).astype(BF)
        hidden_grad = tok_ct[start:stop, :].astype(F32) + norm_back(grad, gain, xhat, inverse)
        hg_ref[start:stop, :] = hidden_grad
        gain_sum += jnp.sum(grad * xhat, axis=0, keepdims=True)
        bias_sum += jnp.sum(hidden_grad, axis=0, keepdims=True)
    sg_ref[0:experts, :] = mm(logits, act_own[0:lanes, 0:D], 1, 0)
    sg_ref[experts : experts + 1, :] = gain_sum
    sg_ref[experts + 1 : experts + 2, :] = bias_sum
    for copy in copies:
        copy.wait_send()

    def finish(d, carry):
        remote(dx_s.at[d], back.at[d], ss.at[d], rs.at[d], {"dp": (me + n - d) % n}).wait_send()
        return carry

    lax.fori_loop(1, n, finish, 0)
    for j in range(4):
        ys(batches - 1, j).wait()
    for r in range(1, steps):
        out_b(r).wait()
    little.wait()
    for copy in swaps:
        copy.wait()


def expert(x, ct_rows, wi, wb, bi, bb, idx, probs, hid, ct, small, n, half):
    slots = x.shape[1]
    rows = n * slots
    hidden = wi[0].shape[1]
    experts, lanes = probs.shape
    tr = up(ct.shape[0], 16)
    chunks = len(row_chunks(tr))
    shape = jax.ShapeDtypeStruct
    sem = pltpu.SemaphoreType.DMA
    vmem = pltpu.VMEM
    far = pl.BlockSpec(memory_space=pl.ANY)
    return pl.pallas_call(
        functools.partial(expert_kernel, n, half, experts),
        out_shape=(
            shape(ct.shape, F32), shape((up(experts + 3, 8), D), F32), shape((n, slots, D), BF),
            shape((D, hidden), F32), shape((D, hidden), BF),
            shape((hidden, D), F32), shape((hidden, D), BF),
            shape((8, 2 * hidden + D), F32), shape((8, 2 * hidden + D), F32),
        ),
        in_specs=[whole(), far, far, far, far, far, whole(), whole(), whole(),
                  whole(), whole(), far, whole(), whole()],
        out_specs=(whole(), whole(), far, far, far, far, far, whole(), whole()),
        scratch_shapes=[
            vmem((D, hidden), BF), vmem((D, hidden), BF), vmem((hidden, D), BF), vmem((hidden, D), BF),
            vmem((rows, D), BF),
            vmem((rows, hidden), BF), vmem((rows, hidden), BF),
            vmem((rows, hidden), BF), vmem((rows, hidden), BF),
            vmem((n, slots, D), BF), vmem((n, slots, D), BF),
            vmem((lanes, D), F32), vmem((tr, D), BF),
            vmem((4, slots, D), BF), vmem((4, slots, D), BF),
            vmem((2, hidden // 3, D), F32),
            vmem((experts, lanes), F32), vmem((experts, lanes), F32),
            sem((5,)), sem((2, 4)), sem((3, 3)), sem((n,)), sem((n,)),
            sem((chunks + 1,)), sem((chunks + 1,)), sem((3,)), sem((3,)),
        ],
        compiler_params=params(collective_id=2, has_side_effects=True),
        name="expert",
    )(x, ct_rows, wi[0], wi[1], wb[0], wb[1], bi[0], bi[1], bb, idx, probs, hid, ct, small)


def attend_back_kernel(
    experts, hg_ref, tok_ref, small_ref, w_ref, qkv_ref, att_ref, gi_ref, gi_in, gb_ref, gb_in, little_ref, little_in,
    dn_ref, dw_ref, gi_out, gb_out, gbi_out, gbb_out,
    normed, low, dqkv, pp,
):
    images = normed.shape[0]
    scale = HD ** (-0.5)
    step = pl.program_id(0)
    gi_out[...] = gi_ref[...] + gi_in[...].astype(F32)
    gb_out[...] = gb_ref[...] + gb_in[...].astype(F32)

    @pl.when(step == 0)
    def _():
        hidden = gbi_out.shape[1]
        gbi_out[...] = little_ref[0:1, 0:hidden] + little_in[0:1, hidden : 2 * hidden]
        gbb_out[...] = little_ref[0:1, 2 * hidden :] + little_in[0:1, 2 * hidden :]
        pp[:, SEQ_PAD - 16 : SEQ_PAD, :] = jnp.zeros((images, 16, D), F32)
        for i in range(images):
            pp[i, 0:SEQ, :] = hg_ref[i * SEQ : (i + 1) * SEQ, :]
        low[...] = pp[...].astype(BF)
        for i in range(images):
            pp[i, 0:SEQ, :] = tok_ref[i * SEQ : (i + 1) * SEQ, :].astype(F32)

    @pl.when(step < images)
    def _():
        i = step
        gains = jnp.transpose(small_ref[...].astype(F32))
        gain = gains[experts : experts + 1, :]
        lane = lax.broadcasted_iota(jnp.int32, (1, 2 * HD), 1)
        masks = [jnp.where(lane // HD == h, 1.0, 0.0).astype(BF) for h in range(2)]
        valid = lax.broadcasted_iota(jnp.int32, (1, SEQ_PAD), 1) < SEQ
        xhat, _ = norm_rows(pp[i])
        normed[i] = (xhat * gain).astype(BF)
        grad_att = mm(low[i], w_ref[3], 1, 0).astype(BF)
        for p in range(w_ref.shape[2] // (2 * HD)):
            cols = slice(p * 2 * HD, (p + 1) * 2 * HD)
            q, k, v = (qkv_ref[c, i, :, cols] for c in range(3))
            pair = grad_att[:, cols]
            grads = []
            for h in range(2):
                scores = mm(q * masks[h], k, 1, 1) * scale
                scores = jnp.where(valid, scores, -1e30)
                raised = jnp.exp(scores - jnp.max(scores, axis=-1, keepdims=True))
                weights = raised / jnp.sum(raised, axis=-1, keepdims=True)
                grad_weights = mm(pair * masks[h], v, 1, 1)
                grad_scores = weights * (
                    grad_weights - jnp.sum(grad_weights * weights, axis=-1, keepdims=True)
                )
                scores_low = grad_scores.astype(BF)
                grads.append((
                    mm(scores_low, k, 1, 0) * scale,
                    mm(scores_low, q, 0, 0) * scale,
                    mm(weights.astype(BF), pair, 0, 0),
                ))
            for c in range(3):
                dqkv[c, i, :, cols] = jnp.where(lane < HD, grads[0][c], grads[1][c]).astype(BF)
        total = mm(dqkv[0, i], w_ref[0], 1, 1)
        for c in range(1, 3):
            total += mm(dqkv[c, i], w_ref[c], 1, 1)
        pp[i] = total

    @pl.when(step == images)
    def _():
        for i in range(images):
            dn_ref[i * SEQ : (i + 1) * SEQ, :] = pp[i, 0:SEQ, :]
        rows = images * SEQ_PAD

        def weight(r, carry):
            at = pl.ds(pl.multiple_of(r * 256, 256), 256)
            left = normed[:, :, at].reshape(rows, 256)
            for c in range(3):
                dw_ref[c, at, :] = mm(left, dqkv[c].reshape(rows, -1), 0, 0).astype(BF)
            left = low[:, :, at].reshape(rows, 256)
            dw_ref[3, at, :] = mm(left, att_ref[...].reshape(rows, -1), 0, 0).astype(BF)
            return carry

        lax.fori_loop(0, D // 256, weight, 0)


def attend_back(hg, tok, small, w, qkv, att, gi, gi_in, gb, gb_in, little, little_in, experts):
    images = tok.shape[0] // SEQ
    width = w.shape[2]
    steps = images + 1
    hidden = gi.shape[1]
    line_i = pl.BlockSpec((gi.shape[0] // steps, hidden), lambda k: (k, 0))
    line_b = pl.BlockSpec((hidden // steps, D), lambda k: (k, 0))
    return pl.pallas_call(
        functools.partial(attend_back_kernel, experts),
        grid=(steps,),
        out_shape=(
            jax.ShapeDtypeStruct(tok.shape, F32),
            jax.ShapeDtypeStruct((4, D, width), BF),
            jax.ShapeDtypeStruct(gi.shape, F32),
            jax.ShapeDtypeStruct(gb.shape, F32),
            jax.ShapeDtypeStruct((1, hidden), F32),
            jax.ShapeDtypeStruct((1, D), F32),
        ),
        in_specs=[whole()] * 6 + [line_i, line_i, line_b, line_b, whole(), whole()],
        out_specs=(whole(), whole(), line_i, line_b, whole(), whole()),
        scratch_shapes=[
            pltpu.VMEM((images, SEQ_PAD, D), BF),
            pltpu.VMEM((images, SEQ_PAD, D), BF),
            pltpu.VMEM((3, images, SEQ_PAD, width), BF),
            pltpu.VMEM((images, SEQ_PAD, D), F32),
        ],
        compiler_params=params(dimension_semantics=("arbitrary",)),
        name="attend_back",
    )(hg, tok, small, w, qkv, att, gi, gi_in, gb, gb_in, little, little_in)


def last_kernel(
    n, experts, dw_ref, sg_ref, dn_ref, tok_ref, hg_ref, small_ref, y_ref, idx_ref, hid_ref,
    tg_ref, out_ref, gw_ref, gs_ref,
    own, other, mix, mix_other, sm, r1, q1, s1, t1, r2, q2, acc, hs, hr, as_, ar, bs, br,
):
    me, mine = lax.axis_index("dp"), lax.axis_index("mp")
    plane = n // LINE
    z, q = me // plane, me % plane
    tok = tok_ref.shape[0]
    rp = dw_ref.shape[3]
    sibling = {"mp": 1 - mine}
    zpeer = [((z + d) % LINE) * plane + q for d in range(1, LINE)]
    qpeer = [z * plane + (q + d) % plane for d in range(1, plane)]
    greet([sibling] + [{"dp": p} for p in zpeer + qpeer])
    sends = []
    for d, p in enumerate(qpeer):
        c = remote(dw_ref.at[:, :, (q + d + 1) % plane], r1.at[d], as_.at[d, 0], ar.at[d, 0], {"dp": p})
        c.start()
        sends.append(c)
    copies = []
    own[own.shape[0] - 16 :, :] = jnp.zeros((16, D), BF)
    for c, (start, size) in enumerate(row_chunks(own.shape[0])):
        stop = min(start + size, tok)
        own[start:stop, :] = dn_ref[start:stop, :].astype(BF)
        rows = pl.ds(start, size)
        copy = remote(own.at[rows, :], other.at[rows, :], hs.at[c], hr.at[c], sibling)
        copy.start()
        copies.append(copy)
    gains = jnp.transpose(small_ref[...].astype(F32))
    gain = gains[experts : experts + 1, :]
    gain_sum = jnp.zeros((1, D), F32)
    for c, (start, size) in enumerate(row_chunks(own.shape[0])):
        stop = min(start + size, tok)
        copies[c].wait()
        grad = own[start:stop, :].astype(F32) + other[start:stop, :].astype(F32)
        xhat, inverse = norm_rows(tok_ref[start:stop, :].astype(F32))
        tg_ref[start:stop, :] = (hg_ref[start:stop, :] + norm_back(grad, gain, xhat, inverse)).astype(BF)
        gain_sum += jnp.sum(grad * xhat, axis=0, keepdims=True)
    row = lax.broadcasted_iota(jnp.int32, sg_ref.shape, 0)
    rows = jnp.where(row == experts + 2, gain_sum, sg_ref[...])
    rows = jnp.concatenate([rows, jnp.zeros((128 - rows.shape[0], D), F32)], axis=0)
    turned = jnp.transpose(rows).astype(BF)
    real = turned.shape[0] // n
    for b in range(n):
        at = (b // plane, b % plane)
        if real < rp:
            sm[at[0], at[1]] = jnp.zeros((rp, 128), BF)
        sm[at[0], at[1], 0:real, :] = turned[b * real : (b + 1) * real, :]
    for d, p in enumerate(qpeer):
        c = remote(sm.at[:, (q + d + 1) % plane], q1.at[d], as_.at[d, 1], ar.at[d, 1], {"dp": p})
        c.start()
        sends.append(c)
    slots = y_ref.shape[1]
    acc[...] = jnp.zeros_like(acc)

    def step(b, carry):
        hot = slot_matrix(idx_ref, b * 4 * slots, 4 * slots)
        acc[...] += mm(hot, y_ref[pl.ds(b * 4, 4)].reshape(4 * slots, D), 0, 0)
        return carry

    lax.fori_loop(0, n // 4, step, 0)
    mix[mix.shape[0] - 16 :, :] = jnp.zeros((16, D), BF)
    base = len(copies)
    late = []
    for c, (start, size) in enumerate(row_chunks(own.shape[0])):
        stop = min(start + size, tok)
        mix[start:stop, :] = acc[start:stop, :].astype(BF)
        rows = pl.ds(start, size)
        copy = remote(mix.at[rows, :], mix_other.at[rows, :], hs.at[base + c], hr.at[base + c], sibling)
        copy.start()
        late.append(copy)
    for c, (start, size) in enumerate(row_chunks(own.shape[0])):
        stop = min(start + size, tok)
        late[c].wait()
        both = mix[start:stop, :].astype(F32) + mix_other[start:stop, :].astype(F32)
        out_ref[start:stop, :] = (hid_ref[start:stop, :] + both).astype(BF)
    for d in range(plane - 1):
        remote(dw_ref.at[:, :, 0], r1.at[d], as_.at[d, 0], ar.at[d, 0], {"dp": qpeer[0]}).wait_recv()
        remote(sm.at[:, 0], q1.at[d], as_.at[d, 1], ar.at[d, 1], {"dp": qpeer[0]}).wait_recv()
    for b in range(LINE):
        value = dw_ref[:, b, q].astype(F32)
        little = sm[b, q].astype(F32)
        for d in range(plane - 1):
            value += r1[d, :, b].astype(F32)
            little += q1[d, b].astype(F32)
        s1[b] = value.astype(BF)
        t1[b] = little.astype(BF)
    for d, p in enumerate(zpeer):
        to = (z + d + 1) % LINE
        for i, (a, b) in enumerate(((s1, r2), (t1, q2))):
            c = remote(a.at[to], b.at[d], bs.at[d, i], br.at[d, i], {"dp": p})
            c.start()
            sends.append(c)
    value = s1[z].astype(F32)
    little = t1[z].astype(F32)
    for d in range(LINE - 1):
        for i, (a, b) in enumerate(((s1, r2), (t1, q2))):
            remote(a.at[0], b.at[d], bs.at[d, i], br.at[d, i], {"dp": zpeer[0]}).wait_recv()
        value += r2[d].astype(F32)
        little += q2[d].astype(F32)
    gw_ref[...] = value
    gs_ref[...] = little
    for c in sends:
        c.wait_send()


def last(dw, sg, dn, tok, hg, small, y, idx, hid, n, experts):
    parts, _, rows, width = dw.shape
    rp = rows
    plane = n // LINE
    dw = dw.reshape(parts, LINE, plane, rp, width)
    tr = up(tok.shape[0], 16)
    chunks = len(row_chunks(tr))
    sem = pltpu.SemaphoreType.DMA
    vmem = pltpu.VMEM
    return pl.pallas_call(
        functools.partial(last_kernel, n, experts),
        out_shape=(
            jax.ShapeDtypeStruct(tok.shape, BF),
            jax.ShapeDtypeStruct(tok.shape, BF),
            jax.ShapeDtypeStruct((parts, rp, width), F32),
            jax.ShapeDtypeStruct((rp, 128), F32),
        ),
        in_specs=[whole()] * 9,
        out_specs=(whole(),) * 4,
        scratch_shapes=[
            vmem((tr, D), BF), vmem((tr, D), BF), vmem((tr, D), BF), vmem((tr, D), BF),
            vmem((LINE, plane, rp, 128), BF),
            vmem((plane - 1, parts, LINE, rp, width), BF),
            vmem((plane - 1, LINE, rp, 128), BF),
            vmem((LINE, parts, rp, width), BF),
            vmem((LINE, rp, 128), BF),
            vmem((LINE - 1, parts, rp, width), BF),
            vmem((LINE - 1, rp, 128), BF),
            vmem((idx.shape[1], D), F32),
            sem((2 * chunks,)), sem((2 * chunks,)),
            sem((plane - 1, 2)), sem((plane - 1, 2)), sem((LINE - 1, 2)), sem((LINE - 1, 2)),
        ],
        compiler_params=params(collective_id=3, has_side_effects=True),
        name="last",
    )(dw, sg, dn, tok, hg, small, y, idx, hid)


def body(
    tokens, ln1_gain, w_qkv, w_out, out_bias, ln2_gain, router, w_in, in_bias,
    w_back, back_bias, routes, priority, cotangent,
):
    n = lax.axis_size("dp")
    tok = tokens.shape[0]
    experts = router.shape[1]
    cap = max(2, 5 * tok // (2 * experts))
    half = (cap + 1) // 2
    slots = up(half + FREE, 16)
    lanes = up(tok, 128)
    shard, width = w_qkv.shape[0], w_qkv.shape[2]
    rp = up(shard, 16)
    swap = [(0, 1), (1, 0)]

    wi = (w_in[0], lax.ppermute(w_in[0], "mp", swap))
    wb = (w_back[0], lax.ppermute(w_back[0], "mp", swap))
    bi = (in_bias, lax.ppermute(in_bias, "mp", swap))

    rt = jnp.pad(routes.T, ((0, 0), (0, lanes - tok)), constant_values=-1)
    ranks = jnp.pad(priority[0], (0, lanes - tok), constant_values=1 << 20)
    idx, ct_rows = route(ranks[None, :], ranks[:, None], rt, cotangent, experts, cap, half, slots)

    weights = jnp.concatenate([jnp.swapaxes(w_qkv, 0, 1), w_out.T[None]], axis=0)
    small = jnp.concatenate(
        [router, ln1_gain[:, None], ln2_gain[:, None], out_bias[:, None],
         jnp.zeros((shard, 128 - experts - 3), BF)], axis=1,
    )
    if rp > shard:
        weights = jnp.pad(weights, ((0, 0), (0, rp - shard), (0, 0)))
        small = jnp.pad(small, ((0, rp - shard), (0, 0)))
    weights, small = gather_weights(weights, small, n)
    if rp > shard:
        weights = weights.reshape(4, n, rp, width)[:, :, :shard].reshape(4, D, width)
        small = small.reshape(n, rp, 128)[:, :shard].reshape(D, 128)

    ct_rows, small = lax.optimization_barrier((ct_rows, small))
    ct_rows = lax.all_to_all(ct_rows, "dp", split_axis=0, concat_axis=0, tiled=True)

    qkv, att, part = attend(tokens, small, weights, experts)
    hid, n2, probs, x = dispatch(part, tokens, small, idx, n, experts, half, slots)
    hg, sg, y, gi, gi_in, gb, gb_in, little, little_in = expert(
        x, ct_rows, wi, wb, bi, back_bias, idx, probs, hid, cotangent, small, n, half
    )
    y = lax.all_to_all(y, "dp", split_axis=0, concat_axis=0, tiled=True)
    dn, dw, gi, gb, gbi, gbb = attend_back(
        hg, tokens, small, weights, qkv, att, gi, gi_in, gb, gb_in, little, little_in, experts
    )
    dw = dw.reshape(4, n, shard, width)
    if rp > shard:
        dw = jnp.pad(dw, ((0, 0), (0, 0), (0, rp - shard), (0, 0)))
    tg, out, gw, gs = last(dw, sg, dn, tokens, hg, small, y, idx, hid, n, experts)
    gw, gs = gw[:, :shard], gs[:shard]
    return (
        out,
        tg,
        gs[:, experts + 2],
        jnp.swapaxes(gw[:3], 0, 1),
        gw[3].T,
        gs[:, experts + 1],
        gs[:, experts],
        gs[:, :experts],
        gi[None],
        gbi,
        gb[None],
        gbb,
    )


def solution(mesh):
    return jax.shard_map(
        body,
        mesh=mesh,
        in_specs=(
            P("dp", None),
            P("dp"),
            P("dp", None, "mp"),
            P("mp", "dp"),
            P("dp"),
            P("dp"),
            P("dp", None),
            P("dp", None, "mp"),
            P("dp", "mp"),
            P("dp", "mp", None),
            P("dp", None),
            P("dp", None),
            P("dp", None),
            P("dp", None),
        ),
        out_specs=(
            P("dp", None),
            P("dp", None),
            P("dp"),
            P("dp", None, "mp"),
            P("mp", "dp"),
            P("dp"),
            P("dp"),
            P("dp", None),
            P("dp", None, "mp"),
            P("dp", "mp"),
            P("dp", "mp", None),
            P("dp", None),
        ),
        check_vma=False,
    )
```

```python
import functools

import jax
import jax.numpy as jnp
from jax import lax
from jax.experimental import pallas as pl
from jax.experimental.pallas import tpu as pltpu
from jax.sharding import PartitionSpec as P

D = 768
HD = 64
SEQ = 197
EPS = 1e-06
F32 = jnp.float32
BF = jnp.bfloat16
MESH = pl.DeviceIdType.MESH
VMEM_LIMIT = 62 * 1024 * 1024
LINE = 4
FREE = 3


def up(value, step):
    return (value + step - 1) // step * step


SEQ_PAD = up(SEQ, 16)


def mm(left, right, cl, cr):
    return lax.dot_general(
        left, right, (((cl,), (cr,)), ((), ())), preferred_element_type=F32
    )


def norm_rows(values):
    average = jnp.mean(values, axis=-1, keepdims=True)
    centered = values - average
    inverse = lax.rsqrt(jnp.mean(centered * centered, axis=-1, keepdims=True) + EPS)
    return centered * inverse, inverse


def norm_back(grad, gain, xhat, inverse):
    scaled = grad * gain
    return inverse * (
        scaled
        - jnp.mean(scaled, axis=-1, keepdims=True)
        - xhat * jnp.mean(scaled * xhat, axis=-1, keepdims=True)
    )


def split_two(value):
    high = value.astype(BF)
    return high, (value - high.astype(F32)).astype(BF)


def whole():
    return pl.BlockSpec(memory_space=pltpu.VMEM)


def params(**more):
    return pltpu.CompilerParams(vmem_limit_bytes=VMEM_LIMIT, **more)


def greet(peers):
    barrier = pltpu.get_barrier_semaphore()
    for peer in peers:
        pl.semaphore_signal(barrier, inc=1, device_id=peer, device_id_type=MESH)
    pl.semaphore_wait(barrier, len(peers))


def remote(src, dst, send_sem, recv_sem, peer):
    return pltpu.make_async_remote_copy(
        src_ref=src, dst_ref=dst, send_sem=send_sem, recv_sem=recv_sem,
        device_id=peer, device_id_type=MESH,
    )


def partner(me, n, place, sign=1):
    plane = n // LINE
    groups = plane // 4
    z, q = me // plane, me % plane
    step, j = place // 4, place % 4
    turn, g = step // groups, step % groups
    k = 2 * (1 - turn % 2) + turn // 2
    line = (z // 2 + k // 2) % 2 * 2 + (z % 2 + k % 2) % 2
    return line * plane + (q + plane + sign * (g * 4 + j)) % plane


def slot_matrix(idx_ref, first, rows):
    number = lax.broadcasted_iota(jnp.int32, (rows, idx_ref.shape[1]), 0) + first
    hit = (number == idx_ref[0:1, :]) | (number == idx_ref[1:2, :])
    return jnp.where(hit, 1.0, 0.0).astype(BF)


def begin_kernel(
    n, cap, half, slots,
    wq_ref, wout_ref, rows_ref, gain_refs, rt_ref, rank_ref, ct_ref, tok_ref,
    wo_ref, so_ref, idx_ref, ctx_ref, qkv_ref, att_ref, part_ref,
    gw, gs, mine_w, mine_s, info, ctp, send, xp, pp,
    zs, zr, ps, pr, cs, cr, lsem,
):
    me, mine = lax.axis_index("dp"), lax.axis_index("mp")
    plane = n // LINE
    z, q = me // plane, me % plane
    experts, shard = rows_ref.shape
    tok = tok_ref.shape[0]
    lanes = idx_ref.shape[1]
    rp = mine_w.shape[1]
    zpeer = [((z + d) % LINE) * plane + q for d in range(1, LINE)]
    qpeer = [z * plane + (q + d) % plane for d in range(1, plane)]
    full_w, full_s = (wo_ref, so_ref) if rp == shard else (gw, gs)

    if rp > shard:
        mine_w[...] = jnp.zeros_like(mine_w)
    mine_w[0:3, 0:shard, :] = wq_ref[...]
    mine_w[3, 0:shard, :] = wout_ref[...]
    pp[0, 0:128, 0:128] = jnp.zeros((128, 128), F32)
    pp[0, 0:experts, 0:shard] = rows_ref[...].astype(F32)
    for k, gain_ref in enumerate(gain_refs):
        pp[0, experts + k : experts + k + 1, 0:shard] = gain_ref[...].astype(F32)
    mine_s[...] = jnp.transpose(pp[0, 0:128, 0:128])[0:rp, :].astype(BF)
    greet([{"dp": (me + d) % n} for d in range(1, n)])

    def at(block):
        rows = pl.ds(pl.multiple_of(block * rp, rp), rp)
        return full_w.at[:, rows, :], full_s.at[rows, :]

    own = at(me)
    sends = []
    for d, p in enumerate(zpeer):
        for i, (a, b) in enumerate(zip((mine_w, mine_s), own)):
            sends.append(remote(a, b, zs.at[d, i], zr.at[d, i], {"dp": p}))
            sends[-1].start()
    for d, p in enumerate(qpeer):
        for i, (a, b) in enumerate(zip((mine_w, mine_s), own)):
            sends.append(remote(a, b, ps.at[d, 0, i], pr.at[d, 0, i], {"dp": p}))
            sends[-1].start()
    here = pl.ds(pl.multiple_of(me * rp, rp), rp)
    full_w[:, here, :] = mine_w[...]
    full_s[here, :] = mine_s[...]

    info[0:2, :] = jnp.full((2, lanes), -1, jnp.int32)
    info[2:3, :] = jnp.full((1, lanes), 1 << 20, jnp.int32)
    info[0:2, 0:tok] = rt_ref[...]
    info[2:3, 0:tok] = rank_ref[...]
    number = lax.broadcasted_iota(jnp.int32, (experts, lanes), 0)
    hot = [jnp.where(number == info[j : j + 1, :], 1.0, 0.0) for j in range(2)]
    ranks = info[2:3, :].astype(F32)
    column = jnp.transpose(jnp.broadcast_to(ranks, (128, lanes)))[:, 0:1]
    before = jnp.where(column < ranks, 1.0, 0.0).astype(BF)
    counts = [mm(h.astype(BF), before, 1, 0) for h in hot]
    counts[1] = counts[1] + jnp.sum(hot[0], axis=1, keepdims=True)
    for j in range(2):
        slot = jnp.sum(counts[j] * hot[j], axis=0, keepdims=True).astype(jnp.int32)
        place = slot - mine * half
        expert_id = info[j : j + 1, :]
        kept = (slot < cap) & (place >= 0) & (place < half) & (expert_id >= 0)
        idx_ref[j : j + 1, :] = jnp.where(kept, expert_id * slots + place, -1)
    ctp[lanes - 64 : lanes, :] = jnp.zeros((64, D), BF)
    ctp[0:tok, :] = ct_ref[...]

    def rows_of(b, carry):
        ones = [slot_matrix(idx_ref, partner(me, n, b * 4 + j) * slots, slots) for j in range(4)]
        block = mm(jnp.concatenate(ones, axis=0), ctp[...], 1, 0).astype(BF)
        send[pl.ds(b * 4, 4)] = block.reshape(4, slots, D)
        return carry

    lax.fori_loop(0, n // 4, rows_of, 0)

    for k in range(1, LINE):
        block = at(((z + LINE - k) % LINE) * plane + q)
        for i in range(2):
            remote(block[i], block[i], zs.at[k - 1, i], zr.at[k - 1, i], {"dp": zpeer[0]}).wait_recv()
        for d, p in enumerate(qpeer):
            for i in range(2):
                sends.append(remote(block[i], block[i], ps.at[d, k, i], pr.at[d, k, i], {"dp": p}))
                sends[-1].start()

    local = pltpu.make_async_copy(send.at[plane], ctx_ref.at[plane], lsem.at[0])
    local.start()

    def ship(p, carry):
        @pl.when(p != plane)
        def _():
            remote(send.at[p], ctx_ref.at[p], cs.at[p], cr.at[p], {"dp": partner(me, n, p)}).start()

        return carry

    lax.fori_loop(0, n, ship, 0)

    images = xp.shape[0]
    scale = HD ** (-0.5)
    xp[:, SEQ_PAD - 16 : SEQ_PAD, :] = jnp.zeros((images, 16, D), F32)
    for i in range(images):
        xp[i, 0:SEQ, :] = tok_ref[i * SEQ : (i + 1) * SEQ, :].astype(F32)

    def norm(i, carry):
        xhat, _ = norm_rows(xp[i])
        xp[i] = xhat
        return carry

    lax.fori_loop(0, images, norm, 0)
    for d in range(1, plane):
        for k in range(LINE):
            block = at(((z + LINE - k) % LINE) * plane + (q + plane - d) % plane)
            for i in range(2):
                remote(block[i], block[i], ps.at[d - 1, k, i], pr.at[d - 1, k, i], {"dp": qpeer[0]}).wait_recv()
    if rp > shard:
        line = lax.broadcasted_iota(jnp.int32, (D, n * rp), 0)
        where = lax.broadcasted_iota(jnp.int32, (D, n * rp), 1)
        squeeze = jnp.where(where == line // shard * rp + line % shard, 1.0, 0.0).astype(BF)
        for c in range(4):
            wo_ref[c] = mm(squeeze, gw[c], 1, 0).astype(BF)
        so_ref[...] = mm(squeeze, gs[...], 1, 0).astype(BF)
    gain = jnp.transpose(so_ref[...].astype(F32))[experts : experts + 1, :]
    lane = lax.broadcasted_iota(jnp.int32, (1, 2 * HD), 1)
    masks = [jnp.where(lane // HD == h, 1.0, 0.0).astype(BF) for h in range(2)]
    valid = lax.broadcasted_iota(jnp.int32, (1, SEQ_PAD), 1) < SEQ

    def image(i, carry):
        normed = (xp[i] * gain).astype(BF)
        for c in range(3):
            qkv_ref[c, i] = mm(normed, wo_ref[c], 1, 0).astype(BF)
        for p in range(qkv_ref.shape[3] // (2 * HD)):
            cols = slice(p * 2 * HD, (p + 1) * 2 * HD)
            qs, ks, vs = (qkv_ref[c, i, :, cols] for c in range(3))
            outs = []
            for h in range(2):
                scores = mm(qs * masks[h], ks, 1, 1) * scale
                scores = jnp.where(valid, scores, -1e30)
                raised = jnp.exp(scores - jnp.max(scores, axis=-1, keepdims=True))
                weights = raised / jnp.sum(raised, axis=-1, keepdims=True)
                outs.append(mm(weights.astype(BF), vs, 1, 0))
            att_ref[i, :, cols] = jnp.where(lane < HD, outs[0], outs[1]).astype(BF)
        pp[i] = mm(att_ref[i], wo_ref[3], 1, 1)
        return carry

    lax.fori_loop(0, images, image, 0)
    for i in range(images):
        part_ref[i * SEQ : (i + 1) * SEQ, :] = pp[i, 0:SEQ, :]
    for c in sends:
        c.wait_send()

    def finish(p, carry):
        @pl.when(p != plane)
        def _():
            remote(send.at[p], ctx_ref.at[p], cs.at[p], cr.at[p], {"dp": partner(me, n, p)}).wait()

        return carry

    lax.fori_loop(0, n, finish, 0)
    local.wait()


def begin(wq, wout, rows, gains, rt, rank, ct, tok, n, experts, cap, half, slots):
    images = tok.shape[0] // SEQ
    shard, width = wout.shape
    rp = up(shard, 16)
    lanes = up(tok.shape[0], 128)
    plane = n // LINE
    sem = pltpu.SemaphoreType.DMA
    shape = jax.ShapeDtypeStruct
    vmem = pltpu.VMEM
    spare = n * rp if rp > shard else 16

    def kernel(wq_ref, wout_ref, rows_ref, g1, g2, g3, *rest):
        begin_kernel(n, cap, half, slots, wq_ref, wout_ref, rows_ref, (g1, g2, g3), *rest)

    return pl.pallas_call(
        kernel,
        out_shape=(
            shape((4, D, width), BF), shape((D, 128), BF), shape((2, lanes), jnp.int32),
            shape((n, slots, D), BF), shape((3, images, SEQ_PAD, width), BF),
            shape((images, SEQ_PAD, width), BF), shape((up(tok.shape[0], 16), D), F32),
        ),
        in_specs=[whole()] * 10,
        out_specs=(whole(), whole(), whole(), pl.BlockSpec(memory_space=pl.ANY), whole(), whole(), whole()),
        scratch_shapes=[
            vmem((4, spare, width), BF), vmem((spare, 128), BF),
            vmem((4, rp, width), BF), vmem((rp, 128), BF), vmem((8, lanes), jnp.int32),
            vmem((lanes, D), BF), vmem((n, slots, D), BF),
            vmem((images, SEQ_PAD, D), F32), vmem((images, SEQ_PAD, D), F32),
            sem((LINE - 1, 2)), sem((LINE - 1, 2)),
            sem((plane - 1, LINE, 2)), sem((plane - 1, LINE, 2)),
            sem((n,)), sem((n,)), sem((1,)),
        ],
        compiler_params=params(collective_id=0, has_side_effects=True),
        name="begin",
    )(wq, wout, rows, *gains, rt, rank, ct, tok)


def row_chunks(rows):
    return [(s, min(256, rows - s)) for s in range(0, rows, 256)]


def token_send(n, send, x_ref, xs, xr, p, peer):
    return remote(send.at[p], x_ref.at[p], xs.at[p], xr.at[p], {"dp": peer})


def send_tokens(
    n, half, early, part_ref, tok_ref, small_ref, idx_ref, hid_ref, n2, prob_ref, x_ref,
    own, other, send, p2, hs, hr, xs, xr,
):
    me, mine = lax.axis_index("dp"), lax.axis_index("mp")
    plane = n // LINE
    tok = tok_ref.shape[0]
    slots = send.shape[1]
    experts, lanes = prob_ref.shape
    tr = other.shape[0]
    sibling = {"mp": 1 - mine}
    own[tr - 16 : tr, :] = jnp.zeros((16, D), BF)
    copies = []
    for c, (start, size) in enumerate(row_chunks(tr)):
        stop = min(start + size, tok)
        own[start:stop, :] = part_ref[start:stop, :].astype(BF)
        rows = pl.ds(start, size)
        copy = remote(own.at[rows, :], other.at[rows, :], hs.at[c], hr.at[c], sibling)
        copy.start()
        copies.append(copy)
    gains = jnp.transpose(small_ref[...].astype(F32))
    gain = gains[experts + 1 : experts + 2, :]
    bias = gains[experts + 2 : experts + 3, :]
    n2[lanes - 64 : lanes, 0:D] = jnp.zeros((64, D), BF)
    for c, (start, size) in enumerate(row_chunks(tr)):
        stop = min(start + size, tok)
        copies[c].wait_recv()
        both = own[start:stop, :].astype(F32) + other[start:stop, :].astype(F32)
        hidden = tok_ref[start:stop, :].astype(F32) + both + bias
        hid_ref[start:stop, :] = hidden
        xhat, _ = norm_rows(hidden)
        n2[start:stop, 0:D] = (xhat * gain).astype(BF)
    logits = mm(gains[0:experts, :].astype(BF), n2[0:lanes, 0:D], 1, 1)
    raised = jnp.exp(logits - jnp.max(logits, axis=0, keepdims=True))
    probs = raised / jnp.sum(raised, axis=0, keepdims=True)
    prob_ref[...] = probs
    high, low = split_two(probs)
    p2[0:experts, :] = high
    p2[experts:, :] = low
    place = lax.broadcasted_iota(jnp.int32, (slots, slots), 0)
    number = lax.broadcasted_iota(jnp.int32, (2 * experts, slots), 0)

    def step(b, carry):
        hot = [slot_matrix(idx_ref, partner(me, n, b * 4 + j) * slots, slots) for j in range(4)]
        block = mm(jnp.concatenate(hot, axis=0), n2[0:lanes, 0:D], 1, 0)
        for j in range(4):
            p = b * 4 + j
            peer = partner(me, n, p)
            gates = mm(p2[...], hot[j], 1, 1)
            row_high = jnp.sum(jnp.where(number == peer, gates, 0.0), axis=0, keepdims=True)
            row_low = jnp.sum(jnp.where(number == peer + experts, gates, 0.0), axis=0, keepdims=True)
            rows = block[j * slots : (j + 1) * slots, :]
            left = jnp.where(place == half, row_high, jnp.where(place == half + 1, row_low, rows[:, 0:slots]))
            send[p, :, :] = rows.astype(BF)
            send[p, :, 0:slots] = left.astype(BF)

            @pl.when((p != plane) & (p < early))
            def _():
                token_send(n, send, x_ref, xs, xr, p, peer).start()

        return carry

    lax.fori_loop(0, n // 4, step, 0)
    x_ref[plane] = send[plane]
    for copy in copies:
        copy.wait_send()


def dispatch_kernel(
    n, half, part_ref, tok_ref, small_ref, idx_ref, hid_ref, prob_ref, x_ref,
    n2, own, other, send, p2, hs, hr, xs, xr,
):
    me, mine = lax.axis_index("dp"), lax.axis_index("mp")
    plane = n // LINE
    greet([{"mp": 1 - mine}] + [{"dp": (me + d) % n} for d in range(1, n)])
    send_tokens(
        n, half, n, part_ref, tok_ref, small_ref, idx_ref, hid_ref, n2, prob_ref, x_ref,
        own, other, send, p2, hs, hr, xs, xr,
    )

    def finish(p, carry):
        @pl.when(p != plane)
        def _():
            token_send(n, send, x_ref, xs, xr, p, partner(me, n, p)).wait()

        return carry

    lax.fori_loop(0, n, finish, 0)


def dispatch(part, tok, small, idx, n, experts, half, slots):
    lanes = idx.shape[1]
    tr = up(tok.shape[0], 16)
    sem = pltpu.SemaphoreType.DMA
    vmem = pltpu.VMEM
    chunks = len(row_chunks(tr))
    return pl.pallas_call(
        functools.partial(dispatch_kernel, n, half),
        out_shape=(
            jax.ShapeDtypeStruct(tok.shape, F32),
            jax.ShapeDtypeStruct((experts, lanes), F32),
            jax.ShapeDtypeStruct((n, slots, D), BF),
        ),
        in_specs=[whole()] * 4,
        out_specs=(whole(),) * 3,
        scratch_shapes=[
            vmem((lanes, D), BF), vmem((tr, D), BF), vmem((tr, D), BF), vmem((n, slots, D), BF),
            vmem((2 * experts, lanes), BF),
            sem((chunks,)), sem((chunks,)), sem((n,)), sem((n,)),
        ],
        compiler_params=params(collective_id=1, has_side_effects=True),
        name="dispatch",
    )(part, tok, small, idx)


def expert_kernel(
    n, half, fused,
    first_ref, ct_ref, wi_own, wi_sib, wb_own, wb_sib, bi_own, bi_sib, bb_ref,
    idx_ref, seen_ref, tok_ct, small_ref,
    hg_ref, sg_ref, y_ref, gi_ref, gi_in, gb_ref, gb_in, little_ref, little_in, hid_out, prob_ref,
    vi_own, vi_sib, vb_own, vb_sib, g_s, act_own, act_sib, dp_own, dp_sib, dx_s, back, acc, other,
    ct_s, y_s, stage, gp, gp_other, x_ref, send, p2,
    lsem, ysem, gsem, ss, rs, hs, hr, ms, mr, xs, xr, es, er,
):
    me, mine = lax.axis_index("dp"), lax.axis_index("mp")
    sibling = {"mp": 1 - mine}
    plane = n // LINE
    slots = x_ref.shape[1]
    tok = tok_ct.shape[0]
    experts = prob_ref.shape[0]
    hidden = wi_own.shape[1]
    group = 4 * slots
    batches = n // 4
    tr = other.shape[0]
    early = n // 2 if fused else n
    first = (first_ref, acc.at[pl.ds(0, tr), :]) if fused else (first_ref, x_ref)
    loads = [
        pltpu.make_async_copy(a, b, lsem.at[i])
        for i, (a, b) in enumerate(
            (first, (wi_own, vi_own), (wb_own, vb_own), (wi_sib, vi_sib), (wb_sib, vb_sib))
        )
    ]
    for c in loads:
        c.start()
    greet([sibling] + [{"dp": (me + d) % n} for d in range(1, n)])
    loads[0].wait()
    if fused:
        send_tokens(
            n, half, early, acc, seen_ref, small_ref, idx_ref, hg_ref, act_own, prob_ref, x_ref,
            g_s, other, send, p2, es, er, xs, xr,
        )
        keep = pltpu.make_async_copy(hg_ref, hid_out, lsem.at[5])
    else:
        keep = pltpu.make_async_copy(hid_out, hg_ref, lsem.at[5])
    keep.start()
    little_ref[...] = jnp.zeros_like(little_ref)

    def cts(b, j):
        return pltpu.make_async_copy(ct_ref.at[b * 4 + j], ct_s.at[j], ysem.at[0, j])

    def ys(b, j):
        return pltpu.make_async_copy(y_s.at[j], y_ref.at[partner(me, n, b * 4 + j, -1)], ysem.at[1, j])

    for j in range(4):
        cts(0, j).start()
    for c in loads[1:]:
        c.wait()
    chunk = 768
    row = lax.broadcasted_iota(jnp.int32, (group, 16), 0)
    number = lax.broadcasted_iota(jnp.int32, (group, 16), 1)
    member = jnp.where(row // slots == number, 1.0, 0.0).astype(BF)
    spot = lax.broadcasted_iota(jnp.int32, (group, 128), 0) % slots
    here = spot == lax.broadcasted_iota(jnp.int32, (group, 128), 1)
    row_t = lax.broadcasted_iota(jnp.int32, (16, group), 1)
    number_t = lax.broadcasted_iota(jnp.int32, (16, group), 0)
    pick = jnp.where(
        (row_t == number_t * slots + half) | (row_t == number_t * slots + half + 1), 1.0, 0.0
    ).astype(BF)
    member_t = jnp.where(row_t // slots == number_t, 1.0, 0.0).astype(BF)
    puts = [jnp.where(row == number * slots + half + i, 1.0, 0.0).astype(BF) for i in range(2)]

    def batch(b, carry):
        at = pl.ds(pl.multiple_of(b * group, 16), group)
        if fused:
            for j in range(4):
                p = b * 4 + j

                @pl.when(p != plane)
                def _():
                    token_send(n, send, x_ref, xs, xr, p, partner(me, n, p)).wait_recv()

            @pl.when(b == batches // 4 - 1)
            def _():
                def more(p, carry):
                    token_send(n, send, x_ref, xs, xr, p, partner(me, n, p)).start()
                    return carry

                lax.fori_loop(early, n, more, 0)

        x = x_ref[pl.ds(b * 4, 4)].reshape(group, D)
        high, low = split_two(mm(pick, x[:, 0:128], 1, 0))
        wide = mm(member, high, 1, 0) + mm(member, low, 1, 0)
        gate = jnp.sum(jnp.where(here, wide, 0.0), axis=1, keepdims=True)
        for j in range(4):
            cts(b, j).wait()
        g_s[at, :] = (gate * ct_s[...].reshape(group, D).astype(F32)).astype(BF)
        little_ref[0:1, 2 * hidden :] += jnp.sum(g_s[at, :].astype(F32), axis=0, keepdims=True)
        for part, (vi, vb, bi, acts, dps) in enumerate(
            ((vi_own, vb_own, bi_own, act_own, dp_own), (vi_sib, vb_sib, bi_sib, act_sib, dp_sib))
        ):
            for c in range(hidden // chunk):
                cols = slice(c * chunk, (c + 1) * chunk)
                pre = mm(x_ref[pl.ds(b * 4, 4)].reshape(group, D), vi[:, cols], 1, 0) + bi[:, cols].astype(F32)
                phi = 0.5 * (1.0 + lax.erf(pre * (0.5**0.5)))
                slope = phi + pre * (jnp.exp(-0.5 * pre * pre) * ((2.0 * jnp.pi) ** -0.5))
                acts[at, cols] = (pre * phi).astype(BF)
                grad = (mm(g_s[at, :], vb[cols, :], 1, 1) * slope).astype(BF)
                dps[at, cols] = grad
                place = slice(part * hidden + c * chunk, part * hidden + (c + 1) * chunk)
                little_ref[0:1, place] += jnp.sum(grad.astype(F32), axis=0, keepdims=True)
        dx = mm(dp_own[at, :], vi_own[...], 1, 1) + mm(dp_sib[at, :], vi_sib[...], 1, 1)
        y = mm(act_own[at, :], vb_own[...], 1, 0) + mm(act_sib[at, :], vb_sib[...], 1, 0)
        y = (y + bb_ref[...].astype(F32)).astype(BF).astype(F32)
        dots = jnp.sum(ct_s[...].reshape(group, D).astype(F32) * y, axis=1, keepdims=True)
        high, low = split_two(jnp.where(here, dots, 0.0))
        high, low = mm(member_t, high, 1, 0).astype(BF), mm(member_t, low, 1, 0).astype(BF)
        left = dx[:, 0:128] + mm(puts[0], high, 1, 0) + mm(puts[1], low, 1, 0)
        dx = jnp.concatenate([left, dx[:, 128:]], axis=1)
        dx_s[pl.ds(b * 4, 4)] = dx.astype(BF).reshape(4, slots, D)
        for j in range(4):
            p = b * 4 + j

            @pl.when(p != plane)
            def _():
                remote(dx_s.at[p], back.at[p], ss.at[p], rs.at[p], {"dp": partner(me, n, p, -1)}).start()

        @pl.when(b > 0)
        def _():
            for j in range(4):
                ys(b - 1, j).wait()

        y_s[...] = (gate * y).astype(BF).reshape(4, slots, D)
        for j in range(4):
            ys(b, j).start()

        @pl.when(b + 1 < batches)
        def _():
            for j in range(4):
                cts(b + 1, j).start()

        return carry

    lax.fori_loop(0, batches, batch, 0)
    back[plane] = dx_s[plane]
    little = remote(little_ref, little_in, ms.at[2], mr.at[2], sibling)
    little.start()

    rows_all = n * slots
    steps = 3
    size = D // steps
    wide = hidden // 2
    swaps = []

    def out_i(r, c):
        return pltpu.make_async_copy(
            stage.at[r % 2, c * size : (c + 1) * size, :],
            gi_ref.at[r * size : (r + 1) * size, c * wide : (c + 1) * wide], gsem.at[c, r],
        )

    def out_b(r):
        return pltpu.make_async_copy(
            stage.at[r % 2], gb_ref.at[r * 2 * size : (r + 1) * 2 * size, :], gsem.at[2, r]
        )

    for r in range(steps):
        at = slice(r * size, (r + 1) * size)
        left = x_ref[:, :, at].reshape(rows_all, size)
        vi_sib[at, :] = mm(left, dp_sib[...], 0, 0).astype(BF)
        for c in range(2):
            if r >= 2:
                out_i(r - 2, c).wait()
            stage[r % 2, c * size : (c + 1) * size, :] = mm(left, dp_own[:, c * wide : (c + 1) * wide], 0, 0)
            out_i(r, c).start()
    copy = remote(vi_sib, gi_in, ms.at[0], mr.at[0], sibling)
    copy.start()
    swaps.append(copy)

    acc[...] = jnp.zeros_like(acc)
    gp[...] = jnp.zeros_like(gp)
    place = lax.broadcasted_iota(jnp.int32, (slots, 128), 0)
    count = lax.broadcasted_iota(jnp.int32, (experts, slots), 0)

    def combine(b, carry):
        hot = []
        for j in range(4):
            d = b * 4 + j
            source = partner(me, n, d)

            @pl.when(d != plane)
            def _():
                remote(dx_s.at[d], back.at[d], ss.at[d], rs.at[d], {"dp": source}).wait_recv()

            hot.append(slot_matrix(idx_ref, source * slots, slots))
            extra = back[d, :, 0:128].astype(F32)
            high = jnp.sum(jnp.where(place == half, extra, 0.0), axis=0, keepdims=True)[:, 0:slots]
            low = jnp.sum(jnp.where(place == half + 1, extra, 0.0), axis=0, keepdims=True)[:, 0:slots]
            for value in (high, low):
                gp[...] += mm(jnp.where(count == source, value, 0.0).astype(BF), hot[j], 1, 0)
        block = back[pl.ds(b * 4, 4)].reshape(group, D)
        acc[...] += mm(jnp.concatenate(hot, axis=0), block, 0, 0)
        return carry

    lax.fori_loop(0, batches // 2, combine, 0)
    for r in range(steps):
        at = slice(r * 2 * size, (r + 1) * 2 * size)
        vb_sib[at, :] = mm(act_sib[:, at], g_s[...], 0, 0).astype(BF)
        if r == 0:
            for c in range(2):
                out_i(1, c).wait()
                out_i(2, c).wait()
        if r >= 2:
            out_b(r - 2).wait()
        stage[r % 2] = mm(act_own[:, at], g_s[...], 0, 0)
        out_b(r).start()
    copy = remote(vb_sib, gb_in, ms.at[1], mr.at[1], sibling)
    copy.start()
    swaps.append(copy)
    lax.fori_loop(batches // 2, batches, combine, 0)

    little.wait()
    copies = []
    own = g_s
    own[other.shape[0] - 16 : other.shape[0], :] = jnp.zeros((16, D), BF)
    for c, (start, length) in enumerate(row_chunks(other.shape[0])):
        stop = min(start + length, tok)
        own[start:stop, :] = acc[start:stop, :].astype(BF)
        rows = pl.ds(start, length)
        copy = remote(own.at[rows, :], other.at[rows, :], hs.at[c], hr.at[c], sibling)
        copy.start()
        copies.append(copy)
    copy = remote(gp, gp_other, hs.at[len(copies)], hr.at[len(copies)], sibling)
    copy.start()
    copy.wait()
    probs = prob_ref[...] if fused else seen_ref[...]
    grad_probs = gp[...] + gp_other[...]
    logits = (probs * (grad_probs - jnp.sum(grad_probs * probs, axis=0, keepdims=True))).astype(BF)
    gains = jnp.transpose(small_ref[...].astype(F32))
    gain = gains[experts + 1 : experts + 2, :]
    acc[...] = mm(logits, gains[0:experts, :].astype(BF), 0, 0)
    sg_ref[...] = jnp.zeros_like(sg_ref)
    gain_sum = jnp.zeros((1, D), F32)
    bias_sum = jnp.zeros((1, D), F32)
    lanes = acc.shape[0]
    act_own[lanes - 64 : lanes, 0:D] = jnp.zeros((64, D), BF)
    keep.wait()
    for c, (start, length) in enumerate(row_chunks(other.shape[0])):
        stop = min(start + length, tok)
        copies[c].wait_recv()
        grad = own[start:stop, :].astype(F32) + other[start:stop, :].astype(F32) + acc[start:stop, :]
        xhat, inverse = norm_rows(hg_ref[start:stop, :])
        act_own[start:stop, 0:D] = (xhat * gain).astype(BF)
        hidden_grad = tok_ct[start:stop, :].astype(F32) + norm_back(grad, gain, xhat, inverse)
        hg_ref[start:stop, :] = hidden_grad
        gain_sum += jnp.sum(grad * xhat, axis=0, keepdims=True)
        bias_sum += jnp.sum(hidden_grad, axis=0, keepdims=True)
    sg_ref[0:experts, :] = mm(logits, act_own[0:lanes, 0:D], 1, 0)
    sg_ref[experts : experts + 1, :] = gain_sum
    sg_ref[experts + 1 : experts + 2, :] = bias_sum
    for copy in copies:
        copy.wait_send()

    def finish(p, carry):
        @pl.when(p != plane)
        def _():
            remote(dx_s.at[p], back.at[p], ss.at[p], rs.at[p], {"dp": partner(me, n, p, -1)}).wait_send()
            if fused:
                token_send(n, send, x_ref, xs, xr, p, partner(me, n, p)).wait_send()

        return carry

    lax.fori_loop(0, n, finish, 0)
    for j in range(4):
        ys(batches - 1, j).wait()
    for r in range(1, steps):
        out_b(r).wait()
    for copy in swaps:
        copy.wait()


def expert(first, ct_rows, wi, wb, bi, bb, idx, probs, hid, tok, ct, small, n, half):
    fused = hid is None
    _, slots, _ = ct_rows.shape
    rows = n * slots
    hidden = wi[0].shape[1]
    lanes = idx.shape[1]
    experts = n
    tr = up(ct.shape[0], 16)
    chunks = len(row_chunks(tr))
    shape = jax.ShapeDtypeStruct
    sem = pltpu.SemaphoreType.DMA
    vmem = pltpu.VMEM
    far = pl.BlockSpec(memory_space=pl.ANY)
    outs = [
        shape(ct.shape, F32), shape((up(experts + 3, 8), D), F32), shape((n, slots, D), BF),
        shape((D, hidden), F32), shape((D, hidden), BF),
        shape((hidden, D), F32), shape((hidden, D), BF),
        shape((8, 2 * hidden + D), F32), shape((8, 2 * hidden + D), F32),
    ]
    out_specs = [whole(), whole(), far, far, far, far, far, whole(), whole()]
    ins = [first, ct_rows, wi[0], wi[1], wb[0], wb[1], bi[0], bi[1], bb, idx]
    in_specs = [far, far, far, far, far, far, whole(), whole(), whole(), whole()]
    if fused:
        outs += [shape(ct.shape, F32), shape((experts, lanes), F32)]
        out_specs += [far, whole()]
        ins += [tok, ct, small]
        in_specs += [whole()] * 3
        kernel = functools.partial(expert_kernel, n, half, True)
    else:
        ins += [probs, ct, small, hid]
        in_specs += [whole()] * 3 + [far]

        def kernel(*refs):
            ins, hid_ref, outs, rest = refs[:13], refs[13], refs[14:23], refs[23:]
            expert_kernel(n, half, False, *ins, *outs, hid_ref, ins[10], *rest)

    small_x = (n, slots, D) if fused else (1, 16, 128)
    return pl.pallas_call(
        kernel,
        out_shape=tuple(outs),
        in_specs=in_specs,
        out_specs=tuple(out_specs),
        scratch_shapes=[
            vmem((D, hidden), BF), vmem((D, hidden), BF), vmem((hidden, D), BF), vmem((hidden, D), BF),
            vmem((rows, D), BF),
            vmem((rows, hidden), BF), vmem((rows, hidden), BF),
            vmem((rows, hidden), BF), vmem((rows, hidden), BF),
            vmem((n, slots, D), BF), vmem((n, slots, D), BF),
            vmem((lanes, D), F32), vmem((tr, D), BF),
            vmem((4, slots, D), BF), vmem((4, slots, D), BF),
            vmem((2, hidden // 3, D), F32),
            vmem((experts, lanes), F32), vmem((experts, lanes), F32),
            vmem((n, slots, D), BF), vmem(small_x, BF), vmem((2 * experts, lanes), BF),
            sem((6,)), sem((2, 4)), sem((3, 3)), sem((n,)), sem((n,)),
            sem((chunks + 1,)), sem((chunks + 1,)), sem((3,)), sem((3,)),
            sem((n,)), sem((n,)), sem((chunks,)), sem((chunks,)),
        ],
        compiler_params=params(collective_id=2, has_side_effects=True),
        name="expert",
    )(*ins)


def attend_back_kernel(
    experts, hg_ref, tok_ref, small_ref, w_ref, qkv_ref, att_ref, gi_ref, gi_in, gb_ref, gb_in, little_ref, little_in,
    dn_ref, dw_ref, gi_out, gb_out, gbi_out, gbb_out,
    normed, low, dqkv, pp,
):
    images = normed.shape[0]
    scale = HD ** (-0.5)
    step = pl.program_id(0)
    gi_out[...] = gi_ref[...] + gi_in[...].astype(F32)
    gb_out[...] = gb_ref[...] + gb_in[...].astype(F32)

    @pl.when(step == 0)
    def _():
        hidden = gbi_out.shape[1]
        gbi_out[...] = little_ref[0:1, 0:hidden] + little_in[0:1, hidden : 2 * hidden]
        gbb_out[...] = little_ref[0:1, 2 * hidden :] + little_in[0:1, 2 * hidden :]
        pp[:, SEQ_PAD - 16 : SEQ_PAD, :] = jnp.zeros((images, 16, D), F32)
        for i in range(images):
            pp[i, 0:SEQ, :] = hg_ref[i * SEQ : (i + 1) * SEQ, :]
        low[...] = pp[...].astype(BF)
        for i in range(images):
            pp[i, 0:SEQ, :] = tok_ref[i * SEQ : (i + 1) * SEQ, :].astype(F32)

    @pl.when(step < images)
    def _():
        i = step
        gains = jnp.transpose(small_ref[...].astype(F32))
        gain = gains[experts : experts + 1, :]
        lane = lax.broadcasted_iota(jnp.int32, (1, 2 * HD), 1)
        masks = [jnp.where(lane // HD == h, 1.0, 0.0).astype(BF) for h in range(2)]
        valid = lax.broadcasted_iota(jnp.int32, (1, SEQ_PAD), 1) < SEQ
        xhat, _ = norm_rows(pp[i])
        normed[i] = (xhat * gain).astype(BF)
        grad_att = mm(low[i], w_ref[3], 1, 0).astype(BF)
        for p in range(w_ref.shape[2] // (2 * HD)):
            cols = slice(p * 2 * HD, (p + 1) * 2 * HD)
            q, k, v = (qkv_ref[c, i, :, cols] for c in range(3))
            pair = grad_att[:, cols]
            grads = []
            for h in range(2):
                scores = mm(q * masks[h], k, 1, 1) * scale
                scores = jnp.where(valid, scores, -1e30)
                raised = jnp.exp(scores - jnp.max(scores, axis=-1, keepdims=True))
                weights = raised / jnp.sum(raised, axis=-1, keepdims=True)
                grad_weights = mm(pair * masks[h], v, 1, 1)
                grad_scores = weights * (
                    grad_weights - jnp.sum(grad_weights * weights, axis=-1, keepdims=True)
                )
                scores_low = grad_scores.astype(BF)
                grads.append((
                    mm(scores_low, k, 1, 0) * scale,
                    mm(scores_low, q, 0, 0) * scale,
                    mm(weights.astype(BF), pair, 0, 0),
                ))
            for c in range(3):
                dqkv[c, i, :, cols] = jnp.where(lane < HD, grads[0][c], grads[1][c]).astype(BF)
        total = mm(dqkv[0, i], w_ref[0], 1, 1)
        for c in range(1, 3):
            total += mm(dqkv[c, i], w_ref[c], 1, 1)
        pp[i] = total

    @pl.when(step == images)
    def _():
        for i in range(images):
            dn_ref[i * SEQ : (i + 1) * SEQ, :] = pp[i, 0:SEQ, :]
        rows = images * SEQ_PAD

        def weight(r, carry):
            at = pl.ds(pl.multiple_of(r * 256, 256), 256)
            left = normed[:, :, at].reshape(rows, 256)
            for c in range(3):
                dw_ref[c, at, :] = mm(left, dqkv[c].reshape(rows, -1), 0, 0).astype(BF)
            left = low[:, :, at].reshape(rows, 256)
            dw_ref[3, at, :] = mm(left, att_ref[...].reshape(rows, -1), 0, 0).astype(BF)
            return carry

        lax.fori_loop(0, D // 256, weight, 0)


def attend_back(hg, tok, small, w, qkv, att, gi, gi_in, gb, gb_in, little, little_in, experts):
    images = tok.shape[0] // SEQ
    width = w.shape[2]
    steps = images + 1
    hidden = gi.shape[1]
    line_i = pl.BlockSpec((gi.shape[0] // steps, hidden), lambda k: (k, 0))
    line_b = pl.BlockSpec((hidden // steps, D), lambda k: (k, 0))
    return pl.pallas_call(
        functools.partial(attend_back_kernel, experts),
        grid=(steps,),
        out_shape=(
            jax.ShapeDtypeStruct(tok.shape, F32),
            jax.ShapeDtypeStruct((4, D, width), BF),
            jax.ShapeDtypeStruct(gi.shape, F32),
            jax.ShapeDtypeStruct(gb.shape, F32),
            jax.ShapeDtypeStruct((1, hidden), F32),
            jax.ShapeDtypeStruct((1, D), F32),
        ),
        in_specs=[whole()] * 6 + [line_i, line_i, line_b, line_b, whole(), whole()],
        out_specs=(whole(), whole(), line_i, line_b, whole(), whole()),
        scratch_shapes=[
            pltpu.VMEM((images, SEQ_PAD, D), BF),
            pltpu.VMEM((images, SEQ_PAD, D), BF),
            pltpu.VMEM((3, images, SEQ_PAD, width), BF),
            pltpu.VMEM((images, SEQ_PAD, D), F32),
        ],
        compiler_params=params(dimension_semantics=("arbitrary",)),
        name="attend_back",
    )(hg, tok, small, w, qkv, att, gi, gi_in, gb, gb_in, little, little_in)


def last_kernel(
    n, experts, dw_ref, sg_ref, dn_ref, tok_ref, hg_ref, small_ref, y_ref, idx_ref, hid_ref,
    tg_ref, out_ref, gw_ref, gs_ref,
    own, other, mix, mix_other, sm, r1, q1, s1, t1, r2, q2, acc, hs, hr, as_, ar, bs, br,
):
    me, mine = lax.axis_index("dp"), lax.axis_index("mp")
    plane = n // LINE
    z, q = me // plane, me % plane
    tok = tok_ref.shape[0]
    rp = dw_ref.shape[3]
    sibling = {"mp": 1 - mine}
    zpeer = [((z + d) % LINE) * plane + q for d in range(1, LINE)]
    qpeer = [z * plane + (q + d) % plane for d in range(1, plane)]
    greet([sibling] + [{"dp": p} for p in zpeer + qpeer])
    sends = []
    for d, p in enumerate(qpeer):
        c = remote(dw_ref.at[:, :, (q + d + 1) % plane], r1.at[d], as_.at[d, 0], ar.at[d, 0], {"dp": p})
        c.start()
        sends.append(c)
    copies = []
    own[own.shape[0] - 16 :, :] = jnp.zeros((16, D), BF)
    for c, (start, size) in enumerate(row_chunks(own.shape[0])):
        stop = min(start + size, tok)
        own[start:stop, :] = dn_ref[start:stop, :].astype(BF)
        rows = pl.ds(start, size)
        copy = remote(own.at[rows, :], other.at[rows, :], hs.at[c], hr.at[c], sibling)
        copy.start()
        copies.append(copy)
    gains = jnp.transpose(small_ref[...].astype(F32))
    gain = gains[experts : experts + 1, :]
    gain_sum = jnp.zeros((1, D), F32)
    for c, (start, size) in enumerate(row_chunks(own.shape[0])):
        stop = min(start + size, tok)
        copies[c].wait()
        grad = own[start:stop, :].astype(F32) + other[start:stop, :].astype(F32)
        xhat, inverse = norm_rows(tok_ref[start:stop, :].astype(F32))
        tg_ref[start:stop, :] = (hg_ref[start:stop, :] + norm_back(grad, gain, xhat, inverse)).astype(BF)
        gain_sum += jnp.sum(grad * xhat, axis=0, keepdims=True)
    row = lax.broadcasted_iota(jnp.int32, sg_ref.shape, 0)
    rows = jnp.where(row == experts + 2, gain_sum, sg_ref[...])
    rows = jnp.concatenate([rows, jnp.zeros((128 - rows.shape[0], D), F32)], axis=0)
    turned = jnp.transpose(rows).astype(BF)
    real = turned.shape[0] // n
    for b in range(n):
        at = (b // plane, b % plane)
        if real < rp:
            sm[at[0], at[1]] = jnp.zeros((rp, 128), BF)
        sm[at[0], at[1], 0:real, :] = turned[b * real : (b + 1) * real, :]
    for d, p in enumerate(qpeer):
        c = remote(sm.at[:, (q + d + 1) % plane], q1.at[d], as_.at[d, 1], ar.at[d, 1], {"dp": p})
        c.start()
        sends.append(c)
    slots = y_ref.shape[1]
    acc[...] = jnp.zeros_like(acc)

    def step(b, carry):
        hot = slot_matrix(idx_ref, b * 4 * slots, 4 * slots)
        acc[...] += mm(hot, y_ref[pl.ds(b * 4, 4)].reshape(4 * slots, D), 0, 0)
        return carry

    lax.fori_loop(0, n // 4, step, 0)
    mix[mix.shape[0] - 16 :, :] = jnp.zeros((16, D), BF)
    base = len(copies)
    late = []
    for c, (start, size) in enumerate(row_chunks(own.shape[0])):
        stop = min(start + size, tok)
        mix[start:stop, :] = acc[start:stop, :].astype(BF)
        rows = pl.ds(start, size)
        copy = remote(mix.at[rows, :], mix_other.at[rows, :], hs.at[base + c], hr.at[base + c], sibling)
        copy.start()
        late.append(copy)
    for c, (start, size) in enumerate(row_chunks(own.shape[0])):
        stop = min(start + size, tok)
        late[c].wait()
        both = mix[start:stop, :].astype(F32) + mix_other[start:stop, :].astype(F32)
        out_ref[start:stop, :] = (hid_ref[start:stop, :] + both).astype(BF)
    for d in range(plane - 1):
        remote(dw_ref.at[:, :, 0], r1.at[d], as_.at[d, 0], ar.at[d, 0], {"dp": qpeer[0]}).wait_recv()
        remote(sm.at[:, 0], q1.at[d], as_.at[d, 1], ar.at[d, 1], {"dp": qpeer[0]}).wait_recv()
    for b in range(LINE):
        value = dw_ref[:, b, q].astype(F32)
        little = sm[b, q].astype(F32)
        for d in range(plane - 1):
            value += r1[d, :, b].astype(F32)
            little += q1[d, b].astype(F32)
        s1[b] = value.astype(BF)
        t1[b] = little.astype(BF)
    for d, p in enumerate(zpeer):
        to = (z + d + 1) % LINE
        for i, (a, b) in enumerate(((s1, r2), (t1, q2))):
            c = remote(a.at[to], b.at[d], bs.at[d, i], br.at[d, i], {"dp": p})
            c.start()
            sends.append(c)
    value = s1[z].astype(F32)
    little = t1[z].astype(F32)
    for d in range(LINE - 1):
        for i, (a, b) in enumerate(((s1, r2), (t1, q2))):
            remote(a.at[0], b.at[d], bs.at[d, i], br.at[d, i], {"dp": zpeer[0]}).wait_recv()
        value += r2[d].astype(F32)
        little += q2[d].astype(F32)
    gw_ref[...] = value
    gs_ref[...] = little
    for c in sends:
        c.wait_send()


def last(dw, sg, dn, tok, hg, small, y, idx, hid, n, experts):
    parts, _, rows, width = dw.shape
    rp = rows
    plane = n // LINE
    dw = dw.reshape(parts, LINE, plane, rp, width)
    tr = up(tok.shape[0], 16)
    chunks = len(row_chunks(tr))
    sem = pltpu.SemaphoreType.DMA
    vmem = pltpu.VMEM
    return pl.pallas_call(
        functools.partial(last_kernel, n, experts),
        out_shape=(
            jax.ShapeDtypeStruct(tok.shape, BF),
            jax.ShapeDtypeStruct(tok.shape, BF),
            jax.ShapeDtypeStruct((parts, rp, width), F32),
            jax.ShapeDtypeStruct((rp, 128), F32),
        ),
        in_specs=[whole()] * 9,
        out_specs=(whole(),) * 4,
        scratch_shapes=[
            vmem((tr, D), BF), vmem((tr, D), BF), vmem((tr, D), BF), vmem((tr, D), BF),
            vmem((LINE, plane, rp, 128), BF),
            vmem((plane - 1, parts, LINE, rp, width), BF),
            vmem((plane - 1, LINE, rp, 128), BF),
            vmem((LINE, parts, rp, width), BF),
            vmem((LINE, rp, 128), BF),
            vmem((LINE - 1, parts, rp, width), BF),
            vmem((LINE - 1, rp, 128), BF),
            vmem((idx.shape[1], D), F32),
            sem((2 * chunks,)), sem((2 * chunks,)),
            sem((plane - 1, 2)), sem((plane - 1, 2)), sem((LINE - 1, 2)), sem((LINE - 1, 2)),
        ],
        compiler_params=params(collective_id=3, has_side_effects=True),
        name="last",
    )(dw, sg, dn, tok, hg, small, y, idx, hid)


def body(
    tokens, ln1_gain, w_qkv, w_out, out_bias, ln2_gain, router, w_in, in_bias,
    w_back, back_bias, routes, priority, cotangent,
):
    n = lax.axis_size("dp")
    tok = tokens.shape[0]
    experts = router.shape[1]
    cap = max(2, 5 * tok // (2 * experts))
    half = (cap + 1) // 2
    slots = up(half + FREE, 16)
    shard, width = w_qkv.shape[0], w_qkv.shape[2]
    rp = up(shard, 16)
    swap = [(0, 1), (1, 0)]

    wi = (w_in[0], lax.ppermute(w_in[0], "mp", swap))
    wb = (w_back[0], lax.ppermute(w_back[0], "mp", swap))
    bi = (in_bias, lax.ppermute(in_bias, "mp", swap))

    weights, small, idx, ct_rows, qkv, att, part = begin(
        jnp.swapaxes(w_qkv, 0, 1), w_out.T, router.T,
        (ln1_gain[None], ln2_gain[None], out_bias[None]),
        routes.T, priority, cotangent, tokens, n, experts, cap, half, slots,
    )
    if n * slots <= 1536:
        hg, sg, y, gi, gi_in, gb, gb_in, little, little_in, hid, _ = expert(
            part, ct_rows, wi, wb, bi, back_bias, idx, None, None, tokens, cotangent, small, n, half
        )
    else:
        hid, probs, x = dispatch(part, tokens, small, idx, n, experts, half, slots)
        hg, sg, y, gi, gi_in, gb, gb_in, little, little_in = expert(
            x, ct_rows, wi, wb, bi, back_bias, idx, probs, hid, tokens, cotangent, small, n, half
        )
    y = lax.all_to_all(y, "dp", split_axis=0, concat_axis=0, tiled=True)
    dn, dw, gi, gb, gbi, gbb = attend_back(
        hg, tokens, small, weights, qkv, att, gi, gi_in, gb, gb_in, little, little_in, experts
    )
    dw = dw.reshape(4, n, shard, width)
    if rp > shard:
        dw = jnp.pad(dw, ((0, 0), (0, 0), (0, rp - shard), (0, 0)))
    tg, out, gw, gs = last(dw, sg, dn, tokens, hg, small, y, idx, hid, n, experts)
    gw, gs = gw[:, :shard], gs[:shard]
    return (
        out,
        tg,
        gs[:, experts + 2],
        jnp.swapaxes(gw[:3], 0, 1),
        gw[3].T,
        gs[:, experts + 1],
        gs[:, experts],
        gs[:, :experts],
        gi[None],
        gbi,
        gb[None],
        gbb,
    )


def solution(mesh):
    return jax.shard_map(
        body,
        mesh=mesh,
        in_specs=(
            P("dp", None),
            P("dp"),
            P("dp", None, "mp"),
            P("mp", "dp"),
            P("dp"),
            P("dp"),
            P("dp", None),
            P("dp", None, "mp"),
            P("dp", "mp"),
            P("dp", "mp", None),
            P("dp", None),
            P("dp", None),
            P("dp", None),
            P("dp", None),
        ),
        out_specs=(
            P("dp", None),
            P("dp", None),
            P("dp"),
            P("dp", None, "mp"),
            P("mp", "dp"),
            P("dp"),
            P("dp"),
            P("dp", None),
            P("dp", None, "mp"),
            P("dp", "mp"),
            P("dp", "mp", None),
            P("dp", None),
        ),
        check_vma=False,
    )
```

```python
import functools

import jax
import jax.numpy as jnp
from jax import lax
from jax.experimental import pallas as pl
from jax.experimental.pallas import tpu as pltpu
from jax.sharding import PartitionSpec as P

D = 768
HD = 64
SEQ = 197
EPS = 1e-06
F32 = jnp.float32
BF = jnp.bfloat16
MESH = pl.DeviceIdType.MESH
VMEM_LIMIT = 62 * 1024 * 1024
LINE = 4
FREE = 3


def up(value, step):
    return (value + step - 1) // step * step


SEQ_PAD = up(SEQ, 16)


def mm(left, right, cl, cr):
    return lax.dot_general(
        left, right, (((cl,), (cr,)), ((), ())), preferred_element_type=F32
    )


def norm_rows(values):
    average = jnp.mean(values, axis=-1, keepdims=True)
    centered = values - average
    inverse = lax.rsqrt(jnp.mean(centered * centered, axis=-1, keepdims=True) + EPS)
    return centered * inverse, inverse


def norm_back(grad, gain, xhat, inverse):
    scaled = grad * gain
    return inverse * (
        scaled
        - jnp.mean(scaled, axis=-1, keepdims=True)
        - xhat * jnp.mean(scaled * xhat, axis=-1, keepdims=True)
    )


def split_two(value):
    high = value.astype(BF)
    return high, (value - high.astype(F32)).astype(BF)


def whole():
    return pl.BlockSpec(memory_space=pltpu.VMEM)


def params(**more):
    return pltpu.CompilerParams(vmem_limit_bytes=VMEM_LIMIT, **more)


def greet(peers):
    barrier = pltpu.get_barrier_semaphore()
    for peer in peers:
        pl.semaphore_signal(barrier, inc=1, device_id=peer, device_id_type=MESH)
    pl.semaphore_wait(barrier, len(peers))


def remote(src, dst, send_sem, recv_sem, peer):
    return pltpu.make_async_remote_copy(
        src_ref=src, dst_ref=dst, send_sem=send_sem, recv_sem=recv_sem,
        device_id=peer, device_id_type=MESH,
    )


def partner(me, n, place, sign=1):
    plane = n // LINE
    groups = plane // 4
    z, q = me // plane, me % plane
    step, j = place // 4, place % 4
    turn, g = step // groups, step % groups
    k = turn % 2 * 2 + turn // 2
    line = (z // 2 + k // 2) % 2 * 2 + (z % 2 + k % 2) % 2
    return line * plane + (q + plane + sign * (g * 4 + j)) % plane


def slot_matrix(idx_ref, first, rows):
    number = lax.broadcasted_iota(jnp.int32, (rows, idx_ref.shape[1]), 0) + first
    hit = (number == idx_ref[0:1, :]) | (number == idx_ref[1:2, :])
    return jnp.where(hit, 1.0, 0.0).astype(BF)


def begin_part(
    n, cap, half, slots, more_peers, started,
    wq_ref, wout_ref, rows_ref, gain_refs, rt_ref, rank_ref, ct_ref, tok_ref,
    wo_ref, so_ref, idx_ref, ctx_ref, qkv_ref, att_ref, part_ref,
    gw, gs, mine_w, mine_s, info, ctp, cc, send, xp, pp,
    zs, zr, ps, pr, cs, cr, lsem,
):
    me, mine = lax.axis_index("dp"), lax.axis_index("mp")
    plane = n // LINE
    z, q = me // plane, me % plane
    experts, shard = rows_ref.shape
    tok = tok_ref.shape[0]
    lanes = idx_ref.shape[1]
    rp = mine_w.shape[1]
    zpeer = [((z + d) % LINE) * plane + q for d in range(1, LINE)]
    qpeer = [z * plane + (q + d) % plane for d in range(1, plane)]
    full_w, full_s = (wo_ref, so_ref) if rp == shard else (gw, gs)

    if rp > shard:
        mine_w[...] = jnp.zeros_like(mine_w)
    mine_w[0:3, 0:shard, :] = wq_ref[...]
    mine_w[3, 0:shard, :] = wout_ref[...]
    pp[0:128, 0:128] = jnp.zeros((128, 128), F32)
    pp[0:experts, 0:shard] = rows_ref[...].astype(F32)
    for k, gain_ref in enumerate(gain_refs):
        pp[experts + k : experts + k + 1, 0:shard] = gain_ref[...].astype(F32)
    mine_s[...] = jnp.transpose(pp[0:128, 0:128])[0:rp, :].astype(BF)
    greet(more_peers + [{"dp": (me + d) % n} for d in range(1, n)])
    started()

    def at(block):
        rows = pl.ds(pl.multiple_of(block * rp, rp), rp)
        return full_w.at[:, rows, :], full_s.at[rows, :]

    own = at(me)
    sends = []
    for d, p in enumerate(zpeer):
        for i, (a, b) in enumerate(zip((mine_w, mine_s), own)):
            sends.append(remote(a, b, zs.at[d, i], zr.at[d, i], {"dp": p}))
            sends[-1].start()
    for d, p in enumerate(qpeer):
        for i, (a, b) in enumerate(zip((mine_w, mine_s), own)):
            sends.append(remote(a, b, ps.at[d, 0, i], pr.at[d, 0, i], {"dp": p}))
            sends[-1].start()
    here = pl.ds(pl.multiple_of(me * rp, rp), rp)
    full_w[:, here, :] = mine_w[...]
    full_s[here, :] = mine_s[...]

    info[0:2, :] = jnp.full((2, lanes), -1, jnp.int32)
    info[2:3, :] = jnp.full((1, lanes), 1 << 20, jnp.int32)
    info[0:2, 0:tok] = rt_ref[...]
    info[2:3, 0:tok] = rank_ref[...]
    number = lax.broadcasted_iota(jnp.int32, (experts, lanes), 0)
    hot = [jnp.where(number == info[j : j + 1, :], 1.0, 0.0) for j in range(2)]
    ranks = info[2:3, :].astype(F32)
    column = jnp.transpose(jnp.broadcast_to(ranks, (128, lanes)))[:, 0:1]
    before = jnp.where(column < ranks, 1.0, 0.0).astype(BF)
    counts = [mm(h.astype(BF), before, 1, 0) for h in hot]
    counts[1] = counts[1] + jnp.sum(hot[0], axis=1, keepdims=True)
    for j in range(2):
        slot = jnp.sum(counts[j] * hot[j], axis=0, keepdims=True).astype(jnp.int32)
        place = slot - mine * half
        expert_id = info[j : j + 1, :]
        kept = (slot < cap) & (place >= 0) & (place < half) & (expert_id >= 0)
        idx_ref[j : j + 1, :] = jnp.where(kept, expert_id * slots + place, -1)
    ctp[lanes - 64 : lanes, cc : cc + D] = jnp.zeros((64, D), BF)
    ctp[0:tok, cc : cc + D] = ct_ref[...]

    def rows_of(b, carry):
        ones = [slot_matrix(idx_ref, partner(me, n, b * 4 + j) * slots, slots) for j in range(4)]
        block = mm(jnp.concatenate(ones, axis=0), ctp[0:lanes, cc : cc + D], 1, 0).astype(BF)
        send[pl.ds(pl.multiple_of(b * 4 * slots, 16), 4 * slots), 0:D] = block
        return carry

    lax.fori_loop(0, n // 4, rows_of, 0)

    for k in range(1, LINE):
        block = at(((z + LINE - k) % LINE) * plane + q)
        for i in range(2):
            remote(block[i], block[i], zs.at[k - 1, i], zr.at[k - 1, i], {"dp": zpeer[0]}).wait_recv()
        for d, p in enumerate(qpeer):
            for i in range(2):
                sends.append(remote(block[i], block[i], ps.at[d, k, i], pr.at[d, k, i], {"dp": p}))
                sends[-1].start()

    def block_of(p):
        return send.at[pl.ds(pl.multiple_of(p * slots, 16), slots), pl.ds(0, D)]

    local = pltpu.make_async_copy(block_of(0), ctx_ref.at[0], lsem.at[0])
    local.start()

    def ship(p, carry):
        @pl.when(p != 0)
        def _():
            remote(block_of(p), ctx_ref.at[p], cs.at[p], cr.at[p], {"dp": partner(me, n, p)}).start()

        return carry

    lax.fori_loop(0, n, ship, 0)

    images = tok // SEQ
    width = wo_ref.shape[2]
    scale = HD ** (-0.5)
    for i in range(images):
        xp[(i + 1) * SEQ_PAD - 16 : (i + 1) * SEQ_PAD, :] = jnp.zeros((16, D), F32)
        xp[i * SEQ_PAD : i * SEQ_PAD + SEQ, :] = tok_ref[i * SEQ : (i + 1) * SEQ, :].astype(F32)

    def norm(i, carry):
        rows = pl.ds(pl.multiple_of(i * SEQ_PAD, 16), SEQ_PAD)
        xhat, _ = norm_rows(xp[rows, :])
        xp[rows, :] = xhat
        return carry

    lax.fori_loop(0, images, norm, 0)
    for d in range(1, plane):
        for k in range(LINE):
            block = at(((z + LINE - k) % LINE) * plane + (q + plane - d) % plane)
            for i in range(2):
                remote(block[i], block[i], ps.at[d - 1, k, i], pr.at[d - 1, k, i], {"dp": qpeer[0]}).wait_recv()
    if rp > shard:
        line = lax.broadcasted_iota(jnp.int32, (D, n * rp), 0)
        where = lax.broadcasted_iota(jnp.int32, (D, n * rp), 1)
        squeeze = jnp.where(where == line // shard * rp + line % shard, 1.0, 0.0).astype(BF)
        for c in range(4):
            wo_ref[c] = mm(squeeze, gw[c], 1, 0).astype(BF)
        so_ref[...] = mm(squeeze, gs[...], 1, 0).astype(BF)
    gain = jnp.transpose(so_ref[...].astype(F32))[experts : experts + 1, :]
    lane = lax.broadcasted_iota(jnp.int32, (1, 2 * HD), 1)
    masks = [jnp.where(lane // HD == h, 1.0, 0.0).astype(BF) for h in range(2)]
    valid = lax.broadcasted_iota(jnp.int32, (1, SEQ_PAD), 1) < SEQ

    def image(i, carry):
        rows = pl.ds(pl.multiple_of(i * SEQ_PAD, 16), SEQ_PAD)
        normed = (xp[rows, :] * gain).astype(BF)
        for c in range(3):
            qkv_ref[rows, c * width : (c + 1) * width] = mm(normed, wo_ref[c], 1, 0).astype(BF)
        for p in range(width // (2 * HD)):
            cols = slice(p * 2 * HD, (p + 1) * 2 * HD)
            qs, ks, vs = (
                qkv_ref[rows, c * width + p * 2 * HD : c * width + (p + 1) * 2 * HD] for c in range(3)
            )
            outs = []
            for h in range(2):
                scores = mm(qs * masks[h], ks, 1, 1) * scale
                scores = jnp.where(valid, scores, -1e30)
                raised = jnp.exp(scores - jnp.max(scores, axis=-1, keepdims=True))
                weights = raised * (1.0 / jnp.sum(raised, axis=-1, keepdims=True))
                outs.append(mm(weights.astype(BF), vs, 1, 0))
            att_ref[rows, cols] = jnp.where(lane < HD, outs[0], outs[1]).astype(BF)
        pp[rows, :] = mm(att_ref[rows, 0:width], wo_ref[3], 1, 1)
        return carry

    lax.fori_loop(0, images, image, 0)
    for i in range(images):
        part_ref[i * SEQ : (i + 1) * SEQ, :] = pp[i * SEQ_PAD : i * SEQ_PAD + SEQ, :]

    def arrived(p):
        @pl.when(p != 0)
        def _():
            remote(block_of(p), ctx_ref.at[p], cs.at[p], cr.at[p], {"dp": partner(me, n, p)}).wait_recv()

    def ended():
        for c in sends:
            c.wait_send()
        local.wait()

        def sent(p, carry):
            @pl.when(p != 0)
            def _():
                remote(block_of(p), ctx_ref.at[p], cs.at[p], cr.at[p], {"dp": partner(me, n, p)}).wait_send()

            return carry

        lax.fori_loop(0, n, sent, 0)

    return arrived, ended


def begin_kernel(n, cap, half, slots, *refs):
    arrived, ended = begin_part(n, cap, half, slots, [], lambda: None, *refs[:21], 0, *refs[21:])

    def finish(p, carry):
        arrived(p)
        return carry

    lax.fori_loop(0, n, finish, 0)
    ended()


def begin(wq, wout, rows, gains, rt, rank, ct, tok, n, experts, cap, half, slots):
    images = tok.shape[0] // SEQ
    shard, width = wout.shape
    rp = up(shard, 16)
    lanes = up(tok.shape[0], 128)
    plane = n // LINE
    sem = pltpu.SemaphoreType.DMA
    shape = jax.ShapeDtypeStruct
    vmem = pltpu.VMEM
    spare = n * rp if rp > shard else 16

    def kernel(wq_ref, wout_ref, rows_ref, g1, g2, g3, *rest):
        begin_kernel(n, cap, half, slots, wq_ref, wout_ref, rows_ref, (g1, g2, g3), *rest)

    return pl.pallas_call(
        kernel,
        out_shape=(
            shape((4, D, width), BF), shape((D, 128), BF), shape((2, lanes), jnp.int32),
            shape((n, slots, D), BF), shape((images * SEQ_PAD, 3 * width), BF),
            shape((images * SEQ_PAD, width), BF), shape((up(tok.shape[0], 16), D), F32),
        ),
        in_specs=[whole()] * 10,
        out_specs=(whole(), whole(), whole(), pl.BlockSpec(memory_space=pl.ANY), whole(), whole(), whole()),
        scratch_shapes=[
            vmem((4, spare, width), BF), vmem((spare, 128), BF),
            vmem((4, rp, width), BF), vmem((rp, 128), BF), vmem((8, lanes), jnp.int32),
            vmem((lanes, D), BF), vmem((n * slots, D), BF),
            vmem((images * SEQ_PAD, D), F32), vmem((images * SEQ_PAD, D), F32),
            sem((LINE - 1, 2)), sem((LINE - 1, 2)),
            sem((plane - 1, LINE, 2)), sem((plane - 1, LINE, 2)),
            sem((n,)), sem((n,)), sem((1,)),
        ],
        compiler_params=params(collective_id=0, has_side_effects=True),
        name="begin",
    )(wq, wout, rows, *gains, rt, rank, ct, tok)


def row_chunks(rows):
    return [(s, min(256, rows - s)) for s in range(0, rows, 256)]


def token_send(n, send, x_ref, xs, xr, p, peer):
    return remote(send.at[p], x_ref.at[p], xs.at[p], xr.at[p], {"dp": peer})


def send_tokens(
    n, half, early, part_ref, tok_ref, small_ref, idx_ref, hid_ref, n2, prob_ref, x_ref,
    own, other, send, p2, hs, hr, xs, xr,
):
    me, mine = lax.axis_index("dp"), lax.axis_index("mp")
    plane = n // LINE
    tok = tok_ref.shape[0]
    slots = send.shape[1]
    experts, lanes = prob_ref.shape
    tr = other.shape[0]
    sibling = {"mp": 1 - mine}
    own[tr - 16 : tr, :] = jnp.zeros((16, D), BF)
    copies = []
    for c, (start, size) in enumerate(row_chunks(tr)):
        stop = min(start + size, tok)
        own[start:stop, :] = part_ref[start:stop, :].astype(BF)
        rows = pl.ds(start, size)
        copy = remote(own.at[rows, :], other.at[rows, :], hs.at[c], hr.at[c], sibling)
        copy.start()
        copies.append(copy)
    gains = jnp.transpose(small_ref[...].astype(F32))
    gain = gains[experts + 1 : experts + 2, :]
    bias = gains[experts + 2 : experts + 3, :]
    n2[lanes - 64 : lanes, 0:D] = jnp.zeros((64, D), BF)
    for c, (start, size) in enumerate(row_chunks(tr)):
        stop = min(start + size, tok)
        copies[c].wait_recv()
        both = own[start:stop, :].astype(F32) + other[start:stop, :].astype(F32)
        hidden = tok_ref[start:stop, :].astype(F32) + both + bias
        hid_ref[start:stop, :] = hidden
        xhat, _ = norm_rows(hidden)
        n2[start:stop, 0:D] = (xhat * gain).astype(BF)
    logits = mm(gains[0:experts, :].astype(BF), n2[0:lanes, 0:D], 1, 1)
    raised = jnp.exp(logits - jnp.max(logits, axis=0, keepdims=True))
    probs = raised / jnp.sum(raised, axis=0, keepdims=True)
    prob_ref[...] = probs
    high, low = split_two(probs)
    p2[0:experts, :] = high
    p2[experts:, :] = low
    place = lax.broadcasted_iota(jnp.int32, (slots, slots), 0)
    number = lax.broadcasted_iota(jnp.int32, (2 * experts, slots), 0)

    def step(b, carry):
        hot = [slot_matrix(idx_ref, partner(me, n, b * 4 + j) * slots, slots) for j in range(4)]
        block = mm(jnp.concatenate(hot, axis=0), n2[0:lanes, 0:D], 1, 0)
        for j in range(4):
            p = b * 4 + j
            peer = partner(me, n, p)
            gates = mm(p2[...], hot[j], 1, 1)
            row_high = jnp.sum(jnp.where(number == peer, gates, 0.0), axis=0, keepdims=True)
            row_low = jnp.sum(jnp.where(number == peer + experts, gates, 0.0), axis=0, keepdims=True)
            rows = block[j * slots : (j + 1) * slots, :]
            left = jnp.where(place == half, row_high, jnp.where(place == half + 1, row_low, rows[:, 0:slots]))
            send[p, :, :] = rows.astype(BF)
            send[p, :, 0:slots] = left.astype(BF)

            @pl.when((p != 0) & (p < early))
            def _():
                token_send(n, send, x_ref, xs, xr, p, peer).start()

        return carry

    lax.fori_loop(0, n // 4, step, 0)
    x_ref[0] = send[0]
    for copy in copies:
        copy.wait_send()


def dispatch_kernel(
    n, half, part_ref, tok_ref, small_ref, idx_ref, hid_ref, prob_ref, x_ref,
    n2, own, other, send, p2, hs, hr, xs, xr,
):
    me, mine = lax.axis_index("dp"), lax.axis_index("mp")
    plane = n // LINE
    greet([{"mp": 1 - mine}] + [{"dp": (me + d) % n} for d in range(1, n)])
    send_tokens(
        n, half, n, part_ref, tok_ref, small_ref, idx_ref, hid_ref, n2, prob_ref, x_ref,
        own, other, send, p2, hs, hr, xs, xr,
    )

    def finish(p, carry):
        @pl.when(p != 0)
        def _():
            token_send(n, send, x_ref, xs, xr, p, partner(me, n, p)).wait()

        return carry

    lax.fori_loop(0, n, finish, 0)


def dispatch(part, tok, small, idx, n, experts, half, slots):
    lanes = idx.shape[1]
    tr = up(tok.shape[0], 16)
    sem = pltpu.SemaphoreType.DMA
    vmem = pltpu.VMEM
    chunks = len(row_chunks(tr))
    return pl.pallas_call(
        functools.partial(dispatch_kernel, n, half),
        out_shape=(
            jax.ShapeDtypeStruct(tok.shape, F32),
            jax.ShapeDtypeStruct((experts, lanes), F32),
            jax.ShapeDtypeStruct((n, slots, D), BF),
        ),
        in_specs=[whole()] * 4,
        out_specs=(whole(),) * 3,
        scratch_shapes=[
            vmem((lanes, D), BF), vmem((tr, D), BF), vmem((tr, D), BF), vmem((n, slots, D), BF),
            vmem((2 * experts, lanes), BF),
            sem((chunks,)), sem((chunks,)), sem((n,)), sem((n,)),
        ],
        compiler_params=params(collective_id=1, has_side_effects=True),
        name="dispatch",
    )(part, tok, small, idx)


def expert_kernel(
    n, cap, half, fused,
    first, ct_ref, wi_own, wi_sib, wb_own, wb_sib, bi_own, bi_sib, bb_ref,
    idx_ref, seen_ref, tok_ct, small_ref,
    hg_ref, sg_ref, y_ref, gi_ref, gi_in, gb_ref, gb_in, little_ref, little_in, hid_out, prob_ref,
    wo_ref, qkv_out, att_out,
    vi_own, vi_sib, vb_own, vb_sib, g_s, act_own, act_sib, dp_own, dp_sib, dx_s, back, acc, other,
    ct_s, y_s, stage, gp, gp_other, x_ref, send, p2, mine_w, mine_s, info, bias_s, bias_in,
    lsem, ysem, gsem, ss, rs, hs, hr, ms, mr, xs, xr, es, er, zs, zr, ps, pr, cs, cr, bsem,
):
    me, mine = lax.axis_index("dp"), lax.axis_index("mp")
    sibling = {"mp": 1 - mine}
    slots = x_ref.shape[1]
    tok = tok_ct.shape[0]
    experts = gp.shape[0]
    hidden = wi_own.shape[1]
    group = 4 * slots
    batches = n // 4
    early = n // 2 if fused else n
    lanes = gp.shape[1]
    owns = [(wi_own, vi_own), (wb_own, vb_own)]
    if not fused:
        owns += [(wi_sib, vi_sib), (wb_sib, vb_sib), (first, x_ref)]
    loads = [pltpu.make_async_copy(a, b, lsem.at[i]) for i, (a, b) in enumerate(owns)]
    for c in loads:
        c.start()
    if fused:
        halves = [
            remote(wi_own, vi_sib, ms.at[3], mr.at[3], sibling),
            remote(wb_own, vb_sib, ms.at[4], mr.at[4], sibling),
            remote(bias_s, bias_in, ms.at[5], mr.at[5], sibling),
        ]
        bias_s[...] = jnp.zeros_like(bias_s)
        bias_s[0:1, :] = bi_own[...].astype(F32)

        def started():
            for c in halves:
                c.start()

        arrived, ended = begin_part(
            n, cap, half, slots, [sibling], started, *first,
            wo_ref, small_ref, idx_ref, ct_ref, act_own, act_sib, hg_ref,
            None, None, mine_w, mine_s, info, act_sib, D, dp_own, acc, stage,
            zs, zr, ps, pr, cs, cr, bsem,
        )
        rows = qkv_out.shape[0]
        kept = [
            pltpu.make_async_copy(act_own.at[pl.ds(0, rows), pl.ds(0, qkv_out.shape[1])], qkv_out, lsem.at[2]),
            pltpu.make_async_copy(act_sib.at[pl.ds(0, rows), pl.ds(0, att_out.shape[1])], att_out, lsem.at[3]),
        ]
        for c in kept:
            c.start()
        send_tokens(
            n, half, early, hg_ref, first[-1], small_ref, idx_ref, hg_ref, dp_sib, prob_ref, x_ref,
            g_s, other, send, p2, es, er, xs, xr,
        )
        keep = pltpu.make_async_copy(hg_ref, hid_out, lsem.at[5])
        keep.start()
        ended()
        for c in kept:
            c.wait()
        for c in halves:
            c.wait()
        bias_own, bias_sib = bi_own[...].astype(F32), bias_in[0:1, :]
    else:
        greet([sibling] + [{"dp": (me + d) % n} for d in range(1, n)])
        keep = pltpu.make_async_copy(hid_out, hg_ref, lsem.at[5])
        keep.start()
        bias_own, bias_sib = bi_own[...].astype(F32), bi_sib[...].astype(F32)
    little_ref[...] = jnp.zeros_like(little_ref)

    def ct_here(b, j):
        if fused:
            arrived(b * 4 + j)

    def cts(b, j):
        return pltpu.make_async_copy(ct_ref.at[b * 4 + j], ct_s.at[j], ysem.at[0, j])

    def ys(b, j):
        return pltpu.make_async_copy(y_s.at[j], y_ref.at[partner(me, n, b * 4 + j, -1)], ysem.at[1, j])

    for j in range(4):
        ct_here(0, j)
        cts(0, j).start()
    for c in loads:
        c.wait()
    chunk = 768
    row = lax.broadcasted_iota(jnp.int32, (group, 16), 0)
    number = lax.broadcasted_iota(jnp.int32, (group, 16), 1)
    member = jnp.where(row // slots == number, 1.0, 0.0).astype(BF)
    spot = lax.broadcasted_iota(jnp.int32, (group, 128), 0) % slots
    here = spot == lax.broadcasted_iota(jnp.int32, (group, 128), 1)
    row_t = lax.broadcasted_iota(jnp.int32, (16, group), 1)
    number_t = lax.broadcasted_iota(jnp.int32, (16, group), 0)
    pick = jnp.where(
        (row_t == number_t * slots + half) | (row_t == number_t * slots + half + 1), 1.0, 0.0
    ).astype(BF)
    member_t = jnp.where(row_t // slots == number_t, 1.0, 0.0).astype(BF)
    puts = [jnp.where(row == number * slots + half + i, 1.0, 0.0).astype(BF) for i in range(2)]

    def batch(b, carry):
        at = pl.ds(pl.multiple_of(b * group, 16), group)
        if fused:
            @pl.when(b == batches // 4)
            def _():
                def more(p, carry):
                    token_send(n, send, x_ref, xs, xr, p, partner(me, n, p)).start()
                    return carry

                lax.fori_loop(early, n, more, 0)

            for j in range(4):
                p = b * 4 + j

                @pl.when(p != 0)
                def _():
                    token_send(n, send, x_ref, xs, xr, p, partner(me, n, p)).wait_recv()

        x = x_ref[pl.ds(b * 4, 4)].reshape(group, D)
        high, low = split_two(mm(pick, x[:, 0:128], 1, 0))
        wide = mm(member, high, 1, 0) + mm(member, low, 1, 0)
        gate = jnp.sum(jnp.where(here, wide, 0.0), axis=1, keepdims=True)
        for j in range(4):
            cts(b, j).wait()
        g_s[at, :] = (gate * ct_s[...].reshape(group, D).astype(F32)).astype(BF)
        little_ref[0:1, 2 * hidden :] += jnp.sum(g_s[at, :].astype(F32), axis=0, keepdims=True)
        for part, (vi, vb, bi, acts, dps) in enumerate(
            ((vi_own, vb_own, bias_own, act_own, dp_own), (vi_sib, vb_sib, bias_sib, act_sib, dp_sib))
        ):
            for c in range(hidden // chunk):
                cols = slice(c * chunk, (c + 1) * chunk)
                pre = mm(x_ref[pl.ds(b * 4, 4)].reshape(group, D), vi[:, cols], 1, 0) + bi[:, cols]
                phi = 0.5 * (1.0 + lax.erf(pre * (0.5**0.5)))
                slope = phi + pre * (jnp.exp(-0.5 * pre * pre) * ((2.0 * jnp.pi) ** -0.5))
                acts[at, cols] = (pre * phi).astype(BF)
                grad = (mm(g_s[at, :], vb[cols, :], 1, 1) * slope).astype(BF)
                dps[at, cols] = grad
                place = slice(part * hidden + c * chunk, part * hidden + (c + 1) * chunk)
                little_ref[0:1, place] += jnp.sum(grad.astype(F32), axis=0, keepdims=True)
        dx = mm(dp_own[at, :], vi_own[...], 1, 1) + mm(dp_sib[at, :], vi_sib[...], 1, 1)
        y = mm(act_own[at, :], vb_own[...], 1, 0) + mm(act_sib[at, :], vb_sib[...], 1, 0)
        y = (y + bb_ref[...].astype(F32)).astype(BF).astype(F32)
        dots = jnp.sum(ct_s[...].reshape(group, D).astype(F32) * y, axis=1, keepdims=True)
        high, low = split_two(jnp.where(here, dots, 0.0))
        high, low = mm(member_t, high, 1, 0).astype(BF), mm(member_t, low, 1, 0).astype(BF)
        left = dx[:, 0:128] + mm(puts[0], high, 1, 0) + mm(puts[1], low, 1, 0)
        dx = jnp.concatenate([left, dx[:, 128:]], axis=1)
        dx_s[pl.ds(b * 4, 4)] = dx.astype(BF).reshape(4, slots, D)
        for j in range(4):
            p = b * 4 + j

            @pl.when(p != 0)
            def _():
                remote(dx_s.at[p], back.at[p], ss.at[p], rs.at[p], {"dp": partner(me, n, p, -1)}).start()

        @pl.when(b > 0)
        def _():
            for j in range(4):
                ys(b - 1, j).wait()

        y_s[...] = (gate * y).astype(BF).reshape(4, slots, D)
        for j in range(4):
            ys(b, j).start()

        @pl.when(b + 1 < batches)
        def _():
            for j in range(4):
                ct_here(b + 1, j)
                cts(b + 1, j).start()

        return carry

    lax.fori_loop(0, batches, batch, 0)
    back[0] = dx_s[0]
    little = remote(little_ref, little_in, ms.at[2], mr.at[2], sibling)
    little.start()

    rows_all = n * slots
    steps = 3
    size = D // steps
    wide = hidden // 2
    swaps = []

    def out_i(r, c):
        return pltpu.make_async_copy(
            stage.at[r % 2 * 2 * size + c * size : r % 2 * 2 * size + (c + 1) * size, :],
            gi_ref.at[r * size : (r + 1) * size, c * wide : (c + 1) * wide], gsem.at[c, r],
        )

    def out_b(r):
        return pltpu.make_async_copy(
            stage.at[r % 2 * 2 * size : (r % 2 + 1) * 2 * size, :], gb_ref.at[r * 2 * size : (r + 1) * 2 * size, :], gsem.at[2, r]
        )

    for r in range(steps):
        at = slice(r * size, (r + 1) * size)
        left = x_ref[:, :, at].reshape(rows_all, size)
        vi_sib[at, :] = mm(left, dp_sib[...], 0, 0).astype(BF)
        for c in range(2):
            if r >= 2:
                out_i(r - 2, c).wait()
            at_s = r % 2 * 2 * size + c * size
            stage[at_s : at_s + size, :] = mm(left, dp_own[:, c * wide : (c + 1) * wide], 0, 0)
            out_i(r, c).start()
    copy = remote(vi_sib, gi_in, ms.at[0], mr.at[0], sibling)
    copy.start()
    swaps.append(copy)

    acc[...] = jnp.zeros_like(acc)
    gp[...] = jnp.zeros_like(gp)
    place = lax.broadcasted_iota(jnp.int32, (slots, 128), 0)
    count = lax.broadcasted_iota(jnp.int32, (experts, slots), 0)

    def combine(b, carry):
        hot = []
        for j in range(4):
            d = b * 4 + j
            source = partner(me, n, d)

            @pl.when(d != 0)
            def _():
                remote(dx_s.at[d], back.at[d], ss.at[d], rs.at[d], {"dp": source}).wait_recv()

            hot.append(slot_matrix(idx_ref, source * slots, slots))
            extra = back[d, :, 0:128].astype(F32)
            high = jnp.sum(jnp.where(place == half, extra, 0.0), axis=0, keepdims=True)[:, 0:slots]
            low = jnp.sum(jnp.where(place == half + 1, extra, 0.0), axis=0, keepdims=True)[:, 0:slots]
            for value in (high, low):
                gp[...] += mm(jnp.where(count == source, value, 0.0).astype(BF), hot[j], 1, 0)
        block = back[pl.ds(b * 4, 4)].reshape(group, D)
        acc[0:lanes, :] += mm(jnp.concatenate(hot, axis=0), block, 0, 0)
        return carry

    lax.fori_loop(0, batches // 2, combine, 0)
    for r in range(steps):
        at = slice(r * 2 * size, (r + 1) * 2 * size)
        vb_sib[at, :] = mm(act_sib[:, at], g_s[...], 0, 0).astype(BF)
        if r == 0:
            for c in range(2):
                out_i(1, c).wait()
                out_i(2, c).wait()
        if r >= 2:
            out_b(r - 2).wait()
        stage[r % 2 * 2 * size : (r % 2 + 1) * 2 * size, :] = mm(act_own[:, at], g_s[...], 0, 0)
        out_b(r).start()
    copy = remote(vb_sib, gb_in, ms.at[1], mr.at[1], sibling)
    copy.start()
    swaps.append(copy)
    lax.fori_loop(batches // 2, batches, combine, 0)

    little.wait()
    copies = []
    own = g_s
    own[other.shape[0] - 16 : other.shape[0], :] = jnp.zeros((16, D), BF)
    for c, (start, length) in enumerate(row_chunks(other.shape[0])):
        stop = min(start + length, tok)
        own[start:stop, :] = acc[start:stop, :].astype(BF)
        rows = pl.ds(start, length)
        copy = remote(own.at[rows, :], other.at[rows, :], hs.at[c], hr.at[c], sibling)
        copy.start()
        copies.append(copy)
    copy = remote(gp, gp_other, hs.at[len(copies)], hr.at[len(copies)], sibling)
    copy.start()
    copy.wait()
    probs = prob_ref[...] if fused else seen_ref[...]
    grad_probs = gp[...] + gp_other[...]
    logits = (probs * (grad_probs - jnp.sum(grad_probs * probs, axis=0, keepdims=True))).astype(BF)
    gains = jnp.transpose(small_ref[...].astype(F32))
    gain = gains[experts + 1 : experts + 2, :]
    acc[0:lanes, :] = mm(logits, gains[0:experts, :].astype(BF), 0, 0)
    sg_ref[...] = jnp.zeros_like(sg_ref)
    gain_sum = jnp.zeros((1, D), F32)
    bias_sum = jnp.zeros((1, D), F32)
    act_own[lanes - 64 : lanes, 0:D] = jnp.zeros((64, D), BF)
    keep.wait()
    for c, (start, length) in enumerate(row_chunks(other.shape[0])):
        stop = min(start + length, tok)
        copies[c].wait_recv()
        grad = own[start:stop, :].astype(F32) + other[start:stop, :].astype(F32) + acc[start:stop, :]
        xhat, inverse = norm_rows(hg_ref[start:stop, :])
        act_own[start:stop, 0:D] = (xhat * gain).astype(BF)
        hidden_grad = tok_ct[start:stop, :].astype(F32) + norm_back(grad, gain, xhat, inverse)
        hg_ref[start:stop, :] = hidden_grad
        gain_sum += jnp.sum(grad * xhat, axis=0, keepdims=True)
        bias_sum += jnp.sum(hidden_grad, axis=0, keepdims=True)
    sg_ref[0:experts, :] = mm(logits, act_own[0:lanes, 0:D], 1, 0)
    sg_ref[experts : experts + 1, :] = gain_sum
    sg_ref[experts + 1 : experts + 2, :] = bias_sum
    for copy in copies:
        copy.wait_send()

    def finish(p, carry):
        @pl.when(p != 0)
        def _():
            remote(dx_s.at[p], back.at[p], ss.at[p], rs.at[p], {"dp": partner(me, n, p, -1)}).wait_send()
            if fused:
                token_send(n, send, x_ref, xs, xr, p, partner(me, n, p)).wait_send()

        return carry

    lax.fori_loop(0, n, finish, 0)
    for j in range(4):
        ys(batches - 1, j).wait()
    for r in range(1, steps):
        out_b(r).wait()
    for copy in swaps:
        copy.wait()


def expert(first, ct_rows, wi, wb, bi, bb, idx, probs, hid, ct, small, n, cap, half, slots):
    fused = hid is None
    rows = n * slots
    hidden = wi[0].shape[1]
    lanes = up(ct.shape[0], 128)
    experts = n
    tr = up(ct.shape[0], 16)
    chunks = len(row_chunks(tr))
    flat = ct.shape[0] // SEQ * SEQ_PAD
    shape = jax.ShapeDtypeStruct
    sem = pltpu.SemaphoreType.DMA
    vmem = pltpu.VMEM
    far = pl.BlockSpec(memory_space=pl.ANY)
    outs = [
        shape(ct.shape, F32), shape((up(experts + 3, 8), D), F32), shape((n, slots, D), BF),
        shape((D, hidden), F32), shape((D, hidden), BF),
        shape((hidden, D), F32), shape((hidden, D), BF),
        shape((8, 2 * hidden + D), F32), shape((8, 2 * hidden + D), F32),
    ]
    out_specs = [whole(), whole(), far, far, far, far, far, whole(), whole()]
    if fused:
        wq, wout, router_t, gains, rt, rank, tok = first
        shard, width = wout.shape
        plane = n // LINE
        ins = [wq, wout, router_t, *gains, rt, rank, ct, tok, wi[0], wb[0], bi[0], bb]
        in_specs = [whole()] * 10 + [far, far, whole(), whole()]
        outs += [
            shape(ct.shape, F32), shape((experts, lanes), F32), shape((4, D, width), BF), shape((D, 128), BF),
            shape((2, lanes), jnp.int32), shape((n, slots, D), BF),
            shape((flat, 3 * width), BF), shape((flat, width), BF),
        ]
        out_specs += [far, whole(), whole(), whole(), whole(), far, far, far]

        def kernel(*refs):
            wq, wout, rows_t, g1, g2, g3, rt, rank, ct, tok, wi, wb, bi, bb = refs[:14]
            main, (hid, prob, wo, so, idx, ctx, qkv, att) = refs[14:23], refs[23:31]
            expert_kernel(
                n, cap, half, True, (wq, wout, rows_t, (g1, g2, g3), rt, rank, ct, tok),
                ctx, wi, None, wb, None, bi, None, bb, idx, None, ct, so,
                *main, hid, prob, wo, qkv, att, *refs[31:],
            )

        spare = [vmem((4, shard, width), BF), vmem((shard, 128), BF), vmem((8, lanes), jnp.int32)]
        spare += [vmem((8, hidden), F32)] * 2
        grid = (plane - 1, LINE, 2)
        send_rows = (n, slots, D)
    else:
        ins = [first, ct_rows, wi[0], wi[1], wb[0], wb[1], bi[0], bi[1], bb, idx, probs, ct, small, hid]
        in_specs = [far] * 6 + [whole()] * 7 + [far]

        def kernel(*refs):
            ins, hid_ref, outs, rest = refs[:13], refs[13], refs[14:23], refs[23:]
            expert_kernel(n, cap, half, False, *ins, *outs, hid_ref, ins[10], None, None, None, *rest)

        spare = [vmem((1, 16, 128), BF), vmem((16, 128), BF), vmem((8, 128), jnp.int32)]
        spare += [vmem((8, 128), F32)] * 2
        grid = (1, 1, 2)
        send_rows = (1, 16, 128)

    return pl.pallas_call(
        kernel,
        out_shape=tuple(outs),
        in_specs=in_specs,
        out_specs=tuple(out_specs),
        scratch_shapes=[
            vmem((D, hidden), BF), vmem((D, hidden), BF), vmem((hidden, D), BF), vmem((hidden, D), BF),
            vmem((rows, D), BF),
            vmem((rows, hidden), BF), vmem((rows, hidden), BF),
            vmem((rows, hidden), BF), vmem((rows, hidden), BF),
            vmem((n, slots, D), BF), vmem((n, slots, D), BF),
            vmem((flat if fused else lanes, D), F32), vmem((tr, D), BF),
            vmem((4, slots, D), BF), vmem((4, slots, D), BF),
            vmem((flat if fused else 1024, D), F32),
            vmem((experts, lanes), F32), vmem((experts, lanes), F32),
            vmem((n, slots, D), BF), vmem(send_rows, BF), vmem((2 * experts, lanes), BF),
            *spare,
            sem((6,)), sem((2, 4)), sem((3, 3)), sem((n,)), sem((n,)),
            sem((chunks + 1,)), sem((chunks + 1,)), sem((6,)), sem((6,)),
            sem((n,)), sem((n,)), sem((chunks,)), sem((chunks,)),
            sem((LINE - 1, 2)), sem((LINE - 1, 2)), sem(grid), sem(grid), sem((n,)), sem((n,)), sem((3,)),
        ],
        compiler_params=params(collective_id=2, has_side_effects=True),
        name="expert",
    )(*ins)


def attend_back_kernel(
    experts, hg_ref, tok_ref, small_ref, w_ref, qkv_ref, att_ref, gi_ref, gi_in, gb_ref, gb_in, little_ref, little_in,
    dn_ref, dw_ref, gi_out, gb_out, gbi_out, gbb_out,
    normed, low, dqkv, pp, flat,
):
    images = normed.shape[0]
    scale = HD ** (-0.5)
    step = pl.program_id(0)
    gi_out[...] = gi_ref[...] + gi_in[...].astype(F32)
    gb_out[...] = gb_ref[...] + gb_in[...].astype(F32)

    @pl.when(step == 0)
    def _():
        hidden = gbi_out.shape[1]
        gbi_out[...] = little_ref[0:1, 0:hidden] + little_in[0:1, hidden : 2 * hidden]
        gbb_out[...] = little_ref[0:1, 2 * hidden :] + little_in[0:1, 2 * hidden :]
        pp[:, SEQ_PAD - 16 : SEQ_PAD, :] = jnp.zeros((images, 16, D), F32)
        for i in range(images):
            pp[i, 0:SEQ, :] = hg_ref[i * SEQ : (i + 1) * SEQ, :]
        low[...] = pp[...].astype(BF)
        for i in range(images):
            pp[i, 0:SEQ, :] = tok_ref[i * SEQ : (i + 1) * SEQ, :].astype(F32)

    @pl.when(step < images)
    def _():
        i = step
        width = w_ref.shape[2]
        mine = pl.ds(pl.multiple_of(i * SEQ_PAD, 16), SEQ_PAD)
        gains = jnp.transpose(small_ref[...].astype(F32))
        gain = gains[experts : experts + 1, :]
        lane = lax.broadcasted_iota(jnp.int32, (1, 2 * HD), 1)
        masks = [jnp.where(lane // HD == h, 1.0, 0.0).astype(BF) for h in range(2)]
        valid = lax.broadcasted_iota(jnp.int32, (1, SEQ_PAD), 1) < SEQ
        xhat, _ = norm_rows(pp[i])
        normed[i] = (xhat * gain).astype(BF)
        grad_att = mm(low[i], w_ref[3], 1, 0).astype(BF)
        for p in range(w_ref.shape[2] // (2 * HD)):
            cols = slice(p * 2 * HD, (p + 1) * 2 * HD)
            q, k, v = (
                qkv_ref[mine, c * width + p * 2 * HD : c * width + (p + 1) * 2 * HD] for c in range(3)
            )
            pair = grad_att[:, cols]
            grads = []
            for h in range(2):
                scores = mm(q * masks[h], k, 1, 1) * scale
                scores = jnp.where(valid, scores, -1e30)
                raised = jnp.exp(scores - jnp.max(scores, axis=-1, keepdims=True))
                weights = raised * (1.0 / jnp.sum(raised, axis=-1, keepdims=True))
                grad_weights = mm(pair * masks[h], v, 1, 1)
                product = grad_weights * weights
                grad_scores = product - weights * jnp.sum(product, axis=-1, keepdims=True)
                scores_low = grad_scores.astype(BF)
                grads.append((
                    mm(scores_low, k, 1, 0) * scale,
                    mm(scores_low, q, 0, 0) * scale,
                    mm(weights.astype(BF), pair, 0, 0),
                ))
            for c in range(3):
                dqkv[c, i, :, cols] = jnp.where(lane < HD, grads[0][c], grads[1][c]).astype(BF)
        total = mm(dqkv[0, i], w_ref[0], 1, 1)
        for c in range(1, 3):
            total += mm(dqkv[c, i], w_ref[c], 1, 1)
        pp[i] = total

    @pl.when(step == images)
    def _():
        for i in range(images):
            flat[i * SEQ : (i + 1) * SEQ, :] = pp[i, 0:SEQ, :]
        flat[images * SEQ :, :] = jnp.zeros((flat.shape[0] - images * SEQ, D), F32)
        dn_ref[...] = flat[...].astype(BF)
        rows = images * SEQ_PAD

        def weight(r, carry):
            at = pl.ds(pl.multiple_of(r * 256, 256), 256)
            left = normed[:, :, at].reshape(rows, 256)
            for c in range(3):
                dw_ref[c, at, :] = mm(left, dqkv[c].reshape(rows, -1), 0, 0).astype(BF)
            left = low[:, :, at].reshape(rows, 256)
            dw_ref[3, at, :] = mm(left, att_ref[...], 0, 0).astype(BF)
            return carry

        lax.fori_loop(0, D // 256, weight, 0)


def attend_back(hg, tok, small, w, qkv, att, gi, gi_in, gb, gb_in, little, little_in, experts):
    images = tok.shape[0] // SEQ
    width = w.shape[2]
    steps = images + 1
    hidden = gi.shape[1]
    tr = up(tok.shape[0], 16)
    line_i = pl.BlockSpec((gi.shape[0] // steps, hidden), lambda k: (k, 0))
    line_b = pl.BlockSpec((hidden // steps, D), lambda k: (k, 0))
    return pl.pallas_call(
        functools.partial(attend_back_kernel, experts),
        grid=(steps,),
        out_shape=(
            jax.ShapeDtypeStruct((tr, D), BF),
            jax.ShapeDtypeStruct((4, D, width), BF),
            jax.ShapeDtypeStruct(gi.shape, F32),
            jax.ShapeDtypeStruct(gb.shape, F32),
            jax.ShapeDtypeStruct((1, hidden), F32),
            jax.ShapeDtypeStruct((1, D), F32),
        ),
        in_specs=[whole()] * 6 + [line_i, line_i, line_b, line_b, whole(), whole()],
        out_specs=(whole(), whole(), line_i, line_b, whole(), whole()),
        scratch_shapes=[
            pltpu.VMEM((images, SEQ_PAD, D), BF),
            pltpu.VMEM((images, SEQ_PAD, D), BF),
            pltpu.VMEM((3, images, SEQ_PAD, width), BF),
            pltpu.VMEM((images, SEQ_PAD, D), F32),
            pltpu.VMEM((tr, D), F32),
        ],
        compiler_params=params(dimension_semantics=("arbitrary",)),
        name="attend_back",
    )(hg, tok, small, w, qkv, att, gi, gi_in, gb, gb_in, little, little_in)


def last_kernel(
    n, experts, by_place, dw_ref, sg_ref, dn_ref, small_ref, idx_ref, tok_ref, hg_ref, y_ref, hid_ref,
    tg_ref, out_ref, gw_ref, gs_ref,
    other, mix, mix_other, sm, r1, q1, s1, t1, r2, q2, acc, own_w, hg_s, y_s, hid_s, tok_s,
    hs, hr, as_, ar, bs, br, lsem,
):
    me, mine = lax.axis_index("dp"), lax.axis_index("mp")
    plane = n // LINE
    z, q = me // plane, me % plane
    tok = tok_s.shape[0]
    rp = own_w.shape[2]
    tr = other.shape[0]
    sibling = {"mp": 1 - mine}
    zpeer = [((z + d) % LINE) * plane + q for d in range(1, LINE)]
    qpeer = [z * plane + (q + d) % plane for d in range(1, plane)]
    loads = [
        pltpu.make_async_copy(a, b, lsem.at[i])
        for i, (a, b) in enumerate(
            ((tok_ref, tok_s), (hg_ref, hg_s), (y_ref, y_s), (hid_ref, hid_s), (dw_ref.at[:, :, q], own_w))
        )
    ]
    for c in loads:
        c.start()
    greet([sibling] + [{"dp": p} for p in zpeer + qpeer])
    copies = []
    for c, (start, size) in enumerate(row_chunks(tr)):
        rows = pl.ds(start, size)
        copy = remote(dn_ref.at[rows, :], other.at[rows, :], hs.at[c], hr.at[c], sibling)
        copy.start()
        copies.append(copy)
    sends = []
    for d, p in enumerate(qpeer):
        c = remote(dw_ref.at[:, :, (q + d + 1) % plane], r1.at[d], as_.at[d, 0], ar.at[d, 0], {"dp": p})
        c.start()
        sends.append(c)
    gains = jnp.transpose(small_ref[...].astype(F32))
    gain = gains[experts : experts + 1, :]
    gain_sum = jnp.zeros((1, D), F32)
    loads[0].wait()
    loads[1].wait()
    for c, (start, size) in enumerate(row_chunks(tr)):
        stop = min(start + size, tok)
        copies[c].wait()
        grad = dn_ref[start:stop, :].astype(F32) + other[start:stop, :].astype(F32)
        xhat, inverse = norm_rows(tok_s[start:stop, :].astype(F32))
        tg_ref[start:stop, :] = (hg_s[start:stop, :] + norm_back(grad, gain, xhat, inverse)).astype(BF)
        gain_sum += jnp.sum(grad * xhat, axis=0, keepdims=True)
    row = lax.broadcasted_iota(jnp.int32, sg_ref.shape, 0)
    rows = jnp.where(row == experts + 2, gain_sum, sg_ref[...])
    rows = jnp.concatenate([rows, jnp.zeros((128 - rows.shape[0], D), F32)], axis=0)
    turned = jnp.transpose(rows).astype(BF)
    real = turned.shape[0] // n
    for b in range(n):
        at = (b // plane, b % plane)
        if real < rp:
            sm[at[0], at[1]] = jnp.zeros((rp, 128), BF)
        sm[at[0], at[1], 0:real, :] = turned[b * real : (b + 1) * real, :]
    for d, p in enumerate(qpeer):
        c = remote(sm.at[:, (q + d + 1) % plane], q1.at[d], as_.at[d, 1], ar.at[d, 1], {"dp": p})
        c.start()
        sends.append(c)
    slots = y_s.shape[1]
    loads[2].wait()
    acc[...] = jnp.zeros_like(acc)

    def step(b, carry):
        source = [partner(me, n, b * 4 + j) if by_place else b * 4 + j for j in range(4)]
        hot = jnp.concatenate([slot_matrix(idx_ref, p * slots, slots) for p in source], axis=0)
        acc[...] += mm(hot, y_s[pl.ds(b * 4, 4)].reshape(4 * slots, D), 0, 0)
        return carry

    lax.fori_loop(0, n // 4, step, 0)
    mix[tr - 16 : tr, :] = jnp.zeros((16, D), BF)
    base = len(copies)
    late = []
    for c, (start, size) in enumerate(row_chunks(tr)):
        stop = min(start + size, tok)
        mix[start:stop, :] = acc[start:stop, :].astype(BF)
        rows = pl.ds(start, size)
        copy = remote(mix.at[rows, :], mix_other.at[rows, :], hs.at[base + c], hr.at[base + c], sibling)
        copy.start()
        late.append(copy)
    loads[4].wait()
    for d in range(plane - 1):
        remote(dw_ref.at[:, :, 0], r1.at[d], as_.at[d, 0], ar.at[d, 0], {"dp": qpeer[0]}).wait_recv()
        remote(sm.at[:, 0], q1.at[d], as_.at[d, 1], ar.at[d, 1], {"dp": qpeer[0]}).wait_recv()
    for b in range(LINE):
        value = own_w[:, b].astype(F32)
        little = sm[b, q].astype(F32)
        for d in range(plane - 1):
            value += r1[d, :, b].astype(F32)
            little += q1[d, b].astype(F32)
        s1[b] = value.astype(BF)
        t1[b] = little.astype(BF)
    for d, p in enumerate(zpeer):
        to = (z + d + 1) % LINE
        for i, (a, b) in enumerate(((s1, r2), (t1, q2))):
            c = remote(a.at[to], b.at[d], bs.at[d, i], br.at[d, i], {"dp": p})
            c.start()
            sends.append(c)
    loads[3].wait()
    for c, (start, size) in enumerate(row_chunks(tr)):
        stop = min(start + size, tok)
        late[c].wait()
        both = mix[start:stop, :].astype(F32) + mix_other[start:stop, :].astype(F32)
        out_ref[start:stop, :] = (hid_s[start:stop, :] + both).astype(BF)
    value = s1[z].astype(F32)
    little = t1[z].astype(F32)
    for d in range(LINE - 1):
        for i, (a, b) in enumerate(((s1, r2), (t1, q2))):
            remote(a.at[0], b.at[d], bs.at[d, i], br.at[d, i], {"dp": zpeer[0]}).wait_recv()
        value += r2[d].astype(F32)
        little += q2[d].astype(F32)
    gw_ref[...] = value
    gs_ref[...] = little
    for c in sends:
        c.wait_send()


def last(dw, sg, dn, tok, hg, small, y, idx, hid, n, experts, by_place):
    parts, _, rp, width = dw.shape
    plane = n // LINE
    dw = dw.reshape(parts, LINE, plane, rp, width)
    tr = up(tok.shape[0], 16)
    chunks = len(row_chunks(tr))
    sem = pltpu.SemaphoreType.DMA
    vmem = pltpu.VMEM
    far = pl.BlockSpec(memory_space=pl.ANY)
    return pl.pallas_call(
        functools.partial(last_kernel, n, experts, by_place),
        out_shape=(
            jax.ShapeDtypeStruct(tok.shape, BF),
            jax.ShapeDtypeStruct(tok.shape, BF),
            jax.ShapeDtypeStruct((parts, rp, width), F32),
            jax.ShapeDtypeStruct((rp, 128), F32),
        ),
        in_specs=[far] + [whole()] * 4 + [far] * 4,
        out_specs=(whole(),) * 4,
        scratch_shapes=[
            vmem((tr, D), BF), vmem((tr, D), BF), vmem((tr, D), BF),
            vmem((LINE, plane, rp, 128), BF),
            vmem((plane - 1, parts, LINE, rp, width), BF),
            vmem((plane - 1, LINE, rp, 128), BF),
            vmem((LINE, parts, rp, width), BF),
            vmem((LINE, rp, 128), BF),
            vmem((LINE - 1, parts, rp, width), BF),
            vmem((LINE - 1, rp, 128), BF),
            vmem((idx.shape[1], D), F32),
            vmem((parts, LINE, rp, width), BF),
            vmem(tok.shape, F32), vmem(y.shape, BF), vmem(tok.shape, F32), vmem(tok.shape, BF),
            sem((2 * chunks,)), sem((2 * chunks,)),
            sem((plane - 1, 2)), sem((plane - 1, 2)), sem((LINE - 1, 2)), sem((LINE - 1, 2)),
            sem((5,)),
        ],
        compiler_params=params(collective_id=3, has_side_effects=True),
        name="last",
    )(dw, sg, dn, small, idx, tok, hg, y, hid)


def body(
    tokens, ln1_gain, w_qkv, w_out, out_bias, ln2_gain, router, w_in, in_bias,
    w_back, back_bias, routes, priority, cotangent,
):
    n = lax.axis_size("dp")
    tok = tokens.shape[0]
    experts = router.shape[1]
    cap = max(2, 5 * tok // (2 * experts))
    half = (cap + 1) // 2
    slots = up(half + FREE, 16)
    shard, width = w_qkv.shape[0], w_qkv.shape[2]
    rp = up(shard, 16)
    swap = [(0, 1), (1, 0)]

    start = (
        jnp.swapaxes(w_qkv, 0, 1), w_out.T, router.T,
        (ln1_gain[None], ln2_gain[None], out_bias[None]), routes.T, priority,
    )
    if n * slots <= 1536:
        (hg, sg, y, gi, gi_in, gb, gb_in, little, little_in, hid, _, weights, small, idx, _, qkv, att) = expert(
            (*start, tokens), None, (w_in[0],), (w_back[0],), (in_bias,), back_bias, None, None, None,
            cotangent, None, n, cap, half, slots,
        )
    else:
        wi = (w_in[0], lax.ppermute(w_in[0], "mp", swap))
        wb = (w_back[0], lax.ppermute(w_back[0], "mp", swap))
        bi = (in_bias, lax.ppermute(in_bias, "mp", swap))
        weights, small, idx, ct_rows, qkv, att, part = begin(
            *start, cotangent, tokens, n, experts, cap, half, slots
        )
        hid, probs, x = dispatch(part, tokens, small, idx, n, experts, half, slots)
        hg, sg, y, gi, gi_in, gb, gb_in, little, little_in = expert(
            x, ct_rows, wi, wb, bi, back_bias, idx, probs, hid, cotangent, small, n, cap, half, slots
        )
    y = lax.all_to_all(y, "dp", split_axis=0, concat_axis=0, tiled=True)
    dn, dw, gi, gb, gbi, gbb = attend_back(
        hg, tokens, small, weights, qkv, att, gi, gi_in, gb, gb_in, little, little_in, experts
    )
    dw = dw.reshape(4, n, shard, width)
    if rp > shard:
        dw = jnp.pad(dw, ((0, 0), (0, 0), (0, rp - shard), (0, 0)))
    tg, out, gw, gs = last(dw, sg, dn, tokens, hg, small, y, idx, hid, n, experts, False)
    gw, gs = gw[:, :shard], gs[:shard]
    return (
        out,
        tg,
        gs[:, experts + 2],
        jnp.swapaxes(gw[:3], 0, 1),
        gw[3].T,
        gs[:, experts + 1],
        gs[:, experts],
        gs[:, :experts],
        gi[None],
        gbi,
        gb[None],
        gbb,
    )


def solution(mesh):
    return jax.shard_map(
        body,
        mesh=mesh,
        in_specs=(
            P("dp", None),
            P("dp"),
            P("dp", None, "mp"),
            P("mp", "dp"),
            P("dp"),
            P("dp"),
            P("dp", None),
            P("dp", None, "mp"),
            P("dp", "mp"),
            P("dp", "mp", None),
            P("dp", None),
            P("dp", None),
            P("dp", None),
            P("dp", None),
        ),
        out_specs=(
            P("dp", None),
            P("dp", None),
            P("dp"),
            P("dp", None, "mp"),
            P("mp", "dp"),
            P("dp"),
            P("dp"),
            P("dp", None),
            P("dp", None, "mp"),
            P("dp", "mp"),
            P("dp", "mp", None),
            P("dp", None),
        ),
        check_vma=False,
    )
```

```python
import functools

import jax
import jax.numpy as jnp
from jax import lax
from jax.experimental import pallas as pl
from jax.experimental.pallas import tpu as pltpu
from jax.sharding import PartitionSpec as P

D = 768
HD = 64
SEQ = 197
EPS = 1e-06
F32 = jnp.float32
BF = jnp.bfloat16
MESH = pl.DeviceIdType.MESH
VMEM_LIMIT = 62 * 1024 * 1024
LINE = 4
FREE = 3


def up(value, step):
    return (value + step - 1) // step * step


SEQ_PAD = up(SEQ, 16)


def mm(left, right, cl, cr):
    return lax.dot_general(
        left, right, (((cl,), (cr,)), ((), ())), preferred_element_type=F32
    )


def norm_rows(values):
    average = jnp.mean(values, axis=-1, keepdims=True)
    centered = values - average
    inverse = lax.rsqrt(jnp.mean(centered * centered, axis=-1, keepdims=True) + EPS)
    return centered * inverse, inverse


def norm_back(grad, gain, xhat, inverse):
    scaled = grad * gain
    return inverse * (
        scaled
        - jnp.mean(scaled, axis=-1, keepdims=True)
        - xhat * jnp.mean(scaled * xhat, axis=-1, keepdims=True)
    )


def split_two(value):
    high = value.astype(BF)
    return high, (value - high.astype(F32)).astype(BF)


def whole():
    return pl.BlockSpec(memory_space=pltpu.VMEM)


def params(**more):
    return pltpu.CompilerParams(vmem_limit_bytes=VMEM_LIMIT, **more)


def greet(peers):
    barrier = pltpu.get_barrier_semaphore()
    for peer in peers:
        pl.semaphore_signal(barrier, inc=1, device_id=peer, device_id_type=MESH)
    pl.semaphore_wait(barrier, len(peers))


def remote(src, dst, send_sem, recv_sem, peer):
    return pltpu.make_async_remote_copy(
        src_ref=src, dst_ref=dst, send_sem=send_sem, recv_sem=recv_sem,
        device_id=peer, device_id_type=MESH,
    )


def partner(me, n, place, sign=1):
    plane = n // LINE
    groups = plane // 4
    z, q = me // plane, me % plane
    step, j = place // 4, place % 4
    turn, g = step // groups, step % groups
    k = turn % 2 * 2 + turn // 2
    line = (z // 2 + k // 2) % 2 * 2 + (z % 2 + k % 2) % 2
    return line * plane + (q + plane + sign * (g * 4 + j)) % plane


def slot_matrix(idx_ref, first, rows):
    number = lax.broadcasted_iota(jnp.int32, (rows, idx_ref.shape[1]), 0) + first
    hit = (number == idx_ref[0:1, :]) | (number == idx_ref[1:2, :])
    return jnp.where(hit, 1.0, 0.0).astype(BF)


def begin_part(
    n, cap, half, slots, more_peers, started,
    wq_ref, wout_ref, rows_ref, gain_refs, rt_ref, rank_ref, ct_ref, tok_ref,
    wo_ref, so_ref, idx_ref, ctx_ref, qkv_ref, att_ref, part_ref,
    gw, gs, mine_w, mine_s, info, ctp, cc, send, xp, pp,
    zs, zr, ps, pr, cs, cr, lsem,
):
    me, mine = lax.axis_index("dp"), lax.axis_index("mp")
    plane = n // LINE
    z, q = me // plane, me % plane
    experts, shard = rows_ref.shape
    tok = tok_ref.shape[0]
    lanes = idx_ref.shape[1]
    rp = mine_w.shape[1]
    zpeer = [((z + d) % LINE) * plane + q for d in range(1, LINE)]
    qpeer = [z * plane + (q + d) % plane for d in range(1, plane)]
    full_w, full_s = (wo_ref, so_ref) if rp == shard else (gw, gs)

    if rp > shard:
        mine_w[...] = jnp.zeros_like(mine_w)
    mine_w[0:3, 0:shard, :] = wq_ref[...]
    mine_w[3, 0:shard, :] = wout_ref[...]
    pp[0:128, 0:128] = jnp.zeros((128, 128), F32)
    pp[0:experts, 0:shard] = rows_ref[...].astype(F32)
    for k, gain_ref in enumerate(gain_refs):
        pp[experts + k : experts + k + 1, 0:shard] = gain_ref[...].astype(F32)
    mine_s[...] = jnp.transpose(pp[0:128, 0:128])[0:rp, :].astype(BF)
    greet(more_peers + [{"dp": (me + d) % n} for d in range(1, n)])
    started()

    def at(block):
        rows = pl.ds(pl.multiple_of(block * rp, rp), rp)
        return full_w.at[:, rows, :], full_s.at[rows, :]

    own = at(me)
    sends = []
    for d, p in enumerate(zpeer):
        for i, (a, b) in enumerate(zip((mine_w, mine_s), own)):
            sends.append(remote(a, b, zs.at[d, i], zr.at[d, i], {"dp": p}))
            sends[-1].start()
    for d, p in enumerate(qpeer):
        for i, (a, b) in enumerate(zip((mine_w, mine_s), own)):
            sends.append(remote(a, b, ps.at[d, 0, i], pr.at[d, 0, i], {"dp": p}))
            sends[-1].start()
    here = pl.ds(pl.multiple_of(me * rp, rp), rp)
    full_w[:, here, :] = mine_w[...]
    full_s[here, :] = mine_s[...]

    info[0:2, :] = jnp.full((2, lanes), -1, jnp.int32)
    info[2:3, :] = jnp.full((1, lanes), 1 << 20, jnp.int32)
    info[0:2, 0:tok] = rt_ref[...]
    info[2:3, 0:tok] = rank_ref[...]
    number = lax.broadcasted_iota(jnp.int32, (experts, lanes), 0)
    hot = [jnp.where(number == info[j : j + 1, :], 1.0, 0.0) for j in range(2)]
    ranks = info[2:3, :].astype(F32)
    column = jnp.transpose(jnp.broadcast_to(ranks, (128, lanes)))[:, 0:1]
    before = jnp.where(column < ranks, 1.0, 0.0).astype(BF)
    counts = [mm(h.astype(BF), before, 1, 0) for h in hot]
    counts[1] = counts[1] + jnp.sum(hot[0], axis=1, keepdims=True)
    for j in range(2):
        slot = jnp.sum(counts[j] * hot[j], axis=0, keepdims=True).astype(jnp.int32)
        place = slot - mine * half
        expert_id = info[j : j + 1, :]
        kept = (slot < cap) & (place >= 0) & (place < half) & (expert_id >= 0)
        idx_ref[j : j + 1, :] = jnp.where(kept, expert_id * slots + place, -1)
    ctp[lanes - 64 : lanes, cc : cc + D] = jnp.zeros((64, D), BF)
    ctp[0:tok, cc : cc + D] = ct_ref[...]

    def rows_of(b, carry):
        ones = [slot_matrix(idx_ref, partner(me, n, b * 4 + j) * slots, slots) for j in range(4)]
        block = mm(jnp.concatenate(ones, axis=0), ctp[0:lanes, cc : cc + D], 1, 0).astype(BF)
        send[pl.ds(pl.multiple_of(b * 4 * slots, 16), 4 * slots), 0:D] = block
        return carry

    lax.fori_loop(0, n // 4, rows_of, 0)

    for k in range(1, LINE):
        block = at(((z + LINE - k) % LINE) * plane + q)
        for i in range(2):
            remote(block[i], block[i], zs.at[k - 1, i], zr.at[k - 1, i], {"dp": zpeer[0]}).wait_recv()
        for d, p in enumerate(qpeer):
            for i in range(2):
                sends.append(remote(block[i], block[i], ps.at[d, k, i], pr.at[d, k, i], {"dp": p}))
                sends[-1].start()

    def block_of(p):
        return send.at[pl.ds(pl.multiple_of(p * slots, 16), slots), pl.ds(0, D)]

    local = pltpu.make_async_copy(block_of(0), ctx_ref.at[0], lsem.at[0])
    local.start()

    def ship(p, carry):
        @pl.when(p != 0)
        def _():
            remote(block_of(p), ctx_ref.at[p], cs.at[p], cr.at[p], {"dp": partner(me, n, p)}).start()

        return carry

    lax.fori_loop(0, n, ship, 0)

    images = tok // SEQ
    width = wo_ref.shape[2]
    scale = HD ** (-0.5)
    for i in range(images):
        xp[(i + 1) * SEQ_PAD - 16 : (i + 1) * SEQ_PAD, :] = jnp.zeros((16, D), F32)
        xp[i * SEQ_PAD : i * SEQ_PAD + SEQ, :] = tok_ref[i * SEQ : (i + 1) * SEQ, :].astype(F32)

    def norm(i, carry):
        rows = pl.ds(pl.multiple_of(i * SEQ_PAD, 16), SEQ_PAD)
        xhat, _ = norm_rows(xp[rows, :])
        xp[rows, :] = xhat
        return carry

    lax.fori_loop(0, images, norm, 0)
    for d in range(1, plane):
        for k in range(LINE):
            block = at(((z + LINE - k) % LINE) * plane + (q + plane - d) % plane)
            for i in range(2):
                remote(block[i], block[i], ps.at[d - 1, k, i], pr.at[d - 1, k, i], {"dp": qpeer[0]}).wait_recv()
    if rp > shard:
        line = lax.broadcasted_iota(jnp.int32, (D, n * rp), 0)
        where = lax.broadcasted_iota(jnp.int32, (D, n * rp), 1)
        squeeze = jnp.where(where == line // shard * rp + line % shard, 1.0, 0.0).astype(BF)
        for c in range(4):
            wo_ref[c] = mm(squeeze, gw[c], 1, 0).astype(BF)
        so_ref[...] = mm(squeeze, gs[...], 1, 0).astype(BF)
    gain = jnp.transpose(so_ref[...].astype(F32))[experts : experts + 1, :]
    lane = lax.broadcasted_iota(jnp.int32, (1, 2 * HD), 1)
    masks = [jnp.where(lane // HD == h, 1.0, 0.0).astype(BF) for h in range(2)]
    valid = lax.broadcasted_iota(jnp.int32, (1, SEQ_PAD), 1) < SEQ

    def image(i, carry):
        rows = pl.ds(pl.multiple_of(i * SEQ_PAD, 16), SEQ_PAD)
        normed = (xp[rows, :] * gain).astype(BF)
        for c in range(3):
            qkv_ref[rows, c * width : (c + 1) * width] = mm(normed, wo_ref[c], 1, 0).astype(BF)
        for p in range(width // (2 * HD)):
            cols = slice(p * 2 * HD, (p + 1) * 2 * HD)
            qs, ks, vs = (
                qkv_ref[rows, c * width + p * 2 * HD : c * width + (p + 1) * 2 * HD] for c in range(3)
            )
            outs = []
            for h in range(2):
                scores = mm(qs * masks[h], ks, 1, 1) * scale
                scores = jnp.where(valid, scores, -1e30)
                raised = jnp.exp(scores - jnp.max(scores, axis=-1, keepdims=True))
                weights = raised * (1.0 / jnp.sum(raised, axis=-1, keepdims=True))
                outs.append(mm(weights.astype(BF), vs, 1, 0))
            att_ref[rows, cols] = jnp.where(lane < HD, outs[0], outs[1]).astype(BF)
        pp[rows, :] = mm(att_ref[rows, 0:width], wo_ref[3], 1, 1)
        return carry

    lax.fori_loop(0, images, image, 0)
    for i in range(images):
        part_ref[i * SEQ : (i + 1) * SEQ, :] = pp[i * SEQ_PAD : i * SEQ_PAD + SEQ, :]

    def arrived(p):
        @pl.when(p != 0)
        def _():
            remote(block_of(p), ctx_ref.at[p], cs.at[p], cr.at[p], {"dp": partner(me, n, p)}).wait_recv()

    def ended():
        for c in sends:
            c.wait_send()
        local.wait()

        def sent(p, carry):
            @pl.when(p != 0)
            def _():
                remote(block_of(p), ctx_ref.at[p], cs.at[p], cr.at[p], {"dp": partner(me, n, p)}).wait_send()

            return carry

        lax.fori_loop(0, n, sent, 0)

    return arrived, ended


def begin_kernel(n, cap, half, slots, *refs):
    arrived, ended = begin_part(n, cap, half, slots, [], lambda: None, *refs[:21], 0, *refs[21:])

    def finish(p, carry):
        arrived(p)
        return carry

    lax.fori_loop(0, n, finish, 0)
    ended()


def begin(wq, wout, rows, gains, rt, rank, ct, tok, n, experts, cap, half, slots):
    images = tok.shape[0] // SEQ
    shard, width = wout.shape
    rp = up(shard, 16)
    lanes = up(tok.shape[0], 128)
    plane = n // LINE
    sem = pltpu.SemaphoreType.DMA
    shape = jax.ShapeDtypeStruct
    vmem = pltpu.VMEM
    spare = n * rp if rp > shard else 16

    def kernel(wq_ref, wout_ref, rows_ref, g1, g2, g3, *rest):
        begin_kernel(n, cap, half, slots, wq_ref, wout_ref, rows_ref, (g1, g2, g3), *rest)

    return pl.pallas_call(
        kernel,
        out_shape=(
            shape((4, D, width), BF), shape((D, 128), BF), shape((2, lanes), jnp.int32),
            shape((n, slots, D), BF), shape((images * SEQ_PAD, 3 * width), BF),
            shape((images * SEQ_PAD, width), BF), shape((up(tok.shape[0], 16), D), F32),
        ),
        in_specs=[whole()] * 10,
        out_specs=(whole(), whole(), whole(), pl.BlockSpec(memory_space=pl.ANY), whole(), whole(), whole()),
        scratch_shapes=[
            vmem((4, spare, width), BF), vmem((spare, 128), BF),
            vmem((4, rp, width), BF), vmem((rp, 128), BF), vmem((8, lanes), jnp.int32),
            vmem((lanes, D), BF), vmem((n * slots, D), BF),
            vmem((images * SEQ_PAD, D), F32), vmem((images * SEQ_PAD, D), F32),
            sem((LINE - 1, 2)), sem((LINE - 1, 2)),
            sem((plane - 1, LINE, 2)), sem((plane - 1, LINE, 2)),
            sem((n,)), sem((n,)), sem((1,)),
        ],
        compiler_params=params(collective_id=0, has_side_effects=True),
        name="begin",
    )(wq, wout, rows, *gains, rt, rank, ct, tok)


def row_chunks(rows):
    return [(s, min(256, rows - s)) for s in range(0, rows, 256)]


def token_send(n, send, x_ref, xs, xr, p, peer):
    return remote(send.at[p], x_ref.at[p], xs.at[p], xr.at[p], {"dp": peer})


def send_tokens(
    n, half, early, part_ref, tok_ref, small_ref, idx_ref, hid_ref, n2, prob_ref, x_ref,
    own, other, send, p2, hs, hr, xs, xr,
):
    me, mine = lax.axis_index("dp"), lax.axis_index("mp")
    plane = n // LINE
    tok = tok_ref.shape[0]
    slots = send.shape[1]
    experts, lanes = prob_ref.shape
    tr = other.shape[0]
    sibling = {"mp": 1 - mine}
    own[tr - 16 : tr, :] = jnp.zeros((16, D), BF)
    copies = []
    for c, (start, size) in enumerate(row_chunks(tr)):
        stop = min(start + size, tok)
        own[start:stop, :] = part_ref[start:stop, :].astype(BF)
        rows = pl.ds(start, size)
        copy = remote(own.at[rows, :], other.at[rows, :], hs.at[c], hr.at[c], sibling)
        copy.start()
        copies.append(copy)
    gains = jnp.transpose(small_ref[...].astype(F32))
    gain = gains[experts + 1 : experts + 2, :]
    bias = gains[experts + 2 : experts + 3, :]
    n2[lanes - 64 : lanes, 0:D] = jnp.zeros((64, D), BF)
    for c, (start, size) in enumerate(row_chunks(tr)):
        stop = min(start + size, tok)
        copies[c].wait_recv()
        both = own[start:stop, :].astype(F32) + other[start:stop, :].astype(F32)
        hidden = tok_ref[start:stop, :].astype(F32) + both + bias
        hid_ref[start:stop, :] = hidden
        xhat, _ = norm_rows(hidden)
        n2[start:stop, 0:D] = (xhat * gain).astype(BF)
    logits = mm(gains[0:experts, :].astype(BF), n2[0:lanes, 0:D], 1, 1)
    raised = jnp.exp(logits - jnp.max(logits, axis=0, keepdims=True))
    probs = raised / jnp.sum(raised, axis=0, keepdims=True)
    prob_ref[...] = probs
    high, low = split_two(probs)
    p2[0:experts, :] = high
    p2[experts:, :] = low
    place = lax.broadcasted_iota(jnp.int32, (slots, slots), 0)
    number = lax.broadcasted_iota(jnp.int32, (2 * experts, slots), 0)

    def step(b, carry):
        hot = [slot_matrix(idx_ref, partner(me, n, b * 4 + j) * slots, slots) for j in range(4)]
        block = mm(jnp.concatenate(hot, axis=0), n2[0:lanes, 0:D], 1, 0)
        for j in range(4):
            p = b * 4 + j
            peer = partner(me, n, p)
            gates = mm(p2[...], hot[j], 1, 1)
            row_high = jnp.sum(jnp.where(number == peer, gates, 0.0), axis=0, keepdims=True)
            row_low = jnp.sum(jnp.where(number == peer + experts, gates, 0.0), axis=0, keepdims=True)
            rows = block[j * slots : (j + 1) * slots, :]
            left = jnp.where(place == half, row_high, jnp.where(place == half + 1, row_low, rows[:, 0:slots]))
            send[p, :, :] = rows.astype(BF)
            send[p, :, 0:slots] = left.astype(BF)

            @pl.when((p != 0) & (p < early))
            def _():
                token_send(n, send, x_ref, xs, xr, p, peer).start()

        return carry

    lax.fori_loop(0, n // 4, step, 0)
    x_ref[0] = send[0]
    for copy in copies:
        copy.wait_send()


def dispatch_kernel(
    n, half, part_ref, tok_ref, small_ref, idx_ref, hid_ref, prob_ref, x_ref,
    n2, own, other, send, p2, hs, hr, xs, xr,
):
    me, mine = lax.axis_index("dp"), lax.axis_index("mp")
    plane = n // LINE
    greet([{"mp": 1 - mine}] + [{"dp": (me + d) % n} for d in range(1, n)])
    send_tokens(
        n, half, n, part_ref, tok_ref, small_ref, idx_ref, hid_ref, n2, prob_ref, x_ref,
        own, other, send, p2, hs, hr, xs, xr,
    )

    def finish(p, carry):
        @pl.when(p != 0)
        def _():
            token_send(n, send, x_ref, xs, xr, p, partner(me, n, p)).wait()

        return carry

    lax.fori_loop(0, n, finish, 0)


def dispatch(part, tok, small, idx, n, experts, half, slots):
    lanes = idx.shape[1]
    tr = up(tok.shape[0], 16)
    sem = pltpu.SemaphoreType.DMA
    vmem = pltpu.VMEM
    chunks = len(row_chunks(tr))
    return pl.pallas_call(
        functools.partial(dispatch_kernel, n, half),
        out_shape=(
            jax.ShapeDtypeStruct(tok.shape, F32),
            jax.ShapeDtypeStruct((experts, lanes), F32),
            jax.ShapeDtypeStruct((n, slots, D), BF),
        ),
        in_specs=[whole()] * 4,
        out_specs=(whole(),) * 3,
        scratch_shapes=[
            vmem((lanes, D), BF), vmem((tr, D), BF), vmem((tr, D), BF), vmem((n, slots, D), BF),
            vmem((2 * experts, lanes), BF),
            sem((chunks,)), sem((chunks,)), sem((n,)), sem((n,)),
        ],
        compiler_params=params(collective_id=1, has_side_effects=True),
        name="dispatch",
    )(part, tok, small, idx)


def expert_kernel(
    n, cap, half, fused,
    first, ct_ref, wi_own, wi_sib, wb_own, wb_sib, bi_own, bi_sib, bb_ref,
    idx_ref, seen_ref, tok_ct, small_ref,
    hg_ref, sg_ref, y_ref, gi_ref, gi_in, gb_ref, gb_in, little_ref, little_in, hid_out, prob_ref,
    wo_ref, qkv_out, att_out,
    vi_own, vi_sib, vb_own, vb_sib, g_s, act_own, act_sib, dp_own, dp_sib, dx_s, back, acc, other,
    ct_s, y_s, stage, gp, gp_other, x_ref, send, p2, mine_w, mine_s, info, bias_s, bias_in,
    lsem, ysem, gsem, ss, rs, hs, hr, ms, mr, xs, xr, es, er, zs, zr, ps, pr, cs, cr, bsem,
):
    me, mine = lax.axis_index("dp"), lax.axis_index("mp")
    sibling = {"mp": 1 - mine}
    slots = x_ref.shape[1]
    tok = tok_ct.shape[0]
    experts = gp.shape[0]
    hidden = wi_own.shape[1]
    group = 4 * slots
    batches = n // 4
    early = n // 2 if fused else n
    lanes = gp.shape[1]
    owns = [(wi_own, vi_own), (wb_own, vb_own)]
    if not fused:
        owns += [(wi_sib, vi_sib), (wb_sib, vb_sib), (first, x_ref)]
    loads = [pltpu.make_async_copy(a, b, lsem.at[i]) for i, (a, b) in enumerate(owns)]
    for c in loads:
        c.start()
    if fused:
        halves = [
            remote(wi_own, vi_sib, ms.at[3], mr.at[3], sibling),
            remote(wb_own, vb_sib, ms.at[4], mr.at[4], sibling),
            remote(bias_s, bias_in, ms.at[5], mr.at[5], sibling),
        ]
        bias_s[...] = jnp.zeros_like(bias_s)
        bias_s[0:1, :] = bi_own[...].astype(F32)

        def started():
            for c in halves:
                c.start()

        arrived, ended = begin_part(
            n, cap, half, slots, [sibling], started, *first,
            wo_ref, small_ref, idx_ref, ct_ref, act_own, act_sib, hg_ref,
            None, None, mine_w, mine_s, info, act_sib, D, dp_own, acc, stage,
            zs, zr, ps, pr, cs, cr, bsem,
        )
        rows = qkv_out.shape[0]
        kept = [
            pltpu.make_async_copy(act_own.at[pl.ds(0, rows), pl.ds(0, qkv_out.shape[1])], qkv_out, lsem.at[2]),
            pltpu.make_async_copy(act_sib.at[pl.ds(0, rows), pl.ds(0, att_out.shape[1])], att_out, lsem.at[3]),
        ]
        for c in kept:
            c.start()
        send_tokens(
            n, half, early, hg_ref, first[-1], small_ref, idx_ref, hg_ref, dp_sib, prob_ref, x_ref,
            g_s, other, send, p2, es, er, xs, xr,
        )
        keep = pltpu.make_async_copy(hg_ref, hid_out, lsem.at[5])
        keep.start()
        ended()
        for c in kept:
            c.wait()
        for c in halves:
            c.wait()
        bias_own, bias_sib = bi_own[...].astype(F32), bias_in[0:1, :]
    else:
        greet([sibling] + [{"dp": (me + d) % n} for d in range(1, n)])
        keep = pltpu.make_async_copy(hid_out, hg_ref, lsem.at[5])
        keep.start()
        bias_own, bias_sib = bi_own[...].astype(F32), bi_sib[...].astype(F32)
    little_ref[...] = jnp.zeros_like(little_ref)

    def ct_here(b, j):
        if fused:
            arrived(b * 4 + j)

    def cts(b, j):
        return pltpu.make_async_copy(ct_ref.at[b * 4 + j], ct_s.at[j], ysem.at[0, j])

    def ys(b, j):
        return pltpu.make_async_copy(y_s.at[j], y_ref.at[b * 4 + j], ysem.at[1, j])

    for j in range(4):
        ct_here(0, j)
        cts(0, j).start()
    for c in loads:
        c.wait()
    chunk = 768
    row = lax.broadcasted_iota(jnp.int32, (group, 16), 0)
    number = lax.broadcasted_iota(jnp.int32, (group, 16), 1)
    member = jnp.where(row // slots == number, 1.0, 0.0).astype(BF)
    spot = lax.broadcasted_iota(jnp.int32, (group, 128), 0) % slots
    here = spot == lax.broadcasted_iota(jnp.int32, (group, 128), 1)
    row_t = lax.broadcasted_iota(jnp.int32, (16, group), 1)
    number_t = lax.broadcasted_iota(jnp.int32, (16, group), 0)
    pick = jnp.where(
        (row_t == number_t * slots + half) | (row_t == number_t * slots + half + 1), 1.0, 0.0
    ).astype(BF)
    member_t = jnp.where(row_t // slots == number_t, 1.0, 0.0).astype(BF)
    puts = [jnp.where(row == number * slots + half + i, 1.0, 0.0).astype(BF) for i in range(2)]

    def batch(b, carry):
        at = pl.ds(pl.multiple_of(b * group, 16), group)
        if fused:
            @pl.when(b == batches // 4)
            def _():
                def more(p, carry):
                    token_send(n, send, x_ref, xs, xr, p, partner(me, n, p)).start()
                    return carry

                lax.fori_loop(early, n, more, 0)

            for j in range(4):
                p = b * 4 + j

                @pl.when(p != 0)
                def _():
                    token_send(n, send, x_ref, xs, xr, p, partner(me, n, p)).wait_recv()

        x = x_ref[pl.ds(b * 4, 4)].reshape(group, D)
        high, low = split_two(mm(pick, x[:, 0:128], 1, 0))
        wide = mm(member, high, 1, 0) + mm(member, low, 1, 0)
        gate = jnp.sum(jnp.where(here, wide, 0.0), axis=1, keepdims=True)
        for j in range(4):
            cts(b, j).wait()
        g_s[at, :] = (gate * ct_s[...].reshape(group, D).astype(F32)).astype(BF)
        little_ref[0:1, 2 * hidden :] += jnp.sum(g_s[at, :].astype(F32), axis=0, keepdims=True)
        for part, (vi, vb, bi, acts, dps) in enumerate(
            ((vi_own, vb_own, bias_own, act_own, dp_own), (vi_sib, vb_sib, bias_sib, act_sib, dp_sib))
        ):
            for c in range(hidden // chunk):
                cols = slice(c * chunk, (c + 1) * chunk)
                pre = mm(x_ref[pl.ds(b * 4, 4)].reshape(group, D), vi[:, cols], 1, 0) + bi[:, cols]
                phi = 0.5 * (1.0 + lax.erf(pre * (0.5**0.5)))
                slope = phi + pre * (jnp.exp(-0.5 * pre * pre) * ((2.0 * jnp.pi) ** -0.5))
                acts[at, cols] = (pre * phi).astype(BF)
                grad = (mm(g_s[at, :], vb[cols, :], 1, 1) * slope).astype(BF)
                dps[at, cols] = grad
                place = slice(part * hidden + c * chunk, part * hidden + (c + 1) * chunk)
                little_ref[0:1, place] += jnp.sum(grad.astype(F32), axis=0, keepdims=True)
        dx = mm(dp_own[at, :], vi_own[...], 1, 1) + mm(dp_sib[at, :], vi_sib[...], 1, 1)
        y = mm(act_own[at, :], vb_own[...], 1, 0) + mm(act_sib[at, :], vb_sib[...], 1, 0)
        y = (y + bb_ref[...].astype(F32)).astype(BF).astype(F32)
        dots = jnp.sum(ct_s[...].reshape(group, D).astype(F32) * y, axis=1, keepdims=True)
        high, low = split_two(jnp.where(here, dots, 0.0))
        high, low = mm(member_t, high, 1, 0).astype(BF), mm(member_t, low, 1, 0).astype(BF)
        left = dx[:, 0:128] + mm(puts[0], high, 1, 0) + mm(puts[1], low, 1, 0)
        dx = jnp.concatenate([left, dx[:, 128:]], axis=1)
        dx_s[pl.ds(b * 4, 4)] = dx.astype(BF).reshape(4, slots, D)
        for j in range(4):
            p = b * 4 + j

            @pl.when(p != 0)
            def _():
                remote(dx_s.at[p], back.at[p], ss.at[p], rs.at[p], {"dp": partner(me, n, p, -1)}).start()

        @pl.when(b > 0)
        def _():
            for j in range(4):
                ys(b - 1, j).wait()

        y_s[...] = (gate * y).astype(BF).reshape(4, slots, D)
        for j in range(4):
            ys(b, j).start()

        @pl.when(b + 1 < batches)
        def _():
            for j in range(4):
                ct_here(b + 1, j)
                cts(b + 1, j).start()

        return carry

    lax.fori_loop(0, batches, batch, 0)
    back[0] = dx_s[0]
    little = remote(little_ref, little_in, ms.at[2], mr.at[2], sibling)
    little.start()

    rows_all = n * slots
    steps = 3
    size = D // steps
    wide = hidden // 2
    swaps = []

    def out_i(r, c):
        return pltpu.make_async_copy(
            stage.at[r % 2 * 2 * size + c * size : r % 2 * 2 * size + (c + 1) * size, :],
            gi_ref.at[r * size : (r + 1) * size, c * wide : (c + 1) * wide], gsem.at[c, r],
        )

    def out_b(r):
        return pltpu.make_async_copy(
            stage.at[r % 2 * 2 * size : (r % 2 + 1) * 2 * size, :], gb_ref.at[r * 2 * size : (r + 1) * 2 * size, :], gsem.at[2, r]
        )

    for r in range(steps):
        at = slice(r * size, (r + 1) * size)
        left = x_ref[:, :, at].reshape(rows_all, size)
        vi_sib[at, :] = mm(left, dp_sib[...], 0, 0).astype(BF)
        for c in range(2):
            if r >= 2:
                out_i(r - 2, c).wait()
            at_s = r % 2 * 2 * size + c * size
            stage[at_s : at_s + size, :] = mm(left, dp_own[:, c * wide : (c + 1) * wide], 0, 0)
            out_i(r, c).start()
    copy = remote(vi_sib, gi_in, ms.at[0], mr.at[0], sibling)
    copy.start()
    swaps.append(copy)

    acc[...] = jnp.zeros_like(acc)
    gp[...] = jnp.zeros_like(gp)
    place = lax.broadcasted_iota(jnp.int32, (slots, 128), 0)
    count = lax.broadcasted_iota(jnp.int32, (experts, slots), 0)

    def combine(b, carry):
        hot = []
        for j in range(4):
            d = b * 4 + j
            source = partner(me, n, d)

            @pl.when(d != 0)
            def _():
                remote(dx_s.at[d], back.at[d], ss.at[d], rs.at[d], {"dp": source}).wait_recv()

            hot.append(slot_matrix(idx_ref, source * slots, slots))
            extra = back[d, :, 0:128].astype(F32)
            high = jnp.sum(jnp.where(place == half, extra, 0.0), axis=0, keepdims=True)[:, 0:slots]
            low = jnp.sum(jnp.where(place == half + 1, extra, 0.0), axis=0, keepdims=True)[:, 0:slots]
            for value in (high, low):
                gp[...] += mm(jnp.where(count == source, value, 0.0).astype(BF), hot[j], 1, 0)
        block = back[pl.ds(b * 4, 4)].reshape(group, D)
        acc[0:lanes, :] += mm(jnp.concatenate(hot, axis=0), block, 0, 0)
        return carry

    lax.fori_loop(0, batches // 2, combine, 0)
    for r in range(steps):
        at = slice(r * 2 * size, (r + 1) * 2 * size)
        vb_sib[at, :] = mm(act_sib[:, at], g_s[...], 0, 0).astype(BF)
        if r == 0:
            for c in range(2):
                out_i(1, c).wait()
                out_i(2, c).wait()
        if r >= 2:
            out_b(r - 2).wait()
        stage[r % 2 * 2 * size : (r % 2 + 1) * 2 * size, :] = mm(act_own[:, at], g_s[...], 0, 0)
        out_b(r).start()
    copy = remote(vb_sib, gb_in, ms.at[1], mr.at[1], sibling)
    copy.start()
    swaps.append(copy)
    lax.fori_loop(batches // 2, batches, combine, 0)

    little.wait()
    copies = []
    own = g_s
    own[other.shape[0] - 16 : other.shape[0], :] = jnp.zeros((16, D), BF)
    for c, (start, length) in enumerate(row_chunks(other.shape[0])):
        stop = min(start + length, tok)
        own[start:stop, :] = acc[start:stop, :].astype(BF)
        rows = pl.ds(start, length)
        copy = remote(own.at[rows, :], other.at[rows, :], hs.at[c], hr.at[c], sibling)
        copy.start()
        copies.append(copy)
    copy = remote(gp, gp_other, hs.at[len(copies)], hr.at[len(copies)], sibling)
    copy.start()
    copy.wait()
    probs = prob_ref[...] if fused else seen_ref[...]
    grad_probs = gp[...] + gp_other[...]
    logits = (probs * (grad_probs - jnp.sum(grad_probs * probs, axis=0, keepdims=True))).astype(BF)
    gains = jnp.transpose(small_ref[...].astype(F32))
    gain = gains[experts + 1 : experts + 2, :]
    acc[0:lanes, :] = mm(logits, gains[0:experts, :].astype(BF), 0, 0)
    sg_ref[...] = jnp.zeros_like(sg_ref)
    gain_sum = jnp.zeros((1, D), F32)
    bias_sum = jnp.zeros((1, D), F32)
    act_own[lanes - 64 : lanes, 0:D] = jnp.zeros((64, D), BF)
    keep.wait()
    for c, (start, length) in enumerate(row_chunks(other.shape[0])):
        stop = min(start + length, tok)
        copies[c].wait_recv()
        grad = own[start:stop, :].astype(F32) + other[start:stop, :].astype(F32) + acc[start:stop, :]
        xhat, inverse = norm_rows(hg_ref[start:stop, :])
        act_own[start:stop, 0:D] = (xhat * gain).astype(BF)
        hidden_grad = tok_ct[start:stop, :].astype(F32) + norm_back(grad, gain, xhat, inverse)
        hg_ref[start:stop, :] = hidden_grad
        gain_sum += jnp.sum(grad * xhat, axis=0, keepdims=True)
        bias_sum += jnp.sum(hidden_grad, axis=0, keepdims=True)
    sg_ref[0:experts, :] = mm(logits, act_own[0:lanes, 0:D], 1, 0)
    sg_ref[experts : experts + 1, :] = gain_sum
    sg_ref[experts + 1 : experts + 2, :] = bias_sum
    for copy in copies:
        copy.wait_send()

    def finish(p, carry):
        @pl.when(p != 0)
        def _():
            remote(dx_s.at[p], back.at[p], ss.at[p], rs.at[p], {"dp": partner(me, n, p, -1)}).wait_send()
            if fused:
                token_send(n, send, x_ref, xs, xr, p, partner(me, n, p)).wait_send()

        return carry

    lax.fori_loop(0, n, finish, 0)
    for j in range(4):
        ys(batches - 1, j).wait()
    for r in range(1, steps):
        out_b(r).wait()
    for copy in swaps:
        copy.wait()


def expert(first, ct_rows, wi, wb, bi, bb, idx, probs, hid, ct, small, n, cap, half, slots):
    fused = hid is None
    rows = n * slots
    hidden = wi[0].shape[1]
    lanes = up(ct.shape[0], 128)
    experts = n
    tr = up(ct.shape[0], 16)
    chunks = len(row_chunks(tr))
    flat = ct.shape[0] // SEQ * SEQ_PAD
    shape = jax.ShapeDtypeStruct
    sem = pltpu.SemaphoreType.DMA
    vmem = pltpu.VMEM
    far = pl.BlockSpec(memory_space=pl.ANY)
    outs = [
        shape(ct.shape, F32), shape((up(experts + 3, 8), D), F32), shape((n, slots, D), BF),
        shape((D, hidden), F32), shape((D, hidden), BF),
        shape((hidden, D), F32), shape((hidden, D), BF),
        shape((8, 2 * hidden + D), F32), shape((8, 2 * hidden + D), F32),
    ]
    out_specs = [whole(), whole(), far, far, far, far, far, whole(), whole()]
    if fused:
        wq, wout, router_t, gains, rt, rank, tok = first
        shard, width = wout.shape
        plane = n // LINE
        ins = [wq, wout, router_t, *gains, rt, rank, ct, tok, wi[0], wb[0], bi[0], bb]
        in_specs = [whole()] * 10 + [far, far, whole(), whole()]
        outs += [
            shape(ct.shape, F32), shape((experts, lanes), F32), shape((4, D, width), BF), shape((D, 128), BF),
            shape((2, lanes), jnp.int32), shape((n, slots, D), BF),
            shape((flat, 3 * width), BF), shape((flat, width), BF),
        ]
        out_specs += [far, whole(), whole(), whole(), whole(), far, far, far]

        def kernel(*refs):
            wq, wout, rows_t, g1, g2, g3, rt, rank, ct, tok, wi, wb, bi, bb = refs[:14]
            main, (hid, prob, wo, so, idx, ctx, qkv, att) = refs[14:23], refs[23:31]
            expert_kernel(
                n, cap, half, True, (wq, wout, rows_t, (g1, g2, g3), rt, rank, ct, tok),
                ctx, wi, None, wb, None, bi, None, bb, idx, None, ct, so,
                *main, hid, prob, wo, qkv, att, *refs[31:],
            )

        spare = [vmem((4, shard, width), BF), vmem((shard, 128), BF), vmem((8, lanes), jnp.int32)]
        spare += [vmem((8, hidden), F32)] * 2
        grid = (plane - 1, LINE, 2)
        send_rows = (n, slots, D)
    else:
        ins = [first, ct_rows, wi[0], wi[1], wb[0], wb[1], bi[0], bi[1], bb, idx, probs, ct, small, hid]
        in_specs = [far] * 6 + [whole()] * 7 + [far]

        def kernel(*refs):
            ins, hid_ref, outs, rest = refs[:13], refs[13], refs[14:23], refs[23:]
            expert_kernel(n, cap, half, False, *ins, *outs, hid_ref, ins[10], None, None, None, *rest)

        spare = [vmem((1, 16, 128), BF), vmem((16, 128), BF), vmem((8, 128), jnp.int32)]
        spare += [vmem((8, 128), F32)] * 2
        grid = (1, 1, 2)
        send_rows = (1, 16, 128)

    return pl.pallas_call(
        kernel,
        out_shape=tuple(outs),
        in_specs=in_specs,
        out_specs=tuple(out_specs),
        scratch_shapes=[
            vmem((D, hidden), BF), vmem((D, hidden), BF), vmem((hidden, D), BF), vmem((hidden, D), BF),
            vmem((rows, D), BF),
            vmem((rows, hidden), BF), vmem((rows, hidden), BF),
            vmem((rows, hidden), BF), vmem((rows, hidden), BF),
            vmem((n, slots, D), BF), vmem((n, slots, D), BF),
            vmem((flat if fused else lanes, D), F32), vmem((tr, D), BF),
            vmem((4, slots, D), BF), vmem((4, slots, D), BF),
            vmem((flat if fused else 1024, D), F32),
            vmem((experts, lanes), F32), vmem((experts, lanes), F32),
            vmem((n, slots, D), BF), vmem(send_rows, BF), vmem((2 * experts, lanes), BF),
            *spare,
            sem((6,)), sem((2, 4)), sem((3, 3)), sem((n,)), sem((n,)),
            sem((chunks + 1,)), sem((chunks + 1,)), sem((6,)), sem((6,)),
            sem((n,)), sem((n,)), sem((chunks,)), sem((chunks,)),
            sem((LINE - 1, 2)), sem((LINE - 1, 2)), sem(grid), sem(grid), sem((n,)), sem((n,)), sem((3,)),
        ],
        compiler_params=params(collective_id=2, has_side_effects=True),
        name="expert",
    )(*ins)


def join_kernel(gi_ref, gi_in, gb_ref, gb_in, little_ref, little_in, gi_out, gb_out, gbi_out, gbb_out):
    gi_out[...] = gi_ref[...] + gi_in[...].astype(F32)
    gb_out[...] = gb_ref[...] + gb_in[...].astype(F32)
    hidden = gbi_out.shape[1]
    gbi_out[...] = little_ref[0:1, 0:hidden] + little_in[0:1, hidden : 2 * hidden]
    gbb_out[...] = little_ref[0:1, 2 * hidden :] + little_in[0:1, 2 * hidden :]


def join(gi, gi_in, gb, gb_in, little, little_in):
    steps = 6
    hidden = gi.shape[1]
    line_i = pl.BlockSpec((gi.shape[0] // steps, hidden), lambda k: (k, 0))
    line_b = pl.BlockSpec((hidden // steps, D), lambda k: (k, 0))
    shape = jax.ShapeDtypeStruct
    return pl.pallas_call(
        join_kernel,
        grid=(steps,),
        out_shape=(shape(gi.shape, F32), shape(gb.shape, F32), shape((1, hidden), F32), shape((1, D), F32)),
        in_specs=[line_i, line_i, line_b, line_b, whole(), whole()],
        out_specs=(line_i, line_b, whole(), whole()),
        compiler_params=params(dimension_semantics=("arbitrary",)),
        name="join",
    )(gi, gi_in, gb, gb_in, little, little_in)


def end_kernel(
    n, experts, shard,
    hg_ref, tok_ref, w_ref, qkv_ref, att_ref, y_ref, hid_ref, small_ref, idx_ref, sg_ref,
    tg_ref, out_ref, gw_ref, gs_ref,
    hg_s, tok_s, w_s, qkv_s, att_s, hid_s, normed, low, dqkv, pp, flat, dn, other, mix, mix_other,
    y_s, acc, dw, r1, s1, r2, sm, q1, t1, q2,
    lsem, us, ur, hs, hr, as_, ar, bs, br,
):
    me, mine = lax.axis_index("dp"), lax.axis_index("mp")
    plane = n // LINE
    z, q = me // plane, me % plane
    tok = tok_s.shape[0]
    images = tok // SEQ
    width = w_s.shape[2]
    rp = dw.shape[3]
    tr = other.shape[0]
    slots = y_s.shape[1]
    scale = HD ** (-0.5)
    sibling = {"mp": 1 - mine}
    zpeer = [((z + d) % LINE) * plane + q for d in range(1, LINE)]
    qpeer = [z * plane + (q + d) % plane for d in range(1, plane)]
    loads = [
        pltpu.make_async_copy(a, b, lsem.at[i])
        for i, (a, b) in enumerate(
            ((hg_ref, hg_s), (tok_ref, tok_s), (w_ref, w_s), (qkv_ref, qkv_s), (att_ref, att_s), (hid_ref, hid_s),
             (y_ref.at[0], y_s.at[0]))
        )
    ]
    for c in loads:
        c.start()
    greet([sibling] + [{"dp": (me + d) % n} for d in range(1, n)])

    def y_copy(p, sign):
        return remote(y_ref.at[p], y_s.at[p], us.at[p], ur.at[p], {"dp": partner(me, n, p, sign)})

    def y_start(p, carry):
        y_copy(p, -1).start()
        return carry

    lax.fori_loop(1, n, y_start, 0)
    loads[0].wait()
    for i in range(images):
        pp[(i + 1) * SEQ_PAD - 16 : (i + 1) * SEQ_PAD, :] = jnp.zeros((16, D), F32)
        pp[i * SEQ_PAD : i * SEQ_PAD + SEQ, :] = hg_s[i * SEQ : (i + 1) * SEQ, :]
    low[...] = pp[...].astype(BF)
    loads[1].wait()
    for i in range(images):
        pp[i * SEQ_PAD : i * SEQ_PAD + SEQ, :] = tok_s[i * SEQ : (i + 1) * SEQ, :].astype(F32)
    for c in loads[2:5]:
        c.wait()

    def spread(value):
        value = value.astype(BF)
        if rp > shard:
            line = lax.broadcasted_iota(jnp.int32, (n * rp, D), 0)
            where = lax.broadcasted_iota(jnp.int32, (n * rp, D), 1)
            fits = (where == line // rp * shard + line % rp) & (line % rp < shard)
            value = mm(jnp.where(fits, 1.0, 0.0).astype(BF), value, 1, 0).astype(BF)
        return value.reshape(LINE, plane, rp, width)

    sends = []

    def plane_send(k, a, b):
        for d, p in enumerate(qpeer):
            to = (q + d + 1) % plane
            c = remote(a(to), b(d), as_.at[d, k], ar.at[d, k], {"dp": p})
            c.start()
            sends.append(c)

    dw[3] = spread(mm(low[...], att_s[...], 0, 0))
    plane_send(0, lambda to: dw.at[3, :, to], lambda d: r1.at[d, 3])
    gains = jnp.transpose(small_ref[...].astype(F32))
    gain = gains[experts : experts + 1, :]
    lane = lax.broadcasted_iota(jnp.int32, (1, 2 * HD), 1)
    masks = [jnp.where(lane // HD == h, 1.0, 0.0).astype(BF) for h in range(2)]
    valid = lax.broadcasted_iota(jnp.int32, (1, SEQ_PAD), 1) < SEQ

    def image(i, carry):
        rows = pl.ds(pl.multiple_of(i * SEQ_PAD, 16), SEQ_PAD)
        xhat, _ = norm_rows(pp[rows, :])
        normed[rows, :] = (xhat * gain).astype(BF)
        grad_att = mm(low[rows, :], w_s[3], 1, 0).astype(BF)
        for p in range(width // (2 * HD)):
            cols = [slice(c * width + p * 2 * HD, c * width + (p + 1) * 2 * HD) for c in range(3)]
            qs, ks, vs = (qkv_s[rows, c] for c in cols)
            pair = grad_att[:, p * 2 * HD : (p + 1) * 2 * HD]
            grads = []
            for h in range(2):
                scores = mm(qs * masks[h], ks, 1, 1) * scale
                scores = jnp.where(valid, scores, -1e30)
                raised = jnp.exp(scores - jnp.max(scores, axis=-1, keepdims=True))
                weights = raised * (1.0 / jnp.sum(raised, axis=-1, keepdims=True))
                product = mm(pair * masks[h], vs, 1, 1) * weights
                grad_scores = product - weights * jnp.sum(product, axis=-1, keepdims=True)
                scores_low = grad_scores.astype(BF)
                grads.append((
                    mm(scores_low, ks, 1, 0) * scale,
                    mm(scores_low, qs, 0, 0) * scale,
                    mm(weights.astype(BF), pair, 0, 0),
                ))
            for c in range(3):
                dqkv[rows, cols[c]] = jnp.where(lane < HD, grads[0][c], grads[1][c]).astype(BF)
        total = mm(dqkv[rows, 0:width], w_s[0], 1, 1)
        for c in range(1, 3):
            total += mm(dqkv[rows, c * width : (c + 1) * width], w_s[c], 1, 1)
        pp[rows, :] = total
        return carry

    lax.fori_loop(0, images, image, 0)
    for c in range(3):
        dw[c] = spread(mm(normed[...], dqkv[:, c * width : (c + 1) * width], 0, 0))
        plane_send(1 + c, lambda to: dw.at[c, :, to], lambda d: r1.at[d, c])
    for i in range(images):
        flat[i * SEQ : (i + 1) * SEQ, :] = pp[i * SEQ_PAD : i * SEQ_PAD + SEQ, :]
    dn[tr - 16 : tr, :] = jnp.zeros((16, D), BF)
    copies = []
    for c, (start, size) in enumerate(row_chunks(tr)):
        stop = min(start + size, tok)
        dn[start:stop, :] = flat[start:stop, :].astype(BF)
        rows = pl.ds(start, size)
        copy = remote(dn.at[rows, :], other.at[rows, :], hs.at[c], hr.at[c], sibling)
        copy.start()
        copies.append(copy)
    gain_sum = jnp.zeros((1, D), F32)
    for c, (start, size) in enumerate(row_chunks(tr)):
        stop = min(start + size, tok)
        copies[c].wait()
        grad = dn[start:stop, :].astype(F32) + other[start:stop, :].astype(F32)
        xhat, inverse = norm_rows(tok_s[start:stop, :].astype(F32))
        tg_ref[start:stop, :] = (hg_s[start:stop, :] + norm_back(grad, gain, xhat, inverse)).astype(BF)
        gain_sum += jnp.sum(grad * xhat, axis=0, keepdims=True)
    row = lax.broadcasted_iota(jnp.int32, sg_ref.shape, 0)
    rows = jnp.where(row == experts + 2, gain_sum, sg_ref[...])
    rows = jnp.concatenate([rows, jnp.zeros((128 - rows.shape[0], D), F32)], axis=0)
    turned = jnp.transpose(rows).astype(BF)
    for b in range(n):
        at = (b // plane, b % plane)
        if shard < rp:
            sm[at[0], at[1]] = jnp.zeros((rp, 128), BF)
        sm[at[0], at[1], 0:shard, :] = turned[b * shard : (b + 1) * shard, :]
    plane_send(4, lambda to: sm.at[:, to], lambda d: q1.at[d])
    acc[...] = jnp.zeros_like(acc)
    loads[6].wait()

    def step(b, carry):
        for j in range(4):
            p = b * 4 + j

            @pl.when(p != 0)
            def _():
                y_copy(p, 1).wait_recv()

        hot = jnp.concatenate(
            [slot_matrix(idx_ref, partner(me, n, b * 4 + j) * slots, slots) for j in range(4)], axis=0
        )
        acc[...] += mm(hot, y_s[pl.ds(b * 4, 4)].reshape(4 * slots, D), 0, 0)
        return carry

    lax.fori_loop(0, n // 4, step, 0)
    mix[tr - 16 : tr, :] = jnp.zeros((16, D), BF)
    base = len(copies)
    late = []
    for c, (start, size) in enumerate(row_chunks(tr)):
        stop = min(start + size, tok)
        mix[start:stop, :] = acc[start:stop, :].astype(BF)
        rows = pl.ds(start, size)
        copy = remote(mix.at[rows, :], mix_other.at[rows, :], hs.at[base + c], hr.at[base + c], sibling)
        copy.start()
        late.append(copy)
    for d in range(plane - 1):
        for k, (a, b) in enumerate(
            [(dw.at[3, :, 0], r1.at[d, 3])] + [(dw.at[c, :, 0], r1.at[d, c]) for c in range(3)]
            + [(sm.at[:, 0], q1.at[d])]
        ):
            remote(a, b, as_.at[d, k], ar.at[d, k], {"dp": qpeer[0]}).wait_recv()
    for b in range(LINE):
        value = dw[:, b, q].astype(F32)
        little = sm[b, q].astype(F32)
        for d in range(plane - 1):
            value += r1[d, :, b].astype(F32)
            little += q1[d, b].astype(F32)
        s1[b] = value.astype(BF)
        t1[b] = little.astype(BF)
    for d, p in enumerate(zpeer):
        to = (z + d + 1) % LINE
        for i, (a, b) in enumerate(((s1, r2), (t1, q2))):
            c = remote(a.at[to], b.at[d], bs.at[d, i], br.at[d, i], {"dp": p})
            c.start()
            sends.append(c)
    loads[5].wait()
    for c, (start, size) in enumerate(row_chunks(tr)):
        stop = min(start + size, tok)
        late[c].wait()
        both = mix[start:stop, :].astype(F32) + mix_other[start:stop, :].astype(F32)
        out_ref[start:stop, :] = (hid_s[start:stop, :] + both).astype(BF)
    value = s1[z].astype(F32)
    little = t1[z].astype(F32)
    for d in range(LINE - 1):
        for i, (a, b) in enumerate(((s1, r2), (t1, q2))):
            remote(a.at[0], b.at[d], bs.at[d, i], br.at[d, i], {"dp": zpeer[0]}).wait_recv()
        value += r2[d].astype(F32)
        little += q2[d].astype(F32)
    gw_ref[...] = value
    gs_ref[...] = little
    for c in sends:
        c.wait_send()

    def y_end(p, carry):
        y_copy(p, -1).wait_send()
        return carry

    lax.fori_loop(1, n, y_end, 0)


def end(hg, tok, w, qkv, att, y, hid, small, idx, sg, n, experts):
    parts, _, width = w.shape
    shard = D // n
    rp = up(shard, 16)
    plane = n // LINE
    tr = up(tok.shape[0], 16)
    chunks = len(row_chunks(tr))
    rows = qkv.shape[0]
    sem = pltpu.SemaphoreType.DMA
    vmem = pltpu.VMEM
    shape = jax.ShapeDtypeStruct
    far = pl.BlockSpec(memory_space=pl.ANY)
    return pl.pallas_call(
        functools.partial(end_kernel, n, experts, shard),
        out_shape=(
            shape(tok.shape, BF), shape(tok.shape, BF), shape((parts, rp, width), F32), shape((rp, 128), F32),
        ),
        in_specs=[far] * 7 + [whole()] * 3,
        out_specs=(whole(),) * 4,
        scratch_shapes=[
            vmem(tok.shape, F32), vmem(tok.shape, BF), vmem(w.shape, BF), vmem(qkv.shape, BF), vmem(att.shape, BF),
            vmem(tok.shape, F32),
            vmem((rows, D), BF), vmem((rows, D), BF), vmem(qkv.shape, BF), vmem((rows, D), F32), vmem((tr, D), F32),
            vmem((tr, D), BF), vmem((tr, D), BF), vmem((tr, D), BF), vmem((tr, D), BF),
            vmem(y.shape, BF), vmem((idx.shape[1], D), F32),
            vmem((parts, LINE, plane, rp, width), BF),
            vmem((plane - 1, parts, LINE, rp, width), BF),
            vmem((LINE, parts, rp, width), BF),
            vmem((LINE - 1, parts, rp, width), BF),
            vmem((LINE, plane, rp, 128), BF),
            vmem((plane - 1, LINE, rp, 128), BF),
            vmem((LINE, rp, 128), BF),
            vmem((LINE - 1, rp, 128), BF),
            sem((7,)), sem((n,)), sem((n,)), sem((2 * chunks,)), sem((2 * chunks,)),
            sem((plane - 1, 5)), sem((plane - 1, 5)), sem((LINE - 1, 2)), sem((LINE - 1, 2)),
        ],
        compiler_params=params(collective_id=3, has_side_effects=True),
        name="end",
    )(hg, tok, w, qkv, att, y, hid, small, idx, sg)


def body(
    tokens, ln1_gain, w_qkv, w_out, out_bias, ln2_gain, router, w_in, in_bias,
    w_back, back_bias, routes, priority, cotangent,
):
    n = lax.axis_size("dp")
    tok = tokens.shape[0]
    experts = router.shape[1]
    cap = max(2, 5 * tok // (2 * experts))
    half = (cap + 1) // 2
    slots = up(half + FREE, 16)
    shard, width = w_qkv.shape[0], w_qkv.shape[2]
    rp = up(shard, 16)
    swap = [(0, 1), (1, 0)]

    start = (
        jnp.swapaxes(w_qkv, 0, 1), w_out.T, router.T,
        (ln1_gain[None], ln2_gain[None], out_bias[None]), routes.T, priority,
    )
    if n * slots <= 1536:
        (hg, sg, y, gi, gi_in, gb, gb_in, little, little_in, hid, _, weights, small, idx, _, qkv, att) = expert(
            (*start, tokens), None, (w_in[0],), (w_back[0],), (in_bias,), back_bias, None, None, None,
            cotangent, None, n, cap, half, slots,
        )
    else:
        wi = (w_in[0], lax.ppermute(w_in[0], "mp", swap))
        wb = (w_back[0], lax.ppermute(w_back[0], "mp", swap))
        bi = (in_bias, lax.ppermute(in_bias, "mp", swap))
        weights, small, idx, ct_rows, qkv, att, part = begin(
            *start, cotangent, tokens, n, experts, cap, half, slots
        )
        hid, probs, x = dispatch(part, tokens, small, idx, n, experts, half, slots)
        hg, sg, y, gi, gi_in, gb, gb_in, little, little_in = expert(
            x, ct_rows, wi, wb, bi, back_bias, idx, probs, hid, cotangent, small, n, cap, half, slots
        )
    gi, gb, gbi, gbb = join(gi, gi_in, gb, gb_in, little, little_in)
    tg, out, gw, gs = end(hg, tokens, weights, qkv, att, y, hid, small, idx, sg, n, experts)
    gw, gs = gw[:, :shard], gs[:shard]
    return (
        out,
        tg,
        gs[:, experts + 2],
        jnp.swapaxes(gw[:3], 0, 1),
        gw[3].T,
        gs[:, experts + 1],
        gs[:, experts],
        gs[:, :experts],
        gi[None],
        gbi,
        gb[None],
        gbb,
    )


def solution(mesh):
    return jax.shard_map(
        body,
        mesh=mesh,
        in_specs=(
            P("dp", None),
            P("dp"),
            P("dp", None, "mp"),
            P("mp", "dp"),
            P("dp"),
            P("dp"),
            P("dp", None),
            P("dp", None, "mp"),
            P("dp", "mp"),
            P("dp", "mp", None),
            P("dp", None),
            P("dp", None),
            P("dp", None),
            P("dp", None),
        ),
        out_specs=(
            P("dp", None),
            P("dp", None),
            P("dp"),
            P("dp", None, "mp"),
            P("mp", "dp"),
            P("dp"),
            P("dp"),
            P("dp", None),
            P("dp", None, "mp"),
            P("dp", "mp"),
            P("dp", "mp", None),
            P("dp", None),
        ),
        check_vma=False,
    )
```

```python
import functools

import jax
import jax.numpy as jnp
from jax import lax
from jax.experimental import pallas as pl
from jax.experimental.pallas import tpu as pltpu
from jax.sharding import PartitionSpec as P

D = 768
HD = 64
SEQ = 197
EPS = 1e-06
F32 = jnp.float32
BF = jnp.bfloat16
MESH = pl.DeviceIdType.MESH
VMEM_LIMIT = 62 * 1024 * 1024
LINE = 4
FREE = 3


def up(value, step):
    return (value + step - 1) // step * step


SEQ_PAD = up(SEQ, 16)


def mm(left, right, cl, cr):
    return lax.dot_general(
        left, right, (((cl,), (cr,)), ((), ())), preferred_element_type=F32
    )


def norm_rows(values):
    average = jnp.mean(values, axis=-1, keepdims=True)
    centered = values - average
    inverse = lax.rsqrt(jnp.mean(centered * centered, axis=-1, keepdims=True) + EPS)
    return centered * inverse, inverse


def norm_back(grad, gain, xhat, inverse):
    scaled = grad * gain
    return inverse * (
        scaled
        - jnp.mean(scaled, axis=-1, keepdims=True)
        - xhat * jnp.mean(scaled * xhat, axis=-1, keepdims=True)
    )


def split_two(value):
    high = value.astype(BF)
    return high, (value - high.astype(F32)).astype(BF)


def whole():
    return pl.BlockSpec(memory_space=pltpu.VMEM)


def params(**more):
    return pltpu.CompilerParams(vmem_limit_bytes=VMEM_LIMIT, **more)


def greet(peers):
    barrier = pltpu.get_barrier_semaphore()
    for peer in peers:
        pl.semaphore_signal(barrier, inc=1, device_id=peer, device_id_type=MESH)
    pl.semaphore_wait(barrier, len(peers))


def remote(src, dst, send_sem, recv_sem, peer):
    return pltpu.make_async_remote_copy(
        src_ref=src, dst_ref=dst, send_sem=send_sem, recv_sem=recv_sem,
        device_id=peer, device_id_type=MESH,
    )


def partner(me, n, place, sign=1):
    plane = n // LINE
    groups = plane // 4
    z, q = me // plane, me % plane
    step, j = place // 4, place % 4
    turn, g = step // groups, step % groups
    k = turn % 2 * 2 + turn // 2
    line = (z // 2 + k // 2) % 2 * 2 + (z % 2 + k % 2) % 2
    return line * plane + (q + plane + sign * (g * 4 + j)) % plane


def slot_matrix(idx_ref, first, rows):
    number = lax.broadcasted_iota(jnp.int32, (rows, idx_ref.shape[1]), 0) + first
    hit = (number == idx_ref[0:1, :]) | (number == idx_ref[1:2, :])
    return jnp.where(hit, 1.0, 0.0).astype(BF)


def begin_part(
    n, cap, half, slots, more_peers, started,
    wq_ref, wout_ref, rows_ref, gain_refs, rt_ref, rank_ref, ct_ref, tok_ref,
    wo_ref, so_ref, idx_ref, ctx_ref, qkv_ref, att_ref, part_ref, soft_ref,
    gw, gs, mine_w, mine_s, info, ctp, cc, send, xp, pp, soft, early_sum,
    zs, zr, ps, pr, cs, cr, lsem,
):
    me, mine = lax.axis_index("dp"), lax.axis_index("mp")
    plane = n // LINE
    z, q = me // plane, me % plane
    experts, shard = rows_ref.shape
    tok = tok_ref.shape[0]
    lanes = idx_ref.shape[1]
    rp = mine_w.shape[1]
    zpeer = [((z + d) % LINE) * plane + q for d in range(1, LINE)]
    qpeer = [z * plane + (q + d) % plane for d in range(1, plane)]
    full_w, full_s = (wo_ref, so_ref) if rp == shard else (gw, gs)

    if rp > shard:
        mine_w[...] = jnp.zeros_like(mine_w)
    mine_w[0:3, 0:shard, :] = wq_ref[...]
    mine_w[3, 0:shard, :] = wout_ref[...]
    pp[0:128, 0:128] = jnp.zeros((128, 128), F32)
    pp[0:experts, 0:shard] = rows_ref[...].astype(F32)
    for k, gain_ref in enumerate(gain_refs):
        pp[experts + k : experts + k + 1, 0:shard] = gain_ref[...].astype(F32)
    mine_s[...] = jnp.transpose(pp[0:128, 0:128])[0:rp, :].astype(BF)
    greet(more_peers + [{"dp": (me + d) % n} for d in range(1, n)])
    started()

    def at(block):
        rows = pl.ds(pl.multiple_of(block * rp, rp), rp)
        return full_w.at[:, rows, :], full_s.at[rows, :]

    own = at(me)
    sends = []
    for d, p in enumerate(zpeer):
        for i, (a, b) in enumerate(zip((mine_w, mine_s), own)):
            sends.append(remote(a, b, zs.at[d, i], zr.at[d, i], {"dp": p}))
            sends[-1].start()
    for d, p in enumerate(qpeer):
        for i, (a, b) in enumerate(zip((mine_w, mine_s), own)):
            sends.append(remote(a, b, ps.at[d, 0, i], pr.at[d, 0, i], {"dp": p}))
            sends[-1].start()
    here = pl.ds(pl.multiple_of(me * rp, rp), rp)
    full_w[:, here, :] = mine_w[...]
    full_s[here, :] = mine_s[...]

    info[0:2, :] = jnp.full((2, lanes), -1, jnp.int32)
    info[2:3, :] = jnp.full((1, lanes), 1 << 20, jnp.int32)
    info[0:2, 0:tok] = rt_ref[...]
    info[2:3, 0:tok] = rank_ref[...]
    number = lax.broadcasted_iota(jnp.int32, (experts, lanes), 0)
    hot = [jnp.where(number == info[j : j + 1, :], 1.0, 0.0) for j in range(2)]
    ranks = info[2:3, :].astype(F32)
    column = jnp.transpose(jnp.broadcast_to(ranks, (128, lanes)))[:, 0:1]
    before = jnp.where(column < ranks, 1.0, 0.0).astype(BF)
    counts = [mm(h.astype(BF), before, 1, 0) for h in hot]
    counts[1] = counts[1] + jnp.sum(hot[0], axis=1, keepdims=True)
    for j in range(2):
        slot = jnp.sum(counts[j] * hot[j], axis=0, keepdims=True).astype(jnp.int32)
        place = slot - mine * half
        expert_id = info[j : j + 1, :]
        kept = (slot < cap) & (place >= 0) & (place < half) & (expert_id >= 0)
        idx_ref[j : j + 1, :] = jnp.where(kept, expert_id * slots + place, -1)
    ctp[lanes - 64 : lanes, cc : cc + D] = jnp.zeros((64, D), BF)
    ctp[0:tok, cc : cc + D] = ct_ref[...]

    def rows_of(b, carry):
        ones = [slot_matrix(idx_ref, partner(me, n, b * 4 + j) * slots, slots) for j in range(4)]
        block = mm(jnp.concatenate(ones, axis=0), ctp[0:lanes, cc : cc + D], 1, 0).astype(BF)
        send[pl.ds(pl.multiple_of(b * 4 * slots, 16), 4 * slots), 0:D] = block
        return carry

    lax.fori_loop(0, n // 4, rows_of, 0)

    for k in range(1, LINE):
        block = at(((z + LINE - k) % LINE) * plane + q)
        for i in range(2):
            remote(block[i], block[i], zs.at[k - 1, i], zr.at[k - 1, i], {"dp": zpeer[0]}).wait_recv()
        for d, p in enumerate(qpeer):
            for i in range(2):
                sends.append(remote(block[i], block[i], ps.at[d, k, i], pr.at[d, k, i], {"dp": p}))
                sends[-1].start()

    def block_of(p):
        return send.at[pl.ds(pl.multiple_of(p * slots, 16), slots), pl.ds(0, D)]

    local = pltpu.make_async_copy(block_of(0), ctx_ref.at[0], lsem.at[0])
    local.start()

    def ship(p, carry):
        @pl.when(p != 0)
        def _():
            remote(block_of(p), ctx_ref.at[p], cs.at[p], cr.at[p], {"dp": partner(me, n, p)}).start()

        return carry

    lax.fori_loop(1, n, ship, 0)

    images = tok // SEQ
    width = wo_ref.shape[2]
    scale = HD ** (-0.5)
    for i in range(images):
        xp[(i + 1) * SEQ_PAD - 16 : (i + 1) * SEQ_PAD, :] = jnp.zeros((16, D), F32)
        xp[i * SEQ_PAD : i * SEQ_PAD + SEQ, :] = tok_ref[i * SEQ : (i + 1) * SEQ, :].astype(F32)

    def norm(i, carry):
        rows = pl.ds(pl.multiple_of(i * SEQ_PAD, 16), SEQ_PAD)
        xhat, _ = norm_rows(xp[rows, :])
        xp[rows, :] = xhat
        return carry

    lax.fori_loop(0, images, norm, 0)
    for d in range(1, plane):
        for k in range(LINE):
            block = at(((z + LINE - k) % LINE) * plane + (q + plane - d) % plane)
            for i in range(2):
                remote(block[i], block[i], ps.at[d - 1, k, i], pr.at[d - 1, k, i], {"dp": qpeer[0]}).wait_recv()
    if rp > shard:
        line = lax.broadcasted_iota(jnp.int32, (D, n * rp), 0)
        where = lax.broadcasted_iota(jnp.int32, (D, n * rp), 1)
        squeeze = jnp.where(where == line // shard * rp + line % shard, 1.0, 0.0).astype(BF)
        for c in range(4):
            wo_ref[c] = mm(squeeze, gw[c], 1, 0).astype(BF)
        so_ref[...] = mm(squeeze, gs[...], 1, 0).astype(BF)
    gain = jnp.transpose(so_ref[...].astype(F32))[experts : experts + 1, :]
    lane = lax.broadcasted_iota(jnp.int32, (1, 2 * HD), 1)
    masks = [jnp.where(lane // HD == h, scale, 0.0).astype(BF) for h in range(2)]
    valid = lax.broadcasted_iota(jnp.int32, (1, SEQ_PAD), 1) < SEQ

    def keep(i):
        return pltpu.make_async_copy(soft.at[i % 2], soft_ref.at[i], lsem.at[1 + i % 2])

    def image(i, carry):
        @pl.when(i >= 2)
        def _():
            keep(i - 2).wait()

        rows = pl.ds(pl.multiple_of(i * SEQ_PAD, 16), SEQ_PAD)
        normed = (xp[rows, :] * gain).astype(BF)
        for c in range(3):
            qkv_ref[rows, c * width : (c + 1) * width] = mm(normed, wo_ref[c], 1, 0).astype(BF)
        for p in range(width // (2 * HD)):
            cols = slice(p * 2 * HD, (p + 1) * 2 * HD)
            qs, ks, vs = (
                qkv_ref[rows, c * width + p * 2 * HD : c * width + (p + 1) * 2 * HD] for c in range(3)
            )
            outs = []
            for h in range(2):
                scores = jnp.where(valid, mm(qs * masks[h], ks, 1, 1), -1e30)
                raised = jnp.exp(scores - jnp.max(scores, axis=-1, keepdims=True))
                weights = raised * (1.0 / jnp.sum(raised, axis=-1, keepdims=True))
                soft[i % 2, 2 * p + h] = weights
                outs.append(mm(weights.astype(BF), vs, 1, 0))
            att_ref[rows, cols] = jnp.where(lane < HD, outs[0], outs[1]).astype(BF)
        partial = mm(att_ref[rows, 0:width], wo_ref[3], 1, 1)
        if early_sum is None:
            pp[rows, :] = partial
        else:
            early_sum[0][rows, :] = partial.astype(BF)
            early_copy(i).start()
        keep(i).start()
        return carry

    def early_copy(i):
        own, other, es, er = early_sum
        rows = pl.ds(pl.multiple_of(i * SEQ_PAD, 16), SEQ_PAD)
        return remote(own.at[rows, :], other.at[rows, :], es.at[i], er.at[i], {"mp": 1 - mine})

    lax.fori_loop(0, images, image, 0)
    for i in range(images):
        rows = slice(i * SEQ_PAD, i * SEQ_PAD + SEQ)
        if early_sum is None:
            total = pp[rows, :]
        else:
            early_copy(i).wait()
            total = early_sum[0][rows, :].astype(F32) + early_sum[1][rows, :].astype(F32)
        part_ref[i * SEQ : (i + 1) * SEQ, :] = total

    def arrived(p):
        @pl.when(p != 0)
        def _():
            remote(block_of(p), ctx_ref.at[p], cs.at[p], cr.at[p], {"dp": partner(me, n, p)}).wait_recv()

    def ended():
        for c in sends:
            c.wait_send()
        local.wait()
        for i in range(max(0, images - 2), images):
            keep(i).wait()

        def sent(p, carry):
            @pl.when(p != 0)
            def _():
                remote(block_of(p), ctx_ref.at[p], cs.at[p], cr.at[p], {"dp": partner(me, n, p)}).wait_send()

            return carry

        lax.fori_loop(0, n, sent, 0)

    return arrived, ended


def begin_kernel(n, cap, half, slots, *refs):
    arrived, ended = begin_part(n, cap, half, slots, [], lambda: None, *refs[:22], 0, *refs[22:26], None, *refs[26:])

    def finish(p, carry):
        arrived(p)
        return carry

    lax.fori_loop(0, n, finish, 0)
    ended()


def begin(wq, wout, rows, gains, rt, rank, ct, tok, n, experts, cap, half, slots):
    images = tok.shape[0] // SEQ
    shard, width = wout.shape
    rp = up(shard, 16)
    lanes = up(tok.shape[0], 128)
    plane = n // LINE
    sem = pltpu.SemaphoreType.DMA
    shape = jax.ShapeDtypeStruct
    vmem = pltpu.VMEM
    spare = n * rp if rp > shard else 16

    def kernel(wq_ref, wout_ref, rows_ref, g1, g2, g3, *rest):
        begin_kernel(n, cap, half, slots, wq_ref, wout_ref, rows_ref, (g1, g2, g3), *rest)

    return pl.pallas_call(
        kernel,
        out_shape=(
            shape((4, D, width), BF), shape((D, 128), BF), shape((2, lanes), jnp.int32),
            shape((n, slots, D), BF), shape((images * SEQ_PAD, 3 * width), BF),
            shape((images * SEQ_PAD, width), BF), shape((up(tok.shape[0], 16), D), F32),
            shape((images, width // HD, SEQ_PAD, SEQ_PAD), F32),
        ),
        in_specs=[whole()] * 10,
        out_specs=(whole(), whole(), whole(), pl.BlockSpec(memory_space=pl.ANY), whole(), whole(), whole(),
                   pl.BlockSpec(memory_space=pl.ANY)),
        scratch_shapes=[
            vmem((4, spare, width), BF), vmem((spare, 128), BF),
            vmem((4, rp, width), BF), vmem((rp, 128), BF), vmem((8, lanes), jnp.int32),
            vmem((lanes, D), BF), vmem((n * slots, D), BF),
            vmem((images * SEQ_PAD, D), F32), vmem((images * SEQ_PAD, D), F32),
            vmem((2, width // HD, SEQ_PAD, SEQ_PAD), F32),
            sem((LINE - 1, 2)), sem((LINE - 1, 2)),
            sem((plane - 1, LINE, 2)), sem((plane - 1, LINE, 2)),
            sem((n,)), sem((n,)), sem((1,)),
        ],
        compiler_params=params(collective_id=0, has_side_effects=True),
        name="begin",
    )(wq, wout, rows, *gains, rt, rank, ct, tok)


def row_chunks(rows):
    return [(s, min(256, rows - s)) for s in range(0, rows, 256)]


def token_send(n, send, x_ref, xs, xr, p, peer):
    return remote(send.at[p], x_ref.at[p], xs.at[p], xr.at[p], {"dp": peer})


def send_tokens(
    n, half, early, part_ref, tok_ref, small_ref, idx_ref, hid_ref, n2, prob_ref, x_ref,
    own, other, send, p2, hs, hr, xs, xr,
):
    me, mine = lax.axis_index("dp"), lax.axis_index("mp")
    plane = n // LINE
    tok = tok_ref.shape[0]
    slots = send.shape[1]
    experts, lanes = prob_ref.shape
    tr = up(tok, 16)
    sibling = {"mp": 1 - mine}
    copies = []
    if own is not None:
        own[tr - 16 : tr, :] = jnp.zeros((16, D), BF)
        for c, (start, size) in enumerate(row_chunks(tr)):
            stop = min(start + size, tok)
            own[start:stop, :] = part_ref[start:stop, :].astype(BF)
            rows = pl.ds(start, size)
            copy = remote(own.at[rows, :], other.at[rows, :], hs.at[c], hr.at[c], sibling)
            copy.start()
            copies.append(copy)
    gains = jnp.transpose(small_ref[...].astype(F32))
    gain = gains[experts + 1 : experts + 2, :]
    bias = gains[experts + 2 : experts + 3, :]
    n2[lanes - 64 : lanes, 0:D] = jnp.zeros((64, D), BF)
    for c, (start, size) in enumerate(row_chunks(tr)):
        stop = min(start + size, tok)
        if own is None:
            both = part_ref[start:stop, :]
        else:
            copies[c].wait_recv()
            both = own[start:stop, :].astype(F32) + other[start:stop, :].astype(F32)
        hidden = tok_ref[start:stop, :].astype(F32) + both + bias
        hid_ref[start:stop, :] = hidden
        xhat, _ = norm_rows(hidden)
        n2[start:stop, 0:D] = (xhat * gain).astype(BF)
    logits = mm(gains[0:experts, :].astype(BF), n2[0:lanes, 0:D], 1, 1)
    raised = jnp.exp(logits - jnp.max(logits, axis=0, keepdims=True))
    probs = raised / jnp.sum(raised, axis=0, keepdims=True)
    prob_ref[...] = probs
    high, low = split_two(probs)
    p2[0:experts, :] = high
    p2[experts:, :] = low
    place = lax.broadcasted_iota(jnp.int32, (slots, slots), 0)
    number = lax.broadcasted_iota(jnp.int32, (2 * experts, slots), 0)

    def step(b, carry):
        hot = [slot_matrix(idx_ref, partner(me, n, b * 4 + j) * slots, slots) for j in range(4)]
        block = mm(jnp.concatenate(hot, axis=0), n2[0:lanes, 0:D], 1, 0)
        for j in range(4):
            p = b * 4 + j
            peer = partner(me, n, p)
            gates = mm(p2[...], hot[j], 1, 1)
            row_high = jnp.sum(jnp.where(number == peer, gates, 0.0), axis=0, keepdims=True)
            row_low = jnp.sum(jnp.where(number == peer + experts, gates, 0.0), axis=0, keepdims=True)
            rows = block[j * slots : (j + 1) * slots, :]
            left = jnp.where(place == half, row_high, jnp.where(place == half + 1, row_low, rows[:, 0:slots]))
            send[p, :, :] = rows.astype(BF)
            send[p, :, 0:slots] = left.astype(BF)

            @pl.when((p != 0) & (p < early))
            def _():
                token_send(n, send, x_ref, xs, xr, p, peer).start()

        return carry

    lax.fori_loop(0, n // 4, step, 0)
    x_ref[0] = send[0]
    for copy in copies:
        copy.wait_send()


def dispatch_kernel(
    n, half, part_ref, tok_ref, small_ref, idx_ref, hid_ref, prob_ref, x_ref,
    n2, own, other, send, p2, hs, hr, xs, xr,
):
    me, mine = lax.axis_index("dp"), lax.axis_index("mp")
    plane = n // LINE
    greet([{"mp": 1 - mine}] + [{"dp": (me + d) % n} for d in range(1, n)])
    send_tokens(
        n, half, n, part_ref, tok_ref, small_ref, idx_ref, hid_ref, n2, prob_ref, x_ref,
        own, other, send, p2, hs, hr, xs, xr,
    )

    def finish(p, carry):
        @pl.when(p != 0)
        def _():
            token_send(n, send, x_ref, xs, xr, p, partner(me, n, p)).wait()

        return carry

    lax.fori_loop(0, n, finish, 0)


def dispatch(part, tok, small, idx, n, experts, half, slots):
    lanes = idx.shape[1]
    tr = up(tok.shape[0], 16)
    sem = pltpu.SemaphoreType.DMA
    vmem = pltpu.VMEM
    chunks = len(row_chunks(tr))
    return pl.pallas_call(
        functools.partial(dispatch_kernel, n, half),
        out_shape=(
            jax.ShapeDtypeStruct(tok.shape, F32),
            jax.ShapeDtypeStruct((experts, lanes), F32),
            jax.ShapeDtypeStruct((n, slots, D), BF),
        ),
        in_specs=[whole()] * 4,
        out_specs=(whole(),) * 3,
        scratch_shapes=[
            vmem((lanes, D), BF), vmem((tr, D), BF), vmem((tr, D), BF), vmem((n, slots, D), BF),
            vmem((2 * experts, lanes), BF),
            sem((chunks,)), sem((chunks,)), sem((n,)), sem((n,)),
        ],
        compiler_params=params(collective_id=1, has_side_effects=True),
        name="dispatch",
    )(part, tok, small, idx)


def expert_kernel(
    n, cap, half, fused,
    first, ct_ref, wi_own, wi_sib, wb_own, wb_sib, bi_own, bi_sib, bb_ref,
    idx_ref, seen_ref, tok_ct, small_ref,
    hg_ref, sg_ref, y_ref, gi_ref, gi_in, gb_ref, gb_in, little_ref, little_in, hid_out, prob_ref,
    wo_ref, qkv_out, att_out, soft_out,
    vi_own, vi_sib, vb_own, vb_sib, g_s, act_own, act_sib, dp_own, dp_sib, dx_s, back, acc, other,
    ct_s, y_s, stage, gp, gp_other, x_ref, send, p2, mine_w, mine_s, info, bias_s, bias_in, soft,
    lsem, ysem, gsem, ss, rs, hs, hr, ms, mr, xs, xr, es, er, zs, zr, ps, pr, cs, cr, bsem,
):
    me, mine = lax.axis_index("dp"), lax.axis_index("mp")
    sibling = {"mp": 1 - mine}
    slots = x_ref.shape[1]
    tok = tok_ct.shape[0]
    tr = up(tok, 16)
    experts = gp.shape[0]
    hidden = wi_own.shape[1]
    group = 4 * slots
    batches = n // 4
    early = n // 2 if fused else n
    lanes = gp.shape[1]
    owns = [(wi_own, vi_own), (wb_own, vb_own)]
    if not fused:
        owns += [(wi_sib, vi_sib), (wb_sib, vb_sib), (first, x_ref)]
    loads = [pltpu.make_async_copy(a, b, lsem.at[i]) for i, (a, b) in enumerate(owns)]
    for c in loads:
        c.start()
    if fused:
        halves = [
            remote(wi_own, vi_sib, ms.at[3], mr.at[3], sibling),
            remote(wb_own, vb_sib, ms.at[4], mr.at[4], sibling),
            remote(bias_s, bias_in, ms.at[5], mr.at[5], sibling),
        ]
        bias_s[...] = jnp.zeros_like(bias_s)
        bias_s[0:1, :] = bi_own[...].astype(F32)

        def started():
            for c in halves:
                c.start()

        arrived, ended = begin_part(
            n, cap, half, slots, [sibling], started, *first,
            wo_ref, small_ref, idx_ref, ct_ref, act_own, act_sib, hg_ref, soft_out,
            None, None, mine_w, mine_s, info, act_sib, D, dp_own, acc, stage, soft, (g_s, other, es, er),
            zs, zr, ps, pr, cs, cr, bsem,
        )
        rows = qkv_out.shape[0]
        kept = [
            pltpu.make_async_copy(act_own.at[pl.ds(0, rows), pl.ds(0, qkv_out.shape[1])], qkv_out, lsem.at[2]),
            pltpu.make_async_copy(act_sib.at[pl.ds(0, rows), pl.ds(0, att_out.shape[1])], att_out, lsem.at[3]),
        ]
        for c in kept:
            c.start()
        send_tokens(
            n, half, early, hg_ref, first[-1], small_ref, idx_ref, hg_ref, dp_sib, prob_ref, x_ref,
            None, None, send, p2, None, None, xs, xr,
        )
        keep = pltpu.make_async_copy(hg_ref, hid_out, lsem.at[5])
        keep.start()
        ended()
        for c in kept:
            c.wait()
        for c in halves:
            c.wait()
        bias_own, bias_sib = bi_own[...].astype(F32), bias_in[0:1, :]
    else:
        greet([sibling] + [{"dp": (me + d) % n} for d in range(1, n)])
        keep = pltpu.make_async_copy(hid_out, hg_ref, lsem.at[5])
        keep.start()
        bias_own, bias_sib = bi_own[...].astype(F32), bi_sib[...].astype(F32)
    little_ref[...] = jnp.zeros_like(little_ref)

    def ct_here(b, j):
        if fused:
            arrived(b * 4 + j)

    def cts(b, j):
        return pltpu.make_async_copy(ct_ref.at[b * 4 + j], ct_s.at[j], ysem.at[0, j])

    def ys(b, j):
        return pltpu.make_async_copy(y_s.at[j], y_ref.at[b * 4 + j], ysem.at[1, j])

    for j in range(4):
        ct_here(0, j)
        cts(0, j).start()
    for c in loads:
        c.wait()
    chunk = 768
    row = lax.broadcasted_iota(jnp.int32, (group, 16), 0)
    number = lax.broadcasted_iota(jnp.int32, (group, 16), 1)
    member = jnp.where(row // slots == number, 1.0, 0.0).astype(BF)
    spot = lax.broadcasted_iota(jnp.int32, (group, 128), 0) % slots
    here = spot == lax.broadcasted_iota(jnp.int32, (group, 128), 1)
    row_t = lax.broadcasted_iota(jnp.int32, (16, group), 1)
    number_t = lax.broadcasted_iota(jnp.int32, (16, group), 0)
    pick = jnp.where(
        (row_t == number_t * slots + half) | (row_t == number_t * slots + half + 1), 1.0, 0.0
    ).astype(BF)
    member_t = jnp.where(row_t // slots == number_t, 1.0, 0.0).astype(BF)
    puts = [jnp.where(row == number * slots + half + i, 1.0, 0.0).astype(BF) for i in range(2)]

    def batch(b, carry):
        at = pl.ds(pl.multiple_of(b * group, 16), group)
        if fused:
            @pl.when(b == batches // 4)
            def _():
                def more(p, carry):
                    token_send(n, send, x_ref, xs, xr, p, partner(me, n, p)).start()
                    return carry

                lax.fori_loop(early, n, more, 0)

            for j in range(4):
                p = b * 4 + j

                @pl.when(p != 0)
                def _():
                    token_send(n, send, x_ref, xs, xr, p, partner(me, n, p)).wait_recv()

        x = x_ref[pl.ds(b * 4, 4)].reshape(group, D)
        high, low = split_two(mm(pick, x[:, 0:128], 1, 0))
        wide = mm(member, high, 1, 0) + mm(member, low, 1, 0)
        gate = jnp.sum(jnp.where(here, wide, 0.0), axis=1, keepdims=True)
        for j in range(4):
            cts(b, j).wait()
        g_s[at, :] = (gate * ct_s[...].reshape(group, D).astype(F32)).astype(BF)
        little_ref[0:1, 2 * hidden :] += jnp.sum(g_s[at, :].astype(F32), axis=0, keepdims=True)
        for part, (vi, vb, bi, acts, dps) in enumerate(
            ((vi_own, vb_own, bias_own, act_own, dp_own), (vi_sib, vb_sib, bias_sib, act_sib, dp_sib))
        ):
            for c in range(hidden // chunk):
                cols = slice(c * chunk, (c + 1) * chunk)
                pre = mm(x_ref[pl.ds(b * 4, 4)].reshape(group, D), vi[:, cols], 1, 0) + bi[:, cols]
                phi = 0.5 * (1.0 + lax.erf(pre * (0.5**0.5)))
                slope = phi + pre * (jnp.exp(-0.5 * pre * pre) * ((2.0 * jnp.pi) ** -0.5))
                acts[at, cols] = (pre * phi).astype(BF)
                grad = (mm(g_s[at, :], vb[cols, :], 1, 1) * slope).astype(BF)
                dps[at, cols] = grad
                place = slice(part * hidden + c * chunk, part * hidden + (c + 1) * chunk)
                little_ref[0:1, place] += jnp.sum(grad.astype(F32), axis=0, keepdims=True)
        dx = mm(dp_own[at, :], vi_own[...], 1, 1) + mm(dp_sib[at, :], vi_sib[...], 1, 1)
        y = mm(act_own[at, :], vb_own[...], 1, 0) + mm(act_sib[at, :], vb_sib[...], 1, 0)
        y = (y + bb_ref[...].astype(F32)).astype(BF).astype(F32)
        dots = jnp.sum(ct_s[...].reshape(group, D).astype(F32) * y, axis=1, keepdims=True)
        high, low = split_two(jnp.where(here, dots, 0.0))
        high, low = mm(member_t, high, 1, 0).astype(BF), mm(member_t, low, 1, 0).astype(BF)
        left = dx[:, 0:128] + mm(puts[0], high, 1, 0) + mm(puts[1], low, 1, 0)
        dx = jnp.concatenate([left, dx[:, 128:]], axis=1)
        dx_s[pl.ds(b * 4, 4)] = dx.astype(BF).reshape(4, slots, D)
        for j in range(4):
            p = b * 4 + j

            @pl.when(p != 0)
            def _():
                remote(dx_s.at[p], back.at[p], ss.at[p], rs.at[p], {"dp": partner(me, n, p, -1)}).start()

        @pl.when(b > 0)
        def _():
            for j in range(4):
                ys(b - 1, j).wait()

        y_s[...] = (gate * y).astype(BF).reshape(4, slots, D)
        for j in range(4):
            ys(b, j).start()

        @pl.when(b + 1 < batches)
        def _():
            for j in range(4):
                ct_here(b + 1, j)
                cts(b + 1, j).start()

        return carry

    lax.fori_loop(0, batches, batch, 0)
    back[0] = dx_s[0]
    little = remote(little_ref, little_in, ms.at[2], mr.at[2], sibling)
    little.start()

    rows_all = n * slots
    steps = 3
    size = D // steps
    wide = hidden // 2
    swaps = []

    def out_i(r, c):
        return pltpu.make_async_copy(
            stage.at[r % 2 * 2 * size + c * size : r % 2 * 2 * size + (c + 1) * size, :],
            gi_ref.at[r * size : (r + 1) * size, c * wide : (c + 1) * wide], gsem.at[c, r],
        )

    def out_b(r):
        return pltpu.make_async_copy(
            stage.at[r % 2 * 2 * size : (r % 2 + 1) * 2 * size, :], gb_ref.at[r * 2 * size : (r + 1) * 2 * size, :], gsem.at[2, r]
        )

    for r in range(steps):
        at = slice(r * size, (r + 1) * size)
        left = x_ref[:, :, at].reshape(rows_all, size)
        vi_sib[at, :] = mm(left, dp_sib[...], 0, 0).astype(BF)
        for c in range(2):
            if r >= 2:
                out_i(r - 2, c).wait()
            at_s = r % 2 * 2 * size + c * size
            stage[at_s : at_s + size, :] = mm(left, dp_own[:, c * wide : (c + 1) * wide], 0, 0)
            out_i(r, c).start()
    copy = remote(vi_sib, gi_in, ms.at[0], mr.at[0], sibling)
    copy.start()
    swaps.append(copy)

    acc[...] = jnp.zeros_like(acc)
    gp[...] = jnp.zeros_like(gp)
    place = lax.broadcasted_iota(jnp.int32, (slots, 128), 0)
    count = lax.broadcasted_iota(jnp.int32, (experts, slots), 0)

    def combine(b, carry):
        hot = []
        for j in range(4):
            d = b * 4 + j
            source = partner(me, n, d)

            @pl.when(d != 0)
            def _():
                remote(dx_s.at[d], back.at[d], ss.at[d], rs.at[d], {"dp": source}).wait_recv()

            hot.append(slot_matrix(idx_ref, source * slots, slots))
            extra = back[d, :, 0:128].astype(F32)
            high = jnp.sum(jnp.where(place == half, extra, 0.0), axis=0, keepdims=True)[:, 0:slots]
            low = jnp.sum(jnp.where(place == half + 1, extra, 0.0), axis=0, keepdims=True)[:, 0:slots]
            for value in (high, low):
                gp[...] += mm(jnp.where(count == source, value, 0.0).astype(BF), hot[j], 1, 0)
        block = back[pl.ds(b * 4, 4)].reshape(group, D)
        acc[0:lanes, :] += mm(jnp.concatenate(hot, axis=0), block, 0, 0)
        return carry

    lax.fori_loop(0, batches // 2, combine, 0)
    for r in range(steps):
        at = slice(r * 2 * size, (r + 1) * 2 * size)
        vb_sib[at, :] = mm(act_sib[:, at], g_s[...], 0, 0).astype(BF)
        if r == 0:
            for c in range(2):
                out_i(1, c).wait()
                out_i(2, c).wait()
        if r >= 2:
            out_b(r - 2).wait()
        stage[r % 2 * 2 * size : (r % 2 + 1) * 2 * size, :] = mm(act_own[:, at], g_s[...], 0, 0)
        out_b(r).start()
    copy = remote(vb_sib, gb_in, ms.at[1], mr.at[1], sibling)
    copy.start()
    swaps.append(copy)
    lax.fori_loop(batches // 2, batches, combine, 0)

    little.wait()
    copies = []
    own = g_s
    own[tr - 16 : tr, :] = jnp.zeros((16, D), BF)
    for c, (start, length) in enumerate(row_chunks(tr)):
        stop = min(start + length, tok)
        own[start:stop, :] = acc[start:stop, :].astype(BF)
        rows = pl.ds(start, length)
        copy = remote(own.at[rows, :], other.at[rows, :], hs.at[c], hr.at[c], sibling)
        copy.start()
        copies.append(copy)
    copy = remote(gp, gp_other, hs.at[len(copies)], hr.at[len(copies)], sibling)
    copy.start()
    copy.wait()
    probs = prob_ref[...] if fused else seen_ref[...]
    grad_probs = gp[...] + gp_other[...]
    logits = (probs * (grad_probs - jnp.sum(grad_probs * probs, axis=0, keepdims=True))).astype(BF)
    gains = jnp.transpose(small_ref[...].astype(F32))
    gain = gains[experts + 1 : experts + 2, :]
    acc[0:lanes, :] = mm(logits, gains[0:experts, :].astype(BF), 0, 0)
    sg_ref[...] = jnp.zeros_like(sg_ref)
    gain_sum = jnp.zeros((1, D), F32)
    bias_sum = jnp.zeros((1, D), F32)
    act_own[lanes - 64 : lanes, 0:D] = jnp.zeros((64, D), BF)
    keep.wait()
    for c, (start, length) in enumerate(row_chunks(tr)):
        stop = min(start + length, tok)
        copies[c].wait_recv()
        grad = own[start:stop, :].astype(F32) + other[start:stop, :].astype(F32) + acc[start:stop, :]
        xhat, inverse = norm_rows(hg_ref[start:stop, :])
        act_own[start:stop, 0:D] = (xhat * gain).astype(BF)
        hidden_grad = tok_ct[start:stop, :].astype(F32) + norm_back(grad, gain, xhat, inverse)
        hg_ref[start:stop, :] = hidden_grad
        gain_sum += jnp.sum(grad * xhat, axis=0, keepdims=True)
        bias_sum += jnp.sum(hidden_grad, axis=0, keepdims=True)
    sg_ref[0:experts, :] = mm(logits, act_own[0:lanes, 0:D], 1, 0)
    sg_ref[experts : experts + 1, :] = gain_sum
    sg_ref[experts + 1 : experts + 2, :] = bias_sum
    for copy in copies:
        copy.wait_send()

    def finish(p, carry):
        @pl.when(p != 0)
        def _():
            remote(dx_s.at[p], back.at[p], ss.at[p], rs.at[p], {"dp": partner(me, n, p, -1)}).wait_send()
            if fused:
                token_send(n, send, x_ref, xs, xr, p, partner(me, n, p)).wait_send()

        return carry

    lax.fori_loop(0, n, finish, 0)
    for j in range(4):
        ys(batches - 1, j).wait()
    for r in range(1, steps):
        out_b(r).wait()
    for copy in swaps:
        copy.wait()


def expert(first, ct_rows, wi, wb, bi, bb, idx, probs, hid, ct, small, n, cap, half, slots):
    fused = hid is None
    rows = n * slots
    hidden = wi[0].shape[1]
    lanes = up(ct.shape[0], 128)
    experts = n
    tr = up(ct.shape[0], 16)
    chunks = len(row_chunks(tr))
    flat = ct.shape[0] // SEQ * SEQ_PAD
    shape = jax.ShapeDtypeStruct
    sem = pltpu.SemaphoreType.DMA
    vmem = pltpu.VMEM
    far = pl.BlockSpec(memory_space=pl.ANY)
    outs = [
        shape(ct.shape, F32), shape((up(experts + 3, 8), D), F32), shape((n, slots, D), BF),
        shape((D, hidden), F32), shape((D, hidden), BF),
        shape((hidden, D), F32), shape((hidden, D), BF),
        shape((8, 2 * hidden + D), F32), shape((8, 2 * hidden + D), F32),
    ]
    out_specs = [whole(), whole(), far, far, far, far, far, whole(), whole()]
    if fused:
        wq, wout, router_t, gains, rt, rank, tok = first
        shard, width = wout.shape
        plane = n // LINE
        ins = [wq, wout, router_t, *gains, rt, rank, ct, tok, wi[0], wb[0], bi[0], bb]
        in_specs = [whole()] * 10 + [far, far, whole(), whole()]
        outs += [
            shape(ct.shape, F32), shape((experts, lanes), F32), shape((4, D, width), BF), shape((D, 128), BF),
            shape((2, lanes), jnp.int32), shape((n, slots, D), BF),
            shape((flat, 3 * width), BF), shape((flat, width), BF),
            shape((flat // SEQ_PAD, width // HD, SEQ_PAD, SEQ_PAD), F32),
        ]
        out_specs += [far, whole(), whole(), whole(), whole(), far, far, far, far]

        def kernel(*refs):
            wq, wout, rows_t, g1, g2, g3, rt, rank, ct, tok, wi, wb, bi, bb = refs[:14]
            main, (hid, prob, wo, so, idx, ctx, qkv, att, soft) = refs[14:23], refs[23:32]
            expert_kernel(
                n, cap, half, True, (wq, wout, rows_t, (g1, g2, g3), rt, rank, ct, tok),
                ctx, wi, None, wb, None, bi, None, bb, idx, None, ct, so,
                *main, hid, prob, wo, qkv, att, soft, *refs[32:],
            )

        spare = [vmem((4, shard, width), BF), vmem((shard, 128), BF), vmem((8, lanes), jnp.int32)]
        spare += [vmem((8, hidden), F32)] * 2 + [vmem((2, width // HD, SEQ_PAD, SEQ_PAD), F32)]
        grid = (plane - 1, LINE, 2)
        send_rows = (n, slots, D)
    else:
        ins = [first, ct_rows, wi[0], wi[1], wb[0], wb[1], bi[0], bi[1], bb, idx, probs, ct, small, hid]
        in_specs = [far] * 6 + [whole()] * 7 + [far]

        def kernel(*refs):
            ins, hid_ref, outs, rest = refs[:13], refs[13], refs[14:23], refs[23:]
            expert_kernel(n, cap, half, False, *ins, *outs, hid_ref, ins[10], None, None, None, None, *rest)

        spare = [vmem((1, 16, 128), BF), vmem((16, 128), BF), vmem((8, 128), jnp.int32)]
        spare += [vmem((8, 128), F32)] * 3
        grid = (1, 1, 2)
        send_rows = (1, 16, 128)

    return pl.pallas_call(
        kernel,
        out_shape=tuple(outs),
        in_specs=in_specs,
        out_specs=tuple(out_specs),
        scratch_shapes=[
            vmem((D, hidden), BF), vmem((D, hidden), BF), vmem((hidden, D), BF), vmem((hidden, D), BF),
            vmem((rows, D), BF),
            vmem((rows, hidden), BF), vmem((rows, hidden), BF),
            vmem((rows, hidden), BF), vmem((rows, hidden), BF),
            vmem((n, slots, D), BF), vmem((n, slots, D), BF),
            vmem((flat if fused else lanes, D), F32), vmem((flat if fused else tr, D), BF),
            vmem((4, slots, D), BF), vmem((4, slots, D), BF),
            vmem((flat if fused else 1024, D), F32),
            vmem((experts, lanes), F32), vmem((experts, lanes), F32),
            vmem((n, slots, D), BF), vmem(send_rows, BF), vmem((2 * experts, lanes), BF),
            *spare,
            sem((6,)), sem((2, 4)), sem((3, 3)), sem((n,)), sem((n,)),
            sem((chunks + 1,)), sem((chunks + 1,)), sem((6,)), sem((6,)),
            sem((n,)), sem((n,)), sem((flat // SEQ_PAD,)), sem((flat // SEQ_PAD,)),
            sem((LINE - 1, 2)), sem((LINE - 1, 2)), sem(grid), sem(grid), sem((n,)), sem((n,)), sem((3,)),
        ],
        compiler_params=params(collective_id=2, has_side_effects=True),
        name="expert",
    )(*ins)


def join_kernel(
    gi_ref, gi_in, gb_ref, gb_in, little_ref, little_in, gw_ref, gs_ref,
    gi_out, gb_out, gbi_out, gbb_out, gq_out, go_out, gr_out, g1_out, g2_out, g3_out,
):
    gi_out[...] = gi_ref[...] + gi_in[...].astype(F32)
    gb_out[...] = gb_ref[...] + gb_in[...].astype(F32)

    @pl.when(pl.program_id(0) == 0)
    def _():
        hidden = gbi_out.shape[1]
        shard = go_out.shape[0]
        experts = gr_out.shape[0]
        gbi_out[...] = little_ref[0:1, 0:hidden] + little_in[0:1, hidden : 2 * hidden]
        gbb_out[...] = little_ref[0:1, 2 * hidden :] + little_in[0:1, 2 * hidden :]
        gq_out[...] = gw_ref[0:3, 0:shard, :]
        go_out[...] = gw_ref[3, 0:shard, :]
        turned = jnp.transpose(gs_ref[...])
        gr_out[...] = turned[0:experts, 0:shard]
        for k, out in enumerate((g2_out, g3_out, g1_out)):
            out[...] = turned[experts + k : experts + k + 1, 0:shard]


def join(gi, gi_in, gb, gb_in, little, little_in, gw, gs, shard, experts):
    steps = 6
    width = gw.shape[2]
    hidden = gi.shape[1]
    line_i = pl.BlockSpec((gi.shape[0] // steps, hidden), lambda k: (k, 0))
    line_b = pl.BlockSpec((hidden // steps, D), lambda k: (k, 0))
    shape = jax.ShapeDtypeStruct
    return pl.pallas_call(
        join_kernel,
        grid=(steps,),
        out_shape=(shape(gi.shape, F32), shape(gb.shape, F32), shape((1, hidden), F32), shape((1, D), F32),
                   shape((3, shard, width), F32), shape((shard, width), F32), shape((experts, shard), F32),
                   *[shape((1, shard), F32)] * 3),
        in_specs=[line_i, line_i, line_b, line_b] + [whole()] * 4,
        out_specs=(line_i, line_b) + (whole(),) * 8,
        compiler_params=params(dimension_semantics=("arbitrary",)),
        name="join",
    )(gi, gi_in, gb, gb_in, little, little_in, gw, gs)


def end_kernel(
    n, experts, shard,
    hg_ref, tok_ref, w_ref, qkv_ref, att_ref, soft_ref, y_ref, hid_ref, small_ref, idx_ref, sg_ref,
    tg_ref, out_ref, gw_ref, gs_ref,
    hg_s, tok_s, w_s, qkv_s, att_s, hid_s, normed, low, dqkv, pp, flat, dn, other, mix, mix_other,
    y_s, acc, soft, dw, r1, s1, r2, sm, q1, t1, q2,
    lsem, us, ur, hs, hr, as_, ar, bs, br,
):
    me, mine = lax.axis_index("dp"), lax.axis_index("mp")
    plane = n // LINE
    z, q = me // plane, me % plane
    tok = tok_s.shape[0]
    images = tok // SEQ
    width = w_s.shape[2]
    rp = dw.shape[3]
    tr = other.shape[0]
    slots = y_s.shape[1]
    scale = HD ** (-0.5)
    sibling = {"mp": 1 - mine}
    zpeer = [((z + d) % LINE) * plane + q for d in range(1, LINE)]
    qpeer = [z * plane + (q + d) % plane for d in range(1, plane)]
    loads = [
        pltpu.make_async_copy(a, b, lsem.at[i])
        for i, (a, b) in enumerate(
            ((hg_ref, hg_s), (tok_ref, tok_s), (w_ref, w_s), (qkv_ref, qkv_s), (att_ref, att_s), (hid_ref, hid_s),
             (y_ref.at[0], y_s.at[0]))
        )
    ]
    for c in loads:
        c.start()
    greet([sibling] + [{"dp": (me + d) % n} for d in range(1, n)])

    def y_copy(p, sign):
        return remote(y_ref.at[p], y_s.at[p], us.at[p], ur.at[p], {"dp": partner(me, n, p, sign)})

    def y_start(p, carry):
        y_copy(p, -1).start()
        return carry

    lax.fori_loop(1, n, y_start, 0)
    loads[0].wait()
    for i in range(images):
        pp[(i + 1) * SEQ_PAD - 16 : (i + 1) * SEQ_PAD, :] = jnp.zeros((16, D), F32)
        pp[i * SEQ_PAD : i * SEQ_PAD + SEQ, :] = hg_s[i * SEQ : (i + 1) * SEQ, :]
    low[...] = pp[...].astype(BF)
    loads[1].wait()
    for i in range(images):
        pp[i * SEQ_PAD : i * SEQ_PAD + SEQ, :] = tok_s[i * SEQ : (i + 1) * SEQ, :].astype(F32)
    for c in loads[2:5]:
        c.wait()

    def spread(value):
        value = value.astype(BF)
        if rp > shard:
            line = lax.broadcasted_iota(jnp.int32, (n * rp, D), 0)
            where = lax.broadcasted_iota(jnp.int32, (n * rp, D), 1)
            fits = (where == line // rp * shard + line % rp) & (line % rp < shard)
            value = mm(jnp.where(fits, 1.0, 0.0).astype(BF), value, 1, 0).astype(BF)
        return value.reshape(LINE, plane, rp, width)

    sends = []

    def plane_send(k, a, b):
        for d, p in enumerate(qpeer):
            to = (q + d + 1) % plane
            c = remote(a(to), b(d), as_.at[d, k], ar.at[d, k], {"dp": p})
            c.start()
            sends.append(c)

    dw[3] = spread(mm(low[...], att_s[...], 0, 0))
    plane_send(0, lambda to: dw.at[3, :, to], lambda d: r1.at[d, 3])
    gains = jnp.transpose(small_ref[...].astype(F32))
    gain = gains[experts : experts + 1, :]
    lane = lax.broadcasted_iota(jnp.int32, (1, 2 * HD), 1)
    masks = [jnp.where(lane // HD == h, 1.0, 0.0).astype(BF) for h in range(2)]

    def fetch(i):
        return pltpu.make_async_copy(soft_ref.at[i], soft.at[i % 2], lsem.at[7 + i % 2])

    fetch(0).start()

    def image(i, carry):
        rows = pl.ds(pl.multiple_of(i * SEQ_PAD, 16), SEQ_PAD)
        fetch(i).wait()

        @pl.when(i + 1 < images)
        def _():
            fetch(i + 1).start()

        xhat, _ = norm_rows(pp[rows, :])
        normed[rows, :] = (xhat * gain).astype(BF)
        grad_att = mm(low[rows, :], w_s[3], 1, 0).astype(BF)
        for p in range(width // (2 * HD)):
            cols = [slice(c * width + p * 2 * HD, c * width + (p + 1) * 2 * HD) for c in range(3)]
            qs, ks, vs = (qkv_s[rows, c] for c in cols)
            pair = grad_att[:, p * 2 * HD : (p + 1) * 2 * HD]
            grads = []
            for h in range(2):
                weights = soft[i % 2, 2 * p + h]
                product = mm(pair * masks[h], vs, 1, 1) * weights
                grad_scores = product - weights * jnp.sum(product, axis=-1, keepdims=True)
                scores_low = grad_scores.astype(BF)
                grads.append((
                    mm(scores_low, ks, 1, 0) * scale,
                    mm(scores_low, qs, 0, 0) * scale,
                    mm(weights.astype(BF), pair, 0, 0),
                ))
            for c in range(3):
                dqkv[rows, cols[c]] = jnp.where(lane < HD, grads[0][c], grads[1][c]).astype(BF)
        total = mm(dqkv[rows, 0:width], w_s[0], 1, 1)
        for c in range(1, 3):
            total += mm(dqkv[rows, c * width : (c + 1) * width], w_s[c], 1, 1)
        pp[rows, :] = total
        return carry

    lax.fori_loop(0, images, image, 0)
    for c in range(3):
        dw[c] = spread(mm(normed[...], dqkv[:, c * width : (c + 1) * width], 0, 0))
        plane_send(1 + c, lambda to: dw.at[c, :, to], lambda d: r1.at[d, c])
    for i in range(images):
        flat[i * SEQ : (i + 1) * SEQ, :] = pp[i * SEQ_PAD : i * SEQ_PAD + SEQ, :]
    dn[tr - 16 : tr, :] = jnp.zeros((16, D), BF)
    copies = []
    for c, (start, size) in enumerate(row_chunks(tr)):
        stop = min(start + size, tok)
        dn[start:stop, :] = flat[start:stop, :].astype(BF)
        rows = pl.ds(start, size)
        copy = remote(dn.at[rows, :], other.at[rows, :], hs.at[c], hr.at[c], sibling)
        copy.start()
        copies.append(copy)
    gain_sum = jnp.zeros((1, D), F32)
    for c, (start, size) in enumerate(row_chunks(tr)):
        stop = min(start + size, tok)
        copies[c].wait()
        grad = dn[start:stop, :].astype(F32) + other[start:stop, :].astype(F32)
        xhat, inverse = norm_rows(tok_s[start:stop, :].astype(F32))
        tg_ref[start:stop, :] = (hg_s[start:stop, :] + norm_back(grad, gain, xhat, inverse)).astype(BF)
        gain_sum += jnp.sum(grad * xhat, axis=0, keepdims=True)
    row = lax.broadcasted_iota(jnp.int32, sg_ref.shape, 0)
    rows = jnp.where(row == experts + 2, gain_sum, sg_ref[...])
    rows = jnp.concatenate([rows, jnp.zeros((128 - rows.shape[0], D), F32)], axis=0)
    turned = jnp.transpose(rows).astype(BF)
    for b in range(n):
        at = (b // plane, b % plane)
        if shard < rp:
            sm[at[0], at[1]] = jnp.zeros((rp, 128), BF)
        sm[at[0], at[1], 0:shard, :] = turned[b * shard : (b + 1) * shard, :]
    plane_send(4, lambda to: sm.at[:, to], lambda d: q1.at[d])
    acc[...] = jnp.zeros_like(acc)
    loads[6].wait()

    def step(b, carry):
        for j in range(4):
            p = b * 4 + j

            @pl.when(p != 0)
            def _():
                y_copy(p, 1).wait_recv()

        hot = jnp.concatenate(
            [slot_matrix(idx_ref, partner(me, n, b * 4 + j) * slots, slots) for j in range(4)], axis=0
        )
        acc[...] += mm(hot, y_s[pl.ds(b * 4, 4)].reshape(4 * slots, D), 0, 0)
        return carry

    lax.fori_loop(0, n // 4, step, 0)
    mix[tr - 16 : tr, :] = jnp.zeros((16, D), BF)
    base = len(copies)
    late = []
    for c, (start, size) in enumerate(row_chunks(tr)):
        stop = min(start + size, tok)
        mix[start:stop, :] = acc[start:stop, :].astype(BF)
        rows = pl.ds(start, size)
        copy = remote(mix.at[rows, :], mix_other.at[rows, :], hs.at[base + c], hr.at[base + c], sibling)
        copy.start()
        late.append(copy)
    for d in range(plane - 1):
        for k, (a, b) in enumerate(
            [(dw.at[3, :, 0], r1.at[d, 3])] + [(dw.at[c, :, 0], r1.at[d, c]) for c in range(3)]
            + [(sm.at[:, 0], q1.at[d])]
        ):
            remote(a, b, as_.at[d, k], ar.at[d, k], {"dp": qpeer[0]}).wait_recv()
    for b in range(LINE):
        value = dw[:, b, q].astype(F32)
        little = sm[b, q].astype(F32)
        for d in range(plane - 1):
            value += r1[d, :, b].astype(F32)
            little += q1[d, b].astype(F32)
        s1[b] = value.astype(BF)
        t1[b] = little.astype(BF)
    for d, p in enumerate(zpeer):
        to = (z + d + 1) % LINE
        for i, (a, b) in enumerate(((s1, r2), (t1, q2))):
            c = remote(a.at[to], b.at[d], bs.at[d, i], br.at[d, i], {"dp": p})
            c.start()
            sends.append(c)
    loads[5].wait()
    for c, (start, size) in enumerate(row_chunks(tr)):
        stop = min(start + size, tok)
        late[c].wait()
        both = mix[start:stop, :].astype(F32) + mix_other[start:stop, :].astype(F32)
        out_ref[start:stop, :] = (hid_s[start:stop, :] + both).astype(BF)
    value = s1[z].astype(F32)
    little = t1[z].astype(F32)
    for d in range(LINE - 1):
        for i, (a, b) in enumerate(((s1, r2), (t1, q2))):
            remote(a.at[0], b.at[d], bs.at[d, i], br.at[d, i], {"dp": zpeer[0]}).wait_recv()
        value += r2[d].astype(F32)
        little += q2[d].astype(F32)
    gw_ref[...] = value
    gs_ref[...] = little
    for c in sends:
        c.wait_send()

    def y_end(p, carry):
        y_copy(p, -1).wait_send()
        return carry

    lax.fori_loop(1, n, y_end, 0)


def end(hg, tok, w, qkv, att, soft, y, hid, small, idx, sg, n, experts):
    parts, _, width = w.shape
    shard = D // n
    rp = up(shard, 16)
    plane = n // LINE
    tr = up(tok.shape[0], 16)
    chunks = len(row_chunks(tr))
    rows = qkv.shape[0]
    sem = pltpu.SemaphoreType.DMA
    vmem = pltpu.VMEM
    shape = jax.ShapeDtypeStruct
    far = pl.BlockSpec(memory_space=pl.ANY)
    return pl.pallas_call(
        functools.partial(end_kernel, n, experts, shard),
        out_shape=(
            shape(tok.shape, BF), shape(tok.shape, BF), shape((parts, rp, width), F32), shape((rp, 128), F32),
        ),
        in_specs=[far] * 8 + [whole()] * 3,
        out_specs=(whole(),) * 4,
        scratch_shapes=[
            vmem(tok.shape, F32), vmem(tok.shape, BF), vmem(w.shape, BF), vmem(qkv.shape, BF), vmem(att.shape, BF),
            vmem(tok.shape, F32),
            vmem((rows, D), BF), vmem((rows, D), BF), vmem(qkv.shape, BF), vmem((rows, D), F32), vmem((tr, D), F32),
            vmem((tr, D), BF), vmem((tr, D), BF), vmem((tr, D), BF), vmem((tr, D), BF),
            vmem(y.shape, BF), vmem((idx.shape[1], D), F32),
            vmem((2,) + soft.shape[1:], F32),
            vmem((parts, LINE, plane, rp, width), BF),
            vmem((plane - 1, parts, LINE, rp, width), BF),
            vmem((LINE, parts, rp, width), BF),
            vmem((LINE - 1, parts, rp, width), BF),
            vmem((LINE, plane, rp, 128), BF),
            vmem((plane - 1, LINE, rp, 128), BF),
            vmem((LINE, rp, 128), BF),
            vmem((LINE - 1, rp, 128), BF),
            sem((9,)), sem((n,)), sem((n,)), sem((2 * chunks,)), sem((2 * chunks,)),
            sem((plane - 1, 5)), sem((plane - 1, 5)), sem((LINE - 1, 2)), sem((LINE - 1, 2)),
        ],
        compiler_params=params(collective_id=3, has_side_effects=True),
        name="end",
    )(hg, tok, w, qkv, att, soft, y, hid, small, idx, sg)


def body(
    tokens, ln1_gain, w_qkv, w_out, out_bias, ln2_gain, router, w_in, in_bias,
    w_back, back_bias, routes, priority, cotangent,
):
    n = lax.axis_size("dp")
    tok = tokens.shape[0]
    experts = router.shape[1]
    cap = max(2, 5 * tok // (2 * experts))
    half = (cap + 1) // 2
    slots = up(half + FREE, 16)
    shard, width = w_qkv.shape[0], w_qkv.shape[2]
    rp = up(shard, 16)
    swap = [(0, 1), (1, 0)]

    start = (
        jnp.swapaxes(w_qkv, 0, 1), w_out.T, router.T,
        (ln1_gain[None], ln2_gain[None], out_bias[None]), routes.T, priority,
    )
    if n * slots <= 1536:
        (hg, sg, y, gi, gi_in, gb, gb_in, little, little_in, hid, _, weights, small, idx, _, qkv, att, soft) = expert(
            (*start, tokens), None, (w_in[0],), (w_back[0],), (in_bias,), back_bias, None, None, None,
            cotangent, None, n, cap, half, slots,
        )
    else:
        wi = (w_in[0], lax.ppermute(w_in[0], "mp", swap))
        wb = (w_back[0], lax.ppermute(w_back[0], "mp", swap))
        bi = (in_bias, lax.ppermute(in_bias, "mp", swap))
        weights, small, idx, ct_rows, qkv, att, part, soft = begin(
            *start, cotangent, tokens, n, experts, cap, half, slots
        )
        hid, probs, x = dispatch(part, tokens, small, idx, n, experts, half, slots)
        hg, sg, y, gi, gi_in, gb, gb_in, little, little_in = expert(
            x, ct_rows, wi, wb, bi, back_bias, idx, probs, hid, cotangent, small, n, cap, half, slots
        )
    tg, out, gw, gs = end(hg, tokens, weights, qkv, att, soft, y, hid, small, idx, sg, n, experts)
    gi, gb, gbi, gbb, gq, go, gr, g1, g2, g3 = join(gi, gi_in, gb, gb_in, little, little_in, gw, gs, shard, experts)
    return (
        out,
        tg,
        g1[0],
        jnp.swapaxes(gq, 0, 1),
        go.T,
        g3[0],
        g2[0],
        gr.T,
        gi[None],
        gbi,
        gb[None],
        gbb,
    )


def solution(mesh):
    return jax.shard_map(
        body,
        mesh=mesh,
        in_specs=(
            P("dp", None),
            P("dp"),
            P("dp", None, "mp"),
            P("mp", "dp"),
            P("dp"),
            P("dp"),
            P("dp", None),
            P("dp", None, "mp"),
            P("dp", "mp"),
            P("dp", "mp", None),
            P("dp", None),
            P("dp", None),
            P("dp", None),
            P("dp", None),
        ),
        out_specs=(
            P("dp", None),
            P("dp", None),
            P("dp"),
            P("dp", None, "mp"),
            P("mp", "dp"),
            P("dp"),
            P("dp"),
            P("dp", None),
            P("dp", None, "mp"),
            P("dp", "mp"),
            P("dp", "mp", None),
            P("dp", None),
        ),
        check_vma=False,
    )
```

```python
import functools

import jax
import jax.numpy as jnp
from jax import lax
from jax.experimental import pallas as pl
from jax.experimental.pallas import tpu as pltpu
from jax.sharding import PartitionSpec as P

D = 768
HD = 64
SEQ = 197
EPS = 1e-06
F32 = jnp.float32
BF = jnp.bfloat16
MESH = pl.DeviceIdType.MESH
VMEM_LIMIT = 62 * 1024 * 1024
LINE = 4
FREE = 3


def up(value, step):
    return (value + step - 1) // step * step


SEQ_PAD = up(SEQ, 16)


def mm(left, right, cl, cr):
    return lax.dot_general(
        left, right, (((cl,), (cr,)), ((), ())), preferred_element_type=F32
    )


def norm_rows(values):
    average = jnp.mean(values, axis=-1, keepdims=True)
    centered = values - average
    inverse = lax.rsqrt(jnp.mean(centered * centered, axis=-1, keepdims=True) + EPS)
    return centered * inverse, inverse


def norm_back(grad, gain, xhat, inverse):
    scaled = grad * gain
    return inverse * (
        scaled
        - jnp.mean(scaled, axis=-1, keepdims=True)
        - xhat * jnp.mean(scaled * xhat, axis=-1, keepdims=True)
    )


def split_two(value):
    high = value.astype(BF)
    return high, (value - high.astype(F32)).astype(BF)


def whole():
    return pl.BlockSpec(memory_space=pltpu.VMEM)


def params(**more):
    return pltpu.CompilerParams(vmem_limit_bytes=VMEM_LIMIT, **more)


def greet(peers):
    barrier = pltpu.get_barrier_semaphore()
    for peer in peers:
        pl.semaphore_signal(barrier, inc=1, device_id=peer, device_id_type=MESH)
    pl.semaphore_wait(barrier, len(peers))


def remote(src, dst, send_sem, recv_sem, peer):
    return pltpu.make_async_remote_copy(
        src_ref=src, dst_ref=dst, send_sem=send_sem, recv_sem=recv_sem,
        device_id=peer, device_id_type=MESH,
    )


def partner(me, n, place, sign=1):
    plane = n // LINE
    groups = plane // 4
    z, q = me // plane, me % plane
    step, j = place // 4, place % 4
    turn, g = step // groups, step % groups
    k = turn % 2 * 2 + turn // 2
    line = (z // 2 + k // 2) % 2 * 2 + (z % 2 + k % 2) % 2
    return line * plane + (q + plane + sign * (g * 4 + j)) % plane


def slot_matrix(idx_ref, first, rows):
    number = lax.broadcasted_iota(jnp.int32, (rows, idx_ref.shape[1]), 0) + first
    hit = (number == idx_ref[0:1, :]) | (number == idx_ref[1:2, :])
    return jnp.where(hit, 1.0, 0.0).astype(BF)


def begin_part(
    n, cap, half, slots, more_peers, started,
    wq_ref, wout_ref, rows_ref, gain_refs, rt_ref, rank_ref, ct_ref, tok_ref,
    wo_ref, so_ref, idx_ref, ctx_ref, qkv_ref, att_ref, part_ref, soft_ref,
    gw, gs, mine_w, mine_s, info, ctp, cc, send, xp, pp, soft, early_sum,
    zs, zr, ps, pr, cs, cr, lsem,
):
    me, mine = lax.axis_index("dp"), lax.axis_index("mp")
    plane = n // LINE
    z, q = me // plane, me % plane
    experts, shard = rows_ref.shape
    tok = tok_ref.shape[0]
    lanes = idx_ref.shape[1]
    rp = mine_w.shape[1]
    zpeer = [((z + d) % LINE) * plane + q for d in range(1, LINE)]
    qpeer = [z * plane + (q + d) % plane for d in range(1, plane)]
    full_w, full_s = (wo_ref, so_ref) if rp == shard else (gw, gs)

    if rp > shard:
        mine_w[...] = jnp.zeros_like(mine_w)
    mine_w[0:3, 0:shard, :] = wq_ref[...]
    mine_w[3, 0:shard, :] = wout_ref[...]
    pp[0:128, 0:128] = jnp.zeros((128, 128), F32)
    pp[0:experts, 0:shard] = rows_ref[...].astype(F32)
    for k, gain_ref in enumerate(gain_refs):
        pp[experts + k : experts + k + 1, 0:shard] = gain_ref[...].astype(F32)
    mine_s[...] = jnp.transpose(pp[0:128, 0:128])[0:rp, :].astype(BF)
    greet(more_peers + [{"dp": (me + d) % n} for d in range(1, n)])
    started()

    def at(block):
        rows = pl.ds(pl.multiple_of(block * rp, rp), rp)
        return full_w.at[:, rows, :], full_s.at[rows, :]

    own = at(me)
    sends = []
    for d, p in enumerate(zpeer):
        for i, (a, b) in enumerate(zip((mine_w, mine_s), own)):
            sends.append(remote(a, b, zs.at[d, i], zr.at[d, i], {"dp": p}))
            sends[-1].start()
    for d, p in enumerate(qpeer):
        for i, (a, b) in enumerate(zip((mine_w, mine_s), own)):
            sends.append(remote(a, b, ps.at[d, 0, i], pr.at[d, 0, i], {"dp": p}))
            sends[-1].start()
    here = pl.ds(pl.multiple_of(me * rp, rp), rp)
    full_w[:, here, :] = mine_w[...]
    full_s[here, :] = mine_s[...]

    info[0:2, :] = jnp.full((2, lanes), -1, jnp.int32)
    info[2:3, :] = jnp.full((1, lanes), 1 << 20, jnp.int32)
    info[0:2, 0:tok] = rt_ref[...]
    info[2:3, 0:tok] = rank_ref[...]
    number = lax.broadcasted_iota(jnp.int32, (experts, lanes), 0)
    hot = [jnp.where(number == info[j : j + 1, :], 1.0, 0.0) for j in range(2)]
    ranks = info[2:3, :].astype(F32)
    column = jnp.transpose(jnp.broadcast_to(ranks, (128, lanes)))[:, 0:1]
    before = jnp.where(column < ranks, 1.0, 0.0).astype(BF)
    counts = [mm(h.astype(BF), before, 1, 0) for h in hot]
    counts[1] = counts[1] + jnp.sum(hot[0], axis=1, keepdims=True)
    for j in range(2):
        slot = jnp.sum(counts[j] * hot[j], axis=0, keepdims=True).astype(jnp.int32)
        place = slot - mine * half
        expert_id = info[j : j + 1, :]
        kept = (slot < cap) & (place >= 0) & (place < half) & (expert_id >= 0)
        idx_ref[j : j + 1, :] = jnp.where(kept, expert_id * slots + place, -1)
    ctp[lanes - 64 : lanes, cc : cc + D] = jnp.zeros((64, D), BF)
    ctp[0:tok, cc : cc + D] = ct_ref[...]

    def rows_of(b, carry):
        ones = [slot_matrix(idx_ref, partner(me, n, b * 4 + j) * slots, slots) for j in range(4)]
        block = mm(jnp.concatenate(ones, axis=0), ctp[0:lanes, cc : cc + D], 1, 0).astype(BF)
        send[pl.ds(pl.multiple_of(b * 4 * slots, 16), 4 * slots), 0:D] = block
        return carry

    lax.fori_loop(0, n // 4, rows_of, 0)

    for k in range(1, LINE):
        block = at(((z + LINE - k) % LINE) * plane + q)
        for i in range(2):
            remote(block[i], block[i], zs.at[k - 1, i], zr.at[k - 1, i], {"dp": zpeer[0]}).wait_recv()
        for d, p in enumerate(qpeer):
            for i in range(2):
                sends.append(remote(block[i], block[i], ps.at[d, k, i], pr.at[d, k, i], {"dp": p}))
                sends[-1].start()

    def block_of(p):
        return send.at[pl.ds(pl.multiple_of(p * slots, 16), slots), pl.ds(0, D)]

    local = pltpu.make_async_copy(block_of(0), ctx_ref.at[0], lsem.at[0])
    local.start()

    def ship(p, carry):
        @pl.when(p != 0)
        def _():
            remote(block_of(p), ctx_ref.at[p], cs.at[p], cr.at[p], {"dp": partner(me, n, p)}).start()

        return carry

    lax.fori_loop(1, n, ship, 0)

    images = tok // SEQ
    width = wo_ref.shape[2]
    scale = HD ** (-0.5)
    for i in range(images):
        xp[(i + 1) * SEQ_PAD - 16 : (i + 1) * SEQ_PAD, :] = jnp.zeros((16, D), F32)
        xp[i * SEQ_PAD : i * SEQ_PAD + SEQ, :] = tok_ref[i * SEQ : (i + 1) * SEQ, :].astype(F32)

    def norm(i, carry):
        rows = pl.ds(pl.multiple_of(i * SEQ_PAD, 16), SEQ_PAD)
        xhat, _ = norm_rows(xp[rows, :])
        xp[rows, :] = xhat
        return carry

    lax.fori_loop(0, images, norm, 0)
    for d in range(1, plane):
        for k in range(LINE):
            block = at(((z + LINE - k) % LINE) * plane + (q + plane - d) % plane)
            for i in range(2):
                remote(block[i], block[i], ps.at[d - 1, k, i], pr.at[d - 1, k, i], {"dp": qpeer[0]}).wait_recv()
    if rp > shard:
        line = lax.broadcasted_iota(jnp.int32, (D, n * rp), 0)
        where = lax.broadcasted_iota(jnp.int32, (D, n * rp), 1)
        squeeze = jnp.where(where == line // shard * rp + line % shard, 1.0, 0.0).astype(BF)
        for c in range(4):
            wo_ref[c] = mm(squeeze, gw[c], 1, 0).astype(BF)
        so_ref[...] = mm(squeeze, gs[...], 1, 0).astype(BF)
    gain = jnp.transpose(so_ref[...].astype(F32))[experts : experts + 1, :]
    lane = lax.broadcasted_iota(jnp.int32, (1, 2 * HD), 1)
    masks = [jnp.where(lane // HD == h, scale, 0.0).astype(BF) for h in range(2)]
    valid = lax.broadcasted_iota(jnp.int32, (1, SEQ_PAD), 1) < SEQ

    def keep(i):
        return pltpu.make_async_copy(soft.at[i % 2], soft_ref.at[i], lsem.at[1 + i % 2])

    def image(i, carry):
        @pl.when(i >= 2)
        def _():
            keep(i - 2).wait()

        rows = pl.ds(pl.multiple_of(i * SEQ_PAD, 16), SEQ_PAD)
        normed = (xp[rows, :] * gain).astype(BF)
        for c in range(3):
            qkv_ref[rows, c * width : (c + 1) * width] = mm(normed, wo_ref[c], 1, 0).astype(BF)
        for p in range(width // (2 * HD)):
            cols = slice(p * 2 * HD, (p + 1) * 2 * HD)
            qs, ks, vs = (
                qkv_ref[rows, c * width + p * 2 * HD : c * width + (p + 1) * 2 * HD] for c in range(3)
            )
            outs = []
            for h in range(2):
                scores = jnp.where(valid, mm(qs * masks[h], ks, 1, 1), -1e30)
                raised = jnp.exp(scores - jnp.max(scores, axis=-1, keepdims=True))
                weights = raised * (1.0 / jnp.sum(raised, axis=-1, keepdims=True))
                soft[i % 2, 2 * p + h] = weights
                outs.append(mm(weights.astype(BF), vs, 1, 0))
            att_ref[rows, cols] = jnp.where(lane < HD, outs[0], outs[1]).astype(BF)
        partial = mm(att_ref[rows, 0:width], wo_ref[3], 1, 1)
        if early_sum is None:
            pp[rows, :] = partial
        else:
            early_sum[0][rows, :] = partial.astype(BF)
            early_copy(i).start()
        keep(i).start()
        return carry

    def early_copy(i):
        own, other, es, er = early_sum
        rows = pl.ds(pl.multiple_of(i * SEQ_PAD, 16), SEQ_PAD)
        return remote(own.at[rows, :], other.at[rows, :], es.at[i], er.at[i], {"mp": 1 - mine})

    lax.fori_loop(0, images, image, 0)
    for i in range(images):
        rows = slice(i * SEQ_PAD, i * SEQ_PAD + SEQ)
        if early_sum is None:
            total = pp[rows, :]
        else:
            early_copy(i).wait()
            total = early_sum[0][rows, :].astype(F32) + early_sum[1][rows, :].astype(F32)
        part_ref[i * SEQ : (i + 1) * SEQ, :] = total

    def arrived(p):
        @pl.when(p != 0)
        def _():
            remote(block_of(p), ctx_ref.at[p], cs.at[p], cr.at[p], {"dp": partner(me, n, p)}).wait_recv()

    def ended():
        for c in sends:
            c.wait_send()
        local.wait()
        for i in range(max(0, images - 2), images):
            keep(i).wait()

        def sent(p, carry):
            @pl.when(p != 0)
            def _():
                remote(block_of(p), ctx_ref.at[p], cs.at[p], cr.at[p], {"dp": partner(me, n, p)}).wait_send()

            return carry

        lax.fori_loop(0, n, sent, 0)

    return arrived, ended


def begin_kernel(n, cap, half, slots, *refs):
    arrived, ended = begin_part(n, cap, half, slots, [], lambda: None, *refs[:22], 0, *refs[22:26], None, *refs[26:])

    def finish(p, carry):
        arrived(p)
        return carry

    lax.fori_loop(0, n, finish, 0)
    ended()


def begin(wq, wout, rows, gains, rt, rank, ct, tok, n, experts, cap, half, slots):
    images = tok.shape[0] // SEQ
    shard, width = wout.shape
    rp = up(shard, 16)
    lanes = up(tok.shape[0], 128)
    plane = n // LINE
    sem = pltpu.SemaphoreType.DMA
    shape = jax.ShapeDtypeStruct
    vmem = pltpu.VMEM
    spare = n * rp if rp > shard else 16

    def kernel(wq_ref, wout_ref, rows_ref, g1, g2, g3, *rest):
        begin_kernel(n, cap, half, slots, wq_ref, wout_ref, rows_ref, (g1, g2, g3), *rest)

    return pl.pallas_call(
        kernel,
        out_shape=(
            shape((4, D, width), BF), shape((D, 128), BF), shape((2, lanes), jnp.int32),
            shape((n, slots, D), BF), shape((images * SEQ_PAD, 3 * width), BF),
            shape((images * SEQ_PAD, width), BF), shape((up(tok.shape[0], 16), D), F32),
            shape((images, width // HD, SEQ_PAD, SEQ_PAD), F32),
        ),
        in_specs=[whole()] * 10,
        out_specs=(whole(), whole(), whole(), pl.BlockSpec(memory_space=pl.ANY), whole(), whole(), whole(),
                   pl.BlockSpec(memory_space=pl.ANY)),
        scratch_shapes=[
            vmem((4, spare, width), BF), vmem((spare, 128), BF),
            vmem((4, rp, width), BF), vmem((rp, 128), BF), vmem((8, lanes), jnp.int32),
            vmem((lanes, D), BF), vmem((n * slots, D), BF),
            vmem((images * SEQ_PAD, D), F32), vmem((images * SEQ_PAD, D), F32),
            vmem((2, width // HD, SEQ_PAD, SEQ_PAD), F32),
            sem((LINE - 1, 2)), sem((LINE - 1, 2)),
            sem((plane - 1, LINE, 2)), sem((plane - 1, LINE, 2)),
            sem((n,)), sem((n,)), sem((1,)),
        ],
        compiler_params=params(collective_id=0, has_side_effects=True),
        name="begin",
    )(wq, wout, rows, *gains, rt, rank, ct, tok)


def row_chunks(rows):
    return [(s, min(256, rows - s)) for s in range(0, rows, 256)]


def token_send(n, send, x_ref, xs, xr, p, peer):
    return remote(send.at[p], x_ref.at[p], xs.at[p], xr.at[p], {"dp": peer})


def send_tokens(
    n, half, early, part_ref, tok_ref, small_ref, idx_ref, hid_ref, n2, prob_ref, x_ref,
    own, other, send, p2, hs, hr, xs, xr,
):
    me, mine = lax.axis_index("dp"), lax.axis_index("mp")
    plane = n // LINE
    tok = tok_ref.shape[0]
    slots = send.shape[1]
    experts, lanes = prob_ref.shape
    tr = up(tok, 16)
    sibling = {"mp": 1 - mine}
    copies = []
    if own is not None:
        own[tr - 16 : tr, :] = jnp.zeros((16, D), BF)
        for c, (start, size) in enumerate(row_chunks(tr)):
            stop = min(start + size, tok)
            own[start:stop, :] = part_ref[start:stop, :].astype(BF)
            rows = pl.ds(start, size)
            copy = remote(own.at[rows, :], other.at[rows, :], hs.at[c], hr.at[c], sibling)
            copy.start()
            copies.append(copy)
    gains = jnp.transpose(small_ref[...].astype(F32))
    gain = gains[experts + 1 : experts + 2, :]
    bias = gains[experts + 2 : experts + 3, :]
    n2[lanes - 64 : lanes, 0:D] = jnp.zeros((64, D), BF)
    for c, (start, size) in enumerate(row_chunks(tr)):
        stop = min(start + size, tok)
        if own is None:
            both = part_ref[start:stop, :]
        else:
            copies[c].wait_recv()
            both = own[start:stop, :].astype(F32) + other[start:stop, :].astype(F32)
        hidden = tok_ref[start:stop, :].astype(F32) + both + bias
        hid_ref[start:stop, :] = hidden
        xhat, _ = norm_rows(hidden)
        n2[start:stop, 0:D] = (xhat * gain).astype(BF)
    logits = mm(gains[0:experts, :].astype(BF), n2[0:lanes, 0:D], 1, 1)
    raised = jnp.exp(logits - jnp.max(logits, axis=0, keepdims=True))
    probs = raised / jnp.sum(raised, axis=0, keepdims=True)
    prob_ref[...] = probs
    high, low = split_two(probs)
    p2[0:experts, :] = high
    p2[experts:, :] = low
    place = lax.broadcasted_iota(jnp.int32, (slots, slots), 0)
    number = lax.broadcasted_iota(jnp.int32, (2 * experts, slots), 0)

    def step(turn, carry):
        b = turn + 1 - 2 * (turn % 2)
        hot = [slot_matrix(idx_ref, partner(me, n, b * 4 + j) * slots, slots) for j in range(4)]
        block = mm(jnp.concatenate(hot, axis=0), n2[0:lanes, 0:D], 1, 0)
        for j in range(4):
            p = b * 4 + j
            peer = partner(me, n, p)
            gates = mm(p2[...], hot[j], 1, 1)
            row_high = jnp.sum(jnp.where(number == peer, gates, 0.0), axis=0, keepdims=True)
            row_low = jnp.sum(jnp.where(number == peer + experts, gates, 0.0), axis=0, keepdims=True)
            rows = block[j * slots : (j + 1) * slots, :]
            left = jnp.where(place == half, row_high, jnp.where(place == half + 1, row_low, rows[:, 0:slots]))
            send[p, :, :] = rows.astype(BF)
            send[p, :, 0:slots] = left.astype(BF)

            @pl.when((p != 0) & (p < early))
            def _():
                token_send(n, send, x_ref, xs, xr, p, peer).start()

        return carry

    lax.fori_loop(0, n // 4, step, 0)
    x_ref[0] = send[0]
    for copy in copies:
        copy.wait_send()


def dispatch_kernel(
    n, half, part_ref, tok_ref, small_ref, idx_ref, hid_ref, prob_ref, x_ref,
    n2, own, other, send, p2, hs, hr, xs, xr,
):
    me, mine = lax.axis_index("dp"), lax.axis_index("mp")
    plane = n // LINE
    greet([{"mp": 1 - mine}] + [{"dp": (me + d) % n} for d in range(1, n)])
    send_tokens(
        n, half, n, part_ref, tok_ref, small_ref, idx_ref, hid_ref, n2, prob_ref, x_ref,
        own, other, send, p2, hs, hr, xs, xr,
    )

    def finish(p, carry):
        @pl.when(p != 0)
        def _():
            token_send(n, send, x_ref, xs, xr, p, partner(me, n, p)).wait()

        return carry

    lax.fori_loop(0, n, finish, 0)


def dispatch(part, tok, small, idx, n, experts, half, slots):
    lanes = idx.shape[1]
    tr = up(tok.shape[0], 16)
    sem = pltpu.SemaphoreType.DMA
    vmem = pltpu.VMEM
    chunks = len(row_chunks(tr))
    return pl.pallas_call(
        functools.partial(dispatch_kernel, n, half),
        out_shape=(
            jax.ShapeDtypeStruct(tok.shape, F32),
            jax.ShapeDtypeStruct((experts, lanes), F32),
            jax.ShapeDtypeStruct((n, slots, D), BF),
        ),
        in_specs=[whole()] * 4,
        out_specs=(whole(),) * 3,
        scratch_shapes=[
            vmem((lanes, D), BF), vmem((tr, D), BF), vmem((tr, D), BF), vmem((n, slots, D), BF),
            vmem((2 * experts, lanes), BF),
            sem((chunks,)), sem((chunks,)), sem((n,)), sem((n,)),
        ],
        compiler_params=params(collective_id=1, has_side_effects=True),
        name="dispatch",
    )(part, tok, small, idx)


def expert_kernel(
    n, cap, half, fused,
    first, ct_ref, wi_own, wi_sib, wb_own, wb_sib, bi_own, bi_sib, bb_ref,
    idx_ref, seen_ref, tok_ct, small_ref,
    hg_ref, sg_ref, y_ref, gi_ref, gi_in, gb_ref, gb_in, little_ref, little_in, hid_out, prob_ref,
    wo_ref, qkv_out, att_out, soft_out,
    vi_own, vi_sib, vb_own, vb_sib, g_s, act_own, act_sib, dp_own, dp_sib, dx_s, back, acc, other,
    ct_s, y_s, stage, gp, gp_other, x_ref, send, p2, mine_w, mine_s, info, bias_s, bias_in, soft,
    lsem, ysem, gsem, ss, rs, hs, hr, ms, mr, xs, xr, es, er, zs, zr, ps, pr, cs, cr, bsem,
):
    me, mine = lax.axis_index("dp"), lax.axis_index("mp")
    sibling = {"mp": 1 - mine}
    slots = x_ref.shape[1]
    tok = tok_ct.shape[0]
    tr = up(tok, 16)
    experts = gp.shape[0]
    hidden = wi_own.shape[1]
    group = 4 * slots
    batches = n // 4
    early = n // 2 if fused else n
    lanes = gp.shape[1]
    owns = [(wi_own, vi_own), (wb_own, vb_own)]
    if not fused:
        owns += [(wi_sib, vi_sib), (wb_sib, vb_sib), (first, x_ref)]
    loads = [pltpu.make_async_copy(a, b, lsem.at[i]) for i, (a, b) in enumerate(owns)]
    for c in loads:
        c.start()
    if fused:
        halves = [
            remote(wi_own, vi_sib, ms.at[3], mr.at[3], sibling),
            remote(wb_own, vb_sib, ms.at[4], mr.at[4], sibling),
            remote(bias_s, bias_in, ms.at[5], mr.at[5], sibling),
        ]
        bias_s[...] = jnp.zeros_like(bias_s)
        bias_s[0:1, :] = bi_own[...].astype(F32)

        def started():
            for c in halves:
                c.start()

        arrived, ended = begin_part(
            n, cap, half, slots, [sibling], started, *first,
            wo_ref, small_ref, idx_ref, ct_ref, act_own, act_sib, hg_ref, soft_out,
            None, None, mine_w, mine_s, info, act_sib, D, dp_own, acc, stage, soft, (g_s, other, es, er),
            zs, zr, ps, pr, cs, cr, bsem,
        )
        rows = qkv_out.shape[0]
        kept = [
            pltpu.make_async_copy(act_own.at[pl.ds(0, rows), pl.ds(0, qkv_out.shape[1])], qkv_out, lsem.at[2]),
            pltpu.make_async_copy(act_sib.at[pl.ds(0, rows), pl.ds(0, att_out.shape[1])], att_out, lsem.at[3]),
        ]
        for c in kept:
            c.start()
        send_tokens(
            n, half, early, hg_ref, first[-1], small_ref, idx_ref, hg_ref, dp_sib, prob_ref, x_ref,
            None, None, send, p2, None, None, xs, xr,
        )
        keep = pltpu.make_async_copy(hg_ref, hid_out, lsem.at[5])
        keep.start()
        ended()
        for c in kept:
            c.wait()
        for c in halves:
            c.wait()
        bias_own, bias_sib = bi_own[...].astype(F32), bias_in[0:1, :]
    else:
        greet([sibling] + [{"dp": (me + d) % n} for d in range(1, n)])
        keep = pltpu.make_async_copy(hid_out, hg_ref, lsem.at[5])
        keep.start()
        bias_own, bias_sib = bi_own[...].astype(F32), bi_sib[...].astype(F32)
    little_ref[...] = jnp.zeros_like(little_ref)

    def ct_here(b, j):
        if fused:
            arrived(b * 4 + j)

    def cts(b, j):
        return pltpu.make_async_copy(ct_ref.at[b * 4 + j], ct_s.at[j], ysem.at[0, j])

    def ys(b, j):
        return pltpu.make_async_copy(y_s.at[j], y_ref.at[b * 4 + j], ysem.at[1, j])

    for j in range(4):
        ct_here(0, j)
        cts(0, j).start()
    for c in loads:
        c.wait()
    chunk = 768
    row = lax.broadcasted_iota(jnp.int32, (group, 16), 0)
    number = lax.broadcasted_iota(jnp.int32, (group, 16), 1)
    member = jnp.where(row // slots == number, 1.0, 0.0).astype(BF)
    spot = lax.broadcasted_iota(jnp.int32, (group, 128), 0) % slots
    here = spot == lax.broadcasted_iota(jnp.int32, (group, 128), 1)
    row_t = lax.broadcasted_iota(jnp.int32, (16, group), 1)
    number_t = lax.broadcasted_iota(jnp.int32, (16, group), 0)
    pick = jnp.where(
        (row_t == number_t * slots + half) | (row_t == number_t * slots + half + 1), 1.0, 0.0
    ).astype(BF)
    member_t = jnp.where(row_t // slots == number_t, 1.0, 0.0).astype(BF)
    puts = [jnp.where(row == number * slots + half + i, 1.0, 0.0).astype(BF) for i in range(2)]

    def batch(b, carry):
        at = pl.ds(pl.multiple_of(b * group, 16), group)
        if fused:
            @pl.when(b == batches // 4)
            def _():
                def more(p, carry):
                    token_send(n, send, x_ref, xs, xr, p, partner(me, n, p)).start()
                    return carry

                lax.fori_loop(early, n, more, 0)

            for j in range(4):
                p = b * 4 + j

                @pl.when(p != 0)
                def _():
                    token_send(n, send, x_ref, xs, xr, p, partner(me, n, p)).wait_recv()

        x = x_ref[pl.ds(b * 4, 4)].reshape(group, D)
        high, low = split_two(mm(pick, x[:, 0:128], 1, 0))
        wide = mm(member, high, 1, 0) + mm(member, low, 1, 0)
        gate = jnp.sum(jnp.where(here, wide, 0.0), axis=1, keepdims=True)
        for j in range(4):
            cts(b, j).wait()
        g_s[at, :] = (gate * ct_s[...].reshape(group, D).astype(F32)).astype(BF)
        little_ref[0:1, 2 * hidden :] += jnp.sum(g_s[at, :].astype(F32), axis=0, keepdims=True)
        for part, (vi, vb, bi, acts, dps) in enumerate(
            ((vi_own, vb_own, bias_own, act_own, dp_own), (vi_sib, vb_sib, bias_sib, act_sib, dp_sib))
        ):
            for c in range(hidden // chunk):
                cols = slice(c * chunk, (c + 1) * chunk)
                pre = mm(x_ref[pl.ds(b * 4, 4)].reshape(group, D), vi[:, cols], 1, 0) + bi[:, cols]
                phi = 0.5 * (1.0 + lax.erf(pre * (0.5**0.5)))
                slope = phi + pre * (jnp.exp(-0.5 * pre * pre) * ((2.0 * jnp.pi) ** -0.5))
                acts[at, cols] = (pre * phi).astype(BF)
                grad = (mm(g_s[at, :], vb[cols, :], 1, 1) * slope).astype(BF)
                dps[at, cols] = grad
                place = slice(part * hidden + c * chunk, part * hidden + (c + 1) * chunk)
                little_ref[0:1, place] += jnp.sum(grad.astype(F32), axis=0, keepdims=True)
        dx = mm(dp_own[at, :], vi_own[...], 1, 1) + mm(dp_sib[at, :], vi_sib[...], 1, 1)
        y = mm(act_own[at, :], vb_own[...], 1, 0) + mm(act_sib[at, :], vb_sib[...], 1, 0)
        y = (y + bb_ref[...].astype(F32)).astype(BF).astype(F32)
        dots = jnp.sum(ct_s[...].reshape(group, D).astype(F32) * y, axis=1, keepdims=True)
        high, low = split_two(jnp.where(here, dots, 0.0))
        high, low = mm(member_t, high, 1, 0).astype(BF), mm(member_t, low, 1, 0).astype(BF)
        left = dx[:, 0:128] + mm(puts[0], high, 1, 0) + mm(puts[1], low, 1, 0)
        dx = jnp.concatenate([left, dx[:, 128:]], axis=1)
        dx_s[pl.ds(b * 4, 4)] = dx.astype(BF).reshape(4, slots, D)
        for j in range(4):
            p = b * 4 + j

            @pl.when(p != 0)
            def _():
                remote(dx_s.at[p], back.at[p], ss.at[p], rs.at[p], {"dp": partner(me, n, p, -1)}).start()

        @pl.when(b > 0)
        def _():
            for j in range(4):
                ys(b - 1, j).wait()

        y_s[...] = (gate * y).astype(BF).reshape(4, slots, D)
        for j in range(4):
            ys(b, j).start()

        @pl.when(b + 1 < batches)
        def _():
            for j in range(4):
                ct_here(b + 1, j)
                cts(b + 1, j).start()

        return carry

    lax.fori_loop(0, batches, batch, 0)
    back[0] = dx_s[0]
    little = remote(little_ref, little_in, ms.at[2], mr.at[2], sibling)
    little.start()

    rows_all = n * slots
    steps = 3
    size = D // steps
    wide = hidden // 2
    swaps = []

    def out_i(r, c):
        return pltpu.make_async_copy(
            stage.at[r % 2 * 2 * size + c * size : r % 2 * 2 * size + (c + 1) * size, :],
            gi_ref.at[r * size : (r + 1) * size, c * wide : (c + 1) * wide], gsem.at[c, r],
        )

    def out_b(r):
        return pltpu.make_async_copy(
            stage.at[r % 2 * 2 * size : (r % 2 + 1) * 2 * size, :], gb_ref.at[r * 2 * size : (r + 1) * 2 * size, :], gsem.at[2, r]
        )

    for r in range(steps):
        at = slice(r * size, (r + 1) * size)
        left = x_ref[:, :, at].reshape(rows_all, size)
        vi_sib[at, :] = mm(left, dp_sib[...], 0, 0).astype(BF)
        for c in range(2):
            if r >= 2:
                out_i(r - 2, c).wait()
            at_s = r % 2 * 2 * size + c * size
            stage[at_s : at_s + size, :] = mm(left, dp_own[:, c * wide : (c + 1) * wide], 0, 0)
            out_i(r, c).start()
    copy = remote(vi_sib, gi_in, ms.at[0], mr.at[0], sibling)
    copy.start()
    swaps.append(copy)

    acc[...] = jnp.zeros_like(acc)
    gp[...] = jnp.zeros_like(gp)
    place = lax.broadcasted_iota(jnp.int32, (slots, 128), 0)
    count = lax.broadcasted_iota(jnp.int32, (experts, slots), 0)

    def combine(b, carry):
        hot = []
        for j in range(4):
            d = b * 4 + j
            source = partner(me, n, d)

            @pl.when(d != 0)
            def _():
                remote(dx_s.at[d], back.at[d], ss.at[d], rs.at[d], {"dp": source}).wait_recv()

            hot.append(slot_matrix(idx_ref, source * slots, slots))
            extra = back[d, :, 0:128].astype(F32)
            high = jnp.sum(jnp.where(place == half, extra, 0.0), axis=0, keepdims=True)[:, 0:slots]
            low = jnp.sum(jnp.where(place == half + 1, extra, 0.0), axis=0, keepdims=True)[:, 0:slots]
            for value in (high, low):
                gp[...] += mm(jnp.where(count == source, value, 0.0).astype(BF), hot[j], 1, 0)
        block = back[pl.ds(b * 4, 4)].reshape(group, D)
        acc[0:lanes, :] += mm(jnp.concatenate(hot, axis=0), block, 0, 0)
        return carry

    lax.fori_loop(0, batches // 2, combine, 0)
    for r in range(steps):
        at = slice(r * 2 * size, (r + 1) * 2 * size)
        vb_sib[at, :] = mm(act_sib[:, at], g_s[...], 0, 0).astype(BF)
        if r == 0:
            for c in range(2):
                out_i(1, c).wait()
                out_i(2, c).wait()
        if r >= 2:
            out_b(r - 2).wait()
        stage[r % 2 * 2 * size : (r % 2 + 1) * 2 * size, :] = mm(act_own[:, at], g_s[...], 0, 0)
        out_b(r).start()
    copy = remote(vb_sib, gb_in, ms.at[1], mr.at[1], sibling)
    copy.start()
    swaps.append(copy)
    lax.fori_loop(batches // 2, batches, combine, 0)

    little.wait()
    copies = []
    own = g_s
    own[tr - 16 : tr, :] = jnp.zeros((16, D), BF)
    for c, (start, length) in enumerate(row_chunks(tr)):
        stop = min(start + length, tok)
        own[start:stop, :] = acc[start:stop, :].astype(BF)
        rows = pl.ds(start, length)
        copy = remote(own.at[rows, :], other.at[rows, :], hs.at[c], hr.at[c], sibling)
        copy.start()
        copies.append(copy)
    copy = remote(gp, gp_other, hs.at[len(copies)], hr.at[len(copies)], sibling)
    copy.start()
    copy.wait()
    probs = prob_ref[...] if fused else seen_ref[...]
    grad_probs = gp[...] + gp_other[...]
    logits = (probs * (grad_probs - jnp.sum(grad_probs * probs, axis=0, keepdims=True))).astype(BF)
    gains = jnp.transpose(small_ref[...].astype(F32))
    gain = gains[experts + 1 : experts + 2, :]
    acc[0:lanes, :] = mm(logits, gains[0:experts, :].astype(BF), 0, 0)
    sg_ref[...] = jnp.zeros_like(sg_ref)
    gain_sum = jnp.zeros((1, D), F32)
    bias_sum = jnp.zeros((1, D), F32)
    act_own[lanes - 64 : lanes, 0:D] = jnp.zeros((64, D), BF)
    keep.wait()
    for c, (start, length) in enumerate(row_chunks(tr)):
        stop = min(start + length, tok)
        copies[c].wait_recv()
        grad = own[start:stop, :].astype(F32) + other[start:stop, :].astype(F32) + acc[start:stop, :]
        xhat, inverse = norm_rows(hg_ref[start:stop, :])
        act_own[start:stop, 0:D] = (xhat * gain).astype(BF)
        hidden_grad = tok_ct[start:stop, :].astype(F32) + norm_back(grad, gain, xhat, inverse)
        hg_ref[start:stop, :] = hidden_grad
        gain_sum += jnp.sum(grad * xhat, axis=0, keepdims=True)
        bias_sum += jnp.sum(hidden_grad, axis=0, keepdims=True)
    sg_ref[0:experts, :] = mm(logits, act_own[0:lanes, 0:D], 1, 0)
    sg_ref[experts : experts + 1, :] = gain_sum
    sg_ref[experts + 1 : experts + 2, :] = bias_sum
    for copy in copies:
        copy.wait_send()

    def finish(p, carry):
        @pl.when(p != 0)
        def _():
            remote(dx_s.at[p], back.at[p], ss.at[p], rs.at[p], {"dp": partner(me, n, p, -1)}).wait_send()
            if fused:
                token_send(n, send, x_ref, xs, xr, p, partner(me, n, p)).wait_send()

        return carry

    lax.fori_loop(0, n, finish, 0)
    for j in range(4):
        ys(batches - 1, j).wait()
    for r in range(1, steps):
        out_b(r).wait()
    for copy in swaps:
        copy.wait()


def expert(first, ct_rows, wi, wb, bi, bb, idx, probs, hid, ct, small, n, cap, half, slots):
    fused = hid is None
    rows = n * slots
    hidden = wi[0].shape[1]
    lanes = up(ct.shape[0], 128)
    experts = n
    tr = up(ct.shape[0], 16)
    chunks = len(row_chunks(tr))
    flat = ct.shape[0] // SEQ * SEQ_PAD
    shape = jax.ShapeDtypeStruct
    sem = pltpu.SemaphoreType.DMA
    vmem = pltpu.VMEM
    far = pl.BlockSpec(memory_space=pl.ANY)
    outs = [
        shape(ct.shape, F32), shape((up(experts + 3, 8), D), F32), shape((n, slots, D), BF),
        shape((D, hidden), F32), shape((D, hidden), BF),
        shape((hidden, D), F32), shape((hidden, D), BF),
        shape((8, 2 * hidden + D), F32), shape((8, 2 * hidden + D), F32),
    ]
    out_specs = [whole(), whole(), far, far, far, far, far, whole(), whole()]
    if fused:
        wq, wout, router_t, gains, rt, rank, tok = first
        shard, width = wout.shape
        plane = n // LINE
        ins = [wq, wout, router_t, *gains, rt, rank, ct, tok, wi[0], wb[0], bi[0], bb]
        in_specs = [whole()] * 10 + [far, far, whole(), whole()]
        outs += [
            shape(ct.shape, F32), shape((experts, lanes), F32), shape((4, D, width), BF), shape((D, 128), BF),
            shape((2, lanes), jnp.int32), shape((n, slots, D), BF),
            shape((flat, 3 * width), BF), shape((flat, width), BF),
            shape((flat // SEQ_PAD, width // HD, SEQ_PAD, SEQ_PAD), F32),
        ]
        out_specs += [far, whole(), whole(), whole(), whole(), far, far, far, far]

        def kernel(*refs):
            wq, wout, rows_t, g1, g2, g3, rt, rank, ct, tok, wi, wb, bi, bb = refs[:14]
            main, (hid, prob, wo, so, idx, ctx, qkv, att, soft) = refs[14:23], refs[23:32]
            expert_kernel(
                n, cap, half, True, (wq, wout, rows_t, (g1, g2, g3), rt, rank, ct, tok),
                ctx, wi, None, wb, None, bi, None, bb, idx, None, ct, so,
                *main, hid, prob, wo, qkv, att, soft, *refs[32:],
            )

        spare = [vmem((4, shard, width), BF), vmem((shard, 128), BF), vmem((8, lanes), jnp.int32)]
        spare += [vmem((8, hidden), F32)] * 2 + [vmem((2, width // HD, SEQ_PAD, SEQ_PAD), F32)]
        grid = (plane - 1, LINE, 2)
        send_rows = (n, slots, D)
    else:
        ins = [first, ct_rows, wi[0], wi[1], wb[0], wb[1], bi[0], bi[1], bb, idx, probs, ct, small, hid]
        in_specs = [far] * 6 + [whole()] * 7 + [far]

        def kernel(*refs):
            ins, hid_ref, outs, rest = refs[:13], refs[13], refs[14:23], refs[23:]
            expert_kernel(n, cap, half, False, *ins, *outs, hid_ref, ins[10], None, None, None, None, *rest)

        spare = [vmem((1, 16, 128), BF), vmem((16, 128), BF), vmem((8, 128), jnp.int32)]
        spare += [vmem((8, 128), F32)] * 3
        grid = (1, 1, 2)
        send_rows = (1, 16, 128)

    return pl.pallas_call(
        kernel,
        out_shape=tuple(outs),
        in_specs=in_specs,
        out_specs=tuple(out_specs),
        scratch_shapes=[
            vmem((D, hidden), BF), vmem((D, hidden), BF), vmem((hidden, D), BF), vmem((hidden, D), BF),
            vmem((rows, D), BF),
            vmem((rows, hidden), BF), vmem((rows, hidden), BF),
            vmem((rows, hidden), BF), vmem((rows, hidden), BF),
            vmem((n, slots, D), BF), vmem((n, slots, D), BF),
            vmem((flat if fused else lanes, D), F32), vmem((flat if fused else tr, D), BF),
            vmem((4, slots, D), BF), vmem((4, slots, D), BF),
            vmem((flat if fused else 1024, D), F32),
            vmem((experts, lanes), F32), vmem((experts, lanes), F32),
            vmem((n, slots, D), BF), vmem(send_rows, BF), vmem((2 * experts, lanes), BF),
            *spare,
            sem((6,)), sem((2, 4)), sem((3, 3)), sem((n,)), sem((n,)),
            sem((chunks + 1,)), sem((chunks + 1,)), sem((6,)), sem((6,)),
            sem((n,)), sem((n,)), sem((flat // SEQ_PAD,)), sem((flat // SEQ_PAD,)),
            sem((LINE - 1, 2)), sem((LINE - 1, 2)), sem(grid), sem(grid), sem((n,)), sem((n,)), sem((3,)),
        ],
        compiler_params=params(collective_id=2, has_side_effects=True),
        name="expert",
    )(*ins)


def join_kernel(
    gi_ref, gi_in, gb_ref, gb_in, little_ref, little_in, gw_ref, gs_ref,
    gi_out, gb_out, gbi_out, gbb_out, gq_out, go_out, gr_out, g1_out, g2_out, g3_out,
):
    gi_out[...] = gi_ref[...] + gi_in[...].astype(F32)
    gb_out[...] = gb_ref[...] + gb_in[...].astype(F32)

    @pl.when(pl.program_id(0) == 0)
    def _():
        hidden = gbi_out.shape[1]
        shard = go_out.shape[0]
        experts = gr_out.shape[0]
        gbi_out[...] = little_ref[0:1, 0:hidden] + little_in[0:1, hidden : 2 * hidden]
        gbb_out[...] = little_ref[0:1, 2 * hidden :] + little_in[0:1, 2 * hidden :]
        gq_out[...] = gw_ref[0:3, 0:shard, :]
        go_out[...] = gw_ref[3, 0:shard, :]
        turned = jnp.transpose(gs_ref[...])
        gr_out[...] = turned[0:experts, 0:shard]
        for k, out in enumerate((g2_out, g3_out, g1_out)):
            out[...] = turned[experts + k : experts + k + 1, 0:shard]


def join(gi, gi_in, gb, gb_in, little, little_in, gw, gs, shard, experts):
    steps = 6
    width = gw.shape[2]
    hidden = gi.shape[1]
    line_i = pl.BlockSpec((gi.shape[0] // steps, hidden), lambda k: (k, 0))
    line_b = pl.BlockSpec((hidden // steps, D), lambda k: (k, 0))
    shape = jax.ShapeDtypeStruct
    return pl.pallas_call(
        join_kernel,
        grid=(steps,),
        out_shape=(shape(gi.shape, F32), shape(gb.shape, F32), shape((1, hidden), F32), shape((1, D), F32),
                   shape((3, shard, width), F32), shape((shard, width), F32), shape((experts, shard), F32),
                   *[shape((1, shard), F32)] * 3),
        in_specs=[line_i, line_i, line_b, line_b] + [whole()] * 4,
        out_specs=(line_i, line_b) + (whole(),) * 8,
        compiler_params=params(dimension_semantics=("arbitrary",)),
        name="join",
    )(gi, gi_in, gb, gb_in, little, little_in, gw, gs)


def end_kernel(
    n, experts, shard,
    hg_ref, tok_ref, w_ref, qkv_ref, att_ref, soft_ref, y_ref, hid_ref, small_ref, idx_ref, sg_ref,
    tg_ref, out_ref, gw_ref, gs_ref,
    hg_s, tok_s, w_s, qkv_s, att_s, hid_s, normed, low, dqkv, pp, flat, dn, other, mix, mix_other,
    y_s, acc, soft, dw, r1, s1, r2, sm, q1, t1, q2,
    lsem, us, ur, hs, hr, as_, ar, bs, br,
):
    me, mine = lax.axis_index("dp"), lax.axis_index("mp")
    plane = n // LINE
    z, q = me // plane, me % plane
    tok = tok_s.shape[0]
    images = tok // SEQ
    width = w_s.shape[2]
    rp = dw.shape[3]
    tr = other.shape[0]
    slots = y_s.shape[1]
    scale = HD ** (-0.5)
    sibling = {"mp": 1 - mine}
    zpeer = [((z + d) % LINE) * plane + q for d in range(1, LINE)]
    qpeer = [z * plane + (q + d) % plane for d in range(1, plane)]
    loads = [
        pltpu.make_async_copy(a, b, lsem.at[i])
        for i, (a, b) in enumerate(
            ((hg_ref, hg_s), (tok_ref, tok_s), (w_ref, w_s), (qkv_ref, qkv_s), (att_ref, att_s), (hid_ref, hid_s),
             (y_ref.at[0], y_s.at[0]))
        )
    ]
    for c in loads:
        c.start()
    greet([sibling] + [{"dp": (me + d) % n} for d in range(1, n)])

    def y_copy(p, sign):
        return remote(y_ref.at[p], y_s.at[p], us.at[p], ur.at[p], {"dp": partner(me, n, p, sign)})

    def y_start(p, carry):
        y_copy(p, -1).start()
        return carry

    lax.fori_loop(1, n, y_start, 0)
    loads[0].wait()
    for i in range(images):
        pp[(i + 1) * SEQ_PAD - 16 : (i + 1) * SEQ_PAD, :] = jnp.zeros((16, D), F32)
        pp[i * SEQ_PAD : i * SEQ_PAD + SEQ, :] = hg_s[i * SEQ : (i + 1) * SEQ, :]
    low[...] = pp[...].astype(BF)
    loads[1].wait()
    for i in range(images):
        pp[i * SEQ_PAD : i * SEQ_PAD + SEQ, :] = tok_s[i * SEQ : (i + 1) * SEQ, :].astype(F32)
    for c in loads[2:5]:
        c.wait()

    def spread(value):
        value = value.astype(BF)
        if rp > shard:
            line = lax.broadcasted_iota(jnp.int32, (n * rp, D), 0)
            where = lax.broadcasted_iota(jnp.int32, (n * rp, D), 1)
            fits = (where == line // rp * shard + line % rp) & (line % rp < shard)
            value = mm(jnp.where(fits, 1.0, 0.0).astype(BF), value, 1, 0).astype(BF)
        return value.reshape(LINE, plane, rp, width)

    sends = []

    def plane_send(k, a, b):
        for d, p in enumerate(qpeer):
            to = (q + d + 1) % plane
            c = remote(a(to), b(d), as_.at[d, k], ar.at[d, k], {"dp": p})
            c.start()
            sends.append(c)

    def line_send(k, a, b):
        for d, p in enumerate(zpeer):
            c = remote(a((z + d + 1) % LINE), b(d), bs.at[d, k], br.at[d, k], {"dp": p})
            c.start()
            sends.append(c)

    def settle(part, k):
        for d in range(plane - 1):
            remote(dw.at[part, :, 0], r1.at[d, part], as_.at[d, k], ar.at[d, k], {"dp": qpeer[0]}).wait_recv()
        for b in range(LINE):
            value = dw[part, b, q].astype(F32)
            for d in range(plane - 1):
                value += r1[d, part, b].astype(F32)
            s1[part, b] = value.astype(BF)
        line_send(part, lambda to: s1.at[part, to], lambda d: r2.at[d, part])

    dw[3] = spread(mm(low[...], att_s[...], 0, 0))
    plane_send(0, lambda to: dw.at[3, :, to], lambda d: r1.at[d, 3])
    gains = jnp.transpose(small_ref[...].astype(F32))
    gain = gains[experts : experts + 1, :]
    lane = lax.broadcasted_iota(jnp.int32, (1, 2 * HD), 1)
    masks = [jnp.where(lane // HD == h, 1.0, 0.0).astype(BF) for h in range(2)]

    def fetch(i):
        return pltpu.make_async_copy(soft_ref.at[i], soft.at[i % 2], lsem.at[7 + i % 2])

    fetch(0).start()

    def image(i, carry):
        rows = pl.ds(pl.multiple_of(i * SEQ_PAD, 16), SEQ_PAD)
        fetch(i).wait()

        @pl.when(i + 1 < images)
        def _():
            fetch(i + 1).start()

        xhat, _ = norm_rows(pp[rows, :])
        normed[rows, :] = (xhat * gain).astype(BF)
        grad_att = mm(low[rows, :], w_s[3], 1, 0).astype(BF)
        for p in range(width // (2 * HD)):
            cols = [slice(c * width + p * 2 * HD, c * width + (p + 1) * 2 * HD) for c in range(3)]
            qs, ks, vs = (qkv_s[rows, c] for c in cols)
            pair = grad_att[:, p * 2 * HD : (p + 1) * 2 * HD]
            grads = []
            for h in range(2):
                weights = soft[i % 2, 2 * p + h]
                product = mm(pair * masks[h], vs, 1, 1) * weights
                grad_scores = product - weights * jnp.sum(product, axis=-1, keepdims=True)
                scores_low = grad_scores.astype(BF)
                grads.append((
                    mm(scores_low, ks, 1, 0) * scale,
                    mm(scores_low, qs, 0, 0) * scale,
                    mm(weights.astype(BF), pair, 0, 0),
                ))
            for c in range(3):
                dqkv[rows, cols[c]] = jnp.where(lane < HD, grads[0][c], grads[1][c]).astype(BF)
        total = mm(dqkv[rows, 0:width], w_s[0], 1, 1)
        for c in range(1, 3):
            total += mm(dqkv[rows, c * width : (c + 1) * width], w_s[c], 1, 1)
        pp[rows, :] = total
        return carry

    lax.fori_loop(0, images, image, 0)
    for c in range(3):
        dw[c] = spread(mm(normed[...], dqkv[:, c * width : (c + 1) * width], 0, 0))
        plane_send(1 + c, lambda to: dw.at[c, :, to], lambda d: r1.at[d, c])
    for i in range(images):
        flat[i * SEQ : (i + 1) * SEQ, :] = pp[i * SEQ_PAD : i * SEQ_PAD + SEQ, :]
    dn[tr - 16 : tr, :] = jnp.zeros((16, D), BF)
    copies = []
    for c, (start, size) in enumerate(row_chunks(tr)):
        stop = min(start + size, tok)
        dn[start:stop, :] = flat[start:stop, :].astype(BF)
        rows = pl.ds(start, size)
        copy = remote(dn.at[rows, :], other.at[rows, :], hs.at[c], hr.at[c], sibling)
        copy.start()
        copies.append(copy)
    settle(3, 0)
    gain_sum = jnp.zeros((1, D), F32)
    for c, (start, size) in enumerate(row_chunks(tr)):
        stop = min(start + size, tok)
        copies[c].wait()
        grad = dn[start:stop, :].astype(F32) + other[start:stop, :].astype(F32)
        xhat, inverse = norm_rows(tok_s[start:stop, :].astype(F32))
        tg_ref[start:stop, :] = (hg_s[start:stop, :] + norm_back(grad, gain, xhat, inverse)).astype(BF)
        gain_sum += jnp.sum(grad * xhat, axis=0, keepdims=True)
    settle(0, 1)
    row = lax.broadcasted_iota(jnp.int32, sg_ref.shape, 0)
    rows = jnp.where(row == experts + 2, gain_sum, sg_ref[...])
    rows = jnp.concatenate([rows, jnp.zeros((128 - rows.shape[0], D), F32)], axis=0)
    turned = jnp.transpose(rows).astype(BF)
    for b in range(n):
        at = (b // plane, b % plane)
        if shard < rp:
            sm[at[0], at[1]] = jnp.zeros((rp, 128), BF)
        sm[at[0], at[1], 0:shard, :] = turned[b * shard : (b + 1) * shard, :]
    plane_send(4, lambda to: sm.at[:, to], lambda d: q1.at[d])
    settle(1, 2)
    acc[...] = jnp.zeros_like(acc)
    loads[6].wait()

    def step(b, carry):
        for j in range(4):
            p = b * 4 + j

            @pl.when(p != 0)
            def _():
                y_copy(p, 1).wait_recv()

        hot = jnp.concatenate(
            [slot_matrix(idx_ref, partner(me, n, b * 4 + j) * slots, slots) for j in range(4)], axis=0
        )
        acc[...] += mm(hot, y_s[pl.ds(b * 4, 4)].reshape(4 * slots, D), 0, 0)
        return carry

    lax.fori_loop(0, n // 4, step, 0)
    mix[tr - 16 : tr, :] = jnp.zeros((16, D), BF)
    base = len(copies)
    late = []
    for c, (start, size) in enumerate(row_chunks(tr)):
        stop = min(start + size, tok)
        mix[start:stop, :] = acc[start:stop, :].astype(BF)
        rows = pl.ds(start, size)
        copy = remote(mix.at[rows, :], mix_other.at[rows, :], hs.at[base + c], hr.at[base + c], sibling)
        copy.start()
        late.append(copy)
    settle(2, 3)
    for d in range(plane - 1):
        remote(sm.at[:, 0], q1.at[d], as_.at[d, 4], ar.at[d, 4], {"dp": qpeer[0]}).wait_recv()
    for b in range(LINE):
        little = sm[b, q].astype(F32)
        for d in range(plane - 1):
            little += q1[d, b].astype(F32)
        t1[b] = little.astype(BF)
    line_send(4, lambda to: t1.at[to], lambda d: q2.at[d])
    loads[5].wait()
    for c, (start, size) in enumerate(row_chunks(tr)):
        stop = min(start + size, tok)
        late[c].wait()
        both = mix[start:stop, :].astype(F32) + mix_other[start:stop, :].astype(F32)
        out_ref[start:stop, :] = (hid_s[start:stop, :] + both).astype(BF)
    for part in (3, 0, 1, 2):
        value = s1[part, z].astype(F32)
        for d in range(LINE - 1):
            remote(s1.at[0, 0], r2.at[d, part], bs.at[d, part], br.at[d, part], {"dp": zpeer[0]}).wait_recv()
            value += r2[d, part].astype(F32)
        gw_ref[part] = value
    little = t1[z].astype(F32)
    for d in range(LINE - 1):
        remote(t1.at[0], q2.at[d], bs.at[d, 4], br.at[d, 4], {"dp": zpeer[0]}).wait_recv()
        little += q2[d].astype(F32)
    gs_ref[...] = little
    for c in sends:
        c.wait_send()

    def y_end(p, carry):
        y_copy(p, -1).wait_send()
        return carry

    lax.fori_loop(1, n, y_end, 0)


def end(hg, tok, w, qkv, att, soft, y, hid, small, idx, sg, n, experts):
    parts, _, width = w.shape
    shard = D // n
    rp = up(shard, 16)
    plane = n // LINE
    tr = up(tok.shape[0], 16)
    chunks = len(row_chunks(tr))
    rows = qkv.shape[0]
    sem = pltpu.SemaphoreType.DMA
    vmem = pltpu.VMEM
    shape = jax.ShapeDtypeStruct
    far = pl.BlockSpec(memory_space=pl.ANY)
    return pl.pallas_call(
        functools.partial(end_kernel, n, experts, shard),
        out_shape=(
            shape(tok.shape, BF), shape(tok.shape, BF), shape((parts, rp, width), F32), shape((rp, 128), F32),
        ),
        in_specs=[far] * 8 + [whole()] * 3,
        out_specs=(whole(),) * 4,
        scratch_shapes=[
            vmem(tok.shape, F32), vmem(tok.shape, BF), vmem(w.shape, BF), vmem(qkv.shape, BF), vmem(att.shape, BF),
            vmem(tok.shape, F32),
            vmem((rows, D), BF), vmem((rows, D), BF), vmem(qkv.shape, BF), vmem((rows, D), F32), vmem((tr, D), F32),
            vmem((tr, D), BF), vmem((tr, D), BF), vmem((tr, D), BF), vmem((tr, D), BF),
            vmem(y.shape, BF), vmem((idx.shape[1], D), F32),
            vmem((2,) + soft.shape[1:], F32),
            vmem((parts, LINE, plane, rp, width), BF),
            vmem((plane - 1, parts, LINE, rp, width), BF),
            vmem((parts, LINE, rp, width), BF),
            vmem((LINE - 1, parts, rp, width), BF),
            vmem((LINE, plane, rp, 128), BF),
            vmem((plane - 1, LINE, rp, 128), BF),
            vmem((LINE, rp, 128), BF),
            vmem((LINE - 1, rp, 128), BF),
            sem((9,)), sem((n,)), sem((n,)), sem((2 * chunks,)), sem((2 * chunks,)),
            sem((plane - 1, 5)), sem((plane - 1, 5)), sem((LINE - 1, 5)), sem((LINE - 1, 5)),
        ],
        compiler_params=params(collective_id=3, has_side_effects=True),
        name="end",
    )(hg, tok, w, qkv, att, soft, y, hid, small, idx, sg)


def body(
    tokens, ln1_gain, w_qkv, w_out, out_bias, ln2_gain, router, w_in, in_bias,
    w_back, back_bias, routes, priority, cotangent,
):
    n = lax.axis_size("dp")
    tok = tokens.shape[0]
    experts = router.shape[1]
    cap = max(2, 5 * tok // (2 * experts))
    half = (cap + 1) // 2
    slots = up(half + FREE, 16)
    shard, width = w_qkv.shape[0], w_qkv.shape[2]
    rp = up(shard, 16)
    swap = [(0, 1), (1, 0)]

    start = (
        jnp.swapaxes(w_qkv, 0, 1), w_out.T, router.T,
        (ln1_gain[None], ln2_gain[None], out_bias[None]), routes.T, priority,
    )
    if n * slots <= 1536:
        (hg, sg, y, gi, gi_in, gb, gb_in, little, little_in, hid, _, weights, small, idx, _, qkv, att, soft) = expert(
            (*start, tokens), None, (w_in[0],), (w_back[0],), (in_bias,), back_bias, None, None, None,
            cotangent, None, n, cap, half, slots,
        )
    else:
        wi = (w_in[0], lax.ppermute(w_in[0], "mp", swap))
        wb = (w_back[0], lax.ppermute(w_back[0], "mp", swap))
        bi = (in_bias, lax.ppermute(in_bias, "mp", swap))
        weights, small, idx, ct_rows, qkv, att, part, soft = begin(
            *start, cotangent, tokens, n, experts, cap, half, slots
        )
        hid, probs, x = dispatch(part, tokens, small, idx, n, experts, half, slots)
        hg, sg, y, gi, gi_in, gb, gb_in, little, little_in = expert(
            x, ct_rows, wi, wb, bi, back_bias, idx, probs, hid, cotangent, small, n, cap, half, slots
        )
    tg, out, gw, gs = end(hg, tokens, weights, qkv, att, soft, y, hid, small, idx, sg, n, experts)
    gi, gb, gbi, gbb, gq, go, gr, g1, g2, g3 = join(gi, gi_in, gb, gb_in, little, little_in, gw, gs, shard, experts)
    return (
        out,
        tg,
        g1[0],
        jnp.swapaxes(gq, 0, 1),
        go.T,
        g3[0],
        g2[0],
        gr.T,
        gi[None],
        gbi,
        gb[None],
        gbb,
    )


def solution(mesh):
    return jax.shard_map(
        body,
        mesh=mesh,
        in_specs=(
            P("dp", None),
            P("dp"),
            P("dp", None, "mp"),
            P("mp", "dp"),
            P("dp"),
            P("dp"),
            P("dp", None),
            P("dp", None, "mp"),
            P("dp", "mp"),
            P("dp", "mp", None),
            P("dp", None),
            P("dp", None),
            P("dp", None),
            P("dp", None),
        ),
        out_specs=(
            P("dp", None),
            P("dp", None),
            P("dp"),
            P("dp", None, "mp"),
            P("mp", "dp"),
            P("dp"),
            P("dp"),
            P("dp", None),
            P("dp", None, "mp"),
            P("dp", "mp"),
            P("dp", "mp", None),
            P("dp", None),
        ),
        check_vma=False,
    )
```

```python
import functools

import jax
import jax.numpy as jnp
from jax import lax
from jax.experimental import pallas as pl
from jax.experimental.pallas import tpu as pltpu
from jax.sharding import PartitionSpec as P

D = 768
HD = 64
SEQ = 197
EPS = 1e-06
F32 = jnp.float32
BF = jnp.bfloat16
MESH = pl.DeviceIdType.MESH
VMEM_LIMIT = 62 * 1024 * 1024
LINE = 4
FREE = 3


def up(value, step):
    return (value + step - 1) // step * step


SEQ_PAD = up(SEQ, 16)


def mm(left, right, cl, cr):
    return lax.dot_general(
        left, right, (((cl,), (cr,)), ((), ())), preferred_element_type=F32
    )


def norm_rows(values):
    average = jnp.mean(values, axis=-1, keepdims=True)
    centered = values - average
    inverse = lax.rsqrt(jnp.mean(centered * centered, axis=-1, keepdims=True) + EPS)
    return centered * inverse, inverse


def norm_back(grad, gain, xhat, inverse):
    scaled = grad * gain
    return inverse * (
        scaled
        - jnp.mean(scaled, axis=-1, keepdims=True)
        - xhat * jnp.mean(scaled * xhat, axis=-1, keepdims=True)
    )


def split_two(value):
    high = value.astype(BF)
    return high, (value - high.astype(F32)).astype(BF)


def whole():
    return pl.BlockSpec(memory_space=pltpu.VMEM)


def params(**more):
    return pltpu.CompilerParams(vmem_limit_bytes=VMEM_LIMIT, **more)


def greet(peers):
    barrier = pltpu.get_barrier_semaphore()
    for peer in peers:
        pl.semaphore_signal(barrier, inc=1, device_id=peer, device_id_type=MESH)
    pl.semaphore_wait(barrier, len(peers))


def remote(src, dst, send_sem, recv_sem, peer):
    return pltpu.make_async_remote_copy(
        src_ref=src, dst_ref=dst, send_sem=send_sem, recv_sem=recv_sem,
        device_id=peer, device_id_type=MESH,
    )


def partner(me, n, place, sign=1):
    plane = n // LINE
    groups = plane // 4
    z, q = me // plane, me % plane
    step, j = place // 4, place % 4
    turn, g = step // groups, step % groups
    k = turn % 2 * 2 + turn // 2
    line = (z // 2 + k // 2) % 2 * 2 + (z % 2 + k % 2) % 2
    return line * plane + (q + plane + sign * (g * 4 + j)) % plane


def slot_matrix(idx_ref, first, rows):
    number = lax.broadcasted_iota(jnp.int32, (rows, idx_ref.shape[1]), 0) + first
    hit = (number == idx_ref[0:1, :]) | (number == idx_ref[1:2, :])
    return jnp.where(hit, 1.0, 0.0).astype(BF)


def begin_part(
    n, cap, half, slots, more_peers, started,
    wq_ref, wout_ref, rows_ref, gain_refs, rt_ref, rank_ref, ct_ref, tok_ref,
    wo_ref, so_ref, idx_ref, ctx_ref, qkv_ref, att_ref, part_ref, soft_ref,
    gw, gs, mine_w, mine_s, info, ctp, cc, send, xp, pp, soft, early_sum,
    zs, zr, ps, pr, cs, cr, lsem,
):
    me, mine = lax.axis_index("dp"), lax.axis_index("mp")
    plane = n // LINE
    z, q = me // plane, me % plane
    experts, shard = rows_ref.shape
    tok = tok_ref.shape[0]
    lanes = idx_ref.shape[1]
    rp = mine_w.shape[1]
    zpeer = [((z + d) % LINE) * plane + q for d in range(1, LINE)]
    qpeer = [z * plane + (q + d) % plane for d in range(1, plane)]
    full_w, full_s = (wo_ref, so_ref) if rp == shard else (gw, gs)

    if rp > shard:
        mine_w[...] = jnp.zeros_like(mine_w)
    mine_w[0:3, 0:shard, :] = wq_ref[...]
    mine_w[3, 0:shard, :] = wout_ref[...]
    pp[0:128, 0:128] = jnp.zeros((128, 128), F32)
    pp[0:experts, 0:shard] = rows_ref[...].astype(F32)
    for k, gain_ref in enumerate(gain_refs):
        pp[experts + k : experts + k + 1, 0:shard] = gain_ref[...].astype(F32)
    mine_s[...] = jnp.transpose(pp[0:128, 0:128])[0:rp, :].astype(BF)
    greet(more_peers + [{"dp": (me + d) % n} for d in range(1, n)])
    started()

    def at(block):
        rows = pl.ds(pl.multiple_of(block * rp, rp), rp)
        return full_w.at[:, rows, :], full_s.at[rows, :]

    own = at(me)
    sends = []
    for d, p in enumerate(zpeer):
        for i, (a, b) in enumerate(zip((mine_w, mine_s), own)):
            sends.append(remote(a, b, zs.at[d, i], zr.at[d, i], {"dp": p}))
            sends[-1].start()
    for d, p in enumerate(qpeer):
        for i, (a, b) in enumerate(zip((mine_w, mine_s), own)):
            sends.append(remote(a, b, ps.at[d, 0, i], pr.at[d, 0, i], {"dp": p}))
            sends[-1].start()
    here = pl.ds(pl.multiple_of(me * rp, rp), rp)
    full_w[:, here, :] = mine_w[...]
    full_s[here, :] = mine_s[...]

    info[0:2, :] = jnp.full((2, lanes), -1, jnp.int32)
    info[2:3, :] = jnp.full((1, lanes), 1 << 20, jnp.int32)
    info[0:2, 0:tok] = rt_ref[...]
    info[2:3, 0:tok] = rank_ref[...]
    number = lax.broadcasted_iota(jnp.int32, (experts, lanes), 0)
    hot = [jnp.where(number == info[j : j + 1, :], 1.0, 0.0) for j in range(2)]
    ranks = info[2:3, :].astype(F32)
    column = jnp.transpose(jnp.broadcast_to(ranks, (128, lanes)))[:, 0:1]
    before = jnp.where(column < ranks, 1.0, 0.0).astype(BF)
    counts = [mm(h.astype(BF), before, 1, 0) for h in hot]
    counts[1] = counts[1] + jnp.sum(hot[0], axis=1, keepdims=True)
    for j in range(2):
        slot = jnp.sum(counts[j] * hot[j], axis=0, keepdims=True).astype(jnp.int32)
        place = slot - mine * half
        expert_id = info[j : j + 1, :]
        kept = (slot < cap) & (place >= 0) & (place < half) & (expert_id >= 0)
        idx_ref[j : j + 1, :] = jnp.where(kept, expert_id * slots + place, -1)
    ctp[lanes - 64 : lanes, cc : cc + D] = jnp.zeros((64, D), BF)
    ctp[0:tok, cc : cc + D] = ct_ref[...]

    def rows_of(b, carry):
        ones = [slot_matrix(idx_ref, partner(me, n, b * 4 + j) * slots, slots) for j in range(4)]
        block = mm(jnp.concatenate(ones, axis=0), ctp[0:lanes, cc : cc + D], 1, 0).astype(BF)
        send[pl.ds(pl.multiple_of(b * 4 * slots, 16), 4 * slots), 0:D] = block
        return carry

    lax.fori_loop(0, n // 4, rows_of, 0)

    for k in range(1, LINE):
        block = at(((z + LINE - k) % LINE) * plane + q)
        for i in range(2):
            remote(block[i], block[i], zs.at[k - 1, i], zr.at[k - 1, i], {"dp": zpeer[0]}).wait_recv()
        for d, p in enumerate(qpeer):
            for i in range(2):
                sends.append(remote(block[i], block[i], ps.at[d, k, i], pr.at[d, k, i], {"dp": p}))
                sends[-1].start()

    def block_of(p):
        return send.at[pl.ds(pl.multiple_of(p * slots, 16), slots), pl.ds(0, D)]

    local = pltpu.make_async_copy(block_of(0), ctx_ref.at[0], lsem.at[0])
    local.start()

    def ship(p, carry):
        @pl.when(p != 0)
        def _():
            remote(block_of(p), ctx_ref.at[p], cs.at[p], cr.at[p], {"dp": partner(me, n, p)}).start()

        return carry

    lax.fori_loop(1, n, ship, 0)

    images = tok // SEQ
    width = wo_ref.shape[2]
    scale = HD ** (-0.5)
    for i in range(images):
        xp[(i + 1) * SEQ_PAD - 16 : (i + 1) * SEQ_PAD, :] = jnp.zeros((16, D), F32)
        xp[i * SEQ_PAD : i * SEQ_PAD + SEQ, :] = tok_ref[i * SEQ : (i + 1) * SEQ, :].astype(F32)

    def norm(i, carry):
        rows = pl.ds(pl.multiple_of(i * SEQ_PAD, 16), SEQ_PAD)
        xhat, _ = norm_rows(xp[rows, :])
        xp[rows, :] = xhat
        return carry

    lax.fori_loop(0, images, norm, 0)
    for d in range(1, plane):
        for k in range(LINE):
            block = at(((z + LINE - k) % LINE) * plane + (q + plane - d) % plane)
            for i in range(2):
                remote(block[i], block[i], ps.at[d - 1, k, i], pr.at[d - 1, k, i], {"dp": qpeer[0]}).wait_recv()
    if rp > shard:
        line = lax.broadcasted_iota(jnp.int32, (D, n * rp), 0)
        where = lax.broadcasted_iota(jnp.int32, (D, n * rp), 1)
        squeeze = jnp.where(where == line // shard * rp + line % shard, 1.0, 0.0).astype(BF)
        for c in range(4):
            wo_ref[c] = mm(squeeze, gw[c], 1, 0).astype(BF)
        so_ref[...] = mm(squeeze, gs[...], 1, 0).astype(BF)
    gain = jnp.transpose(so_ref[...].astype(F32))[experts : experts + 1, :]
    lane = lax.broadcasted_iota(jnp.int32, (1, 2 * HD), 1)
    masks = [jnp.where(lane // HD == h, scale, 0.0).astype(BF) for h in range(2)]
    valid = lax.broadcasted_iota(jnp.int32, (1, SEQ_PAD), 1) < SEQ

    def keep(i):
        return pltpu.make_async_copy(soft.at[i % 2], soft_ref.at[i], lsem.at[1 + i % 2])

    def image(i, carry):
        @pl.when(i >= 2)
        def _():
            keep(i - 2).wait()

        rows = pl.ds(pl.multiple_of(i * SEQ_PAD, 16), SEQ_PAD)
        normed = (xp[rows, :] * gain).astype(BF)
        for c in range(3):
            qkv_ref[rows, c * width : (c + 1) * width] = mm(normed, wo_ref[c], 1, 0).astype(BF)
        for p in range(width // (2 * HD)):
            cols = slice(p * 2 * HD, (p + 1) * 2 * HD)
            qs, ks, vs = (
                qkv_ref[rows, c * width + p * 2 * HD : c * width + (p + 1) * 2 * HD] for c in range(3)
            )
            outs = []
            for h in range(2):
                scores = jnp.where(valid, mm(qs * masks[h], ks, 1, 1), -1e30)
                raised = jnp.exp(scores - jnp.max(scores, axis=-1, keepdims=True))
                weights = raised * (1.0 / jnp.sum(raised, axis=-1, keepdims=True))
                soft[i % 2, 2 * p + h] = weights
                outs.append(mm(weights.astype(BF), vs, 1, 0))
            att_ref[rows, cols] = jnp.where(lane < HD, outs[0], outs[1]).astype(BF)
        partial = mm(att_ref[rows, 0:width], wo_ref[3], 1, 1)
        if early_sum is None:
            pp[rows, :] = partial
        else:
            early_sum[0][rows, :] = partial.astype(BF)
            early_copy(i).start()
        keep(i).start()
        return carry

    def early_copy(i):
        own, other, es, er = early_sum
        rows = pl.ds(pl.multiple_of(i * SEQ_PAD, 16), SEQ_PAD)
        return remote(own.at[rows, :], other.at[rows, :], es.at[i], er.at[i], {"mp": 1 - mine})

    lax.fori_loop(0, images, image, 0)
    for i in range(images):
        rows = slice(i * SEQ_PAD, i * SEQ_PAD + SEQ)
        if early_sum is None:
            total = pp[rows, :]
        else:
            early_copy(i).wait()
            total = early_sum[0][rows, :].astype(F32) + early_sum[1][rows, :].astype(F32)
        part_ref[i * SEQ : (i + 1) * SEQ, :] = total

    def arrived(p):
        @pl.when(p != 0)
        def _():
            remote(block_of(p), ctx_ref.at[p], cs.at[p], cr.at[p], {"dp": partner(me, n, p)}).wait_recv()

    def ended():
        for c in sends:
            c.wait_send()
        local.wait()
        for i in range(max(0, images - 2), images):
            keep(i).wait()

        def sent(p, carry):
            @pl.when(p != 0)
            def _():
                remote(block_of(p), ctx_ref.at[p], cs.at[p], cr.at[p], {"dp": partner(me, n, p)}).wait_send()

            return carry

        lax.fori_loop(0, n, sent, 0)

    return arrived, ended


def begin_kernel(n, cap, half, slots, *refs):
    arrived, ended = begin_part(n, cap, half, slots, [], lambda: None, *refs[:22], 0, *refs[22:26], None, *refs[26:])

    def finish(p, carry):
        arrived(p)
        return carry

    lax.fori_loop(0, n, finish, 0)
    ended()


def begin(wq, wout, rows, gains, rt, rank, ct, tok, n, experts, cap, half, slots):
    images = tok.shape[0] // SEQ
    shard, width = wout.shape
    rp = up(shard, 16)
    lanes = up(tok.shape[0], 128)
    plane = n // LINE
    sem = pltpu.SemaphoreType.DMA
    shape = jax.ShapeDtypeStruct
    vmem = pltpu.VMEM
    spare = n * rp if rp > shard else 16

    def kernel(wq_ref, wout_ref, rows_ref, g1, g2, g3, *rest):
        begin_kernel(n, cap, half, slots, wq_ref, wout_ref, rows_ref, (g1, g2, g3), *rest)

    return pl.pallas_call(
        kernel,
        out_shape=(
            shape((4, D, width), BF), shape((D, 128), BF), shape((2, lanes), jnp.int32),
            shape((n, slots, D), BF), shape((images * SEQ_PAD, 3 * width), BF),
            shape((images * SEQ_PAD, width), BF), shape((up(tok.shape[0], 16), D), F32),
            shape((images, width // HD, SEQ_PAD, SEQ_PAD), F32),
        ),
        in_specs=[whole()] * 10,
        out_specs=(whole(), whole(), whole(), pl.BlockSpec(memory_space=pl.ANY), whole(), whole(), whole(),
                   pl.BlockSpec(memory_space=pl.ANY)),
        scratch_shapes=[
            vmem((4, spare, width), BF), vmem((spare, 128), BF),
            vmem((4, rp, width), BF), vmem((rp, 128), BF), vmem((8, lanes), jnp.int32),
            vmem((lanes, D), BF), vmem((n * slots, D), BF),
            vmem((images * SEQ_PAD, D), F32), vmem((images * SEQ_PAD, D), F32),
            vmem((2, width // HD, SEQ_PAD, SEQ_PAD), F32),
            sem((LINE - 1, 2)), sem((LINE - 1, 2)),
            sem((plane - 1, LINE, 2)), sem((plane - 1, LINE, 2)),
            sem((n,)), sem((n,)), sem((1,)),
        ],
        compiler_params=params(collective_id=0, has_side_effects=True),
        name="begin",
    )(wq, wout, rows, *gains, rt, rank, ct, tok)


def row_chunks(rows):
    return [(s, min(256, rows - s)) for s in range(0, rows, 256)]


def token_send(n, send, x_ref, xs, xr, p, peer):
    return remote(send.at[p], x_ref.at[p], xs.at[p], xr.at[p], {"dp": peer})


def send_tokens(
    n, half, early, part_ref, tok_ref, small_ref, idx_ref, hid_ref, n2, prob_ref, x_ref,
    own, other, send, p2, hs, hr, xs, xr,
):
    me, mine = lax.axis_index("dp"), lax.axis_index("mp")
    plane = n // LINE
    tok = tok_ref.shape[0]
    slots = send.shape[1]
    experts, lanes = prob_ref.shape
    tr = up(tok, 16)
    sibling = {"mp": 1 - mine}
    copies = []
    if own is not None:
        own[tr - 16 : tr, :] = jnp.zeros((16, D), BF)
        for c, (start, size) in enumerate(row_chunks(tr)):
            stop = min(start + size, tok)
            own[start:stop, :] = part_ref[start:stop, :].astype(BF)
            rows = pl.ds(start, size)
            copy = remote(own.at[rows, :], other.at[rows, :], hs.at[c], hr.at[c], sibling)
            copy.start()
            copies.append(copy)
    gains = jnp.transpose(small_ref[...].astype(F32))
    gain = gains[experts + 1 : experts + 2, :]
    bias = gains[experts + 2 : experts + 3, :]
    n2[lanes - 64 : lanes, 0:D] = jnp.zeros((64, D), BF)
    for c, (start, size) in enumerate(row_chunks(tr)):
        stop = min(start + size, tok)
        if own is None:
            both = part_ref[start:stop, :]
        else:
            copies[c].wait_recv()
            both = own[start:stop, :].astype(F32) + other[start:stop, :].astype(F32)
        hidden = tok_ref[start:stop, :].astype(F32) + both + bias
        hid_ref[start:stop, :] = hidden
        xhat, _ = norm_rows(hidden)
        n2[start:stop, 0:D] = (xhat * gain).astype(BF)
    logits = mm(gains[0:experts, :].astype(BF), n2[0:lanes, 0:D], 1, 1)
    raised = jnp.exp(logits - jnp.max(logits, axis=0, keepdims=True))
    probs = raised / jnp.sum(raised, axis=0, keepdims=True)
    prob_ref[...] = probs
    high, low = split_two(probs)
    p2[0:experts, :] = high
    p2[experts:, :] = low
    place = lax.broadcasted_iota(jnp.int32, (slots, slots), 0)
    number = lax.broadcasted_iota(jnp.int32, (2 * experts, slots), 0)

    def step(turn, carry):
        b = turn + 1 - 2 * (turn % 2)
        hot = [slot_matrix(idx_ref, partner(me, n, b * 4 + j) * slots, slots) for j in range(4)]
        block = mm(jnp.concatenate(hot, axis=0), n2[0:lanes, 0:D], 1, 0)
        for j in range(4):
            p = b * 4 + j
            peer = partner(me, n, p)
            gates = mm(p2[...], hot[j], 1, 1)
            row_high = jnp.sum(jnp.where(number == peer, gates, 0.0), axis=0, keepdims=True)
            row_low = jnp.sum(jnp.where(number == peer + experts, gates, 0.0), axis=0, keepdims=True)
            rows = block[j * slots : (j + 1) * slots, :]
            left = jnp.where(place == half, row_high, jnp.where(place == half + 1, row_low, rows[:, 0:slots]))
            send[p, :, :] = rows.astype(BF)
            send[p, :, 0:slots] = left.astype(BF)

            @pl.when((p != 0) & (p < early))
            def _():
                token_send(n, send, x_ref, xs, xr, p, peer).start()

        return carry

    lax.fori_loop(0, n // 4, step, 0)
    x_ref[0] = send[0]
    for copy in copies:
        copy.wait_send()


def dispatch_kernel(
    n, half, part_ref, tok_ref, small_ref, idx_ref, hid_ref, prob_ref, x_ref,
    n2, own, other, send, p2, hs, hr, xs, xr,
):
    me, mine = lax.axis_index("dp"), lax.axis_index("mp")
    plane = n // LINE
    greet([{"mp": 1 - mine}] + [{"dp": (me + d) % n} for d in range(1, n)])
    send_tokens(
        n, half, n, part_ref, tok_ref, small_ref, idx_ref, hid_ref, n2, prob_ref, x_ref,
        own, other, send, p2, hs, hr, xs, xr,
    )

    def finish(p, carry):
        @pl.when(p != 0)
        def _():
            token_send(n, send, x_ref, xs, xr, p, partner(me, n, p)).wait()

        return carry

    lax.fori_loop(0, n, finish, 0)


def dispatch(part, tok, small, idx, n, experts, half, slots):
    lanes = idx.shape[1]
    tr = up(tok.shape[0], 16)
    sem = pltpu.SemaphoreType.DMA
    vmem = pltpu.VMEM
    chunks = len(row_chunks(tr))
    return pl.pallas_call(
        functools.partial(dispatch_kernel, n, half),
        out_shape=(
            jax.ShapeDtypeStruct(tok.shape, F32),
            jax.ShapeDtypeStruct((experts, lanes), F32),
            jax.ShapeDtypeStruct((n, slots, D), BF),
        ),
        in_specs=[whole()] * 4,
        out_specs=(whole(),) * 3,
        scratch_shapes=[
            vmem((lanes, D), BF), vmem((tr, D), BF), vmem((tr, D), BF), vmem((n, slots, D), BF),
            vmem((2 * experts, lanes), BF),
            sem((chunks,)), sem((chunks,)), sem((n,)), sem((n,)),
        ],
        compiler_params=params(collective_id=1, has_side_effects=True),
        name="dispatch",
    )(part, tok, small, idx)


def expert_kernel(
    n, cap, half, fused,
    first, ct_ref, wi_own, wi_sib, wb_own, wb_sib, bi_own, bi_sib, bb_ref,
    idx_ref, seen_ref, tok_ct, small_ref,
    hg_ref, sg_ref, y_ref, gi_ref, gi_in, gb_ref, gb_in, little_ref, little_in, hid_out, prob_ref,
    wo_ref, qkv_out, att_out, soft_out,
    vi_own, vi_sib, vb_own, vb_sib, g_s, act_own, act_sib, dp_own, dp_sib, dx_s, back, acc, other,
    ct_s, y_s, stage, gp, gp_other, x_ref, send, p2, mine_w, mine_s, info, bias_s, bias_in, soft,
    lsem, ysem, gsem, ss, rs, hs, hr, ms, mr, xs, xr, es, er, zs, zr, ps, pr, cs, cr, bsem,
):
    me, mine = lax.axis_index("dp"), lax.axis_index("mp")
    sibling = {"mp": 1 - mine}
    slots = x_ref.shape[1]
    tok = tok_ct.shape[0]
    tr = up(tok, 16)
    experts = gp.shape[0]
    hidden = wi_own.shape[1]
    group = 4 * slots
    batches = n // 4
    early = n // 2 if fused else n
    lanes = gp.shape[1]
    owns = [(wi_own, vi_own), (wb_own, vb_own)]
    if not fused:
        owns += [(wi_sib, vi_sib), (wb_sib, vb_sib), (first, x_ref)]
    loads = [pltpu.make_async_copy(a, b, lsem.at[i]) for i, (a, b) in enumerate(owns)]
    for c in loads:
        c.start()
    if fused:
        halves = [
            remote(wi_own, vi_sib, ms.at[3], mr.at[3], sibling),
            remote(wb_own, vb_sib, ms.at[4], mr.at[4], sibling),
            remote(bias_s, bias_in, ms.at[5], mr.at[5], sibling),
        ]
        bias_s[...] = jnp.zeros_like(bias_s)
        bias_s[0:1, :] = bi_own[...].astype(F32)

        def started():
            for c in halves:
                c.start()

        arrived, ended = begin_part(
            n, cap, half, slots, [sibling], started, *first,
            wo_ref, small_ref, idx_ref, ct_ref, act_own, act_sib, hg_ref, soft_out,
            None, None, mine_w, mine_s, info, act_sib, D, dp_own, acc, stage, soft, (g_s, other, es, er),
            zs, zr, ps, pr, cs, cr, bsem,
        )
        rows = qkv_out.shape[0]
        kept = [
            pltpu.make_async_copy(act_own.at[pl.ds(0, rows), pl.ds(0, qkv_out.shape[1])], qkv_out, lsem.at[2]),
            pltpu.make_async_copy(act_sib.at[pl.ds(0, rows), pl.ds(0, att_out.shape[1])], att_out, lsem.at[3]),
        ]
        for c in kept:
            c.start()
        send_tokens(
            n, half, early, hg_ref, first[-1], small_ref, idx_ref, hg_ref, dp_sib, prob_ref, x_ref,
            None, None, send, p2, None, None, xs, xr,
        )
        keep = pltpu.make_async_copy(hg_ref, hid_out, lsem.at[5])
        keep.start()
        ended()
        for c in kept:
            c.wait()
        for c in halves:
            c.wait()
        bias_own, bias_sib = bi_own[...].astype(F32), bias_in[0:1, :]
    else:
        greet([sibling] + [{"dp": (me + d) % n} for d in range(1, n)])
        keep = pltpu.make_async_copy(hid_out, hg_ref, lsem.at[5])
        keep.start()
        bias_own, bias_sib = bi_own[...].astype(F32), bi_sib[...].astype(F32)
    little_ref[...] = jnp.zeros_like(little_ref)

    def ct_here(b, j):
        if fused:
            arrived(b * 4 + j)

    def cts(b, j):
        return pltpu.make_async_copy(ct_ref.at[b * 4 + j], ct_s.at[j], ysem.at[0, j])

    def ys(b, j):
        return pltpu.make_async_copy(y_s.at[j], y_ref.at[b * 4 + j], ysem.at[1, j])

    for j in range(4):
        ct_here(0, j)
        cts(0, j).start()
    for c in loads:
        c.wait()
    chunk = 768
    row = lax.broadcasted_iota(jnp.int32, (group, 16), 0)
    number = lax.broadcasted_iota(jnp.int32, (group, 16), 1)
    member = jnp.where(row // slots == number, 1.0, 0.0).astype(BF)
    spot = lax.broadcasted_iota(jnp.int32, (group, 128), 0) % slots
    here = spot == lax.broadcasted_iota(jnp.int32, (group, 128), 1)
    row_t = lax.broadcasted_iota(jnp.int32, (16, group), 1)
    number_t = lax.broadcasted_iota(jnp.int32, (16, group), 0)
    pick = jnp.where(
        (row_t == number_t * slots + half) | (row_t == number_t * slots + half + 1), 1.0, 0.0
    ).astype(BF)
    member_t = jnp.where(row_t // slots == number_t, 1.0, 0.0).astype(BF)
    puts = [jnp.where(row == number * slots + half + i, 1.0, 0.0).astype(BF) for i in range(2)]

    def batch(b, carry):
        at = pl.ds(pl.multiple_of(b * group, 16), group)
        if fused:
            @pl.when(b == batches // 4)
            def _():
                def more(p, carry):
                    token_send(n, send, x_ref, xs, xr, p, partner(me, n, p)).start()
                    return carry

                lax.fori_loop(early, n, more, 0)

            for j in range(4):
                p = b * 4 + j

                @pl.when(p != 0)
                def _():
                    token_send(n, send, x_ref, xs, xr, p, partner(me, n, p)).wait_recv()

        x = x_ref[pl.ds(b * 4, 4)].reshape(group, D)
        high, low = split_two(mm(pick, x[:, 0:128], 1, 0))
        wide = mm(member, high, 1, 0) + mm(member, low, 1, 0)
        gate = jnp.sum(jnp.where(here, wide, 0.0), axis=1, keepdims=True)
        for j in range(4):
            cts(b, j).wait()
        g_s[at, :] = (gate * ct_s[...].reshape(group, D).astype(F32)).astype(BF)
        little_ref[0:1, 2 * hidden :] += jnp.sum(g_s[at, :].astype(F32), axis=0, keepdims=True)
        for part, (vi, vb, bi, acts, dps) in enumerate(
            ((vi_own, vb_own, bias_own, act_own, dp_own), (vi_sib, vb_sib, bias_sib, act_sib, dp_sib))
        ):
            for c in range(hidden // chunk):
                cols = slice(c * chunk, (c + 1) * chunk)
                pre = mm(x_ref[pl.ds(b * 4, 4)].reshape(group, D), vi[:, cols], 1, 0) + bi[:, cols]
                phi = 0.5 * (1.0 + lax.erf(pre * (0.5**0.5)))
                slope = phi + pre * (jnp.exp(-0.5 * pre * pre) * ((2.0 * jnp.pi) ** -0.5))
                acts[at, cols] = (pre * phi).astype(BF)
                grad = (mm(g_s[at, :], vb[cols, :], 1, 1) * slope).astype(BF)
                dps[at, cols] = grad
                place = slice(part * hidden + c * chunk, part * hidden + (c + 1) * chunk)
                little_ref[0:1, place] += jnp.sum(grad.astype(F32), axis=0, keepdims=True)
        dx = mm(dp_own[at, :], vi_own[...], 1, 1) + mm(dp_sib[at, :], vi_sib[...], 1, 1)
        y = mm(act_own[at, :], vb_own[...], 1, 0) + mm(act_sib[at, :], vb_sib[...], 1, 0)
        y = (y + bb_ref[...].astype(F32)).astype(BF).astype(F32)
        dots = jnp.sum(ct_s[...].reshape(group, D).astype(F32) * y, axis=1, keepdims=True)
        high, low = split_two(jnp.where(here, dots, 0.0))
        high, low = mm(member_t, high, 1, 0).astype(BF), mm(member_t, low, 1, 0).astype(BF)
        left = dx[:, 0:128] + mm(puts[0], high, 1, 0) + mm(puts[1], low, 1, 0)
        dx = jnp.concatenate([left, dx[:, 128:]], axis=1)
        dx_s[pl.ds(b * 4, 4)] = dx.astype(BF).reshape(4, slots, D)
        for j in range(4):
            p = b * 4 + j

            @pl.when(p != 0)
            def _():
                remote(dx_s.at[p], back.at[p], ss.at[p], rs.at[p], {"dp": partner(me, n, p, -1)}).start()

        @pl.when(b > 0)
        def _():
            for j in range(4):
                ys(b - 1, j).wait()

        y_s[...] = (gate * y).astype(BF).reshape(4, slots, D)
        for j in range(4):
            ys(b, j).start()

        @pl.when(b + 1 < batches)
        def _():
            for j in range(4):
                ct_here(b + 1, j)
                cts(b + 1, j).start()

        return carry

    lax.fori_loop(0, batches, batch, 0)
    back[0] = dx_s[0]
    little = remote(little_ref, little_in, ms.at[2], mr.at[2], sibling)
    little.start()

    rows_all = n * slots
    steps = 3
    size = D // steps
    wide = hidden // 2
    swaps = []

    def out_i(r, c):
        return pltpu.make_async_copy(
            stage.at[r % 2 * 2 * size + c * size : r % 2 * 2 * size + (c + 1) * size, :],
            gi_ref.at[r * size : (r + 1) * size, c * wide : (c + 1) * wide], gsem.at[c, r],
        )

    def out_b(r):
        return pltpu.make_async_copy(
            stage.at[r % 2 * 2 * size : (r % 2 + 1) * 2 * size, :], gb_ref.at[r * 2 * size : (r + 1) * 2 * size, :], gsem.at[2, r]
        )

    for r in range(steps):
        at = slice(r * size, (r + 1) * size)
        left = x_ref[:, :, at].reshape(rows_all, size)
        vi_sib[at, :] = mm(left, dp_sib[...], 0, 0).astype(BF)
        for c in range(2):
            if r >= 2:
                out_i(r - 2, c).wait()
            at_s = r % 2 * 2 * size + c * size
            stage[at_s : at_s + size, :] = mm(left, dp_own[:, c * wide : (c + 1) * wide], 0, 0)
            out_i(r, c).start()
    copy = remote(vi_sib, gi_in, ms.at[0], mr.at[0], sibling)
    copy.start()
    swaps.append(copy)

    acc[...] = jnp.zeros_like(acc)
    gp[...] = jnp.zeros_like(gp)
    place = lax.broadcasted_iota(jnp.int32, (slots, 128), 0)
    count = lax.broadcasted_iota(jnp.int32, (experts, slots), 0)

    def combine(b, carry):
        hot = []
        for j in range(4):
            d = b * 4 + j
            source = partner(me, n, d)

            @pl.when(d != 0)
            def _():
                remote(dx_s.at[d], back.at[d], ss.at[d], rs.at[d], {"dp": source}).wait_recv()

            hot.append(slot_matrix(idx_ref, source * slots, slots))
            extra = back[d, :, 0:128].astype(F32)
            high = jnp.sum(jnp.where(place == half, extra, 0.0), axis=0, keepdims=True)[:, 0:slots]
            low = jnp.sum(jnp.where(place == half + 1, extra, 0.0), axis=0, keepdims=True)[:, 0:slots]
            for value in (high, low):
                gp[...] += mm(jnp.where(count == source, value, 0.0).astype(BF), hot[j], 1, 0)
        block = back[pl.ds(b * 4, 4)].reshape(group, D)
        acc[0:lanes, :] += mm(jnp.concatenate(hot, axis=0), block, 0, 0)
        return carry

    lax.fori_loop(0, batches // 2, combine, 0)
    for r in range(steps):
        at = slice(r * 2 * size, (r + 1) * 2 * size)
        vb_sib[at, :] = mm(act_sib[:, at], g_s[...], 0, 0).astype(BF)
        if r == 0:
            for c in range(2):
                out_i(1, c).wait()
                out_i(2, c).wait()
        if r >= 2:
            out_b(r - 2).wait()
        stage[r % 2 * 2 * size : (r % 2 + 1) * 2 * size, :] = mm(act_own[:, at], g_s[...], 0, 0)
        out_b(r).start()
    copy = remote(vb_sib, gb_in, ms.at[1], mr.at[1], sibling)
    copy.start()
    swaps.append(copy)
    lax.fori_loop(batches // 2, batches, combine, 0)

    little.wait()
    copies = []
    own = g_s
    own[tr - 16 : tr, :] = jnp.zeros((16, D), BF)
    for c, (start, length) in enumerate(row_chunks(tr)):
        stop = min(start + length, tok)
        own[start:stop, :] = acc[start:stop, :].astype(BF)
        rows = pl.ds(start, length)
        copy = remote(own.at[rows, :], other.at[rows, :], hs.at[c], hr.at[c], sibling)
        copy.start()
        copies.append(copy)
    copy = remote(gp, gp_other, hs.at[len(copies)], hr.at[len(copies)], sibling)
    copy.start()
    copy.wait()
    probs = prob_ref[...] if fused else seen_ref[...]
    grad_probs = gp[...] + gp_other[...]
    logits = (probs * (grad_probs - jnp.sum(grad_probs * probs, axis=0, keepdims=True))).astype(BF)
    gains = jnp.transpose(small_ref[...].astype(F32))
    gain = gains[experts + 1 : experts + 2, :]
    acc[0:lanes, :] = mm(logits, gains[0:experts, :].astype(BF), 0, 0)
    sg_ref[...] = jnp.zeros_like(sg_ref)
    gain_sum = jnp.zeros((1, D), F32)
    bias_sum = jnp.zeros((1, D), F32)
    act_own[lanes - 64 : lanes, 0:D] = jnp.zeros((64, D), BF)
    keep.wait()
    for c, (start, length) in enumerate(row_chunks(tr)):
        stop = min(start + length, tok)
        copies[c].wait_recv()
        grad = own[start:stop, :].astype(F32) + other[start:stop, :].astype(F32) + acc[start:stop, :]
        xhat, inverse = norm_rows(hg_ref[start:stop, :])
        act_own[start:stop, 0:D] = (xhat * gain).astype(BF)
        hidden_grad = tok_ct[start:stop, :].astype(F32) + norm_back(grad, gain, xhat, inverse)
        hg_ref[start:stop, :] = hidden_grad
        gain_sum += jnp.sum(grad * xhat, axis=0, keepdims=True)
        bias_sum += jnp.sum(hidden_grad, axis=0, keepdims=True)
    sg_ref[0:experts, :] = mm(logits, act_own[0:lanes, 0:D], 1, 0)
    sg_ref[experts : experts + 1, :] = gain_sum
    sg_ref[experts + 1 : experts + 2, :] = bias_sum
    for copy in copies:
        copy.wait_send()

    def finish(p, carry):
        @pl.when(p != 0)
        def _():
            remote(dx_s.at[p], back.at[p], ss.at[p], rs.at[p], {"dp": partner(me, n, p, -1)}).wait_send()
            if fused:
                token_send(n, send, x_ref, xs, xr, p, partner(me, n, p)).wait_send()

        return carry

    lax.fori_loop(0, n, finish, 0)
    for j in range(4):
        ys(batches - 1, j).wait()
    for r in range(1, steps):
        out_b(r).wait()
    for copy in swaps:
        copy.wait()


def expert(first, ct_rows, wi, wb, bi, bb, idx, probs, hid, ct, small, n, cap, half, slots):
    fused = hid is None
    rows = n * slots
    hidden = wi[0].shape[1]
    lanes = up(ct.shape[0], 128)
    experts = n
    tr = up(ct.shape[0], 16)
    chunks = len(row_chunks(tr))
    flat = ct.shape[0] // SEQ * SEQ_PAD
    shape = jax.ShapeDtypeStruct
    sem = pltpu.SemaphoreType.DMA
    vmem = pltpu.VMEM
    far = pl.BlockSpec(memory_space=pl.ANY)
    outs = [
        shape(ct.shape, F32), shape((up(experts + 3, 8), D), F32), shape((n, slots, D), BF),
        shape((D, hidden), F32), shape((D, hidden), BF),
        shape((hidden, D), F32), shape((hidden, D), BF),
        shape((8, 2 * hidden + D), F32), shape((8, 2 * hidden + D), F32),
    ]
    out_specs = [whole(), whole(), far, far, far, far, far, whole(), whole()]
    if fused:
        wq, wout, router_t, gains, rt, rank, tok = first
        shard, width = wout.shape
        plane = n // LINE
        ins = [wq, wout, router_t, *gains, rt, rank, ct, tok, wi[0], wb[0], bi[0], bb]
        in_specs = [whole()] * 10 + [far, far, whole(), whole()]
        outs += [
            shape(ct.shape, F32), shape((experts, lanes), F32), shape((4, D, width), BF), shape((D, 128), BF),
            shape((2, lanes), jnp.int32), shape((n, slots, D), BF),
            shape((flat, 3 * width), BF), shape((flat, width), BF),
            shape((flat // SEQ_PAD, width // HD, SEQ_PAD, SEQ_PAD), F32),
        ]
        out_specs += [far, whole(), whole(), whole(), whole(), far, far, far, far]

        def kernel(*refs):
            wq, wout, rows_t, g1, g2, g3, rt, rank, ct, tok, wi, wb, bi, bb = refs[:14]
            main, (hid, prob, wo, so, idx, ctx, qkv, att, soft) = refs[14:23], refs[23:32]
            expert_kernel(
                n, cap, half, True, (wq, wout, rows_t, (g1, g2, g3), rt, rank, ct, tok),
                ctx, wi, None, wb, None, bi, None, bb, idx, None, ct, so,
                *main, hid, prob, wo, qkv, att, soft, *refs[32:],
            )

        spare = [vmem((4, shard, width), BF), vmem((shard, 128), BF), vmem((8, lanes), jnp.int32)]
        spare += [vmem((8, hidden), F32)] * 2 + [vmem((2, width // HD, SEQ_PAD, SEQ_PAD), F32)]
        grid = (plane - 1, LINE, 2)
        send_rows = (n, slots, D)
    else:
        ins = [first, ct_rows, wi[0], wi[1], wb[0], wb[1], bi[0], bi[1], bb, idx, probs, ct, small, hid]
        in_specs = [far] * 6 + [whole()] * 7 + [far]

        def kernel(*refs):
            ins, hid_ref, outs, rest = refs[:13], refs[13], refs[14:23], refs[23:]
            expert_kernel(n, cap, half, False, *ins, *outs, hid_ref, ins[10], None, None, None, None, *rest)

        spare = [vmem((1, 16, 128), BF), vmem((16, 128), BF), vmem((8, 128), jnp.int32)]
        spare += [vmem((8, 128), F32)] * 3
        grid = (1, 1, 2)
        send_rows = (1, 16, 128)

    return pl.pallas_call(
        kernel,
        out_shape=tuple(outs),
        in_specs=in_specs,
        out_specs=tuple(out_specs),
        scratch_shapes=[
            vmem((D, hidden), BF), vmem((D, hidden), BF), vmem((hidden, D), BF), vmem((hidden, D), BF),
            vmem((rows, D), BF),
            vmem((rows, hidden), BF), vmem((rows, hidden), BF),
            vmem((rows, hidden), BF), vmem((rows, hidden), BF),
            vmem((n, slots, D), BF), vmem((n, slots, D), BF),
            vmem((flat if fused else lanes, D), F32), vmem((flat if fused else tr, D), BF),
            vmem((4, slots, D), BF), vmem((4, slots, D), BF),
            vmem((flat if fused else 1024, D), F32),
            vmem((experts, lanes), F32), vmem((experts, lanes), F32),
            vmem((n, slots, D), BF), vmem(send_rows, BF), vmem((2 * experts, lanes), BF),
            *spare,
            sem((6,)), sem((2, 4)), sem((3, 3)), sem((n,)), sem((n,)),
            sem((chunks + 1,)), sem((chunks + 1,)), sem((6,)), sem((6,)),
            sem((n,)), sem((n,)), sem((flat // SEQ_PAD,)), sem((flat // SEQ_PAD,)),
            sem((LINE - 1, 2)), sem((LINE - 1, 2)), sem(grid), sem(grid), sem((n,)), sem((n,)), sem((3,)),
        ],
        compiler_params=params(collective_id=2, has_side_effects=True),
        name="expert",
    )(*ins)


def join_kernel(
    gi_ref, gi_in, gb_ref, gb_in, little_ref, little_in, gw_ref, gs_ref,
    gi_out, gb_out, gbi_out, gbb_out, gq_out, go_out, gr_out, g1_out, g2_out, g3_out,
):
    gi_out[...] = gi_ref[...] + gi_in[...].astype(F32)
    gb_out[...] = gb_ref[...] + gb_in[...].astype(F32)

    @pl.when(pl.program_id(0) == 0)
    def _():
        hidden = gbi_out.shape[1]
        shard = go_out.shape[0]
        experts = gr_out.shape[0]
        gbi_out[...] = little_ref[0:1, 0:hidden] + little_in[0:1, hidden : 2 * hidden]
        gbb_out[...] = little_ref[0:1, 2 * hidden :] + little_in[0:1, 2 * hidden :]
        gq_out[...] = gw_ref[0:3, 0:shard, :]
        go_out[...] = gw_ref[3, 0:shard, :]
        turned = jnp.transpose(gs_ref[...])
        gr_out[...] = turned[0:experts, 0:shard]
        for k, out in enumerate((g2_out, g3_out, g1_out)):
            out[...] = turned[experts + k : experts + k + 1, 0:shard]


def join(gi, gi_in, gb, gb_in, little, little_in, gw, gs, shard, experts):
    steps = 6
    width = gw.shape[2]
    hidden = gi.shape[1]
    line_i = pl.BlockSpec((gi.shape[0] // steps, hidden), lambda k: (k, 0))
    line_b = pl.BlockSpec((hidden // steps, D), lambda k: (k, 0))
    shape = jax.ShapeDtypeStruct
    return pl.pallas_call(
        join_kernel,
        grid=(steps,),
        out_shape=(shape(gi.shape, F32), shape(gb.shape, F32), shape((1, hidden), F32), shape((1, D), F32),
                   shape((3, shard, width), F32), shape((shard, width), F32), shape((experts, shard), F32),
                   *[shape((1, shard), F32)] * 3),
        in_specs=[line_i, line_i, line_b, line_b] + [whole()] * 4,
        out_specs=(line_i, line_b) + (whole(),) * 8,
        compiler_params=params(dimension_semantics=("arbitrary",)),
        name="join",
    )(gi, gi_in, gb, gb_in, little, little_in, gw, gs)


def end_kernel(
    n, experts, shard,
    hg_ref, tok_ref, w_ref, qkv_ref, att_ref, soft_ref, y_ref, hid_ref, small_ref, idx_ref, sg_ref,
    tg_ref, out_ref, gw_ref, gs_ref,
    hg_s, tok_s, w_s, qkv_s, att_s, hid_s, normed, low, dqkv, pp, flat, dn, other, mix, mix_other,
    y_s, acc, soft, dw, r1, s1, r2, sm, q1, t1, q2,
    lsem, us, ur, hs, hr, as_, ar, bs, br,
):
    me, mine = lax.axis_index("dp"), lax.axis_index("mp")
    plane = n // LINE
    z, q = me // plane, me % plane
    tok = tok_s.shape[0]
    images = tok // SEQ
    width = w_s.shape[2]
    rp = dw.shape[3]
    tr = other.shape[0]
    slots = y_s.shape[1]
    scale = HD ** (-0.5)
    sibling = {"mp": 1 - mine}
    zpeer = [((z + d) % LINE) * plane + q for d in range(1, LINE)]
    qpeer = [z * plane + (q + d) % plane for d in range(1, plane)]
    loads = [
        pltpu.make_async_copy(a, b, lsem.at[i])
        for i, (a, b) in enumerate(
            ((hg_ref, hg_s), (tok_ref, tok_s), (w_ref, w_s), (qkv_ref, qkv_s), (att_ref, att_s), (hid_ref, hid_s),
             (y_ref.at[0], y_s.at[0]))
        )
    ]
    for c in loads:
        c.start()
    greet([sibling] + [{"dp": (me + d) % n} for d in range(1, n)])

    def y_copy(p, sign):
        return remote(y_ref.at[p], y_s.at[p], us.at[p], ur.at[p], {"dp": partner(me, n, p, sign)})

    def y_start(p, carry):
        y_copy(p, -1).start()
        return carry

    quarter = n // 4
    lax.fori_loop(quarter, 2 * quarter, y_start, 0)
    lax.fori_loop(3 * quarter, n, y_start, 0)
    lax.fori_loop(1, quarter, y_start, 0)
    lax.fori_loop(2 * quarter, 3 * quarter, y_start, 0)
    loads[0].wait()
    for i in range(images):
        pp[(i + 1) * SEQ_PAD - 16 : (i + 1) * SEQ_PAD, :] = jnp.zeros((16, D), F32)
        pp[i * SEQ_PAD : i * SEQ_PAD + SEQ, :] = hg_s[i * SEQ : (i + 1) * SEQ, :]
    low[...] = pp[...].astype(BF)
    loads[1].wait()
    for i in range(images):
        pp[i * SEQ_PAD : i * SEQ_PAD + SEQ, :] = tok_s[i * SEQ : (i + 1) * SEQ, :].astype(F32)
    for c in loads[2:5]:
        c.wait()

    def spread(value):
        value = value.astype(BF)
        if rp > shard:
            line = lax.broadcasted_iota(jnp.int32, (n * rp, D), 0)
            where = lax.broadcasted_iota(jnp.int32, (n * rp, D), 1)
            fits = (where == line // rp * shard + line % rp) & (line % rp < shard)
            value = mm(jnp.where(fits, 1.0, 0.0).astype(BF), value, 1, 0).astype(BF)
        return value.reshape(LINE, plane, rp, width)

    sends = []

    def plane_send(k, a, b):
        for d, p in enumerate(qpeer):
            to = (q + d + 1) % plane
            c = remote(a(to), b(d), as_.at[d, k], ar.at[d, k], {"dp": p})
            c.start()
            sends.append(c)

    def line_send(k, a, b):
        for d, p in enumerate(zpeer):
            c = remote(a((z + d + 1) % LINE), b(d), bs.at[d, k], br.at[d, k], {"dp": p})
            c.start()
            sends.append(c)

    def settle(part, k):
        for d in range(plane - 1):
            remote(dw.at[part, :, 0], r1.at[d, part], as_.at[d, k], ar.at[d, k], {"dp": qpeer[0]}).wait_recv()
        for b in range(LINE):
            value = dw[part, b, q].astype(F32)
            for d in range(plane - 1):
                value += r1[d, part, b].astype(F32)
            s1[part, b] = value.astype(BF)
        line_send(part, lambda to: s1.at[part, to], lambda d: r2.at[d, part])

    dw[3] = spread(mm(low[...], att_s[...], 0, 0))
    plane_send(0, lambda to: dw.at[3, :, to], lambda d: r1.at[d, 3])
    gains = jnp.transpose(small_ref[...].astype(F32))
    gain = gains[experts : experts + 1, :]
    lane = lax.broadcasted_iota(jnp.int32, (1, 2 * HD), 1)
    masks = [jnp.where(lane // HD == h, 1.0, 0.0).astype(BF) for h in range(2)]

    def fetch(i):
        return pltpu.make_async_copy(soft_ref.at[i], soft.at[i % 2], lsem.at[7 + i % 2])

    fetch(0).start()

    def image(i, carry):
        rows = pl.ds(pl.multiple_of(i * SEQ_PAD, 16), SEQ_PAD)
        fetch(i).wait()

        @pl.when(i + 1 < images)
        def _():
            fetch(i + 1).start()

        xhat, _ = norm_rows(pp[rows, :])
        normed[rows, :] = (xhat * gain).astype(BF)
        grad_att = mm(low[rows, :], w_s[3], 1, 0).astype(BF)
        for p in range(width // (2 * HD)):
            cols = [slice(c * width + p * 2 * HD, c * width + (p + 1) * 2 * HD) for c in range(3)]
            qs, ks, vs = (qkv_s[rows, c] for c in cols)
            pair = grad_att[:, p * 2 * HD : (p + 1) * 2 * HD]
            grads = []
            for h in range(2):
                weights = soft[i % 2, 2 * p + h]
                product = mm(pair * masks[h], vs, 1, 1) * weights
                grad_scores = product - weights * jnp.sum(product, axis=-1, keepdims=True)
                scores_low = grad_scores.astype(BF)
                grads.append((
                    mm(scores_low, ks, 1, 0) * scale,
                    mm(scores_low, qs, 0, 0) * scale,
                    mm(weights.astype(BF), pair, 0, 0),
                ))
            for c in range(3):
                dqkv[rows, cols[c]] = jnp.where(lane < HD, grads[0][c], grads[1][c]).astype(BF)
        total = mm(dqkv[rows, 0:width], w_s[0], 1, 1)
        for c in range(1, 3):
            total += mm(dqkv[rows, c * width : (c + 1) * width], w_s[c], 1, 1)
        pp[rows, :] = total
        return carry

    lax.fori_loop(0, images, image, 0)
    for c in range(3):
        dw[c] = spread(mm(normed[...], dqkv[:, c * width : (c + 1) * width], 0, 0))
        plane_send(1 + c, lambda to: dw.at[c, :, to], lambda d: r1.at[d, c])
    for i in range(images):
        flat[i * SEQ : (i + 1) * SEQ, :] = pp[i * SEQ_PAD : i * SEQ_PAD + SEQ, :]
    dn[tr - 16 : tr, :] = jnp.zeros((16, D), BF)
    copies = []
    for c, (start, size) in enumerate(row_chunks(tr)):
        stop = min(start + size, tok)
        dn[start:stop, :] = flat[start:stop, :].astype(BF)
        rows = pl.ds(start, size)
        copy = remote(dn.at[rows, :], other.at[rows, :], hs.at[c], hr.at[c], sibling)
        copy.start()
        copies.append(copy)
    settle(3, 0)
    gain_sum = jnp.zeros((1, D), F32)
    for c, (start, size) in enumerate(row_chunks(tr)):
        stop = min(start + size, tok)
        copies[c].wait()
        grad = dn[start:stop, :].astype(F32) + other[start:stop, :].astype(F32)
        xhat, inverse = norm_rows(tok_s[start:stop, :].astype(F32))
        tg_ref[start:stop, :] = (hg_s[start:stop, :] + norm_back(grad, gain, xhat, inverse)).astype(BF)
        gain_sum += jnp.sum(grad * xhat, axis=0, keepdims=True)
    settle(0, 1)
    row = lax.broadcasted_iota(jnp.int32, sg_ref.shape, 0)
    rows = jnp.where(row == experts + 2, gain_sum, sg_ref[...])
    rows = jnp.concatenate([rows, jnp.zeros((128 - rows.shape[0], D), F32)], axis=0)
    turned = jnp.transpose(rows).astype(BF)
    for b in range(n):
        at = (b // plane, b % plane)
        if shard < rp:
            sm[at[0], at[1]] = jnp.zeros((rp, 128), BF)
        sm[at[0], at[1], 0:shard, :] = turned[b * shard : (b + 1) * shard, :]
    plane_send(4, lambda to: sm.at[:, to], lambda d: q1.at[d])
    settle(1, 2)
    acc[...] = jnp.zeros_like(acc)
    loads[6].wait()

    def step(b, carry):
        for j in range(4):
            p = b * 4 + j

            @pl.when(p != 0)
            def _():
                y_copy(p, 1).wait_recv()

        hot = jnp.concatenate(
            [slot_matrix(idx_ref, partner(me, n, b * 4 + j) * slots, slots) for j in range(4)], axis=0
        )
        acc[...] += mm(hot, y_s[pl.ds(b * 4, 4)].reshape(4 * slots, D), 0, 0)
        return carry

    lax.fori_loop(0, n // 4, step, 0)
    mix[tr - 16 : tr, :] = jnp.zeros((16, D), BF)
    base = len(copies)
    late = []
    for c, (start, size) in enumerate(row_chunks(tr)):
        stop = min(start + size, tok)
        mix[start:stop, :] = acc[start:stop, :].astype(BF)
        rows = pl.ds(start, size)
        copy = remote(mix.at[rows, :], mix_other.at[rows, :], hs.at[base + c], hr.at[base + c], sibling)
        copy.start()
        late.append(copy)
    settle(2, 3)
    for d in range(plane - 1):
        remote(sm.at[:, 0], q1.at[d], as_.at[d, 4], ar.at[d, 4], {"dp": qpeer[0]}).wait_recv()
    for b in range(LINE):
        little = sm[b, q].astype(F32)
        for d in range(plane - 1):
            little += q1[d, b].astype(F32)
        t1[b] = little.astype(BF)
    line_send(4, lambda to: t1.at[to], lambda d: q2.at[d])
    loads[5].wait()
    for c, (start, size) in enumerate(row_chunks(tr)):
        stop = min(start + size, tok)
        late[c].wait()
        both = mix[start:stop, :].astype(F32) + mix_other[start:stop, :].astype(F32)
        out_ref[start:stop, :] = (hid_s[start:stop, :] + both).astype(BF)
    for part in (3, 0, 1, 2):
        value = s1[part, z].astype(F32)
        for d in range(LINE - 1):
            remote(s1.at[0, 0], r2.at[d, part], bs.at[d, part], br.at[d, part], {"dp": zpeer[0]}).wait_recv()
            value += r2[d, part].astype(F32)
        gw_ref[part] = value
    little = t1[z].astype(F32)
    for d in range(LINE - 1):
        remote(t1.at[0], q2.at[d], bs.at[d, 4], br.at[d, 4], {"dp": zpeer[0]}).wait_recv()
        little += q2[d].astype(F32)
    gs_ref[...] = little
    for c in sends:
        c.wait_send()

    def y_end(p, carry):
        y_copy(p, -1).wait_send()
        return carry

    lax.fori_loop(1, n, y_end, 0)


def end(hg, tok, w, qkv, att, soft, y, hid, small, idx, sg, n, experts):
    parts, _, width = w.shape
    shard = D // n
    rp = up(shard, 16)
    plane = n // LINE
    tr = up(tok.shape[0], 16)
    chunks = len(row_chunks(tr))
    rows = qkv.shape[0]
    sem = pltpu.SemaphoreType.DMA
    vmem = pltpu.VMEM
    shape = jax.ShapeDtypeStruct
    far = pl.BlockSpec(memory_space=pl.ANY)
    return pl.pallas_call(
        functools.partial(end_kernel, n, experts, shard),
        out_shape=(
            shape(tok.shape, BF), shape(tok.shape, BF), shape((parts, rp, width), F32), shape((rp, 128), F32),
        ),
        in_specs=[far] * 8 + [whole()] * 3,
        out_specs=(whole(),) * 4,
        scratch_shapes=[
            vmem(tok.shape, F32), vmem(tok.shape, BF), vmem(w.shape, BF), vmem(qkv.shape, BF), vmem(att.shape, BF),
            vmem(tok.shape, F32),
            vmem((rows, D), BF), vmem((rows, D), BF), vmem(qkv.shape, BF), vmem((rows, D), F32), vmem((tr, D), F32),
            vmem((tr, D), BF), vmem((tr, D), BF), vmem((tr, D), BF), vmem((tr, D), BF),
            vmem(y.shape, BF), vmem((idx.shape[1], D), F32),
            vmem((2,) + soft.shape[1:], F32),
            vmem((parts, LINE, plane, rp, width), BF),
            vmem((plane - 1, parts, LINE, rp, width), BF),
            vmem((parts, LINE, rp, width), BF),
            vmem((LINE - 1, parts, rp, width), BF),
            vmem((LINE, plane, rp, 128), BF),
            vmem((plane - 1, LINE, rp, 128), BF),
            vmem((LINE, rp, 128), BF),
            vmem((LINE - 1, rp, 128), BF),
            sem((9,)), sem((n,)), sem((n,)), sem((2 * chunks,)), sem((2 * chunks,)),
            sem((plane - 1, 5)), sem((plane - 1, 5)), sem((LINE - 1, 5)), sem((LINE - 1, 5)),
        ],
        compiler_params=params(collective_id=3, has_side_effects=True),
        name="end",
    )(hg, tok, w, qkv, att, soft, y, hid, small, idx, sg)


def body(
    tokens, ln1_gain, w_qkv, w_out, out_bias, ln2_gain, router, w_in, in_bias,
    w_back, back_bias, routes, priority, cotangent,
):
    n = lax.axis_size("dp")
    tok = tokens.shape[0]
    experts = router.shape[1]
    cap = max(2, 5 * tok // (2 * experts))
    half = (cap + 1) // 2
    slots = up(half + FREE, 16)
    shard, width = w_qkv.shape[0], w_qkv.shape[2]
    rp = up(shard, 16)
    swap = [(0, 1), (1, 0)]

    start = (
        jnp.swapaxes(w_qkv, 0, 1), w_out.T, router.T,
        (ln1_gain[None], ln2_gain[None], out_bias[None]), routes.T, priority,
    )
    if n * slots <= 1536:
        (hg, sg, y, gi, gi_in, gb, gb_in, little, little_in, hid, _, weights, small, idx, _, qkv, att, soft) = expert(
            (*start, tokens), None, (w_in[0],), (w_back[0],), (in_bias,), back_bias, None, None, None,
            cotangent, None, n, cap, half, slots,
        )
    else:
        wi = (w_in[0], lax.ppermute(w_in[0], "mp", swap))
        wb = (w_back[0], lax.ppermute(w_back[0], "mp", swap))
        bi = (in_bias, lax.ppermute(in_bias, "mp", swap))
        weights, small, idx, ct_rows, qkv, att, part, soft = begin(
            *start, cotangent, tokens, n, experts, cap, half, slots
        )
        hid, probs, x = dispatch(part, tokens, small, idx, n, experts, half, slots)
        hg, sg, y, gi, gi_in, gb, gb_in, little, little_in = expert(
            x, ct_rows, wi, wb, bi, back_bias, idx, probs, hid, cotangent, small, n, cap, half, slots
        )
    tg, out, gw, gs = end(hg, tokens, weights, qkv, att, soft, y, hid, small, idx, sg, n, experts)
    gi, gb, gbi, gbb, gq, go, gr, g1, g2, g3 = join(gi, gi_in, gb, gb_in, little, little_in, gw, gs, shard, experts)
    return (
        out,
        tg,
        g1[0],
        jnp.swapaxes(gq, 0, 1),
        go.T,
        g3[0],
        g2[0],
        gr.T,
        gi[None],
        gbi,
        gb[None],
        gbb,
    )


def solution(mesh):
    return jax.shard_map(
        body,
        mesh=mesh,
        in_specs=(
            P("dp", None),
            P("dp"),
            P("dp", None, "mp"),
            P("mp", "dp"),
            P("dp"),
            P("dp"),
            P("dp", None),
            P("dp", None, "mp"),
            P("dp", "mp"),
            P("dp", "mp", None),
            P("dp", None),
            P("dp", None),
            P("dp", None),
            P("dp", None),
        ),
        out_specs=(
            P("dp", None),
            P("dp", None),
            P("dp"),
            P("dp", None, "mp"),
            P("mp", "dp"),
            P("dp"),
            P("dp"),
            P("dp", None),
            P("dp", None, "mp"),
            P("dp", "mp"),
            P("dp", "mp", None),
            P("dp", None),
        ),
        check_vma=False,
    )
```
